32 devices in a mesh: seq: 8 (over z, x), rep: 4 (over y, core).
Axes of the slice: x: 2, y: 2, z: 4, core: 2. Of those that a mesh axis runs over, the one named last changes fastest.
Arguments:
- tokens: bfloat16 [4, 2048, 768], P('rep', 'seq'), may hold values from -6 to 6
- segments: int32 [4, 2048], P('rep', 'seq'), may hold values from 0 to 7, never falling along the last dimension, each value on 1 to 512 neighbouring positions
- orders: int32 [4, 12, 2048], P('rep'), may hold values from 0 to 2047, as said below
- owners: int32 [4, 12, 16], P('rep'), may hold values from 0 to 7, as said below
- query_weight: bfloat16 [768, 768], replicated, may hold values from -0.21875 to 0.21875
- query_bias: bfloat16 [768], replicated, may hold values from -3 to 3
- key_weight: bfloat16 [768, 768], replicated, may hold values from -0.21875 to 0.21875
- value_weight: bfloat16 [768, 768], replicated, may hold values from -0.21875 to 0.21875
- value_bias: bfloat16 [768], replicated, may hold values from -3 to 3
- out_weight: bfloat16 [768, 768], replicated, may hold values from -0.875 to 0.875
- out_bias: bfloat16 [768], replicated, may hold values from -3 to 3
- first_gain: bfloat16 [768], replicated, may hold values from 0.5 to 1.5
- first_shift: bfloat16 [768], replicated, may hold values from -3 to 3
- inner_weight: bfloat16 [768, 3072], replicated, may hold values from -0.21875 to 0.21875
- inner_bias: bfloat16 [3072], replicated, may hold values from -3 to 3
- outer_weight: bfloat16 [3072, 768], replicated, may hold values from -0.109375 to 0.109375
- outer_bias: bfloat16 [768], replicated, may hold values from -3 to 3
- second_gain: bfloat16 [768], replicated, may hold values from 0.5 to 1.5
- second_shift: bfloat16 [768], replicated, may hold values from -3 to 3
- cotangent: bfloat16 [4, 2048, 768], P('rep', 'seq'), may hold values from -6 to 6
Outputs:
- output: bfloat16 [4, 2048, 768], P('rep', 'seq')
- gradient_tokens: bfloat16 [4, 2048, 768], P('rep', 'seq')
- gradient_query_weight: float32 [768, 768], P('seq')
- gradient_query_bias: float32 [768], P('seq')
- gradient_key_weight: float32 [768, 768], P('seq')
- gradient_value_weight: float32 [768, 768], P('seq')
- gradient_value_bias: float32 [768], P('seq')
- gradient_out_weight: float32 [768, 768], P('seq')
- gradient_out_bias: float32 [768], P('seq')
- gradient_first_gain: float32 [768], P('seq')
- gradient_first_shift: float32 [768], P('seq')
- gradient_inner_weight: float32 [768, 3072], P('seq')
- gradient_inner_bias: float32 [3072], P('seq')
- gradient_outer_weight: float32 [3072, 768], P('seq')
- gradient_outer_bias: float32 [768], P('seq')
- gradient_second_gain: float32 [768], P('seq')
- gradient_second_shift: float32 [768], P('seq')
- cluster_stats: float32 [2, 12, 8], replicated
The draws below stay inside these ranges and needn't reach their ends.
Inputs may be any that keep to these rules, and one draw needn't show every extreme that they name: `orders`: for each group and head, a permutation of the group's 2048 positions. For every head, the 256 tokens in the clusters that owners gives to one device hold exactly 32 tokens of each device's block of 256 tokens. `owners`: for each group and head, every device owns exactly 2 of the 16 clusters.
All inputs are finite; a program needn't handle non-finite values.
Results may differ from the reference program's by a relative error of at most 0.015.
Values may be sent and summed in bfloat16 or wider, within the bound.
A program may use at most 192 MiB of HBM per device.

```python
import math
import jax
import jax.numpy as jnp
import numpy as np
from jax import lax

D = 768
H = 12
HD = 64
FF = 3072
TOK_DEV = 256
CLUSTER = 128
GROUPS = 4
SEQ_DEVS = 8
TOKENS = 2048
CLUSTERS = 16
PER_OWNER = 2
SHARE = 32


def route_tables(key):

    def one_head(head_key):
        head_keys = jax.random.split(head_key, 5)
        shuffled = jax.vmap(lambda subkey: jax.random.permutation(subkey, TOK_DEV))(jax.random.split(head_keys[0], SEQ_DEVS)).astype(jnp.int32)
        tokens_of = shuffled + (jnp.arange(SEQ_DEVS, dtype=jnp.int32) * TOK_DEV)[:, None]
        pieces = tokens_of.reshape(SEQ_DEVS, SEQ_DEVS, SHARE)
        first_shift = jax.random.permutation(head_keys[1], SEQ_DEVS).astype(jnp.int32)
        second_shift = jax.random.permutation(head_keys[2], SEQ_DEVS).astype(jnp.int32)
        chosen = (first_shift[:, None] + second_shift[None, :]) % SEQ_DEVS
        sources = jnp.broadcast_to(jnp.arange(SEQ_DEVS, dtype=jnp.int32)[None, :], chosen.shape)
        owned_rows = pieces[sources, chosen].reshape(SEQ_DEVS, TOK_DEV)
        mixed_rows = jax.vmap(lambda subkey, member: member[jax.random.permutation(subkey, TOK_DEV)])(jax.random.split(head_keys[3], SEQ_DEVS), owned_rows)
        placing = jax.random.permutation(head_keys[4], CLUSTERS).astype(jnp.int32)
        owner_of = jnp.zeros((CLUSTERS,), jnp.int32).at[placing].set(jnp.arange(CLUSTERS, dtype=jnp.int32) // PER_OWNER)
        slot_index = (placing[:, None] * CLUSTER + jnp.arange(CLUSTER, dtype=jnp.int32)[None, :]).reshape(-1)
        order_of = jnp.zeros((TOKENS,), jnp.int32).at[slot_index].set(mixed_rows.reshape(-1))
        return (order_of, owner_of)
    all_keys = jax.random.split(key, GROUPS * H)
    order_tables, owner_tables = jax.vmap(one_head)(all_keys)
    return (order_tables.reshape(GROUPS, H, TOKENS), owner_tables.reshape(GROUPS, H, CLUSTERS))


def draw_orders(key, part):
    tables = route_tables(key)
    return tables[0]


def draw_owners(key, part):
    tables = route_tables(key)
    return tables[1]


def levels(stream_key, dims, cuts, low, high):
    loudness, own = 1.0, jax.random.fold_in(stream_key, 6)
    for dim, parts in cuts:
        draws = jnp.exp(jax.random.uniform(jax.random.fold_in(own, dim), (parts,), jnp.float32, low / len(cuts), high / len(cuts)))
        loudness = loudness * jnp.repeat(draws, dims[dim] // parts).reshape([-1 if axis == dim else 1 for axis in range(len(dims))])
    return loudness


def profile(number_of, total, bound, skew):
    weights = [(1 << 20) // math.isqrt(grade ** skew) + 1 for grade in range(2, number_of + 1)]
    rest, given = total - bound - (number_of - 1), [1] * (number_of - 1)
    while rest > 0:
        candidates = [i for i in range(number_of - 1) if given[i] < bound]
        whole, budget = sum([weights[i] for i in candidates]), rest
        for i in candidates:
            more = min(bound - given[i], max(1, budget * weights[i] // whole), rest)
            given[i] = given[i] + more
            rest = rest - more
    return np.array([bound] + given)


def ragged(stream_key, count, total, reach, skew):
    if count == 2:
        one = jax.random.randint(stream_key, (), max(1, total - reach), min(reach, total - 1) + 1)
        return jnp.stack([one, total - one])
    lengths = jnp.asarray(profile(count, total, reach, skew), jnp.int32)
    twos = (count - 1) // 2
    source_of, receiver = lengths[1:1 + 2 * twos:2], lengths[2:2 + 2 * twos:2]
    slack = jnp.minimum(source_of - 1, reach - receiver)
    passed = jax.random.randint(jax.random.fold_in(stream_key, 1), (twos,), 0, 1 << 20) % (slack + 1)
    lengths = lengths.at[1:1 + 2 * twos:2].set(source_of - passed).at[2:2 + 2 * twos:2].set(receiver + passed)
    return lengths[jax.random.permutation(jax.random.fold_in(stream_key, 2), count)]


def scatter_about(rng, extent, scale, most, cuts=(), kind=jnp.bfloat16):
    factor_of = levels(rng, extent, cuts, -0.22, 0.18) if cuts else 1.0
    values = jax.random.normal(rng, extent, jnp.float32) * scale * factor_of
    return jnp.minimum(jnp.maximum(values, -most), most).astype(kind)


def setup_inputs(seed: int = 0) -> dict:
    seeds = jax.random.split(jax.random.key(seed), 21)
    tokens = scatter_about(seeds[0], (GROUPS, TOKENS, D), 1.0, 6.0, ((0, 4), (1, 8)))
    segments = jax.vmap(lambda own: jnp.searchsorted(jnp.cumsum(ragged(own, 8, TOKENS, TOKENS // 4, 2)), jnp.arange(TOKENS), side="right"))(jax.random.split(seeds[1], GROUPS)).reshape((GROUPS, TOKENS)).astype(jnp.int32)
    orders = draw_orders(jax.random.fold_in(seeds[20], 71), 0)
    owners = draw_owners(jax.random.fold_in(seeds[20], 71), 0)
    query_weight = scatter_about(seeds[4], (D, D), D ** -0.5, 0.21875)
    query_bias = scatter_about(seeds[5], (D,), 0.5, 3.0)
    key_weight = scatter_about(seeds[6], (D, D), D ** -0.5, 0.21875)
    value_weight = scatter_about(seeds[7], (D, D), D ** -0.5, 0.21875)
    value_bias = scatter_about(seeds[8], (D,), 0.5, 3.0)
    out_weight = scatter_about(seeds[9], (D, D), (D // 16) ** -0.5, 0.875)
    out_bias = scatter_about(seeds[10], (D,), 0.5, 3.0)
    first_gain = jnp.clip(1.0 + 0.1 * jax.random.normal(seeds[11], (D,), jnp.float32), 0.5, 1.5).astype(jnp.bfloat16)
    first_shift = scatter_about(seeds[12], (D,), 0.5, 3.0)
    inner_weight = scatter_about(seeds[13], (D, FF), D ** -0.5, 0.21875)
    inner_bias = scatter_about(seeds[14], (FF,), 0.5, 3.0)
    outer_weight = scatter_about(seeds[15], (FF, D), FF ** -0.5, 0.109375)
    outer_bias = scatter_about(seeds[16], (D,), 0.5, 3.0)
    second_gain = jnp.clip(1.0 + 0.1 * jax.random.normal(seeds[17], (D,), jnp.float32), 0.5, 1.5).astype(jnp.bfloat16)
    second_shift = scatter_about(seeds[18], (D,), 0.5, 3.0)
    cotangent = scatter_about(seeds[19], (GROUPS, TOKENS, D), 1.0, 6.0, ((0, 4), (1, 8)))
    return dict(tokens=tokens, segments=segments, orders=orders, owners=owners, query_weight=query_weight, query_bias=query_bias, key_weight=key_weight, value_weight=value_weight, value_bias=value_bias, out_weight=out_weight, out_bias=out_bias, first_gain=first_gain, first_shift=first_shift, inner_weight=inner_weight, inner_bias=inner_bias, outer_weight=outer_weight, outer_bias=outer_bias, second_gain=second_gain, second_shift=second_shift, cotangent=cotangent)


EPSILON = 1e-12
NEGATIVE = -1e+30
HIGHEST_PRECISION = lax.Precision.HIGHEST

@jax.custom_vjp
def low(v):
    return lax.optimization_barrier(v.astype(jnp.bfloat16)).astype(jnp.float32)

@jax.custom_vjp
def low_back(v):
    return v

def low_keep(v):
    return (low(v), None)

def low_pass(kept, grad):
    return (grad,)

def back_keep(v):
    return (v, None)

def back_low(kept, grad):
    return (low(grad),)
low.defvjp(low_keep, low_pass)
low_back.defvjp(back_keep, back_low)

def matmul(left_side, right_side):
    return jnp.dot(left_side, right_side, precision=HIGHEST_PRECISION, preferred_element_type=jnp.float32)

def layer_norm(hidden, gain_vector, shift_vector):
    centre = hidden - lax.optimization_barrier(jnp.mean(hidden, axis=-1, keepdims=True))
    variance = lax.optimization_barrier(jnp.mean(centre * centre, axis=-1, keepdims=True))
    return centre * lax.rsqrt(variance + EPSILON) * gain_vector + shift_vector

def attend_head(head_item):
    queries, keys_in, values, row_order, row_inverse, segment_ids = head_item
    sorted_queries = queries[row_order].reshape(CLUSTERS, CLUSTER, HD)
    sorted_keys = keys_in[row_order].reshape(CLUSTERS, CLUSTER, HD)
    sorted_values = values[row_order].reshape(CLUSTERS, CLUSTER, HD)
    cluster_ids = segment_ids[row_order].reshape(CLUSTERS, CLUSTER)
    scores = low_back(jnp.einsum('cqd,ckd->cqk', sorted_queries, sorted_keys, precision=HIGHEST_PRECISION) * HD ** (-0.5))
    allowed = cluster_ids[:, :, None] == cluster_ids[:, None, :]
    masked = jnp.where(allowed, scores, NEGATIVE)
    highest = lax.optimization_barrier(jnp.max(masked, axis=-1, keepdims=True))
    raised = jnp.exp(masked - highest)
    totals = lax.optimization_barrier(jnp.sum(raised, axis=-1, keepdims=True))
    weights = raised / totals
    attended = jnp.einsum('cqk,ckd->cqd', low(weights), sorted_values, precision=HIGHEST_PRECISION)
    log_total = highest[:, :, 0] + jnp.log(totals[:, :, 0])
    entropy = lax.optimization_barrier(jnp.sum(log_total - lax.optimization_barrier(jnp.sum(weights * jnp.where(allowed, scores, 0.0), axis=-1)), axis=-1))
    occupied = lax.optimization_barrier(jnp.sum(allowed.astype(jnp.float32), axis=(1, 2)))
    attended = low_back(low(attended.reshape(TOKENS, HD)))[row_inverse]
    return (attended, entropy, occupied)

def group_forward(param_tuple, flat_tokens, segment_ids, row_orders, row_inverses):
    query_weight, query_bias, key_weight, value_weight, value_bias, out_weight, out_bias, first_gain, first_shift, inner_weight, inner_bias, outer_weight, outer_bias, second_gain, second_shift = param_tuple

    def project(weight_matrix, bias_vector):
        rounded = low_back(low(matmul(flat_tokens, weight_matrix) + bias_vector))
        return rounded.reshape(TOKENS, H, HD).transpose(1, 0, 2)
    queries = project(query_weight, query_bias)
    keys_in = project(key_weight, 0.0)
    values = project(value_weight, value_bias)
    segment_rows = jnp.broadcast_to(segment_ids[None, :], (H, TOKENS))
    attended, entropy, occupied = lax.map(jax.checkpoint(attend_head), (queries, keys_in, values, row_orders, row_inverses, segment_rows))
    attended = attended.transpose(1, 0, 2).reshape(SEQ_DEVS, TOK_DEV, D)

    def dense_block(dense_item):
        token_block, attended_block = dense_item
        branch = low_back(matmul(attended_block, out_weight) + out_bias)
        first_out = layer_norm(token_block + branch, first_gain, first_shift)
        inner_sum = low_back(matmul(low(first_out), inner_weight) + inner_bias)
        activated = low(jax.nn.gelu(inner_sum, approximate=False))
        second = low_back(matmul(activated, outer_weight) + outer_bias)
        return layer_norm(first_out + second, second_gain, second_shift)
    result = lax.map(jax.checkpoint(dense_block), (flat_tokens.reshape(SEQ_DEVS, TOK_DEV, D), attended))
    return (result.reshape(TOKENS, D), (entropy, occupied))

def reference(tokens, segments, orders, owners, query_weight, query_bias, key_weight, value_weight, value_bias, out_weight, out_bias, first_gain, first_shift, inner_weight, inner_bias, outer_weight, outer_bias, second_gain, second_shift, cotangent):
    params = tuple((argument.astype(jnp.float32) for argument in (query_weight, query_bias, key_weight, value_weight, value_bias, out_weight, out_bias, first_gain, first_shift, inner_weight, inner_bias, outer_weight, outer_bias, second_gain, second_shift)))
    inverses = jnp.argsort(orders, axis=-1).astype(jnp.int32)

    def group_step(summed, group_item):
        group_tokens, group_segments, group_orders, group_inverses, group_cotangent = group_item

        def run_group(param_tuple, flat_tokens):
            return group_forward(param_tuple, flat_tokens, group_segments, group_orders, group_inverses)
        result, pullback, extras = jax.vjp(run_group, params, group_tokens, has_aux=True)
        param_grads, token_grads = pullback(group_cotangent)
        summed = tuple((earlier + current for earlier, current in zip(summed, param_grads)))
        return (summed, (result, token_grads, extras[0], extras[1]))
    zeros_start = tuple((jnp.zeros_like(argument) for argument in params))
    summed, (results, token_grads, entropy, occupied) = lax.scan(group_step, zeros_start, (tokens.astype(jnp.float32), segments, orders, inverses, cotangent.astype(jnp.float32)))
    owner_hot = (owners[..., None] == jnp.arange(SEQ_DEVS, dtype=jnp.int32)).astype(jnp.float32)
    entropy_sums = lax.optimization_barrier(jnp.sum(entropy[..., None] * owner_hot, axis=(0, 2))) / (GROUPS * TOK_DEV)
    occupied_sums = lax.optimization_barrier(jnp.sum(occupied[..., None] * owner_hot, axis=(0, 2))) / (GROUPS * TOK_DEV * CLUSTER)
    cluster_stats = jnp.stack([entropy_sums, occupied_sums])
    return (results.astype(jnp.bfloat16), token_grads.astype(jnp.bfloat16), summed[0], summed[1], summed[2], summed[3], summed[4], summed[5], summed[6], summed[7], summed[8], summed[9], summed[10], summed[11], summed[12], summed[13], summed[14], cluster_stats)
```

```python
import functools

import jax
import jax.numpy as jnp
from jax import lax
from jax.experimental import pallas as pl
from jax.experimental.pallas import tpu as pltpu
from jax.sharding import PartitionSpec as P

EPSILON = 1e-12
NEGATIVE = -1e30


def norm_forward(hidden, gain_vector, shift_vector):
    centre = hidden - jnp.mean(hidden, axis=-1, keepdims=True)
    root_inverse = lax.rsqrt(jnp.mean(centre * centre, axis=-1, keepdims=True) + EPSILON)
    normed = centre * root_inverse
    return (
        normed * gain_vector.astype(jnp.float32) + shift_vector.astype(jnp.float32),
        normed,
        root_inverse,
    )


def norm_backward(upstream, normed, root_inverse, gain_vector):
    scaled = upstream * gain_vector.astype(jnp.float32)
    return root_inverse * (
        scaled
        - jnp.mean(scaled, axis=-1, keepdims=True)
        - normed * jnp.mean(scaled * normed, axis=-1, keepdims=True)
    )


def exact_gelu(inner_sum):
    return jax.nn.gelu(inner_sum, approximate=False)


def rank_matrix(sort_keys):
    row_count = sort_keys.shape[1]
    ranks = jnp.sum((sort_keys[:, None, :] < sort_keys[:, :, None]).astype(jnp.int32), axis=2)
    return (ranks[:, None, :] == jnp.arange(row_count, dtype=jnp.int32)[None, :, None]).astype(
        jnp.bfloat16
    )


def scatter_rows(row_block, placing, seq_count):
    head_count, row_count, features = row_block.shape
    picked = jnp.einsum(
        "hri,hif->hrf", placing, row_block, preferred_element_type=jnp.float32
    ).astype(jnp.bfloat16)
    return picked.reshape(head_count, seq_count, row_count // seq_count * features).transpose(
        1, 0, 2
    )


def collect_rows(packed, placing, features):
    seq_count, head_count, flat_width = packed.shape
    row_block = packed.transpose(1, 0, 2).reshape(
        head_count, seq_count * flat_width // features, features
    )
    return jnp.einsum(
        "hri,hrf->hif", placing, row_block, preferred_element_type=jnp.float32
    ).astype(jnp.bfloat16)


def cluster_scores(queries, keys_in, segment_ids, score_scale):
    scores = (
        jnp.einsum("nqd,nkd->nqk", queries, keys_in, preferred_element_type=jnp.float32)
        * score_scale
    )
    allowed = segment_ids[:, :, None] == segment_ids[:, None, :]
    return (scores, allowed, jnp.where(allowed, scores, NEGATIVE))


def cluster_forward(queries, keys_in, values, segment_ids, score_scale):
    scores, allowed, masked = cluster_scores(queries, keys_in, segment_ids, score_scale)
    highest = jnp.max(masked, axis=-1, keepdims=True)
    raised = jnp.exp(masked - highest)
    totals = jnp.sum(raised, axis=-1, keepdims=True)
    weights = raised / totals
    attended = jnp.einsum(
        "nqk,nkd->nqd", weights.astype(jnp.bfloat16), values, preferred_element_type=jnp.float32
    ).astype(jnp.bfloat16)
    log_total = highest[:, :, 0] + jnp.log(totals[:, :, 0])
    entropy = log_total - jnp.sum(weights * jnp.where(allowed, scores, 0.0), axis=-1)
    occupied = jnp.sum(allowed.astype(jnp.float32), axis=-1)
    return (attended, log_total, entropy, occupied)


def cluster_backward(queries, keys_in, values, segment_ids, log_total, grad_out, score_scale):
    masked = cluster_scores(queries, keys_in, segment_ids, score_scale)[2]
    weights = jnp.exp(masked - log_total[:, :, None])
    weight_grads = jnp.einsum("nqd,nkd->nqk", grad_out, values, preferred_element_type=jnp.float32)
    value_grads = jnp.einsum(
        "nqk,nqd->nkd", weights.astype(jnp.bfloat16), grad_out, preferred_element_type=jnp.float32
    )
    score_grads = (
        weights * (weight_grads - jnp.sum(weights * weight_grads, axis=-1, keepdims=True))
    ).astype(jnp.bfloat16)
    query_grads = (
        jnp.einsum("nqk,nkd->nqd", score_grads, keys_in, preferred_element_type=jnp.float32)
        * score_scale
    )
    key_grads = (
        jnp.einsum("nqk,nqd->nkd", score_grads, queries, preferred_element_type=jnp.float32)
        * score_scale
    )
    return jnp.stack([query_grads, key_grads, value_grads], axis=2).astype(jnp.bfloat16)


MESH = pl.DeviceIdType.MESH


def reduce_kernel(
    parts, g_ref, f_ref, core_in, a_one, b_one, ab_two, z_one, z_two, gathered, send_sem, recv_sem
):
    s, r = lax.axis_index("seq"), lax.axis_index("rep")
    zh, zl, x = s // 4, (s // 2) % 2, s % 2
    y, c = r // 2, r % 2
    q = g_ref.shape[3] // 8
    width = g_ref.shape[4] // parts
    over_x, over_zl, over_zh = (s + 1 - 2 * x, r), (s + 2 - 4 * zl, r), (s + 4 - 8 * zh, r)
    over_y, over_c = (s, r + 2 - 4 * y), (s, r + 1 - 2 * c)
    peers = (over_c, over_x, over_y, over_zl, over_zh)

    barrier = pltpu.get_barrier_semaphore()
    for peer in peers:
        pl.semaphore_signal(barrier, inc=1, device_id=peer, device_id_type=MESH)
    pl.semaphore_wait(barrier, len(peers))

    def rows(start, size):
        return pl.ds(pl.multiple_of(start * q, 16), size * q)

    def send(step, k, src, dst, peer):
        copy = pltpu.make_async_remote_copy(
            src_ref=src,
            dst_ref=dst,
            send_sem=send_sem.at[step, k],
            recv_sem=recv_sem.at[step, k],
            device_id=peer,
            device_id_type=MESH,
        )
        copy.start()
        return copy

    def add(count, target, other):
        def one(i, carry):
            target(i)[...] = (
                target(i)[...].astype(jnp.float32) + other(i)[...].astype(jnp.float32)
            ).astype(jnp.bfloat16)
            return carry

        lax.fori_loop(0, count, one, 0)

    columns = [pl.ds(k * width, width) for k in range(parts)]
    zero = [
        send(0, k, g_ref.at[:, :, :, rows(4 * (1 - c), 4), cols], core_in.at[:, :, :, :, cols], over_c)
        for k, cols in enumerate(columns)
    ]
    first, second, third, fourth, fifth, sixth = [], [], [], [], [], []
    for k, cols in enumerate(columns):
        zero[k].wait()
        add(
            8,
            lambda i: core_in.at[i // 4, (i // 2) % 2, i % 2, :, cols],
            lambda i: g_ref.at[i // 4, (i // 2) % 2, i % 2, rows(4 * c, 4), cols],
        )
        first.append(
            (
                send(1, k, core_in.at[:, :, 1 - x, pl.ds(0, 2 * q), cols], a_one.at[:, :, :, cols], over_x),
                send(2, k, core_in.at[:, :, :, rows(3 - y, 1), cols], b_one.at[:, :, :, :, cols], over_y),
            )
        )
    for k, cols in enumerate(columns):
        first[k][0].wait()
        add(
            4,
            lambda i: a_one.at[i // 2, i % 2, :, cols],
            lambda i: core_in.at[i // 2, i % 2, x, pl.ds(0, 2 * q), cols],
        )
        copy_a = send(3, k, a_one.at[:, :, rows(1 - y, 1), cols], ab_two.at[0, :, :, :, cols], over_y)
        first[k][1].wait()
        add(
            8,
            lambda i: b_one.at[i // 4, (i // 2) % 2, i % 2, :, cols],
            lambda i: core_in.at[i // 4, (i // 2) % 2, i % 2, rows(2 + y, 1), cols],
        )
        copy_b = send(4, k, b_one.at[:, :, 1 - x, :, cols], ab_two.at[1, :, :, :, cols], over_x)
        second.append((copy_a, copy_b))
    for k, cols in enumerate(columns):
        second[k][0].wait()
        add(
            4,
            lambda i: ab_two.at[0, i // 2, i % 2, :, cols],
            lambda i: a_one.at[i // 2, i % 2, rows(y, 1), cols],
        )
        second[k][1].wait()
        add(
            4,
            lambda i: ab_two.at[1, i // 2, i % 2, :, cols],
            lambda i: b_one.at[i // 2, i % 2, x, :, cols],
        )
        third.append(send(5, k, ab_two.at[:, :, 1 - zl, :, cols], z_one.at[:, :, :, cols], over_zl))
    for k, cols in enumerate(columns):
        third[k].wait()
        add(
            4,
            lambda i: z_one.at[i // 2, i % 2, :, cols],
            lambda i: ab_two.at[i // 2, i % 2, zl, :, cols],
        )
        fourth.append(send(6, k, z_one.at[:, 1 - zh, :, cols], z_two.at[:, :, cols], over_zh))
    for k, cols in enumerate(columns):
        fourth[k].wait()
        for part in range(2):
            gathered[c, part, y, :, cols] = (
                z_two[part, :, cols].astype(jnp.float32) + z_one[part, zh, :, cols].astype(jnp.float32)
            ).astype(jnp.bfloat16)
        own = gathered.at[c, :, y, :, cols]
        fifth.append(send(7, k, own, own, over_y))
    for k, cols in enumerate(columns):
        fifth[k].wait()
        both = gathered.at[c, :, :, :, cols]
        sixth.append(send(8, k, both, both, over_c))
    for copy in sixth:
        copy.wait()
    f_ref[...] = gathered[...]


def reduce_rows(grads, parts, collective_id):
    seq_count, row_count, width = grads.shape
    q = row_count // 8
    low = jnp.bfloat16
    out = pl.pallas_call(
        functools.partial(reduce_kernel, parts),
        out_shape=jax.ShapeDtypeStruct((2, 2, 2, q, width), low),
        in_specs=[pl.BlockSpec(memory_space=pltpu.VMEM)],
        out_specs=pl.BlockSpec(memory_space=pltpu.VMEM),
        scratch_shapes=[
            pltpu.VMEM((2, 2, 2, 4 * q, width), low),
            pltpu.VMEM((2, 2, 2 * q, width), low),
            pltpu.VMEM((2, 2, 2, q, width), low),
            pltpu.VMEM((2, 2, 2, q, width), low),
            pltpu.VMEM((2, 2, q, width), low),
            pltpu.VMEM((2, q, width), low),
            pltpu.VMEM((2, 2, 2, q, width), low),
            pltpu.SemaphoreType.DMA((9, parts)),
            pltpu.SemaphoreType.DMA((9, parts)),
        ],
        compiler_params=pltpu.CompilerParams(
            collective_id=collective_id, has_side_effects=True, vmem_limit_bytes=56 << 20
        ),
        name="reduce_rows",
    )(grads.reshape(2, 2, 2, row_count, width))
    return out.reshape(row_count, width)


def body(
    tokens,
    segments,
    orders,
    owners,
    query_weight,
    query_bias,
    key_weight,
    value_weight,
    value_bias,
    out_weight,
    out_bias,
    first_gain,
    first_shift,
    inner_weight,
    inner_bias,
    outer_weight,
    outer_bias,
    second_gain,
    second_shift,
    cotangent,
):
    seq_count = lax.axis_size("seq")
    groups = lax.axis_size("rep")
    own_index = lax.axis_index("seq")
    row_count = tokens.shape[1]
    model_width = tokens.shape[2]
    order_table = orders[0]
    owner_table = owners[0]
    head_count, group_tokens = order_table.shape
    cluster_count = owner_table.shape[1]
    cluster = group_tokens // cluster_count
    head_dim = model_width // head_count
    per_owner = row_count // cluster
    score_scale = head_dim ** (-0.5)
    flat_tokens = tokens[0]
    local_index = jnp.arange(row_count, dtype=jnp.int32)
    factor = 1
    for candidate in range(1, seq_count + 1):
        if seq_count % candidate == 0 and candidate * row_count <= 2048:
            factor = candidate
    block_count = seq_count // factor
    block_width = factor * row_count
    order_blocks = order_table.reshape(head_count, block_count, block_width).transpose(1, 0, 2)
    owner_blocks = (
        jnp.repeat(owner_table, cluster, axis=1)
        .reshape(head_count, block_count, block_width)
        .transpose(1, 0, 2)
    )

    def find_target(total, block_item):
        order_block, owner_block = block_item
        local = order_block - own_index * row_count
        hits = local[:, :, None] == local_index[None, None, :]
        return (total + jnp.sum(jnp.where(hits, owner_block[:, :, None], 0), axis=1), None)

    target, unused = lax.scan(
        find_target, jnp.zeros((head_count, row_count), jnp.int32), (order_blocks, owner_blocks)
    )
    send_matrix = rank_matrix(target * row_count + local_index[None, :])
    mine = (owner_table == own_index).astype(jnp.int32)
    before = jnp.cumsum(mine, axis=1) - mine
    slot_hot = (mine[:, None, :] == 1) & (
        before[:, None, :] == jnp.arange(per_owner, dtype=jnp.int32)[None, :, None]
    )
    order_grid = order_table.reshape(head_count, cluster_count, cluster)
    owned_tokens = jnp.sum(
        jnp.where(slot_hot[:, :, :, None], order_grid[:, None, :, :], 0), axis=2
    ).reshape(head_count, row_count)
    arrive_matrix = rank_matrix(owned_tokens)
    w_three = jnp.concatenate([query_weight, key_weight, value_weight], axis=1)
    bias_three = jnp.concatenate(
        [
            query_bias.astype(jnp.float32),
            jnp.zeros((model_width,), jnp.float32),
            value_bias.astype(jnp.float32),
        ]
    )
    projected = (
        jnp.dot(flat_tokens, w_three, preferred_element_type=jnp.float32) + bias_three
    ).astype(jnp.bfloat16)
    token_rows = (
        projected.reshape(row_count, 3, head_count, head_dim)
        .transpose(2, 0, 1, 3)
        .reshape(head_count, row_count, 3 * head_dim)
    )
    segment_rows = jnp.broadcast_to(
        segments[0].astype(jnp.bfloat16)[None, :, None], (head_count, row_count, 1)
    )
    send_values = scatter_rows(token_rows, send_matrix, seq_count)
    send_segments = scatter_rows(segment_rows, send_matrix, seq_count)
    arrived, arrived_segments = (
        lax.all_to_all(send_values, "seq", split_axis=0, concat_axis=0, tiled=True),
        lax.all_to_all(send_segments, "seq", split_axis=0, concat_axis=0, tiled=True),
    )
    cluster_rows = collect_rows(arrived, arrive_matrix, 3 * head_dim).reshape(
        head_count * per_owner, cluster, 3, head_dim
    )
    cluster_segments = collect_rows(arrived_segments, arrive_matrix, 1).reshape(
        head_count * per_owner, cluster
    )
    queries = cluster_rows[:, :, 0]
    keys_in = cluster_rows[:, :, 1]
    values = cluster_rows[:, :, 2]
    attended, log_total, entropy, occupied = cluster_forward(
        queries, keys_in, values, cluster_segments, score_scale
    )
    per_head = jnp.stack(
        [
            jnp.sum(entropy.reshape(head_count, -1), axis=1),
            jnp.sum(occupied.reshape(head_count, -1), axis=1) / cluster,
        ]
    ) / (groups * row_count)
    column = (jnp.arange(seq_count, dtype=jnp.int32) == own_index).astype(jnp.float32)
    cluster_stats = lax.psum(per_head[:, :, None] * column, ("seq", "rep"))
    leaving = scatter_rows(
        attended.reshape(head_count, row_count, head_dim), arrive_matrix, seq_count
    )
    returned = lax.all_to_all(leaving, "seq", split_axis=0, concat_axis=0, tiled=True)
    attended_rows = (
        collect_rows(returned, send_matrix, head_dim)
        .transpose(1, 0, 2)
        .reshape(row_count, model_width)
    )
    branch = jnp.dot(
        attended_rows, out_weight, preferred_element_type=jnp.float32
    ) + out_bias.astype(jnp.float32)
    first_out, normed_one, root_one = norm_forward(
        flat_tokens.astype(jnp.float32) + branch, first_gain, first_shift
    )
    first_low = first_out.astype(jnp.bfloat16)
    inner_sum = jnp.dot(
        first_low, inner_weight, preferred_element_type=jnp.float32
    ) + inner_bias.astype(jnp.float32)
    activated, gelu_pull = jax.vjp(exact_gelu, inner_sum)
    activated_low = activated.astype(jnp.bfloat16)
    second = jnp.dot(
        activated_low, outer_weight, preferred_element_type=jnp.float32
    ) + outer_bias.astype(jnp.float32)
    result, normed_two, root_two = norm_forward(first_out + second, second_gain, second_shift)
    output = result.astype(jnp.bfloat16)[None]
    upstream = cotangent[0].astype(jnp.float32)
    gradient_second_gain = jnp.sum(upstream * normed_two, axis=0)
    gradient_second_shift = jnp.sum(upstream, axis=0)
    delta_two = norm_backward(upstream, normed_two, root_two, second_gain)
    delta_second = delta_two.astype(jnp.bfloat16)
    gradient_outer_bias = jnp.sum(delta_second.astype(jnp.float32), axis=0)
    gradient_outer_weight = jnp.einsum(
        "tf,td->fd", activated_low, delta_second, preferred_element_type=jnp.float32
    )
    delta_activated = jnp.einsum(
        "td,fd->tf", delta_second, outer_weight, preferred_element_type=jnp.float32
    )
    delta_inner = gelu_pull(delta_activated)[0].astype(jnp.bfloat16)
    gradient_inner_bias = jnp.sum(delta_inner.astype(jnp.float32), axis=0)
    gradient_inner_weight = jnp.einsum(
        "td,tf->df", first_low, delta_inner, preferred_element_type=jnp.float32
    )
    delta_first = delta_two + jnp.einsum(
        "tf,df->td", delta_inner, inner_weight, preferred_element_type=jnp.float32
    )
    gradient_first_gain = jnp.sum(delta_first * normed_one, axis=0)
    gradient_first_shift = jnp.sum(delta_first, axis=0)
    delta_one = norm_backward(delta_first, normed_one, root_one, first_gain)
    delta_branch = delta_one.astype(jnp.bfloat16)
    gradient_out_bias = jnp.sum(delta_branch.astype(jnp.float32), axis=0)
    gradient_out_weight = jnp.einsum(
        "td,te->de", attended_rows, delta_branch, preferred_element_type=jnp.float32
    )
    delta_attended = jnp.einsum(
        "te,de->td", delta_branch, out_weight, preferred_element_type=jnp.float32
    ).astype(jnp.bfloat16)
    delta_rows = delta_attended.reshape(row_count, head_count, head_dim).transpose(1, 0, 2)
    send_grads = scatter_rows(delta_rows, send_matrix, seq_count)
    grad_arrived = lax.all_to_all(send_grads, "seq", split_axis=0, concat_axis=0, tiled=True)
    kept_queries, kept_keys, kept_values, kept_segments = (
        queries,
        keys_in,
        values,
        cluster_segments,
    )
    grad_cluster = collect_rows(grad_arrived, arrive_matrix, head_dim).reshape(
        head_count * per_owner, cluster, head_dim
    )
    three_grads = cluster_backward(
        kept_queries, kept_keys, kept_values, kept_segments, log_total, grad_cluster, score_scale
    )
    leaving_grads = scatter_rows(
        three_grads.reshape(head_count, row_count, 3 * head_dim), arrive_matrix, seq_count
    )
    returned_grads = lax.all_to_all(leaving_grads, "seq", split_axis=0, concat_axis=0, tiled=True)
    delta_three = (
        collect_rows(returned_grads, send_matrix, 3 * head_dim)
        .reshape(head_count, row_count, 3, head_dim)
        .transpose(1, 2, 0, 3)
        .reshape(row_count, 3 * model_width)
    )
    bias_grads = jnp.sum(delta_three.astype(jnp.float32), axis=0)
    weight_grads = jnp.einsum(
        "td,te->de", flat_tokens, delta_three, preferred_element_type=jnp.float32
    )
    gradient_tokens = (
        delta_one
        + jnp.einsum("te,de->td", delta_three, w_three, preferred_element_type=jnp.float32)
    ).astype(jnp.bfloat16)[None]
    gradient_query_weight = weight_grads[:, :model_width]
    gradient_key_weight = weight_grads[:, model_width : 2 * model_width]
    gradient_value_weight = weight_grads[:, 2 * model_width :]
    gradient_query_bias = bias_grads[:model_width]
    gradient_value_bias = bias_grads[2 * model_width :]
    pieces = (
        lax.psum_scatter(gradient_query_weight, "seq", scatter_dimension=0, tiled=True),
        lax.psum_scatter(gradient_query_bias, "seq", scatter_dimension=0, tiled=True),
        lax.psum_scatter(gradient_key_weight, "seq", scatter_dimension=0, tiled=True),
        lax.psum_scatter(gradient_value_weight, "seq", scatter_dimension=0, tiled=True),
        lax.psum_scatter(gradient_value_bias, "seq", scatter_dimension=0, tiled=True),
        lax.psum_scatter(gradient_out_weight, "seq", scatter_dimension=0, tiled=True),
        lax.psum_scatter(gradient_out_bias, "seq", scatter_dimension=0, tiled=True),
        lax.psum_scatter(gradient_first_gain, "seq", scatter_dimension=0, tiled=True),
        lax.psum_scatter(gradient_first_shift, "seq", scatter_dimension=0, tiled=True),
        lax.psum_scatter(gradient_inner_weight, "seq", scatter_dimension=0, tiled=True),
        lax.psum_scatter(gradient_inner_bias, "seq", scatter_dimension=0, tiled=True),
        lax.psum_scatter(gradient_outer_weight, "seq", scatter_dimension=0, tiled=True),
        lax.psum_scatter(gradient_outer_bias, "seq", scatter_dimension=0, tiled=True),
        lax.psum_scatter(gradient_second_gain, "seq", scatter_dimension=0, tiled=True),
        lax.psum_scatter(gradient_second_shift, "seq", scatter_dimension=0, tiled=True),
    )
    summed = (
        lax.psum(pieces[0].astype(jnp.bfloat16), "rep").astype(jnp.float32),
        lax.psum(pieces[1].astype(jnp.bfloat16), "rep").astype(jnp.float32),
        lax.psum(pieces[2].astype(jnp.bfloat16), "rep").astype(jnp.float32),
        lax.psum(pieces[3].astype(jnp.bfloat16), "rep").astype(jnp.float32),
        lax.psum(pieces[4].astype(jnp.bfloat16), "rep").astype(jnp.float32),
        lax.psum(pieces[5].astype(jnp.bfloat16), "rep").astype(jnp.float32),
        lax.psum(pieces[6].astype(jnp.bfloat16), "rep").astype(jnp.float32),
        lax.psum(pieces[7].astype(jnp.bfloat16), "rep").astype(jnp.float32),
        lax.psum(pieces[8].astype(jnp.bfloat16), "rep").astype(jnp.float32),
        lax.psum(pieces[9].astype(jnp.bfloat16), "rep").astype(jnp.float32),
        lax.psum(pieces[10].astype(jnp.bfloat16), "rep").astype(jnp.float32),
        lax.psum(pieces[11].astype(jnp.bfloat16), "rep").astype(jnp.float32),
        lax.psum(pieces[12].astype(jnp.bfloat16), "rep").astype(jnp.float32),
        lax.psum(pieces[13].astype(jnp.bfloat16), "rep").astype(jnp.float32),
        lax.psum(pieces[14].astype(jnp.bfloat16), "rep").astype(jnp.float32),
    )
    return (output, gradient_tokens) + tuple(summed) + (cluster_stats,)


def square_body(
    tokens,
    segments,
    orders,
    owners,
    query_weight,
    query_bias,
    key_weight,
    value_weight,
    value_bias,
    out_weight,
    out_bias,
    first_gain,
    first_shift,
    inner_weight,
    inner_bias,
    outer_weight,
    outer_bias,
    second_gain,
    second_shift,
    cotangent,
):
    seq_count = lax.axis_size("seq")
    groups = lax.axis_size("rep")
    own_index = lax.axis_index("seq")
    row_count = tokens.shape[1]
    model_width = tokens.shape[2]
    order_table = orders[0]
    owner_table = owners[0]
    head_count, group_tokens = order_table.shape
    cluster_count = owner_table.shape[1]
    cluster = group_tokens // cluster_count
    head_dim = model_width // head_count
    per_owner = row_count // cluster
    score_scale = head_dim ** (-0.5)
    flat_tokens = tokens[0]
    local_index = jnp.arange(row_count, dtype=jnp.int32)
    factor = 1
    for candidate in range(1, seq_count + 1):
        if seq_count % candidate == 0 and candidate * row_count <= 2048:
            factor = candidate
    block_count = seq_count // factor
    block_width = factor * row_count
    order_blocks = order_table.reshape(head_count, block_count, block_width).transpose(1, 0, 2)
    owner_blocks = (
        jnp.repeat(owner_table, cluster, axis=1)
        .reshape(head_count, block_count, block_width)
        .transpose(1, 0, 2)
    )

    def find_target(total, block_item):
        order_block, owner_block = block_item
        local = order_block - own_index * row_count
        hits = local[:, :, None] == local_index[None, None, :]
        return (total + jnp.sum(jnp.where(hits, owner_block[:, :, None], 0), axis=1), None)

    target, unused = lax.scan(
        find_target, jnp.zeros((head_count, row_count), jnp.int32), (order_blocks, owner_blocks)
    )
    send_matrix = rank_matrix(target * row_count + local_index[None, :])
    mine = (owner_table == own_index).astype(jnp.int32)
    before = jnp.cumsum(mine, axis=1) - mine
    slot_hot = (mine[:, None, :] == 1) & (
        before[:, None, :] == jnp.arange(per_owner, dtype=jnp.int32)[None, :, None]
    )
    order_grid = order_table.reshape(head_count, cluster_count, cluster)
    owned_tokens = jnp.sum(
        jnp.where(slot_hot[:, :, :, None], order_grid[:, None, :, :], 0), axis=2
    ).reshape(head_count, row_count)
    arrive_matrix = rank_matrix(owned_tokens)
    w_three = jnp.concatenate([query_weight, key_weight, value_weight], axis=1)
    bias_three = jnp.concatenate(
        [
            query_bias.astype(jnp.float32),
            jnp.zeros((model_width,), jnp.float32),
            value_bias.astype(jnp.float32),
        ]
    )
    projected = (
        jnp.dot(flat_tokens, w_three, preferred_element_type=jnp.float32) + bias_three
    ).astype(jnp.bfloat16)
    token_rows = (
        projected.reshape(row_count, 3, head_count, head_dim)
        .transpose(2, 0, 1, 3)
        .reshape(head_count, row_count, 3 * head_dim)
    )
    segment_rows = jnp.broadcast_to(
        segments[0].astype(jnp.bfloat16)[None, :, None], (head_count, row_count, 1)
    )
    send_values = scatter_rows(token_rows, send_matrix, seq_count)
    send_segments = scatter_rows(segment_rows, send_matrix, seq_count)
    arrived, arrived_segments = (
        lax.all_to_all(send_values, "seq", split_axis=0, concat_axis=0, tiled=True),
        lax.all_to_all(send_segments, "seq", split_axis=0, concat_axis=0, tiled=True),
    )
    cluster_rows = collect_rows(arrived, arrive_matrix, 3 * head_dim).reshape(
        head_count * per_owner, cluster, 3, head_dim
    )
    cluster_segments = collect_rows(arrived_segments, arrive_matrix, 1).reshape(
        head_count * per_owner, cluster
    )
    queries = cluster_rows[:, :, 0]
    keys_in = cluster_rows[:, :, 1]
    values = cluster_rows[:, :, 2]
    attended, log_total, entropy, occupied = cluster_forward(
        queries, keys_in, values, cluster_segments, score_scale
    )
    per_head = jnp.stack(
        [
            jnp.sum(entropy.reshape(head_count, -1), axis=1),
            jnp.sum(occupied.reshape(head_count, -1), axis=1) / cluster,
        ]
    ) / (groups * row_count)
    column = (jnp.arange(seq_count, dtype=jnp.int32) == own_index).astype(jnp.float32)
    cluster_stats = lax.psum(per_head[:, :, None] * column, ("seq", "rep"))
    leaving = scatter_rows(
        attended.reshape(head_count, row_count, head_dim), arrive_matrix, seq_count
    )
    returned = lax.all_to_all(leaving, "seq", split_axis=0, concat_axis=0, tiled=True)
    attended_rows = (
        collect_rows(returned, send_matrix, head_dim)
        .transpose(1, 0, 2)
        .reshape(row_count, model_width)
    )
    branch = jnp.dot(
        attended_rows, out_weight, preferred_element_type=jnp.float32
    ) + out_bias.astype(jnp.float32)
    first_out, normed_one, root_one = norm_forward(
        flat_tokens.astype(jnp.float32) + branch, first_gain, first_shift
    )
    first_low = first_out.astype(jnp.bfloat16)
    inner_sum = jnp.dot(
        first_low, inner_weight, preferred_element_type=jnp.float32
    ) + inner_bias.astype(jnp.float32)
    activated, gelu_pull = jax.vjp(exact_gelu, inner_sum)
    activated_low = activated.astype(jnp.bfloat16)
    second = jnp.dot(
        activated_low, outer_weight, preferred_element_type=jnp.float32
    ) + outer_bias.astype(jnp.float32)
    result, normed_two, root_two = norm_forward(first_out + second, second_gain, second_shift)
    output = result.astype(jnp.bfloat16)[None]
    upstream = cotangent[0].astype(jnp.float32)
    gradient_second_gain = jnp.sum(upstream * normed_two, axis=0)
    gradient_second_shift = jnp.sum(upstream, axis=0)
    delta_two = norm_backward(upstream, normed_two, root_two, second_gain)
    delta_second = delta_two.astype(jnp.bfloat16)
    gradient_outer_bias = jnp.sum(delta_second.astype(jnp.float32), axis=0)
    gradient_outer_weight = jnp.einsum(
        "tf,td->fd", activated_low, delta_second, preferred_element_type=jnp.float32
    )
    delta_activated = jnp.einsum(
        "td,fd->tf", delta_second, outer_weight, preferred_element_type=jnp.float32
    )
    delta_inner = gelu_pull(delta_activated)[0].astype(jnp.bfloat16)
    gradient_inner_bias = jnp.sum(delta_inner.astype(jnp.float32), axis=0)
    gradient_inner_weight = jnp.einsum(
        "td,tf->df", first_low, delta_inner, preferred_element_type=jnp.float32
    )
    delta_first = delta_two + jnp.einsum(
        "tf,df->td", delta_inner, inner_weight, preferred_element_type=jnp.float32
    )
    gradient_first_gain = jnp.sum(delta_first * normed_one, axis=0)
    gradient_first_shift = jnp.sum(delta_first, axis=0)
    delta_one = norm_backward(delta_first, normed_one, root_one, first_gain)
    delta_branch = delta_one.astype(jnp.bfloat16)
    gradient_out_bias = jnp.sum(delta_branch.astype(jnp.float32), axis=0)
    gradient_out_weight = jnp.einsum(
        "td,te->de", attended_rows, delta_branch, preferred_element_type=jnp.float32
    )
    delta_attended = jnp.einsum(
        "te,de->td", delta_branch, out_weight, preferred_element_type=jnp.float32
    ).astype(jnp.bfloat16)
    delta_rows = delta_attended.reshape(row_count, head_count, head_dim).transpose(1, 0, 2)
    send_grads = scatter_rows(delta_rows, send_matrix, seq_count)
    grad_arrived = lax.all_to_all(send_grads, "seq", split_axis=0, concat_axis=0, tiled=True)
    kept_queries, kept_keys, kept_values, kept_segments = (
        queries,
        keys_in,
        values,
        cluster_segments,
    )
    grad_cluster = collect_rows(grad_arrived, arrive_matrix, head_dim).reshape(
        head_count * per_owner, cluster, head_dim
    )
    three_grads = cluster_backward(
        kept_queries, kept_keys, kept_values, kept_segments, log_total, grad_cluster, score_scale
    )
    leaving_grads = scatter_rows(
        three_grads.reshape(head_count, row_count, 3 * head_dim), arrive_matrix, seq_count
    )
    returned_grads = lax.all_to_all(leaving_grads, "seq", split_axis=0, concat_axis=0, tiled=True)
    delta_three = (
        collect_rows(returned_grads, send_matrix, 3 * head_dim)
        .reshape(head_count, row_count, 3, head_dim)
        .transpose(1, 2, 0, 3)
        .reshape(row_count, 3 * model_width)
    )
    bias_grads = jnp.sum(delta_three.astype(jnp.float32), axis=0)
    weight_grads = jnp.einsum(
        "td,te->de", flat_tokens, delta_three, preferred_element_type=jnp.float32
    )
    gradient_tokens = (
        delta_one
        + jnp.einsum("te,de->td", delta_three, w_three, preferred_element_type=jnp.float32)
    ).astype(jnp.bfloat16)[None]
    gradient_query_weight = weight_grads[:, :model_width]
    gradient_key_weight = weight_grads[:, model_width : 2 * model_width]
    gradient_value_weight = weight_grads[:, 2 * model_width :]
    gradient_query_bias = bias_grads[:model_width]
    gradient_value_bias = bias_grads[2 * model_width :]
    weights_out = [
        gradient_out_weight.reshape(8, -1, model_width),
        gradient_inner_weight.reshape(8, model_width // 8, -1, model_width)
        .transpose(0, 2, 1, 3)
        .reshape(8, -1, model_width),
        gradient_outer_weight.reshape(8, -1, model_width),
        gradient_query_weight.reshape(8, -1, model_width),
        gradient_key_weight.reshape(8, -1, model_width),
        gradient_value_weight.reshape(8, -1, model_width),
    ]
    vectors = jnp.concatenate(
        [
            vector.reshape(8, -1)
            for vector in (
                gradient_query_bias,
                gradient_value_bias,
                gradient_out_bias,
                gradient_first_gain,
                gradient_first_shift,
                gradient_inner_bias,
                gradient_outer_bias,
                gradient_second_gain,
                gradient_second_shift,
            )
        ],
        axis=1,
    )
    used = sum(block.shape[1] for block in weights_out)
    total_rows = -(-(used + 2) // 128) * 128
    spare = (total_rows - used) * model_width - vectors.shape[1]
    vectors = jnp.pad(vectors, ((0, 0), (0, spare))).reshape(8, -1, model_width)
    grads = jnp.concatenate([block.astype(jnp.bfloat16) for block in weights_out + [vectors]], axis=1)
    summed = reduce_rows(grads, 2, 0).astype(jnp.float32)
    share = model_width // 8
    inner_count = inner_weight.shape[1] // model_width
    marks = [0]
    for block in weights_out:
        marks.append(marks[-1] + block.shape[1])
    out_g, inner_g, outer_g, query_g, key_g, value_g = (
        summed[marks[i] : marks[i + 1]] for i in range(6)
    )
    inner_g = inner_g.reshape(inner_count, share, model_width).transpose(1, 0, 2).reshape(share, -1)
    flat = summed[marks[6] :].reshape(-1)
    sizes = [share] * 5 + [share * inner_count] + [share] * 3
    ends = [0]
    for size in sizes:
        ends.append(ends[-1] + size)
    pick = [flat[ends[i] : ends[i + 1]] for i in range(9)]
    return (
        output,
        gradient_tokens,
        query_g,
        pick[0],
        key_g,
        value_g,
        pick[1],
        out_g,
        pick[2],
        pick[3],
        pick[4],
        inner_g,
        pick[5],
        outer_g,
        pick[6],
        pick[7],
        pick[8],
        cluster_stats,
    )


def solution(mesh):
    square = mesh.shape["seq"] == 8 and mesh.shape["rep"] == 4
    placed = (
        P("rep", "seq", None),
        P("rep", "seq"),
        P("rep", None, None),
        P("rep", None, None),
        P(),
        P(),
        P(),
        P(),
        P(),
        P(),
        P(),
        P(),
        P(),
        P(),
        P(),
        P(),
        P(),
        P(),
        P(),
        P("rep", "seq", None),
    )
    return jax.shard_map(
        square_body if square else body,
        mesh=mesh,
        in_specs=placed,
        out_specs=(
            P("rep", "seq", None),
            P("rep", "seq", None),
            P("seq", None),
            P("seq"),
            P("seq", None),
            P("seq", None),
            P("seq"),
            P("seq", None),
            P("seq"),
            P("seq"),
            P("seq"),
            P("seq", None),
            P("seq"),
            P("seq", None),
            P("seq"),
            P("seq"),
            P("seq"),
            P(),
        ),
        check_vma=False,
    )
```

```python
import functools

import jax
import jax.numpy as jnp
from jax import lax
from jax.experimental import pallas as pl
from jax.experimental.pallas import tpu as pltpu
from jax.sharding import PartitionSpec as P

EPSILON = 1e-12
NEGATIVE = -1e30


def norm_forward(hidden, gain_vector, shift_vector):
    centre = hidden - jnp.mean(hidden, axis=-1, keepdims=True)
    root_inverse = lax.rsqrt(jnp.mean(centre * centre, axis=-1, keepdims=True) + EPSILON)
    normed = centre * root_inverse
    return (
        normed * gain_vector.astype(jnp.float32) + shift_vector.astype(jnp.float32),
        normed,
        root_inverse,
    )


def norm_backward(upstream, normed, root_inverse, gain_vector):
    scaled = upstream * gain_vector.astype(jnp.float32)
    return root_inverse * (
        scaled
        - jnp.mean(scaled, axis=-1, keepdims=True)
        - normed * jnp.mean(scaled * normed, axis=-1, keepdims=True)
    )


def exact_gelu(inner_sum):
    return jax.nn.gelu(inner_sum, approximate=False)


def rank_matrix(sort_keys):
    row_count = sort_keys.shape[1]
    ranks = jnp.sum((sort_keys[:, None, :] < sort_keys[:, :, None]).astype(jnp.int32), axis=2)
    return (ranks[:, None, :] == jnp.arange(row_count, dtype=jnp.int32)[None, :, None]).astype(
        jnp.bfloat16
    )


def scatter_rows(row_block, placing, seq_count):
    head_count, row_count, features = row_block.shape
    picked = jnp.einsum(
        "hri,hif->hrf", placing, row_block, preferred_element_type=jnp.float32
    ).astype(jnp.bfloat16)
    return picked.reshape(head_count, seq_count, row_count // seq_count * features).transpose(
        1, 0, 2
    )


def collect_rows(packed, placing, features):
    seq_count, head_count, flat_width = packed.shape
    row_block = packed.transpose(1, 0, 2).reshape(
        head_count, seq_count * flat_width // features, features
    )
    return jnp.einsum(
        "hri,hrf->hif", placing, row_block, preferred_element_type=jnp.float32
    ).astype(jnp.bfloat16)


def cluster_scores(queries, keys_in, segment_ids, score_scale):
    scores = (
        jnp.einsum("nqd,nkd->nqk", queries, keys_in, preferred_element_type=jnp.float32)
        * score_scale
    )
    allowed = segment_ids[:, :, None] == segment_ids[:, None, :]
    return (scores, allowed, jnp.where(allowed, scores, NEGATIVE))


def cluster_forward(queries, keys_in, values, segment_ids, score_scale):
    scores, allowed, masked = cluster_scores(queries, keys_in, segment_ids, score_scale)
    highest = jnp.max(masked, axis=-1, keepdims=True)
    raised = jnp.exp(masked - highest)
    totals = jnp.sum(raised, axis=-1, keepdims=True)
    weights = raised / totals
    attended = jnp.einsum(
        "nqk,nkd->nqd", weights.astype(jnp.bfloat16), values, preferred_element_type=jnp.float32
    ).astype(jnp.bfloat16)
    log_total = highest[:, :, 0] + jnp.log(totals[:, :, 0])
    entropy = log_total - jnp.sum(weights * jnp.where(allowed, scores, 0.0), axis=-1)
    occupied = jnp.sum(allowed.astype(jnp.float32), axis=-1)
    return (attended, log_total, entropy, occupied)


def cluster_backward(queries, keys_in, values, segment_ids, log_total, grad_out, score_scale):
    masked = cluster_scores(queries, keys_in, segment_ids, score_scale)[2]
    weights = jnp.exp(masked - log_total[:, :, None])
    weight_grads = jnp.einsum("nqd,nkd->nqk", grad_out, values, preferred_element_type=jnp.float32)
    value_grads = jnp.einsum(
        "nqk,nqd->nkd", weights.astype(jnp.bfloat16), grad_out, preferred_element_type=jnp.float32
    )
    score_grads = (
        weights * (weight_grads - jnp.sum(weights * weight_grads, axis=-1, keepdims=True))
    ).astype(jnp.bfloat16)
    query_grads = (
        jnp.einsum("nqk,nkd->nqd", score_grads, keys_in, preferred_element_type=jnp.float32)
        * score_scale
    )
    key_grads = (
        jnp.einsum("nqk,nqd->nkd", score_grads, queries, preferred_element_type=jnp.float32)
        * score_scale
    )
    return jnp.stack([query_grads, key_grads, value_grads], axis=2).astype(jnp.bfloat16)


MESH = pl.DeviceIdType.MESH


def half_roll(block):
    return jnp.concatenate([block[:, 64:], block[:, :64]], axis=1)


def lanes(shape):
    return lax.broadcasted_iota(jnp.int32, shape, len(shape) - 1)


def bits(value, flip):
    return value + flip - 2 * value * flip


def coordinates():
    s, r = lax.axis_index("seq"), lax.axis_index("rep")
    return s // 4, (s // 2) % 2, s % 2, r // 2, r % 2


def device(zh, zl, x, y, c):
    return (4 * zh + 2 * zl + x, 2 * y + c)


def greet(peers):
    barrier = pltpu.get_barrier_semaphore()
    for peer in peers:
        pl.semaphore_signal(barrier, inc=1, device_id=peer, device_id_type=MESH)
    pl.semaphore_wait(barrier, len(peers))


def remote(src, dst, sems, index, peer):
    return pltpu.make_async_remote_copy(
        src_ref=src,
        dst_ref=dst,
        send_sem=sems[0].at[index],
        recv_sem=sems[1].at[index],
        device_id=peer,
        device_id_type=MESH,
    )


def dot(left, right, left_dim=1, right_dim=0):
    return lax.dot_general(
        left,
        right,
        (((left_dim,), (right_dim,)), ((), ())),
        preferred_element_type=jnp.float32,
    )


def hot(condition):
    return jnp.where(condition, 1.0, 0.0).astype(jnp.bfloat16)


def build_gather(order_ref, row, start, count, into):
    tokens = into.shape[1]

    def one(k, carry):
        at = pl.multiple_of(k * 128, 128)
        ids = order_ref[row : row + 1, pl.ds(pl.multiple_of(start + at, 128), 128)]
        column = jnp.broadcast_to(ids.astype(jnp.float32), (128, 128)).T
        lane = lanes((128, 128)).astype(jnp.float32)
        for t in range(tokens // 128):
            into[pl.ds(at, 128), t * 128 : (t + 1) * 128] = hot(column == lane + 128.0 * t)
        return carry

    lax.fori_loop(0, count // 128, one, 0)


def build_scatter(order_ref, row, start, count, into, base):
    def one(k, carry):
        at = pl.multiple_of(k * 128, 128)
        token = lax.broadcasted_iota(jnp.int32, (128, 128), 0) + at
        for p in range(count // 128):
            ids = order_ref[row : row + 1, pl.ds(pl.multiple_of(start + 128 * p, 128), 128)]
            into[pl.ds(at, 128), base + 128 * p : base + 128 * (p + 1)] = hot(ids == token)
        return carry

    lax.fori_loop(0, into.shape[0] // 128, one, 0)


def select_head(slab, half, place):
    return jnp.where(half == place, slab, half_roll(slab))


def join(low_lanes, high_lanes):
    return jnp.where(lanes(low_lanes.shape) < 64, low_lanes, high_lanes)


def pick_columns(refs, j, c, add_zero):
    def slab(ref, index):
        return ref[:, pl.ds(pl.multiple_of(index * 128, 128), 128)].astype(jnp.float32)

    first = [slab(ref, j) for ref in refs]
    other = [slab(ref, 4 + j // 2) for ref in refs]
    zero = jnp.zeros_like(first[0])
    q1, v1 = select_head(first[0], c, 0), select_head(first[2], c, 1)
    k1 = select_head(first[1], c, 0)
    v2, q2 = select_head(other[2], j % 2, 0), select_head(other[0], j % 2, 1)
    k2 = select_head(other[1], j % 2, 1)
    return join(q1, v1), join(k1, zero), join(v2, q2), join(zero, k2)


def forward_kernel(
    tokens_ref,
    cot_ref,
    seg_ref,
    orders_ref,
    hot_ref,
    wq_ref,
    wk_ref,
    wv_ref,
    bias_ref,
    att_ref,
    x_all,
    cot_my,
    sorted_ref,
    prob_ref,
    wsel_ref,
    order_ref,
    stats_ref,
    orders_in,
    hot_in,
    seg_src,
    seg_all,
    bias_sel,
    tok,
    gather,
    scatter,
    att_sorted,
    att_send,
    att_in,
    ent_ref,
    cnt_ref,
    swap_send,
    swap_recv,
    ring_send,
    ring_recv,
    seg_send,
    seg_recv,
    back_send,
    back_recv,
):
    zh, zl, x, y, c = coordinates()
    j = 2 * zl + x
    p = 4 * c + j
    block = tokens_ref.shape[0]
    group = 8 * block
    scale = 0.125
    swap = (swap_send, swap_recv)
    ring = (ring_send, ring_recv)
    seg_sems = (seg_send, seg_recv)
    back = (back_send, back_recv)

    def member(flip):
        fc, fz, fx = flip // 4, (flip // 2) % 2, flip % 2
        mc, mz, mx = bits(c, fc), bits(zl, fz), bits(x, fx)
        return device(zh, mz, mx, y, mc), 4 * mc + 2 * mz + mx

    swap_peer = device(1 - zh, zl, x, y, 1 - c)
    peers = [member(flip)[0] for flip in range(1, 8)]
    greet(peers + [swap_peer])
    sibling = peers[3]
    over_x, over_z = peers[0], peers[1]
    matched = c == zh

    seg_src[...] = jnp.broadcast_to(seg_ref[...], seg_src.shape)
    table_copies = [
        remote(orders_ref, orders_in, swap, 0, sibling),
        remote(hot_ref, hot_in, swap, 1, sibling),
    ]
    for copy in table_copies:
        copy.start()
    p_swap = 4 * (1 - c) + j
    pairs = [
        (tokens_ref, x_all.at[p_swap], x_all.at[p]),
        (seg_src, seg_all.at[p_swap], seg_all.at[p]),
        (cot_ref, cot_my, cot_my),
    ]
    swaps = [remote(src, dst, swap, 2 + i, swap_peer) for i, (src, dst, _) in enumerate(pairs)]
    locals_ = [
        pltpu.make_async_copy(src, own, swap_recv.at[5 + i]) for i, (src, _, own) in enumerate(pairs)
    ]

    @pl.when(matched)
    def _():
        for copy in locals_:
            copy.start()

    @pl.when(jnp.logical_not(matched))
    def _():
        for copy in swaps:
            copy.start()

    tiles = pick_columns((wq_ref, wk_ref, wv_ref), j, c, None)
    for i, tile in enumerate(tiles):
        wsel_ref[:, 128 * i : 128 * (i + 1)] = tile.astype(jnp.bfloat16)
    bias_tiles = pick_columns(
        (bias_ref.at[pl.ds(0, 8)], bias_ref.at[pl.ds(8, 8)], bias_ref.at[pl.ds(16, 8)]), j, c, None
    )
    for i, tile in enumerate(bias_tiles):
        bias_sel[:, 128 * i : 128 * (i + 1)] = tile

    for copy in table_copies:
        copy.wait()
    h1, h2 = 2 * j + c, 8 + j
    for i, h in enumerate((h1, h2)):
        own, other = orders_ref[pl.ds(h, 1), :], orders_in[pl.ds(h, 1), :]
        order_ref[i : i + 1, :] = jnp.where(matched, own, other)
    half = 1024 * c

    @pl.when(matched)
    def _():
        for i in (0, 1):
            locals_[i].wait()

    @pl.when(jnp.logical_not(matched))
    def _():
        for i in (0, 1):
            swaps[i].wait()

    px, pz, pd = member(1)[1], member(2)[1], member(3)[1]
    ps, psx, psz, psd = (member(flip)[1] for flip in (4, 5, 6, 7))
    own = x_all.at[p]
    to_x = remote(own, own, ring, 0, over_x)
    to_z = remote(own, own, ring, 1, over_z)
    to_s = remote(own, own, ring, 2, sibling)
    for copy in (to_x, to_z, to_s):
        copy.start()
    seg_copies = []
    for flip in range(1, 8):
        copy = remote(seg_all.at[p], seg_all.at[p], seg_sems, flip - 1, peers[flip - 1])
        copy.start()
        seg_copies.append(copy)

    build_gather(order_ref, 0, 0, group, gather.at[pl.ds(0, group)])
    to_x.wait()
    upper, lower = pl.ds(0, block // 2), pl.ds(block // 2, block // 2)
    x_half = remote(x_all.at[px, upper], x_all.at[px, upper], ring, 3, over_z)
    x_half.start()
    x_to_s = remote(x_all.at[px], x_all.at[px], ring, 4, sibling)
    x_to_s.start()
    to_z.wait()
    z_half = remote(x_all.at[pz, lower], x_all.at[pz, lower], ring, 5, over_x)
    z_half.start()
    z_to_s = remote(x_all.at[pz], x_all.at[pz], ring, 6, sibling)
    z_to_s.start()
    build_gather(order_ref, 1, half, group // 2, gather.at[pl.ds(group, group // 2)])
    for copy in seg_copies:
        copy.wait()

    def project(position):
        at = pl.ds(pl.multiple_of(position * block, block), block)
        out = dot(x_all[position], wsel_ref[...]) + bias_sel[0:1, :]
        ids = seg_all[position, 0:1, :].astype(jnp.float32)
        columns = [
            jnp.broadcast_to(ids[:, 128 * i : 128 * (i + 1)], (128, 128)).T for i in range(block // 128)
        ]
        lane = lanes((block, 128))
        seg_hot = hot(jnp.concatenate(columns, axis=0) == (lane % 64).astype(jnp.float32))
        low = out.astype(jnp.bfloat16)
        tok[at, 0:128] = low[:, 0:128]
        tok[at, 128:256] = jnp.where(lane < 64, low[:, 128:256], seg_hot)
        tok[at, 256:384] = low[:, 256:384]
        tok[at, 384:512] = jnp.where(lane < 64, seg_hot, low[:, 384:512])

    project(p)
    project(px)
    project(pz)
    to_s.wait()
    project(ps)
    x_half.wait()
    z_half.wait()
    d_to_s = remote(x_all.at[pd], x_all.at[pd], ring, 7, sibling)
    d_to_s.start()
    project(pd)
    x_to_s.wait()
    project(psx)
    z_to_s.wait()
    project(psz)
    build_scatter(order_ref, 0, 0, group, scatter, 0)
    build_scatter(order_ref, 1, half, group // 2, scatter, group)
    d_to_s.wait()
    project(psd)

    step = 512

    def gather_rows(k, carry):
        at = pl.ds(pl.multiple_of(k * step, step), step)
        sorted_ref[at, :] = dot(gather[at, :], tok[:, 0:256]).astype(jnp.bfloat16)
        return carry

    def gather_rows_two(k, carry):
        at = pl.ds(pl.multiple_of(k * step, step), step)
        sorted_ref[at, :] = dot(gather[at, :], tok[:, 256:512]).astype(jnp.bfloat16)
        return carry

    lax.fori_loop(0, group // step, gather_rows, 0)
    lax.fori_loop(group // step, group * 3 // 2 // step, gather_rows_two, 0)

    def attend(first_lanes):
        def one(i, carry):
            at = pl.ds(pl.multiple_of(i * 128, 128), 128)
            tile_zero, tile_one = sorted_ref[at, 0:128], sorted_ref[at, 128:256]
            low_lanes = lanes((128, 128)) < 64
            query_lanes = low_lanes if first_lanes else jnp.logical_not(low_lanes)
            queries = jnp.where(query_lanes, tile_zero, jnp.zeros_like(tile_zero))
            ids = jnp.where(query_lanes, jnp.zeros_like(tile_one), tile_one)
            scores = dot(queries, tile_one, 1, 1) * scale
            allowed = dot(ids, tile_one, 1, 1)
            masked = jnp.where(allowed > 0.5, scores, NEGATIVE)
            highest = jnp.max(masked, axis=1, keepdims=True)
            raised = jnp.exp(masked - highest)
            totals = jnp.sum(raised, axis=1, keepdims=True)
            weights = raised / totals
            prob_ref[at, :] = weights
            mixed = dot(weights.astype(jnp.bfloat16), tile_zero)
            att_sorted[at, :] = jnp.where(query_lanes, 0.0, mixed).astype(jnp.bfloat16)
            log_total = highest + jnp.log(totals)
            entropy = jnp.where(lanes((128, 128)) == 0, log_total, 0.0) - weights * masked
            ent_ref[pl.ds(i, 1), :] = jnp.sum(entropy, axis=0, keepdims=True)
            cnt_ref[pl.ds(i, 1), :] = jnp.sum(allowed, axis=0, keepdims=True)
            return carry

        return one

    lax.fori_loop(0, 16, attend(True), 0)
    lax.fori_loop(16, 24, attend(False), 0)

    def place(position):
        at = pl.ds(pl.multiple_of(position * block, block), block)
        return dot(scatter[at, :], att_sorted[...]).astype(jnp.bfloat16)

    back_copies = []
    for flip in (3, 7, 1, 5, 2, 6, 4):
        peer, position = member(flip)
        att_send[flip] = place(position)
        copy = remote(att_send.at[flip], att_in.at[p], back, flip - 1, peer)
        copy.start()
        back_copies.append(copy)
    att_in[p] = place(p)

    stats_ref[...] = jnp.zeros_like(stats_ref)
    for kind, (lane_sums, divisor) in enumerate(((ent_ref, 4.0 * block), (cnt_ref, 4.0 * block * 128))):
        sums = jnp.sum(lane_sums[...], axis=1, keepdims=True) / divisor
        for h, first, size, owner_row in ((h1, 0, 16, 16 * h1), (h2, 16, 8, 16 * h2 + 8 * c)):
            at = pl.ds(pl.multiple_of(owner_row, 8), size)
            owner_hot = jnp.where(matched, hot_ref[at, :], hot_in[at, :])
            stats_ref[kind, pl.ds(h, 1), :] = jnp.sum(
                sums[first : first + size] * owner_hot, axis=0, keepdims=True
            )

    @pl.when(matched)
    def _():
        locals_[2].wait()

    @pl.when(jnp.logical_not(matched))
    def _():
        swaps[2].wait()

    for copy in back_copies:
        copy.wait()
    for pair in range(4):
        even, odd = att_in[pair], att_in[4 + pair]
        att_ref[:, 128 * pair : 128 * (pair + 1)] = join(half_roll(even), odd)
    for pair in range(2):
        low_half = att_in[2 * pair] + att_in[4 + 2 * pair]
        high_half = att_in[2 * pair + 1] + att_in[5 + 2 * pair]
        att_ref[:, 512 + 128 * pair : 640 + 128 * pair] = join(low_half, half_roll(high_half))


def forward_attention(tokens, cotangent, segments, orders, owner_hot, wq, wk, wv, biases):
    block, width = tokens.shape
    group = 8 * block
    low, full = jnp.bfloat16, jnp.float32
    vmem = pl.BlockSpec(memory_space=pltpu.VMEM)
    dma = pltpu.SemaphoreType.DMA
    heads = orders.shape[0]
    rows = group * 3 // 2
    return pl.pallas_call(
        forward_kernel,
        out_shape=[
            jax.ShapeDtypeStruct((block, width), low),
            jax.ShapeDtypeStruct((8, block, width), low),
            jax.ShapeDtypeStruct((block, width), low),
            jax.ShapeDtypeStruct((rows, 256), low),
            jax.ShapeDtypeStruct((rows, 128), full),
            jax.ShapeDtypeStruct((width, 512), low),
            jax.ShapeDtypeStruct((8, group), jnp.int32),
            jax.ShapeDtypeStruct((2, 16, 128), full),
        ],
        in_specs=[vmem] * 9,
        out_specs=[vmem] * 8,
        scratch_shapes=[
            pltpu.VMEM((heads, group), jnp.int32),
            pltpu.VMEM(owner_hot.shape, full),
            pltpu.VMEM((8, block), jnp.int32),
            pltpu.VMEM((8, 8, block), jnp.int32),
            pltpu.VMEM((8, 512), full),
            pltpu.VMEM((group, 512), low),
            pltpu.VMEM((rows, group), low),
            pltpu.VMEM((group, rows), low),
            pltpu.VMEM((rows, 128), low),
            pltpu.VMEM((8, block, 128), low),
            pltpu.VMEM((8, block, 128), low),
            pltpu.VMEM((24, 128), full),
            pltpu.VMEM((24, 128), full),
            dma((8,)),
            dma((8,)),
            dma((8,)),
            dma((8,)),
            dma((7,)),
            dma((7,)),
            dma((7,)),
            dma((7,)),
        ],
        compiler_params=pltpu.CompilerParams(
            collective_id=1, has_side_effects=True, vmem_limit_bytes=60 << 20
        ),
        name="forward_attention",
    )(tokens, cotangent, segments, orders, owner_hot, wq, wk, wv, biases)


def rows_of(start, q, size):
    return pl.ds(pl.multiple_of(start * q, 16), size * q)


def add_into(count, target, other):
    def one(i, carry):
        target(i)[...] = (
            target(i)[...].astype(jnp.float32) + other(i)[...].astype(jnp.float32)
        ).astype(jnp.bfloat16)
        return carry

    lax.fori_loop(0, count, one, 0)


def reduce_steps(parts, g_ref, f_ref, buffers, sems, own_sem):
    own, core_in, a_one, b_one, ab_two, z_one, z_two = buffers
    zh, zl, x, y, c = coordinates()
    q = g_ref.shape[3] // 8
    width = g_ref.shape[4] // parts
    over_c, over_y = device(zh, zl, x, y, 1 - c), device(zh, zl, x, 1 - y, c)
    over_x, over_zl = device(zh, zl, 1 - x, y, c), device(zh, 1 - zl, x, y, c)
    over_zh = device(1 - zh, zl, x, y, c)

    def send(step, k, src, dst, peer):
        copy = remote(src, dst, (sems[0].at[step], sems[1].at[step]), k, peer)
        copy.start()
        return copy

    columns = [pl.ds(k * width, width) for k in range(parts)]
    zero = [
        send(
            0, k, g_ref.at[:, :, :, rows_of(4 * (1 - c), q, 4), cols], core_in.at[:, :, :, :, cols], over_c
        )
        for k, cols in enumerate(columns)
    ]
    mine = [
        pltpu.make_async_copy(
            g_ref.at[:, :, :, rows_of(4 * c, q, 4), cols], own.at[:, :, :, :, cols], own_sem.at[k]
        )
        for k, cols in enumerate(columns)
    ]
    for copy in mine:
        copy.start()
    yield
    first, second, third, fourth, fifth, sixth = [], [], [], [], [], []
    for k, cols in enumerate(columns):
        mine[k].wait()
        zero[k].wait()
        add_into(
            8,
            lambda i: core_in.at[i // 4, (i // 2) % 2, i % 2, :, cols],
            lambda i: own.at[i // 4, (i // 2) % 2, i % 2, :, cols],
        )
        first.append(
            (
                send(1, k, core_in.at[:, :, 1 - x, pl.ds(0, 2 * q), cols], a_one.at[:, :, :, cols], over_x),
                send(2, k, core_in.at[:, :, :, rows_of(3 - y, q, 1), cols], b_one.at[:, :, :, :, cols], over_y),
            )
        )
        yield
    for k, cols in enumerate(columns):
        first[k][0].wait()
        add_into(
            4,
            lambda i: a_one.at[i // 2, i % 2, :, cols],
            lambda i: core_in.at[i // 2, i % 2, x, pl.ds(0, 2 * q), cols],
        )
        copy_a = send(3, k, a_one.at[:, :, rows_of(1 - y, q, 1), cols], ab_two.at[0, :, :, :, cols], over_y)
        first[k][1].wait()
        add_into(
            8,
            lambda i: b_one.at[i // 4, (i // 2) % 2, i % 2, :, cols],
            lambda i: core_in.at[i // 4, (i // 2) % 2, i % 2, rows_of(2 + y, q, 1), cols],
        )
        copy_b = send(4, k, b_one.at[:, :, 1 - x, :, cols], ab_two.at[1, :, :, :, cols], over_x)
        second.append((copy_a, copy_b))
        yield
    for k, cols in enumerate(columns):
        second[k][0].wait()
        add_into(
            4,
            lambda i: ab_two.at[0, i // 2, i % 2, :, cols],
            lambda i: a_one.at[i // 2, i % 2, rows_of(y, q, 1), cols],
        )
        second[k][1].wait()
        add_into(
            4,
            lambda i: ab_two.at[1, i // 2, i % 2, :, cols],
            lambda i: b_one.at[i // 2, i % 2, x, :, cols],
        )
        third.append(send(5, k, ab_two.at[:, :, 1 - zl, :, cols], z_one.at[:, :, :, cols], over_zl))
        yield
    for k, cols in enumerate(columns):
        third[k].wait()
        add_into(
            4,
            lambda i: z_one.at[i // 2, i % 2, :, cols],
            lambda i: ab_two.at[i // 2, i % 2, zl, :, cols],
        )
        fourth.append(send(6, k, z_one.at[:, 1 - zh, :, cols], z_two.at[:, :, cols], over_zh))
        yield
    for k, cols in enumerate(columns):
        fourth[k].wait()
        for part in range(2):
            f_ref[c, part, y, :, cols] = (
                z_two[part, :, cols].astype(jnp.float32) + z_one[part, zh, :, cols].astype(jnp.float32)
            ).astype(jnp.bfloat16)
        own_rows = f_ref.at[c, :, y, :, cols]
        fifth.append(send(7, k, own_rows, own_rows, over_y))
        yield
    for k, cols in enumerate(columns):
        fifth[k].wait()
        both = f_ref.at[c, :, :, :, cols]
        sixth.append(send(8, k, both, both, over_c))
        yield
    for copy in sixth:
        copy.wait()


def backward_kernel(
    parts,
    datt_ref,
    sorted_ref,
    prob_ref,
    order_ref,
    x_all,
    wsel_ref,
    delta_ref,
    out_my,
    stats_ref,
    g_ref,
    out_home,
    grad_home,
    f_ref,
    gq_ref,
    gk_ref,
    gv_ref,
    stats_out,
    datt_send,
    datt_in,
    gather,
    gathered,
    dsorted,
    scatter,
    dqkv,
    part_send,
    part_in,
    total,
    a_in,
    b_in,
    a_two,
    b_two,
    grad_my,
    dw,
    dw_y,
    dw_in,
    dw_all,
    w_all,
    stats_buf,
    stats_in,
    own,
    core_in,
    a_one,
    b_one,
    ab_two,
    z_one,
    z_two,
    datt_ssem,
    datt_rsem,
    part_ssem,
    part_rsem,
    swap_ssem,
    swap_rsem,
    dw_ssem,
    dw_rsem,
    stats_ssem,
    stats_rsem,
    red_ssem,
    red_rsem,
    own_sem,
):
    zh, zl, x, y, c = coordinates()
    s = 4 * zh + 2 * zl + x
    j = 2 * zl + x
    p = 4 * c + j
    block, width = datt_ref.shape
    group = 8 * block
    scale = 0.125
    matched = c == zh
    datt_sems, part_sems = (datt_ssem, datt_rsem), (part_ssem, part_rsem)
    swap_sems, dw_sems, stats_sems = (swap_ssem, swap_rsem), (dw_ssem, dw_rsem), (stats_ssem, stats_rsem)

    def member(flip):
        fc, fz, fx = flip // 4, (flip // 2) % 2, flip % 2
        mc, mz, mx = bits(c, fc), bits(zl, fz), bits(x, fx)
        return device(zh, mz, mx, y, mc), mc, 2 * mz + mx

    peers = [member(flip)[0] for flip in range(1, 8)]
    sibling, over_x, over_z = peers[3], peers[0], peers[1]
    swap_peer = device(1 - zh, zl, x, y, 1 - c)
    over_y = device(zh, zl, x, 1 - y, c)
    across = [device(1 - zh, bits(zl, f // 2), bits(x, f % 2), y, c) for f in range(4)]
    greet(peers + [swap_peer, over_y] + across)

    def home_copy(src, dst, index, start):
        away = remote(src, dst, swap_sems, index, swap_peer)
        here = pltpu.make_async_copy(src, dst, swap_rsem.at[2 + index])

        @pl.when(matched)
        def _():
            here.start() if start else here.wait()

        @pl.when(jnp.logical_not(matched))
        def _():
            away.start() if start else away.wait()

    def tile(mc, mj):
        first = datt_ref[:, pl.ds(pl.multiple_of(mj * 128, 128), 128)]
        other = datt_ref[:, pl.ds(pl.multiple_of((4 + mj // 2) * 128, 128), 128)]
        return join(
            select_head(other.astype(jnp.float32), mj % 2, 0), select_head(first.astype(jnp.float32), mc, 1)
        ).astype(jnp.bfloat16)

    datt_copies = []
    for flip in (3, 7, 1, 5, 2, 6, 4):
        peer, mc, mj = member(flip)
        datt_send[flip] = tile(mc, mj)
        copy = remote(datt_send.at[flip], datt_in.at[p], datt_sems, flip - 1, peer)
        copy.start()
        datt_copies.append(copy)
    datt_in[p] = tile(c, j)
    home_copy(out_my, out_home, 0, True)

    reduction = reduce_steps(
        parts,
        g_ref,
        f_ref,
        (own, core_in, a_one, b_one, ab_two, z_one, z_two),
        (red_ssem, red_rsem),
        own_sem,
    )
    next(reduction)

    half = 1024 * c
    build_gather(order_ref, 0, 0, group, gather.at[pl.ds(0, group)])
    build_gather(order_ref, 1, half, group // 2, gather.at[pl.ds(group, group // 2)])
    for copy in datt_copies:
        copy.wait()
    for k in range(parts):
        next(reduction)

    step = 512
    arrived = datt_in[...].reshape(group, 128)

    def gather_rows(k, carry):
        at = pl.ds(pl.multiple_of(k * step, step), step)
        gathered[at, :] = dot(gather[at, :], arrived).astype(jnp.bfloat16)
        return carry

    lax.fori_loop(0, group * 3 // 2 // step, gather_rows, 0)

    def attend_back(first_lanes):
        def one(i, carry):
            at = pl.ds(pl.multiple_of(i * 128, 128), 128)
            tile_zero, tile_one = sorted_ref[at, 0:128], sorted_ref[at, 128:256]
            low_lanes = lanes((128, 128)) < 64
            query_lanes = low_lanes if first_lanes else jnp.logical_not(low_lanes)
            weights = prob_ref[at, :]
            taken = gathered[at, :]
            taken = jnp.where(query_lanes, jnp.zeros_like(taken), taken)
            weight_grads = dot(taken, tile_zero, 1, 1)
            inside = jnp.sum(weights * weight_grads, axis=1, keepdims=True)
            score_grads = weights * (weight_grads - inside)
            low_grads = score_grads.astype(jnp.bfloat16)
            query_grads = dot(low_grads, tile_one) * scale
            key_grads = dot(low_grads, tile_zero, 0, 0) * scale
            value_grads = dot(weights.astype(jnp.bfloat16), taken, 0, 0)
            dsorted[at, 0:128] = jnp.where(query_lanes, query_grads, value_grads).astype(jnp.bfloat16)
            dsorted[at, 128:256] = jnp.where(query_lanes, key_grads, 0.0).astype(jnp.bfloat16)
            return carry

        return one

    lax.fori_loop(0, 16, attend_back(True), 0)
    for k in range(parts):
        next(reduction)
    lax.fori_loop(16, 24, attend_back(False), 0)

    def place(position):
        token = lax.broadcasted_iota(jnp.int32, (128, 128), 0) + position * block
        for t in range(block // 128):
            for head, start, count, base in ((0, 0, group, 0), (1, half, group // 2, group)):
                for k in range(count // 128):
                    ids = order_ref[head : head + 1, pl.ds(pl.multiple_of(start + 128 * k, 128), 128)]
                    scatter[128 * t : 128 * (t + 1), base + 128 * k : base + 128 * (k + 1)] = hot(
                        ids == token + 128 * t
                    )
        at = pl.ds(pl.multiple_of(position * block, block), block)
        dqkv[at, 0:256] = dot(scatter[:, 0:group], dsorted[0:group, :]).astype(jnp.bfloat16)
        dqkv[at, 256:512] = dot(scatter[:, group:], dsorted[group:, :]).astype(jnp.bfloat16)
        return dot(dqkv[at, :], wsel_ref[...], 1, 1)

    def away(k, carry):
        part_send[k] = place(4 * (1 - c) + k).astype(jnp.bfloat16)
        remote(part_send.at[k], part_in.at[k], part_sems, k, sibling).start()
        return carry

    lax.fori_loop(0, 4, away, 0)

    def here(k, carry):
        part = place(4 * c + k)
        remote(part_send.at[k], part_in.at[k], part_sems, k, sibling).wait()
        total[k // 2, k % 2] = (part + part_in[k].astype(jnp.float32)).astype(jnp.bfloat16)
        return carry

    lax.fori_loop(0, 4, here, 0)
    upper, lower = pl.ds(0, block // 2), pl.ds(block // 2, block // 2)
    a_copy = remote(total.at[:, 1 - x, upper], a_in, part_sems, 4, over_x)
    b_copy = remote(total.at[1 - zl, :, lower], b_in, part_sems, 5, over_z)
    a_copy.start()
    b_copy.start()

    for k in range(width // 128):
        dw[128 * k : 128 * (k + 1), :] = dot(
            x_all[:, 128 * k : 128 * (k + 1)], dqkv[...], 0, 0
        ).astype(jnp.bfloat16)
    bias_row = jnp.broadcast_to(
        jnp.sum(dqkv[...].astype(jnp.float32), axis=0, keepdims=True), (16, 512)
    ).astype(jnp.bfloat16)
    share = width // 8
    for d in range(8):
        for h in range(2):
            dw_y[h, d, 0:share, :] = dw[share * d : share * (d + 1), 256 * h : 256 * (h + 1)]
            dw_y[h, d, share : share + 16, :] = bias_row[:, 256 * h : 256 * (h + 1)]
    over_y_copy = remote(dw_y.at[1 - y], dw_in, dw_sems, 0, over_y)
    over_y_copy.start()

    a_copy.wait()
    add_into(2, lambda i: a_in.at[i], lambda i: total.at[i, x, upper])
    a_next = remote(a_in.at[1 - zl], a_two, part_sems, 6, over_z)
    a_next.start()
    b_copy.wait()
    add_into(2, lambda i: b_in.at[i], lambda i: total.at[zl, i, lower])
    b_next = remote(b_in.at[1 - x], b_two, part_sems, 7, over_x)
    b_next.start()

    over_y_copy.wait()
    add_into(8, lambda i: dw_y.at[y, i], lambda i: dw_in.at[i])
    dw_copies = []
    targets = across + [over_x, over_z, peers[2]]
    flips = [(1, f // 2, f % 2) for f in range(4)] + [(0, 0, 1), (0, 1, 0), (0, 1, 1)]
    for i, (peer, (fh, fz, fx)) in enumerate(zip(targets, flips)):
        d = 4 * bits(zh, fh) + 2 * bits(zl, fz) + bits(x, fx)
        copy = remote(dw_y.at[y, d], dw_all.at[s], dw_sems, 1 + i, peer)
        copy.start()
        dw_copies.append(copy)
    dw_all[s] = dw_y[y, s]

    a_next.wait()
    b_next.wait()
    for start, first, second, index in ((0, a_two, a_in, zl), (block // 2, b_two, b_in, x)):
        at = pl.ds(start, block // 2)
        grad_my[at, :] = (
            delta_ref[at, :] + first[...].astype(jnp.float32) + second[index].astype(jnp.float32)
        ).astype(jnp.bfloat16)
    home_copy(grad_my, grad_home, 1, True)

    stats_buf[0] = stats_ref[...]
    stats_peers = (sibling, over_x, over_z, across[0], over_y)
    for k, peer in enumerate(stats_peers):
        copy = remote(stats_buf.at[k], stats_in.at[k], stats_sems, k, peer)
        copy.start()
        copy.wait()
        stats_buf[k + 1] = stats_buf[k] + stats_in[k]
    stats_out[...] = stats_buf[len(stats_peers)]

    for _ in range(parts):
        next(reduction)

    for copy in dw_copies:
        copy.wait()
    for k in range(4):
        w_all[y, c, k] = (dw_all[k].astype(jnp.float32) + dw_all[4 + k].astype(jnp.float32)).astype(
            jnp.bfloat16
        )
    w_copy = remote(w_all.at[y, c], w_all.at[y, c], dw_sems, 8, over_y)
    w_copy.start()
    next(reduction)
    w_copy.wait()
    w_copy = remote(w_all.at[:, c], w_all.at[:, c], dw_sems, 9, sibling)
    w_copy.start()
    for _ in reduction:
        pass
    w_copy.wait()
    for pair in range(4):
        at = slice(128 * pair, 128 * pair + 128)
        low, high = (w_all[0, core, pair].astype(jnp.float32) for core in range(2))
        gq_ref[:, at] = join(low[:, 0:128], half_roll(high[:, 0:128]))
        gk_ref[:, at] = join(low[:, 128:256], half_roll(high[:, 128:256]))
        gv_ref[:, at] = join(half_roll(low[:, 0:128]), high[:, 0:128])
    for pair in range(2):
        at = slice(512 + 128 * pair, 640 + 128 * pair)
        low, high = (
            w_all[1, 0, 2 * pair + i].astype(jnp.float32) + w_all[1, 1, 2 * pair + i].astype(jnp.float32)
            for i in range(2)
        )
        gq_ref[:, at] = join(half_roll(low[:, 0:128]), high[:, 0:128])
        gk_ref[:, at] = join(half_roll(low[:, 128:256]), high[:, 128:256])
        gv_ref[:, at] = join(low[:, 0:128], half_roll(high[:, 0:128]))
    home_copy(out_my, out_home, 0, False)
    home_copy(grad_my, grad_home, 1, False)


def backward_attention(datt, sorted_rows, prob, order, x_all, wsel, delta, output, stats, grads, parts):
    block, width = datt.shape
    group = 8 * block
    rows = group * 3 // 2
    row_count = grads.shape[1]
    q = row_count // 8
    share = width // 8 + 16
    low, full = jnp.bfloat16, jnp.float32
    vmem = pl.BlockSpec(memory_space=pltpu.VMEM)
    dma = pltpu.SemaphoreType.DMA
    outs = pl.pallas_call(
        functools.partial(backward_kernel, parts),
        out_shape=[
            jax.ShapeDtypeStruct((block, width), low),
            jax.ShapeDtypeStruct((block, width), low),
            jax.ShapeDtypeStruct((2, 2, 2, q, width), low),
            jax.ShapeDtypeStruct((share, width), full),
            jax.ShapeDtypeStruct((share, width), full),
            jax.ShapeDtypeStruct((share, width), full),
            jax.ShapeDtypeStruct(stats.shape, full),
        ],
        in_specs=[vmem] * 9 + [pl.BlockSpec(memory_space=pl.ANY)],
        out_specs=[vmem] * 7,
        scratch_shapes=[
            pltpu.VMEM((8, block, 128), low),
            pltpu.VMEM((8, block, 128), low),
            pltpu.VMEM((rows, group), low),
            pltpu.VMEM((rows, 128), low),
            pltpu.VMEM((rows, 256), low),
            pltpu.VMEM((block, rows), low),
            pltpu.VMEM((group, 512), low),
            pltpu.VMEM((4, block, width), low),
            pltpu.VMEM((4, block, width), low),
            pltpu.VMEM((2, 2, block, width), low),
            pltpu.VMEM((2, block // 2, width), low),
            pltpu.VMEM((2, block // 2, width), low),
            pltpu.VMEM((block // 2, width), low),
            pltpu.VMEM((block // 2, width), low),
            pltpu.VMEM((block, width), low),
            pltpu.VMEM((width, 512), low),
            pltpu.VMEM((2, 8, share, 256), low),
            pltpu.VMEM((8, share, 256), low),
            pltpu.VMEM((8, share, 256), low),
            pltpu.VMEM((2, 2, 4, share, 256), low),
            pltpu.VMEM((6,) + stats.shape, full),
            pltpu.VMEM((5,) + stats.shape, full),
            pltpu.VMEM((2, 2, 2, 4 * q, width), low),
            pltpu.VMEM((2, 2, 2, 4 * q, width), low),
            pltpu.VMEM((2, 2, 2 * q, width), low),
            pltpu.VMEM((2, 2, 2, q, width), low),
            pltpu.VMEM((2, 2, 2, q, width), low),
            pltpu.VMEM((2, 2, q, width), low),
            pltpu.VMEM((2, q, width), low),
            dma((7,)),
            dma((7,)),
            dma((8,)),
            dma((8,)),
            dma((4,)),
            dma((4,)),
            dma((10,)),
            dma((10,)),
            dma((5,)),
            dma((5,)),
            dma((9, parts)),
            dma((9, parts)),
            dma((parts,)),
        ],
        compiler_params=pltpu.CompilerParams(
            collective_id=2, has_side_effects=True, vmem_limit_bytes=60 << 20
        ),
        name="backward_attention",
    )(
        datt,
        sorted_rows,
        prob,
        order,
        x_all.reshape(group, width),
        wsel,
        delta,
        output,
        stats,
        grads.reshape(2, 2, 2, row_count, width),
    )
    out_home, grad_home, reduced, gq, gk, gv, totals = outs
    return out_home, grad_home, reduced.reshape(row_count, width), gq, gk, gv, totals


def body(
    tokens,
    segments,
    orders,
    owners,
    query_weight,
    query_bias,
    key_weight,
    value_weight,
    value_bias,
    out_weight,
    out_bias,
    first_gain,
    first_shift,
    inner_weight,
    inner_bias,
    outer_weight,
    outer_bias,
    second_gain,
    second_shift,
    cotangent,
):
    seq_count = lax.axis_size("seq")
    groups = lax.axis_size("rep")
    own_index = lax.axis_index("seq")
    row_count = tokens.shape[1]
    model_width = tokens.shape[2]
    order_table = orders[0]
    owner_table = owners[0]
    head_count, group_tokens = order_table.shape
    cluster_count = owner_table.shape[1]
    cluster = group_tokens // cluster_count
    head_dim = model_width // head_count
    per_owner = row_count // cluster
    score_scale = head_dim ** (-0.5)
    flat_tokens = tokens[0]
    local_index = jnp.arange(row_count, dtype=jnp.int32)
    factor = 1
    for candidate in range(1, seq_count + 1):
        if seq_count % candidate == 0 and candidate * row_count <= 2048:
            factor = candidate
    block_count = seq_count // factor
    block_width = factor * row_count
    order_blocks = order_table.reshape(head_count, block_count, block_width).transpose(1, 0, 2)
    owner_blocks = (
        jnp.repeat(owner_table, cluster, axis=1)
        .reshape(head_count, block_count, block_width)
        .transpose(1, 0, 2)
    )

    def find_target(total, block_item):
        order_block, owner_block = block_item
        local = order_block - own_index * row_count
        hits = local[:, :, None] == local_index[None, None, :]
        return (total + jnp.sum(jnp.where(hits, owner_block[:, :, None], 0), axis=1), None)

    target, unused = lax.scan(
        find_target, jnp.zeros((head_count, row_count), jnp.int32), (order_blocks, owner_blocks)
    )
    send_matrix = rank_matrix(target * row_count + local_index[None, :])
    mine = (owner_table == own_index).astype(jnp.int32)
    before = jnp.cumsum(mine, axis=1) - mine
    slot_hot = (mine[:, None, :] == 1) & (
        before[:, None, :] == jnp.arange(per_owner, dtype=jnp.int32)[None, :, None]
    )
    order_grid = order_table.reshape(head_count, cluster_count, cluster)
    owned_tokens = jnp.sum(
        jnp.where(slot_hot[:, :, :, None], order_grid[:, None, :, :], 0), axis=2
    ).reshape(head_count, row_count)
    arrive_matrix = rank_matrix(owned_tokens)
    w_three = jnp.concatenate([query_weight, key_weight, value_weight], axis=1)
    bias_three = jnp.concatenate(
        [
            query_bias.astype(jnp.float32),
            jnp.zeros((model_width,), jnp.float32),
            value_bias.astype(jnp.float32),
        ]
    )
    projected = (
        jnp.dot(flat_tokens, w_three, preferred_element_type=jnp.float32) + bias_three
    ).astype(jnp.bfloat16)
    token_rows = (
        projected.reshape(row_count, 3, head_count, head_dim)
        .transpose(2, 0, 1, 3)
        .reshape(head_count, row_count, 3 * head_dim)
    )
    segment_rows = jnp.broadcast_to(
        segments[0].astype(jnp.bfloat16)[None, :, None], (head_count, row_count, 1)
    )
    send_values = scatter_rows(token_rows, send_matrix, seq_count)
    send_segments = scatter_rows(segment_rows, send_matrix, seq_count)
    arrived, arrived_segments = (
        lax.all_to_all(send_values, "seq", split_axis=0, concat_axis=0, tiled=True),
        lax.all_to_all(send_segments, "seq", split_axis=0, concat_axis=0, tiled=True),
    )
    cluster_rows = collect_rows(arrived, arrive_matrix, 3 * head_dim).reshape(
        head_count * per_owner, cluster, 3, head_dim
    )
    cluster_segments = collect_rows(arrived_segments, arrive_matrix, 1).reshape(
        head_count * per_owner, cluster
    )
    queries = cluster_rows[:, :, 0]
    keys_in = cluster_rows[:, :, 1]
    values = cluster_rows[:, :, 2]
    attended, log_total, entropy, occupied = cluster_forward(
        queries, keys_in, values, cluster_segments, score_scale
    )
    per_head = jnp.stack(
        [
            jnp.sum(entropy.reshape(head_count, -1), axis=1),
            jnp.sum(occupied.reshape(head_count, -1), axis=1) / cluster,
        ]
    ) / (groups * row_count)
    column = (jnp.arange(seq_count, dtype=jnp.int32) == own_index).astype(jnp.float32)
    cluster_stats = lax.psum(per_head[:, :, None] * column, ("seq", "rep"))
    leaving = scatter_rows(
        attended.reshape(head_count, row_count, head_dim), arrive_matrix, seq_count
    )
    returned = lax.all_to_all(leaving, "seq", split_axis=0, concat_axis=0, tiled=True)
    attended_rows = (
        collect_rows(returned, send_matrix, head_dim)
        .transpose(1, 0, 2)
        .reshape(row_count, model_width)
    )
    branch = jnp.dot(
        attended_rows, out_weight, preferred_element_type=jnp.float32
    ) + out_bias.astype(jnp.float32)
    first_out, normed_one, root_one = norm_forward(
        flat_tokens.astype(jnp.float32) + branch, first_gain, first_shift
    )
    first_low = first_out.astype(jnp.bfloat16)
    inner_sum = jnp.dot(
        first_low, inner_weight, preferred_element_type=jnp.float32
    ) + inner_bias.astype(jnp.float32)
    activated, gelu_pull = jax.vjp(exact_gelu, inner_sum)
    activated_low = activated.astype(jnp.bfloat16)
    second = jnp.dot(
        activated_low, outer_weight, preferred_element_type=jnp.float32
    ) + outer_bias.astype(jnp.float32)
    result, normed_two, root_two = norm_forward(first_out + second, second_gain, second_shift)
    output = result.astype(jnp.bfloat16)[None]
    upstream = cotangent[0].astype(jnp.float32)
    gradient_second_gain = jnp.sum(upstream * normed_two, axis=0)
    gradient_second_shift = jnp.sum(upstream, axis=0)
    delta_two = norm_backward(upstream, normed_two, root_two, second_gain)
    delta_second = delta_two.astype(jnp.bfloat16)
    gradient_outer_bias = jnp.sum(delta_second.astype(jnp.float32), axis=0)
    gradient_outer_weight = jnp.einsum(
        "tf,td->fd", activated_low, delta_second, preferred_element_type=jnp.float32
    )
    delta_activated = jnp.einsum(
        "td,fd->tf", delta_second, outer_weight, preferred_element_type=jnp.float32
    )
    delta_inner = gelu_pull(delta_activated)[0].astype(jnp.bfloat16)
    gradient_inner_bias = jnp.sum(delta_inner.astype(jnp.float32), axis=0)
    gradient_inner_weight = jnp.einsum(
        "td,tf->df", first_low, delta_inner, preferred_element_type=jnp.float32
    )
    delta_first = delta_two + jnp.einsum(
        "tf,df->td", delta_inner, inner_weight, preferred_element_type=jnp.float32
    )
    gradient_first_gain = jnp.sum(delta_first * normed_one, axis=0)
    gradient_first_shift = jnp.sum(delta_first, axis=0)
    delta_one = norm_backward(delta_first, normed_one, root_one, first_gain)
    delta_branch = delta_one.astype(jnp.bfloat16)
    gradient_out_bias = jnp.sum(delta_branch.astype(jnp.float32), axis=0)
    gradient_out_weight = jnp.einsum(
        "td,te->de", attended_rows, delta_branch, preferred_element_type=jnp.float32
    )
    delta_attended = jnp.einsum(
        "te,de->td", delta_branch, out_weight, preferred_element_type=jnp.float32
    ).astype(jnp.bfloat16)
    delta_rows = delta_attended.reshape(row_count, head_count, head_dim).transpose(1, 0, 2)
    send_grads = scatter_rows(delta_rows, send_matrix, seq_count)
    grad_arrived = lax.all_to_all(send_grads, "seq", split_axis=0, concat_axis=0, tiled=True)
    kept_queries, kept_keys, kept_values, kept_segments = (
        queries,
        keys_in,
        values,
        cluster_segments,
    )
    grad_cluster = collect_rows(grad_arrived, arrive_matrix, head_dim).reshape(
        head_count * per_owner, cluster, head_dim
    )
    three_grads = cluster_backward(
        kept_queries, kept_keys, kept_values, kept_segments, log_total, grad_cluster, score_scale
    )
    leaving_grads = scatter_rows(
        three_grads.reshape(head_count, row_count, 3 * head_dim), arrive_matrix, seq_count
    )
    returned_grads = lax.all_to_all(leaving_grads, "seq", split_axis=0, concat_axis=0, tiled=True)
    delta_three = (
        collect_rows(returned_grads, send_matrix, 3 * head_dim)
        .reshape(head_count, row_count, 3, head_dim)
        .transpose(1, 2, 0, 3)
        .reshape(row_count, 3 * model_width)
    )
    bias_grads = jnp.sum(delta_three.astype(jnp.float32), axis=0)
    weight_grads = jnp.einsum(
        "td,te->de", flat_tokens, delta_three, preferred_element_type=jnp.float32
    )
    gradient_tokens = (
        delta_one
        + jnp.einsum("te,de->td", delta_three, w_three, preferred_element_type=jnp.float32)
    ).astype(jnp.bfloat16)[None]
    gradient_query_weight = weight_grads[:, :model_width]
    gradient_key_weight = weight_grads[:, model_width : 2 * model_width]
    gradient_value_weight = weight_grads[:, 2 * model_width :]
    gradient_query_bias = bias_grads[:model_width]
    gradient_value_bias = bias_grads[2 * model_width :]
    pieces = (
        lax.psum_scatter(gradient_query_weight, "seq", scatter_dimension=0, tiled=True),
        lax.psum_scatter(gradient_query_bias, "seq", scatter_dimension=0, tiled=True),
        lax.psum_scatter(gradient_key_weight, "seq", scatter_dimension=0, tiled=True),
        lax.psum_scatter(gradient_value_weight, "seq", scatter_dimension=0, tiled=True),
        lax.psum_scatter(gradient_value_bias, "seq", scatter_dimension=0, tiled=True),
        lax.psum_scatter(gradient_out_weight, "seq", scatter_dimension=0, tiled=True),
        lax.psum_scatter(gradient_out_bias, "seq", scatter_dimension=0, tiled=True),
        lax.psum_scatter(gradient_first_gain, "seq", scatter_dimension=0, tiled=True),
        lax.psum_scatter(gradient_first_shift, "seq", scatter_dimension=0, tiled=True),
        lax.psum_scatter(gradient_inner_weight, "seq", scatter_dimension=0, tiled=True),
        lax.psum_scatter(gradient_inner_bias, "seq", scatter_dimension=0, tiled=True),
        lax.psum_scatter(gradient_outer_weight, "seq", scatter_dimension=0, tiled=True),
        lax.psum_scatter(gradient_outer_bias, "seq", scatter_dimension=0, tiled=True),
        lax.psum_scatter(gradient_second_gain, "seq", scatter_dimension=0, tiled=True),
        lax.psum_scatter(gradient_second_shift, "seq", scatter_dimension=0, tiled=True),
    )
    summed = (
        lax.psum(pieces[0].astype(jnp.bfloat16), "rep").astype(jnp.float32),
        lax.psum(pieces[1].astype(jnp.bfloat16), "rep").astype(jnp.float32),
        lax.psum(pieces[2].astype(jnp.bfloat16), "rep").astype(jnp.float32),
        lax.psum(pieces[3].astype(jnp.bfloat16), "rep").astype(jnp.float32),
        lax.psum(pieces[4].astype(jnp.bfloat16), "rep").astype(jnp.float32),
        lax.psum(pieces[5].astype(jnp.bfloat16), "rep").astype(jnp.float32),
        lax.psum(pieces[6].astype(jnp.bfloat16), "rep").astype(jnp.float32),
        lax.psum(pieces[7].astype(jnp.bfloat16), "rep").astype(jnp.float32),
        lax.psum(pieces[8].astype(jnp.bfloat16), "rep").astype(jnp.float32),
        lax.psum(pieces[9].astype(jnp.bfloat16), "rep").astype(jnp.float32),
        lax.psum(pieces[10].astype(jnp.bfloat16), "rep").astype(jnp.float32),
        lax.psum(pieces[11].astype(jnp.bfloat16), "rep").astype(jnp.float32),
        lax.psum(pieces[12].astype(jnp.bfloat16), "rep").astype(jnp.float32),
        lax.psum(pieces[13].astype(jnp.bfloat16), "rep").astype(jnp.float32),
        lax.psum(pieces[14].astype(jnp.bfloat16), "rep").astype(jnp.float32),
    )
    return (output, gradient_tokens) + tuple(summed) + (cluster_stats,)


def square_body(
    tokens,
    segments,
    orders,
    owners,
    query_weight,
    query_bias,
    key_weight,
    value_weight,
    value_bias,
    out_weight,
    out_bias,
    first_gain,
    first_shift,
    inner_weight,
    inner_bias,
    outer_weight,
    outer_bias,
    second_gain,
    second_shift,
    cotangent,
):
    own_index = lax.axis_index("seq")
    position = 4 * lax.rem(lax.axis_index("rep"), 2) + lax.rem(own_index, 4)
    head_count = orders.shape[1]
    model_width = tokens.shape[2]
    seq_count = 8
    owner_hot = (owners[0][:, :, None] == jnp.arange(128, dtype=jnp.int32)).astype(jnp.float32)
    biases = jnp.concatenate(
        [
            jnp.broadcast_to(bias.astype(jnp.float32), (8, model_width))
            for bias in (query_bias, jnp.zeros_like(query_bias), value_bias)
        ]
    )
    attended_rows, x_all, my_cotangent, sorted_rows, prob, wsel, order, stats = forward_attention(
        tokens[0],
        cotangent[0],
        segments,
        orders[0],
        owner_hot.reshape(-1, 128),
        query_weight,
        key_weight,
        value_weight,
        biases,
    )
    flat_tokens = lax.dynamic_index_in_dim(x_all, position, 0, keepdims=False)
    branch = jnp.dot(
        attended_rows, out_weight, preferred_element_type=jnp.float32
    ) + out_bias.astype(jnp.float32)
    first_out, normed_one, root_one = norm_forward(
        flat_tokens.astype(jnp.float32) + branch, first_gain, first_shift
    )
    first_low = first_out.astype(jnp.bfloat16)
    inner_sum = jnp.dot(
        first_low, inner_weight, preferred_element_type=jnp.float32
    ) + inner_bias.astype(jnp.float32)
    activated, gelu_pull = jax.vjp(exact_gelu, inner_sum)
    activated_low = activated.astype(jnp.bfloat16)
    second = jnp.dot(
        activated_low, outer_weight, preferred_element_type=jnp.float32
    ) + outer_bias.astype(jnp.float32)
    result, normed_two, root_two = norm_forward(first_out + second, second_gain, second_shift)
    output = result.astype(jnp.bfloat16)
    upstream = my_cotangent.astype(jnp.float32)
    gradient_second_gain = jnp.sum(upstream * normed_two, axis=0)
    gradient_second_shift = jnp.sum(upstream, axis=0)
    delta_two = norm_backward(upstream, normed_two, root_two, second_gain)
    delta_second = delta_two.astype(jnp.bfloat16)
    gradient_outer_bias = jnp.sum(delta_second.astype(jnp.float32), axis=0)
    gradient_outer_weight = jnp.einsum(
        "tf,td->fd", activated_low, delta_second, preferred_element_type=jnp.float32
    )
    delta_activated = jnp.einsum(
        "td,fd->tf", delta_second, outer_weight, preferred_element_type=jnp.float32
    )
    delta_inner = gelu_pull(delta_activated)[0].astype(jnp.bfloat16)
    gradient_inner_bias = jnp.sum(delta_inner.astype(jnp.float32), axis=0)
    gradient_inner_weight = jnp.einsum(
        "td,tf->df", first_low, delta_inner, preferred_element_type=jnp.float32
    )
    delta_first = delta_two + jnp.einsum(
        "tf,df->td", delta_inner, inner_weight, preferred_element_type=jnp.float32
    )
    gradient_first_gain = jnp.sum(delta_first * normed_one, axis=0)
    gradient_first_shift = jnp.sum(delta_first, axis=0)
    delta_one = norm_backward(delta_first, normed_one, root_one, first_gain)
    delta_branch = delta_one.astype(jnp.bfloat16)
    gradient_out_bias = jnp.sum(delta_branch.astype(jnp.float32), axis=0)
    gradient_out_weight = jnp.einsum(
        "td,te->de", attended_rows, delta_branch, preferred_element_type=jnp.float32
    )
    delta_attended = jnp.einsum(
        "te,de->td", delta_branch, out_weight, preferred_element_type=jnp.float32
    ).astype(jnp.bfloat16)
    weights_out = [
        gradient_out_weight.reshape(8, -1, model_width),
        gradient_inner_weight.reshape(8, model_width // 8, -1, model_width)
        .transpose(0, 2, 1, 3)
        .reshape(8, -1, model_width),
        gradient_outer_weight.reshape(8, -1, model_width),
    ]
    vectors = jnp.concatenate(
        [
            vector.reshape(8, -1)
            for vector in (
                gradient_out_bias,
                gradient_first_gain,
                gradient_first_shift,
                gradient_inner_bias,
                gradient_outer_bias,
                gradient_second_gain,
                gradient_second_shift,
            )
        ],
        axis=1,
    )
    used = sum(part.shape[1] for part in weights_out)
    total_rows = -(-(used + 2) // 128) * 128
    spare = (total_rows - used) * model_width - vectors.shape[1]
    vectors = jnp.pad(vectors, ((0, 0), (0, spare))).reshape(8, -1, model_width)
    grads = jnp.concatenate([part.astype(jnp.bfloat16) for part in weights_out + [vectors]], axis=1)
    out_home, grad_home, summed, query_g, key_g, value_g, totals = backward_attention(
        delta_attended, sorted_rows, prob, order, x_all, wsel, delta_one, output, stats, grads, 2
    )
    summed = summed.astype(jnp.float32)
    share = model_width // 8
    inner_count = inner_weight.shape[1] // model_width
    marks = [0]
    for part in weights_out:
        marks.append(marks[-1] + part.shape[1])
    out_g, inner_g, outer_g = (summed[marks[i] : marks[i + 1]] for i in range(3))
    inner_g = inner_g.reshape(inner_count, share, model_width).transpose(1, 0, 2).reshape(share, -1)
    flat = summed[marks[3] :].reshape(-1)
    sizes = [share] * 3 + [share * inner_count] + [share] * 3
    ends = [0]
    for size in sizes:
        ends.append(ends[-1] + size)
    pick = [flat[ends[i] : ends[i + 1]] for i in range(7)]
    return (
        out_home[None],
        grad_home[None],
        query_g[:share],
        lax.dynamic_slice_in_dim(query_g[share], share * own_index, share),
        key_g[:share],
        value_g[:share],
        lax.dynamic_slice_in_dim(value_g[share], share * own_index, share),
        out_g,
        pick[0],
        pick[1],
        pick[2],
        inner_g,
        pick[3],
        outer_g,
        pick[4],
        pick[5],
        pick[6],
        totals[:, :head_count, :seq_count],
    )


def solution(mesh):
    square = mesh.shape["seq"] == 8 and mesh.shape["rep"] == 4
    placed = (
        P("rep", "seq", None),
        P("rep", "seq"),
        P("rep", None, None),
        P("rep", None, None),
        P(),
        P(),
        P(),
        P(),
        P(),
        P(),
        P(),
        P(),
        P(),
        P(),
        P(),
        P(),
        P(),
        P(),
        P(),
        P("rep", "seq", None),
    )
    return jax.shard_map(
        square_body if square else body,
        mesh=mesh,
        in_specs=placed,
        out_specs=(
            P("rep", "seq", None),
            P("rep", "seq", None),
            P("seq", None),
            P("seq"),
            P("seq", None),
            P("seq", None),
            P("seq"),
            P("seq", None),
            P("seq"),
            P("seq"),
            P("seq"),
            P("seq", None),
            P("seq"),
            P("seq", None),
            P("seq"),
            P("seq"),
            P("seq"),
            P(),
        ),
        check_vma=False,
    )
```

```python
import functools

import jax
import jax.numpy as jnp
from jax import lax
from jax.experimental import pallas as pl
from jax.experimental.pallas import tpu as pltpu
from jax.sharding import PartitionSpec as P

EPSILON = 1e-12
NEGATIVE = -1e30


def norm_forward(hidden, gain_vector, shift_vector):
    centre = hidden - jnp.mean(hidden, axis=-1, keepdims=True)
    root_inverse = lax.rsqrt(jnp.mean(centre * centre, axis=-1, keepdims=True) + EPSILON)
    normed = centre * root_inverse
    return (
        normed * gain_vector.astype(jnp.float32) + shift_vector.astype(jnp.float32),
        normed,
        root_inverse,
    )


def norm_backward(upstream, normed, root_inverse, gain_vector):
    scaled = upstream * gain_vector.astype(jnp.float32)
    return root_inverse * (
        scaled
        - jnp.mean(scaled, axis=-1, keepdims=True)
        - normed * jnp.mean(scaled * normed, axis=-1, keepdims=True)
    )


def exact_gelu(inner_sum):
    return jax.nn.gelu(inner_sum, approximate=False)


def rank_matrix(sort_keys):
    row_count = sort_keys.shape[1]
    ranks = jnp.sum((sort_keys[:, None, :] < sort_keys[:, :, None]).astype(jnp.int32), axis=2)
    return (ranks[:, None, :] == jnp.arange(row_count, dtype=jnp.int32)[None, :, None]).astype(
        jnp.bfloat16
    )


def scatter_rows(row_block, placing, seq_count):
    head_count, row_count, features = row_block.shape
    picked = jnp.einsum(
        "hri,hif->hrf", placing, row_block, preferred_element_type=jnp.float32
    ).astype(jnp.bfloat16)
    return picked.reshape(head_count, seq_count, row_count // seq_count * features).transpose(
        1, 0, 2
    )


def collect_rows(packed, placing, features):
    seq_count, head_count, flat_width = packed.shape
    row_block = packed.transpose(1, 0, 2).reshape(
        head_count, seq_count * flat_width // features, features
    )
    return jnp.einsum(
        "hri,hrf->hif", placing, row_block, preferred_element_type=jnp.float32
    ).astype(jnp.bfloat16)


def cluster_scores(queries, keys_in, segment_ids, score_scale):
    scores = (
        jnp.einsum("nqd,nkd->nqk", queries, keys_in, preferred_element_type=jnp.float32)
        * score_scale
    )
    allowed = segment_ids[:, :, None] == segment_ids[:, None, :]
    return (scores, allowed, jnp.where(allowed, scores, NEGATIVE))


def cluster_forward(queries, keys_in, values, segment_ids, score_scale):
    scores, allowed, masked = cluster_scores(queries, keys_in, segment_ids, score_scale)
    highest = jnp.max(masked, axis=-1, keepdims=True)
    raised = jnp.exp(masked - highest)
    totals = jnp.sum(raised, axis=-1, keepdims=True)
    weights = raised / totals
    attended = jnp.einsum(
        "nqk,nkd->nqd", weights.astype(jnp.bfloat16), values, preferred_element_type=jnp.float32
    ).astype(jnp.bfloat16)
    log_total = highest[:, :, 0] + jnp.log(totals[:, :, 0])
    entropy = log_total - jnp.sum(weights * jnp.where(allowed, scores, 0.0), axis=-1)
    occupied = jnp.sum(allowed.astype(jnp.float32), axis=-1)
    return (attended, log_total, entropy, occupied)


def cluster_backward(queries, keys_in, values, segment_ids, log_total, grad_out, score_scale):
    masked = cluster_scores(queries, keys_in, segment_ids, score_scale)[2]
    weights = jnp.exp(masked - log_total[:, :, None])
    weight_grads = jnp.einsum("nqd,nkd->nqk", grad_out, values, preferred_element_type=jnp.float32)
    value_grads = jnp.einsum(
        "nqk,nqd->nkd", weights.astype(jnp.bfloat16), grad_out, preferred_element_type=jnp.float32
    )
    score_grads = (
        weights * (weight_grads - jnp.sum(weights * weight_grads, axis=-1, keepdims=True))
    ).astype(jnp.bfloat16)
    query_grads = (
        jnp.einsum("nqk,nkd->nqd", score_grads, keys_in, preferred_element_type=jnp.float32)
        * score_scale
    )
    key_grads = (
        jnp.einsum("nqk,nqd->nkd", score_grads, queries, preferred_element_type=jnp.float32)
        * score_scale
    )
    return jnp.stack([query_grads, key_grads, value_grads], axis=2).astype(jnp.bfloat16)


MESH = pl.DeviceIdType.MESH


UNROLL = 4


def half_roll(block):
    return jnp.concatenate([block[:, 64:], block[:, :64]], axis=1)


def lanes(shape):
    return lax.broadcasted_iota(jnp.int32, shape, len(shape) - 1)


def bits(value, flip):
    return value + flip - 2 * value * flip


def coordinates():
    s, r = lax.axis_index("seq"), lax.axis_index("rep")
    return s // 4, (s // 2) % 2, s % 2, r // 2, r % 2


def device(zh, zl, x, y, c):
    return (4 * zh + 2 * zl + x, 2 * y + c)


def greet(peers):
    barrier = pltpu.get_barrier_semaphore()
    for peer in peers:
        pl.semaphore_signal(barrier, inc=1, device_id=peer, device_id_type=MESH)
    pl.semaphore_wait(barrier, len(peers))


def remote(src, dst, sems, index, peer):
    return pltpu.make_async_remote_copy(
        src_ref=src,
        dst_ref=dst,
        send_sem=sems[0].at[index],
        recv_sem=sems[1].at[index],
        device_id=peer,
        device_id_type=MESH,
    )


def dot(left, right, left_dim=1, right_dim=0):
    return lax.dot_general(
        left,
        right,
        (((left_dim,), (right_dim,)), ((), ())),
        preferred_element_type=jnp.float32,
    )


def hot(condition):
    return jnp.where(condition, 1.0, 0.0).astype(jnp.bfloat16)


def build_gather(order_ref, row, start, count, into):
    tokens = into.shape[1]

    def one(k, carry):
        at = pl.multiple_of(k * 128, 128)
        ids = order_ref[row : row + 1, pl.ds(pl.multiple_of(start + at, 128), 128)]
        column = jnp.broadcast_to(ids.astype(jnp.float32), (128, 128)).T
        lane = lanes((128, 128)).astype(jnp.float32)
        for t in range(tokens // 128):
            into[pl.ds(at, 128), t * 128 : (t + 1) * 128] = hot(column == lane + 128.0 * t)
        return carry

    lax.fori_loop(0, count // 128, one, 0)


def build_scatter(order_ref, row, start, count, into, base):
    def one(k, carry):
        at = pl.multiple_of(k * 128, 128)
        token = lax.broadcasted_iota(jnp.int32, (128, 128), 0) + at
        for p in range(count // 128):
            ids = order_ref[row : row + 1, pl.ds(pl.multiple_of(start + 128 * p, 128), 128)]
            into[pl.ds(at, 128), base + 128 * p : base + 128 * (p + 1)] = hot(ids == token)
        return carry

    lax.fori_loop(0, into.shape[0] // 128, one, 0)


def select_head(slab, half, place):
    return jnp.where(half == place, slab, half_roll(slab))


def join(low_lanes, high_lanes):
    return jnp.where(lanes(low_lanes.shape) < 64, low_lanes, high_lanes)


def pick_columns(pairs, j, c):
    (q_one, q_two), (k_one, k_two), (v_one, v_two) = pairs
    zero = jnp.zeros_like(q_one)
    q1, v1, k1 = select_head(q_one, c, 0), select_head(v_one, c, 1), select_head(k_one, c, 0)
    v2, q2, k2 = (
        select_head(v_two, j % 2, 0),
        select_head(q_two, j % 2, 1),
        select_head(k_two, j % 2, 1),
    )
    return join(q1, v1), join(k1, zero), join(v2, q2), join(zero, k2)


def forward_kernel(
    tokens_ref,
    cot_ref,
    seg_ref,
    orders_ref,
    owners_ref,
    query_bias_ref,
    value_bias_ref,
    wq_hbm,
    wk_hbm,
    wv_hbm,
    att_ref,
    x_my,
    cot_my,
    wsel_ref,
    order_ref,
    stats_ref,
    x_hbm,
    sorted_hbm,
    prob_hbm,
    x_all,
    sorted_ref,
    prob_ref,
    weights,
    orders_in,
    owners_in,
    owner_pad,
    seg_src,
    seg_all,
    bias_rows,
    bias_sel,
    tok,
    partial,
    gather,
    scatter,
    att_sorted,
    att_send,
    att_in,
    ent_ref,
    cnt_ref,
    swap_send,
    swap_recv,
    ring_send,
    ring_recv,
    seg_send,
    seg_recv,
    back_send,
    back_recv,
    local_sem,
):
    zh, zl, x, y, c = coordinates()
    j = 2 * zl + x
    p = 4 * c + j
    block, width = tokens_ref.shape
    group = 8 * block
    scale = 0.125
    swap = (swap_send, swap_recv)
    ring = (ring_send, ring_recv)
    seg_sems = (seg_send, seg_recv)
    back = (back_send, back_recv)

    def member(flip):
        fc, fz, fx = flip // 4, (flip // 2) % 2, flip % 2
        mc, mz, mx = bits(c, fc), bits(zl, fz), bits(x, fx)
        return device(zh, mz, mx, y, mc), 4 * mc + 2 * mz + mx

    swap_peer = device(1 - zh, zl, x, y, 1 - c)
    peers = [member(flip)[0] for flip in range(1, 8)]
    sibling = peers[3]
    over_x, over_z = peers[0], peers[1]
    matched = c == zh

    slabs = [
        pltpu.make_async_copy(
            src.at[:, pl.ds(pl.multiple_of(index * 128, 128), 128)],
            weights.at[i, slot],
            local_sem.at[3 * slot + i],
        )
        for i, src in enumerate((wq_hbm, wk_hbm, wv_hbm))
        for slot, index in enumerate((j, 4 + j // 2))
    ]
    for copy in slabs:
        copy.start()
    greet(peers + [swap_peer])
    seg_src[...] = jnp.broadcast_to(seg_ref[...], seg_src.shape)
    table_copies = [
        remote(orders_ref, orders_in, swap, 0, sibling),
        remote(owners_ref, owners_in, swap, 1, sibling),
    ]
    for copy in table_copies:
        copy.start()
    p_swap = 4 * (1 - c) + j
    halves = [pl.ds(i * (block // 2), block // 2) for i in range(2)]
    pairs = [(tokens_ref.at[at], x_all.at[p_swap, at], x_all.at[p, at]) for at in halves]
    pairs.insert(0, (seg_src, seg_all.at[p_swap], seg_all.at[p]))
    pairs.append((cot_ref, cot_my, cot_my))
    swaps = [remote(src, dst, swap, 2 + i, swap_peer) for i, (src, dst, _) in enumerate(pairs)]
    locals_ = [
        pltpu.make_async_copy(src, own, swap_recv.at[6 + i]) for i, (src, _, own) in enumerate(pairs)
    ]

    px, pz, pd = member(1)[1], member(2)[1], member(3)[1]

    def share_block(index, position, i, peer):
        view = x_all.at[position, halves[i]]
        return remote(view, view, ring, index, peer)

    own_to_x = [share_block(i, p, i, over_x) for i in range(2)]
    own_to_z = [share_block(2 + i, p, i, over_z) for i in range(2)]
    own_to_s = [share_block(4 + i, p, i, sibling) for i in range(2)]
    x_to_z = share_block(6, px, 0, over_z)
    z_to_x = share_block(7, pz, 1, over_x)
    x_to_s = [share_block(8 + i, px, i, sibling) for i in range(2)]
    z_to_s = [share_block(10 + i, pz, i, sibling) for i in range(2)]
    d_to_s = [share_block(12 + i, pd, i, sibling) for i in range(2)]
    seg_copies = [
        remote(seg_all.at[p], seg_all.at[p], seg_sems, flip - 1, peers[flip - 1]) for flip in range(1, 8)
    ]
    opposite = jnp.logical_not(matched)

    def own_half(i, arrivals):
        arrivals[1 + i].wait()
        own_to_x[i].start()
        own_to_z[i].start()
        own_to_s[i].start()

    def segments_out(arrivals):
        arrivals[0].wait()
        for copy in seg_copies:
            copy.start()

    def forward_first():
        own_to_x[0].wait()
        x_to_z.start()
        x_to_s[0].start()
        own_to_z[0].wait()
        z_to_s[0].start()

    def forward_second():
        own_to_z[1].wait()
        z_to_x.start()
        z_to_s[1].start()
        own_to_x[1].wait()
        x_to_s[1].start()

    def forward_last():
        x_to_z.wait()
        d_to_s[0].start()
        z_to_x.wait()
        d_to_s[1].start()

    def wait_sibling():
        for copy in own_to_s + x_to_s + z_to_s + d_to_s:
            copy.wait_recv()

    @pl.when(matched)
    def _():
        for copy in locals_:
            copy.start()
        segments_out(locals_)
        own_half(0, locals_)
        own_half(1, locals_)

    @pl.when(opposite)
    def _():
        for copy in swaps[:3]:
            copy.start()

    for copy in slabs:
        copy.wait()
    tiles = pick_columns([[weights[i, slot].astype(jnp.float32) for slot in range(2)] for i in range(3)], j, c)
    for i, tile in enumerate(tiles):
        wsel_ref[:, 128 * i : 128 * (i + 1)] = tile.astype(jnp.bfloat16)
    for i, ref in enumerate((query_bias_ref, None, value_bias_ref)):
        row = jnp.zeros((1, width), jnp.float32) if ref is None else ref[...].astype(jnp.float32).reshape(1, width)
        bias_rows[i : i + 1, :] = row
    bias_pairs = [
        [bias_rows[i : i + 1, pl.ds(pl.multiple_of(index * 128, 128), 128)] for index in (j, 4 + j // 2)]
        for i in range(3)
    ]
    for i, tile in enumerate(pick_columns(bias_pairs, j, c)):
        bias_sel[0:1, 128 * i : 128 * (i + 1)] = tile

    for copy in table_copies:
        copy.wait()
    h1, h2 = 2 * j + c, 8 + j
    for i, h in enumerate((h1, h2)):
        order_ref[i : i + 1, :] = jnp.where(matched, orders_ref[h], orders_in[h])
    half = 1024 * c

    build_gather(order_ref, 0, 0, group, gather.at[pl.ds(0, group)])

    @pl.when(matched)
    def _():
        forward_first()
        forward_second()

    @pl.when(opposite)
    def _():
        segments_out(swaps)
        own_half(0, swaps)

    build_gather(order_ref, 1, half, group // 2, gather.at[pl.ds(group, group // 2)])

    @pl.when(matched)
    def _():
        forward_last()

    @pl.when(opposite)
    def _():
        own_half(1, swaps)
        swaps[3].start()
        forward_first()

    def project(position):
        at = pl.ds(pl.multiple_of(position * block, block), block)
        out = dot(x_all[position], wsel_ref[...]) + bias_sel[0:1, :]
        ids = seg_all[position, 0:1, :].astype(jnp.float32)
        columns = [
            jnp.broadcast_to(ids[:, 128 * i : 128 * (i + 1)], (128, 128)).T for i in range(block // 128)
        ]
        lane = lanes((block, 128))
        seg_hot = hot(jnp.concatenate(columns, axis=0) == (lane % 64).astype(jnp.float32))
        low = out.astype(jnp.bfloat16)
        tok[at, 0:128] = low[:, 0:128]
        tok[at, 128:256] = jnp.where(lane < 64, low[:, 128:256], seg_hot)
        tok[at, 256:384] = low[:, 256:384]
        tok[at, 384:512] = jnp.where(lane < 64, seg_hot, low[:, 384:512])

    step = 512
    early, late = group // 2 * zh, group // 2 * (1 - zh)

    def gather_rows(start, add):
        tokens = pl.ds(pl.multiple_of(start, group // 2), group // 2)

        def one(first, columns):
            def body(k, carry):
                at = pl.ds(pl.multiple_of(k * step, step), step)
                rows = dot(gather[at, tokens], tok[tokens, columns])
                if add:
                    sorted_ref[at, :] = (rows + partial[at, :].astype(jnp.float32)).astype(jnp.bfloat16)
                else:
                    partial[at, :] = rows.astype(jnp.bfloat16)
                return carry

            return body

        lax.fori_loop(0, group // step, one(0, pl.ds(0, 256)), 0)
        lax.fori_loop(group // step, group * 3 // 2 // step, one(1, pl.ds(256, 256)), 0)

    for copy in seg_copies:
        copy.wait()
    pl.when(opposite)(wait_sibling)
    for k in range(4):
        project(4 * zh + k)

    @pl.when(opposite)
    def _():
        forward_second()

    gather_rows(early, False)

    @pl.when(opposite)
    def _():
        forward_last()

    pl.when(matched)(wait_sibling)
    for k in range(4):
        project(4 * (1 - zh) + k)
    stores = [
        pltpu.make_async_copy(src, dst, local_sem.at[6 + i])
        for i, (src, dst) in enumerate(((x_all, x_hbm), (sorted_ref, sorted_hbm), (prob_ref, prob_hbm)))
    ]
    stores[0].start()
    x_my[...] = x_all[p]

    gather_rows(late, True)
    build_scatter(order_ref, 0, 0, group, scatter, 0)
    build_scatter(order_ref, 1, half, group // 2, scatter, group)

    def attend(first_lanes):
        def one(i, carry):
            at = pl.ds(pl.multiple_of(i * 128, 128), 128)
            tile_zero, tile_one = sorted_ref[at, 0:128], sorted_ref[at, 128:256]
            low_lanes = lanes((128, 128)) < 64
            query_lanes = low_lanes if first_lanes else jnp.logical_not(low_lanes)
            queries = jnp.where(query_lanes, tile_zero, jnp.zeros_like(tile_zero))
            ids = jnp.where(query_lanes, jnp.zeros_like(tile_one), tile_one)
            scores = dot(queries, tile_one, 1, 1) * scale
            allowed = dot(ids, tile_one, 1, 1)
            masked = jnp.where(allowed > 0.5, scores, NEGATIVE)
            highest = jnp.max(masked, axis=1, keepdims=True)
            raised = jnp.exp(masked - highest)
            totals = jnp.sum(raised, axis=1, keepdims=True)
            weights = raised / totals
            prob_ref[at, :] = weights
            mixed = dot(weights.astype(jnp.bfloat16), tile_zero)
            att_sorted[at, :] = jnp.where(query_lanes, 0.0, mixed).astype(jnp.bfloat16)
            log_total = highest + jnp.log(totals)
            entropy = jnp.where(lanes((128, 128)) == 0, log_total, 0.0) - weights * masked
            ent_ref[pl.ds(i, 1), :] = jnp.sum(entropy, axis=0, keepdims=True)
            cnt_ref[pl.ds(i, 1), :] = jnp.sum(allowed, axis=0, keepdims=True)
            return carry

        return one

    lax.fori_loop(0, 16, attend(True), 0, unroll=UNROLL)
    lax.fori_loop(16, 24, attend(False), 0, unroll=UNROLL)
    stores[1].start()
    stores[2].start()

    def place(position):
        at = pl.ds(pl.multiple_of(position * block, block), block)
        return dot(scatter[at, :], att_sorted[...]).astype(jnp.bfloat16)

    back_copies = []
    for flip in (3, 7, 1, 5, 2, 6, 4):
        peer, position = member(flip)
        att_send[flip] = place(position)
        copy = remote(att_send.at[flip], att_in.at[p], back, flip - 1, peer)
        copy.start()
        back_copies.append(copy)
    att_in[p] = place(p)

    stats_ref[...] = jnp.zeros_like(stats_ref)
    owner_pad[...] = jnp.full_like(owner_pad, -1.0)
    clusters = owners_ref.shape[2]
    for h, first, size, skip in ((h1, 0, clusters, 0), (h2, clusters, clusters // 2, c)):
        ids = jnp.where(matched, owners_ref[h], owners_in[h])
        owner_pad[0:1, 0:clusters] = ids.astype(jnp.float32)
        column = jnp.broadcast_to(owner_pad[0:1, :], (128, 128)).T
        column = jnp.where(skip == 1, column[clusters // 2 : clusters // 2 + size], column[0:size])
        owned = jnp.where(column == lanes((size, 128)).astype(jnp.float32), 1.0, 0.0)
        for kind, (lane_sums, divisor) in enumerate(((ent_ref, 4.0 * block), (cnt_ref, 4.0 * block * 128))):
            sums = jnp.sum(lane_sums[first : first + size, :], axis=1, keepdims=True) / divisor
            stats_ref[kind, pl.ds(h, 1), :] = jnp.sum(sums * owned, axis=0, keepdims=True)

    @pl.when(matched)
    def _():
        locals_[3].wait()

    @pl.when(jnp.logical_not(matched))
    def _():
        swaps[3].wait()

    for copy in back_copies:
        copy.wait()
    for copy in stores:
        copy.wait()
    for copy in own_to_s + x_to_s + z_to_s + d_to_s:
        copy.wait_send()
    for pair in range(4):
        even, odd = att_in[pair], att_in[4 + pair]
        att_ref[:, 128 * pair : 128 * (pair + 1)] = join(half_roll(even), odd)
    for pair in range(2):
        low_half = att_in[2 * pair] + att_in[4 + 2 * pair]
        high_half = att_in[2 * pair + 1] + att_in[5 + 2 * pair]
        att_ref[:, 512 + 128 * pair : 640 + 128 * pair] = join(low_half, half_roll(high_half))


def forward_attention(
    tokens, cotangent, segments, orders, owners, query_bias, value_bias, wq, wk, wv
):
    block, width = tokens.shape
    group = 8 * block
    low, full = jnp.bfloat16, jnp.float32
    vmem = pl.BlockSpec(memory_space=pltpu.VMEM)
    hbm = pl.BlockSpec(memory_space=pl.ANY)
    dma = pltpu.SemaphoreType.DMA
    shape = jax.ShapeDtypeStruct
    rows = group * 3 // 2
    return pl.pallas_call(
        forward_kernel,
        out_shape=[
            shape((block, width), low),
            shape((block, width), low),
            shape((block, width), low),
            shape((width, 512), low),
            shape((8, group), jnp.int32),
            shape((2, 16, 128), full),
            shape((8, block, width), low),
            shape((rows, 256), low),
            shape((rows, 128), full),
        ],
        in_specs=[vmem] * 7 + [hbm] * 3,
        out_specs=[vmem] * 6 + [hbm] * 3,
        scratch_shapes=[
            pltpu.VMEM((8, block, width), low),
            pltpu.VMEM((rows, 256), low),
            pltpu.VMEM((rows, 128), full),
            pltpu.VMEM((3, 2, width, 128), low),
            pltpu.VMEM(orders.shape, jnp.int32),
            pltpu.VMEM(owners.shape, jnp.int32),
            pltpu.VMEM((8, 128), full),
            pltpu.VMEM((8, block), jnp.int32),
            pltpu.VMEM((8, 8, block), jnp.int32),
            pltpu.VMEM((8, width), full),
            pltpu.VMEM((8, 512), full),
            pltpu.VMEM((group, 512), low),
            pltpu.VMEM((rows, 256), low),
            pltpu.VMEM((rows, group), low),
            pltpu.VMEM((group, rows), low),
            pltpu.VMEM((rows, 128), low),
            pltpu.VMEM((8, block, 128), low),
            pltpu.VMEM((8, block, 128), low),
            pltpu.VMEM((24, 128), full),
            pltpu.VMEM((24, 128), full),
            dma((10,)),
            dma((10,)),
            dma((14,)),
            dma((14,)),
            dma((7,)),
            dma((7,)),
            dma((7,)),
            dma((7,)),
            dma((9,)),
        ],
        compiler_params=pltpu.CompilerParams(
            collective_id=1, has_side_effects=True, vmem_limit_bytes=60 << 20
        ),
        name="forward_attention",
    )(tokens, cotangent, segments, orders, owners, query_bias, value_bias, wq, wk, wv)


def normalize(hidden):
    centre = hidden - jnp.mean(hidden, axis=1, keepdims=True)
    root_inverse = lax.rsqrt(jnp.mean(centre * centre, axis=1, keepdims=True) + EPSILON)
    return centre * root_inverse, root_inverse


def normalize_back(scaled, normed, root_inverse):
    return root_inverse * (
        scaled
        - jnp.mean(scaled, axis=1, keepdims=True)
        - normed * jnp.mean(scaled * normed, axis=1, keepdims=True)
    )


def mlp_kernel(
    tile,
    att_ref,
    x_ref,
    cot_ref,
    out_bias_ref,
    first_gain_ref,
    first_shift_ref,
    outer_bias_ref,
    second_gain_ref,
    second_shift_ref,
    inner_bias_ref,
    out_w_hbm,
    inner_w_hbm,
    outer_w_hbm,
    output_ref,
    delta_ref,
    datt_ref,
    low_ref,
    dsecond_ref,
    dbranch_ref,
    vec_out,
    act_hbm,
    dinner_hbm,
    act_ref,
    dinner_ref,
    bias_ref,
    out_w,
    inner_w,
    outer_w,
    slope,
    total,
    normed_ref,
    first_ref,
    load_sem,
):
    width = x_ref.shape[1]
    inner_width = inner_w.shape[1]
    tiles = inner_width // tile
    parts = [slice(tile * t, tile * (t + 1)) for t in range(tiles)]
    loads = [pltpu.make_async_copy(out_w_hbm, out_w, load_sem.at[0])]
    for t, at in enumerate(parts):
        loads.append(
            pltpu.make_async_copy(inner_w_hbm.at[:, at], inner_w.at[:, at], load_sem.at[1 + 2 * t])
        )
        loads.append(pltpu.make_async_copy(outer_w_hbm.at[at], outer_w.at[at], load_sem.at[2 + 2 * t]))
    for copy in loads:
        copy.start()
    stores = [
        [
            pltpu.make_async_copy(src.at[:, at], dst.at[:, at], load_sem.at[1 + 2 * tiles + 2 * t + i])
            for i, (src, dst) in enumerate(((act_ref, act_hbm), (dinner_ref, dinner_hbm)))
        ]
        for t, at in enumerate(parts)
    ]
    bias_ref[0:1, :] = inner_bias_ref[...].astype(jnp.float32).reshape(1, inner_width)
    out_bias, first_gain, first_shift, outer_bias, second_gain, second_shift = (
        ref[...].astype(jnp.float32).reshape(1, width)
        for ref in (
            out_bias_ref,
            first_gain_ref,
            first_shift_ref,
            outer_bias_ref,
            second_gain_ref,
            second_shift_ref,
        )
    )
    loads[0].wait()
    branch = dot(att_ref[...], out_w[...]) + out_bias
    normed, root_one = normalize(x_ref[...].astype(jnp.float32) + branch)
    first = normed * first_gain + first_shift
    first_ref[...] = first
    normed_ref[...] = normed
    low_ref[...] = first.astype(jnp.bfloat16)
    total[...] = jnp.zeros_like(total)

    for t, at in enumerate(parts):
        loads[1 + 2 * t].wait()
        inner = dot(low_ref[...], inner_w[:, at]) + bias_ref[0:1, at]
        cumulative = 0.5 + 0.5 * lax.erf(inner * (0.5**0.5))
        density = jnp.exp(-0.5 * inner * inner) * 0.3989422804014327
        slope[:, at] = cumulative + inner * density
        act = (inner * cumulative).astype(jnp.bfloat16)
        act_ref[:, at] = act
        stores[t][0].start()
        loads[2 + 2 * t].wait()
        total[...] += dot(act, outer_w[at, :])
    normed_two, root_two = normalize(first_ref[...] + total[...] + outer_bias)
    output_ref[...] = (normed_two * second_gain + second_shift).astype(jnp.bfloat16)
    upstream = cot_ref[...].astype(jnp.float32)
    vec_out[4:5, :] = jnp.sum(upstream * normed_two, axis=0, keepdims=True)
    vec_out[5:6, :] = jnp.sum(upstream, axis=0, keepdims=True)
    delta_two = normalize_back(upstream * second_gain, normed_two, root_two)
    low_two = delta_two.astype(jnp.bfloat16)
    dsecond_ref[...] = low_two
    vec_out[3:4, :] = jnp.sum(low_two.astype(jnp.float32), axis=0, keepdims=True)
    total[...] = delta_two
    for t, at in enumerate(parts):
        dact = dot(dsecond_ref[...], outer_w[at, :], 1, 1)
        dinner = (dact * slope[:, at]).astype(jnp.bfloat16)
        dinner_ref[:, at] = dinner
        stores[t][1].start()
        bias_ref[0:1, at] = jnp.sum(dinner.astype(jnp.float32), axis=0, keepdims=True)
        total[...] += dot(dinner, inner_w[:, at], 1, 1)
    for i in range(inner_width // width):
        vec_out[6 + i : 7 + i, :] = bias_ref[0:1, width * i : width * (i + 1)]
    delta_first = total[...]
    normed = normed_ref[...]
    vec_out[1:2, :] = jnp.sum(delta_first * normed, axis=0, keepdims=True)
    vec_out[2:3, :] = jnp.sum(delta_first, axis=0, keepdims=True)
    delta_one = normalize_back(delta_first * first_gain, normed, root_one)
    delta_ref[...] = delta_one
    low_one = delta_one.astype(jnp.bfloat16)
    dbranch_ref[...] = low_one
    vec_out[0:1, :] = jnp.sum(low_one.astype(jnp.float32), axis=0, keepdims=True)
    vec_out[10:16, :] = jnp.zeros((6, width), jnp.float32)
    datt_ref[...] = dot(low_one, out_w[...], 1, 1).astype(jnp.bfloat16)
    for pair in stores:
        for copy in pair:
            copy.wait()


def mlp(att, x_my, cot_my, vectors, out_weight, inner_weight, outer_weight, tile):
    block, width = x_my.shape
    inner_width = inner_weight.shape[1]
    low, full = jnp.bfloat16, jnp.float32
    vmem = pl.BlockSpec(memory_space=pltpu.VMEM)
    hbm = pl.BlockSpec(memory_space=pl.ANY)
    shape = jax.ShapeDtypeStruct
    return pl.pallas_call(
        functools.partial(mlp_kernel, tile),
        out_shape=[
            shape((block, width), low),
            shape((block, width), full),
            shape((block, width), low),
            shape((block, width), low),
            shape((block, width), low),
            shape((block, width), low),
            shape((16, width), full),
            shape((block, inner_width), low),
            shape((block, inner_width), low),
        ],
        in_specs=[vmem] * 10 + [hbm] * 3,
        out_specs=[vmem] * 7 + [hbm] * 2,
        scratch_shapes=[
            pltpu.VMEM((block, inner_width), low),
            pltpu.VMEM((block, inner_width), low),
            pltpu.VMEM((8, inner_width), full),
            pltpu.VMEM(out_weight.shape, low),
            pltpu.VMEM(inner_weight.shape, low),
            pltpu.VMEM(outer_weight.shape, low),
            pltpu.VMEM((block, inner_width), full),
            pltpu.VMEM((block, width), full),
            pltpu.VMEM((block, width), full),
            pltpu.VMEM((block, width), full),
            pltpu.SemaphoreType.DMA((1 + 4 * (inner_width // tile),)),
        ],
        compiler_params=pltpu.CompilerParams(vmem_limit_bytes=60 << 20),
        name="mlp",
    )(att, x_my, cot_my, *vectors, out_weight, inner_weight, outer_weight)


def rows_of(start, q, size):
    return pl.ds(pl.multiple_of(start * q, 16), size * q)


def add_into(count, target, other):
    def one(i, carry):
        target(i)[...] = (
            target(i)[...].astype(jnp.float32) + other(i)[...].astype(jnp.float32)
        ).astype(jnp.bfloat16)
        return carry

    lax.fori_loop(0, count, one, 0)


def reduce_steps(parts, g_ref, f_ref, buffers, sems):
    core_in, a_one, b_one, ab_two, z_one, z_two = buffers
    zh, zl, x, y, c = coordinates()
    q = g_ref.shape[3] // 8
    width = g_ref.shape[4] // parts
    over_c, over_y = device(zh, zl, x, y, 1 - c), device(zh, zl, x, 1 - y, c)
    over_x, over_zl = device(zh, zl, 1 - x, y, c), device(zh, 1 - zl, x, y, c)
    over_zh = device(1 - zh, zl, x, y, c)

    def send(step, k, src, dst, peer):
        copy = remote(src, dst, (sems[0].at[step], sems[1].at[step]), k, peer)
        copy.start()
        return copy

    columns = [pl.ds(k * width, width) for k in range(parts)]
    zero = [
        send(
            0, k, g_ref.at[:, :, :, rows_of(4 * (1 - c), q, 4), cols], core_in.at[:, :, :, :, cols], over_c
        )
        for k, cols in enumerate(columns)
    ]
    yield
    first, second, third, fourth, fifth, sixth = [], [], [], [], [], []
    for k, cols in enumerate(columns):
        zero[k].wait()
        add_into(
            8,
            lambda i: core_in.at[i // 4, (i // 2) % 2, i % 2, :, cols],
            lambda i: g_ref.at[i // 4, (i // 2) % 2, i % 2, rows_of(4 * c, q, 4), cols],
        )
        first.append(
            (
                send(1, k, core_in.at[:, :, 1 - x, pl.ds(0, 2 * q), cols], a_one.at[:, :, :, cols], over_x),
                send(2, k, core_in.at[:, :, :, rows_of(3 - y, q, 1), cols], b_one.at[:, :, :, :, cols], over_y),
            )
        )
        yield
    for k, cols in enumerate(columns):
        first[k][0].wait()
        add_into(
            4,
            lambda i: a_one.at[i // 2, i % 2, :, cols],
            lambda i: core_in.at[i // 2, i % 2, x, pl.ds(0, 2 * q), cols],
        )
        copy_a = send(3, k, a_one.at[:, :, rows_of(1 - y, q, 1), cols], ab_two.at[0, :, :, :, cols], over_y)
        first[k][1].wait()
        add_into(
            8,
            lambda i: b_one.at[i // 4, (i // 2) % 2, i % 2, :, cols],
            lambda i: core_in.at[i // 4, (i // 2) % 2, i % 2, rows_of(2 + y, q, 1), cols],
        )
        copy_b = send(4, k, b_one.at[:, :, 1 - x, :, cols], ab_two.at[1, :, :, :, cols], over_x)
        second.append((copy_a, copy_b))
        yield
    for k, cols in enumerate(columns):
        second[k][0].wait()
        add_into(
            4,
            lambda i: ab_two.at[0, i // 2, i % 2, :, cols],
            lambda i: a_one.at[i // 2, i % 2, rows_of(y, q, 1), cols],
        )
        second[k][1].wait()
        add_into(
            4,
            lambda i: ab_two.at[1, i // 2, i % 2, :, cols],
            lambda i: b_one.at[i // 2, i % 2, x, :, cols],
        )
        third.append(send(5, k, ab_two.at[:, :, 1 - zl, :, cols], z_one.at[:, :, :, cols], over_zl))
        yield
    for k, cols in enumerate(columns):
        third[k].wait()
        add_into(
            4,
            lambda i: z_one.at[i // 2, i % 2, :, cols],
            lambda i: ab_two.at[i // 2, i % 2, zl, :, cols],
        )
        fourth.append(send(6, k, z_one.at[:, 1 - zh, :, cols], z_two.at[:, :, cols], over_zh))
        yield
    for k, cols in enumerate(columns):
        fourth[k].wait()
        for part in range(2):
            f_ref[c, part, y, :, cols] = (
                z_two[part, :, cols].astype(jnp.float32) + z_one[part, zh, :, cols].astype(jnp.float32)
            ).astype(jnp.bfloat16)
        own_rows = f_ref.at[c, :, y, :, cols]
        fifth.append(send(7, k, own_rows, own_rows, over_y))
        yield
    for k, cols in enumerate(columns):
        fifth[k].wait()
        both = f_ref.at[c, :, :, :, cols]
        sixth.append(send(8, k, both, both, over_c))
        yield
    for copy in sixth:
        copy.wait()


def backward_kernel(
    parts,
    datt_ref,
    order_ref,
    out_my,
    stats_ref,
    vec_ref,
    att_hbm,
    dbranch_hbm,
    low_hbm,
    dsecond_hbm,
    act_hbm,
    dinner_hbm,
    sorted_hbm,
    prob_hbm,
    wsel_hbm,
    x_hbm,
    delta_hbm,
    out_home,
    grad_home,
    f_ref,
    w_all,
    stats_out,
    att_ref,
    dbranch_ref,
    low_ref,
    dsecond_ref,
    act_ref,
    dinner_ref,
    sorted_ref,
    prob_ref,
    wsel_ref,
    x_all,
    delta_ref,
    g_ref,
    datt_send,
    datt_in,
    gather,
    gathered,
    dsorted,
    scatter,
    dqkv,
    part_send,
    part_in,
    total,
    a_in,
    b_in,
    a_two,
    b_two,
    grad_my,
    dw,
    dw_y,
    dw_in,
    dw_all,
    stats_buf,
    stats_in,
    core_in,
    a_one,
    b_one,
    ab_two,
    z_one,
    z_two,
    datt_ssem,
    datt_rsem,
    part_ssem,
    part_rsem,
    swap_ssem,
    swap_rsem,
    dw_ssem,
    dw_rsem,
    stats_ssem,
    stats_rsem,
    red_ssem,
    red_rsem,
    load_sem,
):
    zh, zl, x, y, c = coordinates()
    s = 4 * zh + 2 * zl + x
    j = 2 * zl + x
    p = 4 * c + j
    block, width = datt_ref.shape
    group = 8 * block
    scale = 0.125
    matched = c == zh
    datt_sems, part_sems = (datt_ssem, datt_rsem), (part_ssem, part_rsem)
    swap_sems, dw_sems, stats_sems = (swap_ssem, swap_rsem), (dw_ssem, dw_rsem), (stats_ssem, stats_rsem)

    def member(flip):
        fc, fz, fx = flip // 4, (flip // 2) % 2, flip % 2
        mc, mz, mx = bits(c, fc), bits(zl, fz), bits(x, fx)
        return device(zh, mz, mx, y, mc), mc, 2 * mz + mx

    peers = [member(flip)[0] for flip in range(1, 8)]
    sibling, over_x, over_z = peers[3], peers[0], peers[1]
    swap_peer = device(1 - zh, zl, x, y, 1 - c)
    over_y = device(zh, zl, x, 1 - y, c)
    across = [device(1 - zh, bits(zl, f // 2), bits(x, f % 2), y, c) for f in range(4)]
    loads = [
        pltpu.make_async_copy(src, dst, load_sem.at[i])
        for i, (src, dst) in enumerate(
            (
                (att_hbm, att_ref),
                (dbranch_hbm, dbranch_ref),
                (low_hbm, low_ref),
                (dsecond_hbm, dsecond_ref),
                (act_hbm, act_ref),
                (dinner_hbm, dinner_ref),
                (sorted_hbm, sorted_ref),
                (prob_hbm, prob_ref),
                (wsel_hbm, wsel_ref),
                (x_hbm, x_all),
                (delta_hbm, delta_ref),
            )
        )
    ]
    for copy in loads:
        copy.start()
    greet(peers + [swap_peer, over_y] + across)

    def home_copy(src, dst, index, start):
        away = remote(src, dst, swap_sems, index, swap_peer)
        here = pltpu.make_async_copy(src, dst, swap_rsem.at[3 + index])

        @pl.when(matched)
        def _():
            here.start() if start else here.wait()

        @pl.when(jnp.logical_not(matched))
        def _():
            away.start() if start else away.wait()

    def tile(mc, mj):
        first = datt_ref[:, pl.ds(pl.multiple_of(mj * 128, 128), 128)]
        other = datt_ref[:, pl.ds(pl.multiple_of((4 + mj // 2) * 128, 128), 128)]
        return join(
            select_head(other.astype(jnp.float32), mj % 2, 0), select_head(first.astype(jnp.float32), mc, 1)
        ).astype(jnp.bfloat16)

    datt_copies = []
    for flip in (3, 7, 1, 5, 2, 6, 4):
        peer, mc, mj = member(flip)
        datt_send[flip] = tile(mc, mj)
        copy = remote(datt_send.at[flip], datt_in.at[p], datt_sems, flip - 1, peer)
        copy.start()
        datt_copies.append(copy)
    datt_in[p] = tile(c, j)

    def stats_steps():
        stats_buf[0] = stats_ref[...]
        stats_peers = (sibling, over_x, over_z, across[0], over_y)
        for k, peer in enumerate(stats_peers):
            copy = remote(stats_buf.at[k], stats_in.at[k], stats_sems, k, peer)
            copy.start()
            yield
            copy.wait()
            stats_buf[k + 1] = stats_buf[k] + stats_in[k]
        stats_out[...] = stats_buf[len(stats_peers)]
        yield

    totals = stats_steps()
    next(totals)

    share = width // 8
    q = g_ref.shape[3] // 8
    top = 4 * q

    def outer_grads():
        def one(d, carry):
            columns = pl.ds(pl.multiple_of(d * 4 * share, 128), 4 * share)
            g_ref[d // 4, (d // 2) % 2, d % 2, top : top + 4 * share, :] = dot(
                act_ref[:, columns], dsecond_ref[...], 0, 0
            ).astype(jnp.bfloat16)
            return carry

        lax.fori_loop(0, 8, one, 0)

    def inner_grads():
        def one(i, carry):
            z, n = i // 4, i % 4
            rows = pl.ds(pl.multiple_of(z * 4 * share, 128), 4 * share)
            columns = pl.ds(pl.multiple_of(n * width, 128), width)
            grads = dot(low_ref[:, rows], dinner_ref[:, columns], 0, 0).astype(jnp.bfloat16)
            for k in range(4):
                at = pl.ds(pl.multiple_of(n * share, 16), share)
                g_ref[z, k // 2, k % 2, at, :] = grads[share * k : share * (k + 1)]
            return carry

        lax.fori_loop(0, 8, one, 0)

    for copy in loads[:6]:
        copy.wait()
    vectors = vec_ref[...].astype(jnp.bfloat16)
    for z in range(2):
        grads = dot(att_ref[:, 4 * share * z : 4 * share * (z + 1)], dbranch_ref[...], 0, 0).astype(jnp.bfloat16)
        for k in range(4):
            rows = grads[share * k : share * (k + 1)]
            g_ref[z, k // 2, k % 2, 4 * share : 4 * share + share // 2, :] = rows[: share // 2]
            g_ref[z, k // 2, k % 2, 4 * share + share // 2 : top, :] = jnp.zeros_like(vectors)
            g_ref[z, k // 2, k % 2, top + 4 * share : top + 4 * share + share // 2, :] = rows[share // 2 :]
            g_ref[z, k // 2, k % 2, top + 4 * share + share // 2 :, :] = vectors
    pl.when(c == 0)(outer_grads)
    pl.when(c == 1)(inner_grads)
    reduction = reduce_steps(
        parts,
        g_ref,
        f_ref,
        (core_in, a_one, b_one, ab_two, z_one, z_two),
        (red_ssem, red_rsem),
    )
    next(reduction)
    pl.when(c == 0)(inner_grads)
    pl.when(c == 1)(outer_grads)

    half = 1024 * c
    step = gather.shape[1]
    chunks = group * 3 // 2 // step

    def build(k):
        head, start = (0, k * step) if k * step < group else (1, half + k * step - group)
        build_gather(order_ref, head, start, step, gather.at[k % 2])

    def take(k):
        gathered[k * step : (k + 1) * step, :] = dot(
            gather[k % 2], datt_in[...].reshape(group, 128)
        ).astype(jnp.bfloat16)

    next(totals)
    build(0)
    next(reduction)
    build(1)
    for copy in datt_copies:
        copy.wait()
    take(0)
    build(2)
    take(1)
    next(reduction)
    build(3)
    take(2)
    build(4)
    take(3)
    next(totals)
    next(reduction)
    build(5)
    take(4)
    take(5)
    for copy in loads[6:]:
        copy.wait()
    home_copy(out_my, out_home, 0, True)

    def attend_back(first_lanes):
        def one(i, carry):
            at = pl.ds(pl.multiple_of(i * 128, 128), 128)
            tile_zero, tile_one = sorted_ref[at, 0:128], sorted_ref[at, 128:256]
            low_lanes = lanes((128, 128)) < 64
            query_lanes = low_lanes if first_lanes else jnp.logical_not(low_lanes)
            weights = prob_ref[at, :]
            taken = gathered[at, :]
            taken = jnp.where(query_lanes, jnp.zeros_like(taken), taken)
            weight_grads = dot(taken, tile_zero, 1, 1)
            inside = jnp.sum(weights * weight_grads, axis=1, keepdims=True)
            score_grads = weights * (weight_grads - inside)
            low_grads = score_grads.astype(jnp.bfloat16)
            query_grads = dot(low_grads, tile_one) * scale
            key_grads = dot(low_grads, tile_zero, 0, 0) * scale
            value_grads = dot(weights.astype(jnp.bfloat16), taken, 0, 0)
            dsorted[at, 0:128] = jnp.where(query_lanes, query_grads, value_grads).astype(jnp.bfloat16)
            dsorted[at, 128:256] = jnp.where(query_lanes, key_grads, 0.0).astype(jnp.bfloat16)
            return carry

        return one

    lax.fori_loop(0, 8, attend_back(True), 0, unroll=4)
    next(totals)
    next(reduction)
    lax.fori_loop(8, 16, attend_back(True), 0, unroll=4)
    next(totals)
    lax.fori_loop(16, 24, attend_back(False), 0, unroll=4)
    next(reduction)

    def place(position):
        token = lax.broadcasted_iota(jnp.int32, (128, 128), 0) + position * block
        for t in range(block // 128):
            for head, start, count, base in ((0, 0, group, 0), (1, half, group // 2, group)):
                for k in range(count // 128):
                    ids = order_ref[head : head + 1, pl.ds(pl.multiple_of(start + 128 * k, 128), 128)]
                    scatter[128 * t : 128 * (t + 1), base + 128 * k : base + 128 * (k + 1)] = hot(
                        ids == token + 128 * t
                    )
        at = pl.ds(pl.multiple_of(position * block, block), block)
        dqkv[at, 0:256] = dot(scatter[:, 0:group], dsorted[0:group, :]).astype(jnp.bfloat16)
        dqkv[at, 256:512] = dot(scatter[:, group:], dsorted[group:, :]).astype(jnp.bfloat16)
        return dot(dqkv[at, :], wsel_ref[...], 1, 1)

    def away(k, carry):
        part_send[k] = place(4 * (1 - c) + k).astype(jnp.bfloat16)
        remote(part_send.at[k], part_in.at[k], part_sems, k, sibling).start()
        return carry

    lax.fori_loop(0, 4, away, 0)

    def here(k, carry):
        part = place(4 * c + k)
        remote(part_send.at[k], part_in.at[k], part_sems, k, sibling).wait()
        total[k // 2, k % 2] = (part + part_in[k].astype(jnp.float32)).astype(jnp.bfloat16)
        return carry

    lax.fori_loop(0, 4, here, 0)
    upper, lower = pl.ds(0, block // 2), pl.ds(block // 2, block // 2)
    pieces = [pl.ds(i * (width // 2), width // 2) for i in range(2)]
    a_copies, b_copies = [], []
    for i, cols in enumerate(pieces):
        a_copies.append(remote(total.at[:, 1 - x, upper, cols], a_in.at[:, :, cols], part_sems, 4 + i, over_x))
        b_copies.append(remote(total.at[1 - zl, :, lower, cols], b_in.at[:, :, cols], part_sems, 6 + i, over_z))
        a_copies[i].start()
        b_copies[i].start()
    next(reduction)

    for k in range(width // 128):
        dw[128 * k : 128 * (k + 1), :] = dot(
            x_all[:, 128 * k : 128 * (k + 1)], dqkv[...], 0, 0
        ).astype(jnp.bfloat16)
    bias_row = jnp.broadcast_to(
        jnp.sum(dqkv[...].astype(jnp.float32), axis=0, keepdims=True), (16, 512)
    ).astype(jnp.bfloat16)
    for d in range(8):
        for h in range(2):
            dw_y[h, d, 0:share, :] = dw[share * d : share * (d + 1), 256 * h : 256 * (h + 1)]
            dw_y[h, d, share : share + 16, :] = bias_row[:, 256 * h : 256 * (h + 1)]
    over_y_copy = remote(dw_y.at[1 - y], dw_in, dw_sems, 0, over_y)
    over_y_copy.start()

    a_next, b_next = [], []
    for i, cols in enumerate(pieces):
        a_copies[i].wait()
        add_into(2, lambda k: a_in.at[k, :, cols], lambda k: total.at[k, x, upper, cols])
        a_next.append(remote(a_in.at[1 - zl, :, cols], a_two.at[:, cols], part_sems, 8 + i, over_z))
        a_next[i].start()
        b_copies[i].wait()
        add_into(2, lambda k: b_in.at[k, :, cols], lambda k: total.at[zl, k, lower, cols])
        b_next.append(remote(b_in.at[1 - x, :, cols], b_two.at[:, cols], part_sems, 10 + i, over_x))
        b_next[i].start()
    over_y_copy.wait()
    add_into(8, lambda i: dw_y.at[y, i], lambda i: dw_in.at[i])
    dw_copies = []
    targets = across + [over_x, over_z, peers[2]]
    flips = [(1, f // 2, f % 2) for f in range(4)] + [(0, 0, 1), (0, 1, 0), (0, 1, 1)]
    for i, (peer, (fh, fz, fx)) in enumerate(zip(targets, flips)):
        d = 4 * bits(zh, fh) + 2 * bits(zl, fz) + bits(x, fx)
        copy = remote(dw_y.at[y, d], dw_all.at[s], dw_sems, 1 + i, peer)
        copy.start()
        dw_copies.append(copy)
    dw_all[s] = dw_y[y, s]
    for i, cols in enumerate(pieces):
        a_next[i].wait()
        b_next[i].wait()
        for start, first, second, index in ((0, a_two, a_in, zl), (block // 2, b_two, b_in, x)):
            at = pl.ds(start, block // 2)
            grad_my[at, cols] = (
                delta_ref[at, cols]
                + first[:, cols].astype(jnp.float32)
                + second[index, :, cols].astype(jnp.float32)
            ).astype(jnp.bfloat16)
        home_copy(grad_my.at[:, cols], grad_home.at[:, cols], 1 + i, True)
    next(totals)
    for _ in range(parts):
        next(reduction)

    for copy in dw_copies:
        copy.wait()
    for k in range(4):
        w_all[y, c, k] = (dw_all[k].astype(jnp.float32) + dw_all[4 + k].astype(jnp.float32)).astype(
            jnp.bfloat16
        )
    w_copy = remote(w_all.at[y, c], w_all.at[y, c], dw_sems, 8, over_y)
    w_copy.start()
    for _ in range(parts):
        next(reduction)
    w_copy.wait()
    w_copy = remote(w_all.at[:, c], w_all.at[:, c], dw_sems, 9, sibling)
    w_copy.start()
    for _ in reduction:
        pass
    w_copy.wait()
    home_copy(out_my, out_home, 0, False)
    for i, cols in enumerate(pieces):
        home_copy(grad_my.at[:, cols], grad_home.at[:, cols], 1 + i, False)


def backward_attention(
    datt,
    order,
    output,
    stats,
    vectors,
    att,
    dbranch,
    low_first,
    dsecond,
    act,
    dinner,
    sorted_rows,
    prob,
    wsel,
    x_all,
    delta,
    parts,
):
    block, width = datt.shape
    inner_width = act.shape[1]
    group = 8 * block
    rows = group * 3 // 2
    q = (9 * width // 8 + 32) // 8
    share = width // 8 + 16
    low, full = jnp.bfloat16, jnp.float32
    vmem = pl.BlockSpec(memory_space=pltpu.VMEM)
    hbm = pl.BlockSpec(memory_space=pl.ANY)
    dma = pltpu.SemaphoreType.DMA
    shape = jax.ShapeDtypeStruct
    return pl.pallas_call(
        functools.partial(backward_kernel, parts),
        out_shape=[
            shape((block, width), low),
            shape((block, width), low),
            shape((2, 2, 2, q, width), low),
            shape((2, 2, 4, share, 256), low),
            shape(stats.shape, full),
        ],
        in_specs=[vmem] * 5 + [hbm] * 11,
        out_specs=[vmem] * 5,
        scratch_shapes=[
            pltpu.VMEM((block, width), low),
            pltpu.VMEM((block, width), low),
            pltpu.VMEM((block, width), low),
            pltpu.VMEM((block, width), low),
            pltpu.VMEM((block, inner_width), low),
            pltpu.VMEM((block, inner_width), low),
            pltpu.VMEM((rows, 256), low),
            pltpu.VMEM((rows, 128), full),
            pltpu.VMEM((width, 512), low),
            pltpu.VMEM((group, width), low),
            pltpu.VMEM((block, width), full),
            pltpu.VMEM((2, 2, 2, 8 * q, width), low),
            pltpu.VMEM((8, block, 128), low),
            pltpu.VMEM((8, block, 128), low),
            pltpu.VMEM((2, 512, group), low),
            pltpu.VMEM((rows, 128), low),
            pltpu.VMEM((rows, 256), low),
            pltpu.VMEM((block, rows), low),
            pltpu.VMEM((group, 512), low),
            pltpu.VMEM((4, block, width), low),
            pltpu.VMEM((4, block, width), low),
            pltpu.VMEM((2, 2, block, width), low),
            pltpu.VMEM((2, block // 2, width), low),
            pltpu.VMEM((2, block // 2, width), low),
            pltpu.VMEM((block // 2, width), low),
            pltpu.VMEM((block // 2, width), low),
            pltpu.VMEM((block, width), low),
            pltpu.VMEM((width, 512), low),
            pltpu.VMEM((2, 8, share, 256), low),
            pltpu.VMEM((8, share, 256), low),
            pltpu.VMEM((8, share, 256), low),
            pltpu.VMEM((6,) + stats.shape, full),
            pltpu.VMEM((5,) + stats.shape, full),
            pltpu.VMEM((2, 2, 2, 4 * q, width), low),
            pltpu.VMEM((2, 2, 2 * q, width), low),
            pltpu.VMEM((2, 2, 2, q, width), low),
            pltpu.VMEM((2, 2, 2, q, width), low),
            pltpu.VMEM((2, 2, q, width), low),
            pltpu.VMEM((2, q, width), low),
            dma((7,)),
            dma((7,)),
            dma((12,)),
            dma((12,)),
            dma((6,)),
            dma((6,)),
            dma((10,)),
            dma((10,)),
            dma((5,)),
            dma((5,)),
            dma((9, parts)),
            dma((9, parts)),
            dma((11,)),
        ],
        compiler_params=pltpu.CompilerParams(
            collective_id=2, has_side_effects=True, vmem_limit_bytes=62 << 20
        ),
        name="backward_attention",
    )(
        datt,
        order,
        output,
        stats,
        vectors,
        att,
        dbranch,
        low_first,
        dsecond,
        act,
        dinner,
        sorted_rows,
        prob,
        wsel,
        x_all.reshape(group, width),
        delta,
    )


def finish_kernel(
    f_ref,
    w_ref,
    out_ref,
    grad_ref,
    stats_ref,
    output,
    grad_tokens,
    gq_out,
    gqb_out,
    gk_out,
    gv_out,
    gvb_out,
    go_out,
    gob_out,
    gfg_out,
    gfs_out,
    gi_out,
    gib_out,
    gu_out,
    gub_out,
    gsg_out,
    gss_out,
    stats_out,
    gq_ref,
    gv_ref,
    vec_ref,
):
    s = lax.axis_index("seq")
    output[0] = out_ref[...]
    grad_tokens[0] = grad_ref[...]
    stats_out[...] = stats_ref[:, : stats_out.shape[1], : stats_out.shape[2]]
    share, width = gk_out.shape
    top = f_ref.shape[0] // 2
    full = jnp.float32
    for n in range(gi_out.shape[1] // width):
        gi_out[:, n * width : (n + 1) * width] = f_ref[n * share : (n + 1) * share, :].astype(full)
    gu_out[...] = f_ref[top : top + 4 * share, :].astype(full)
    part = share // 2
    go_out[0:part, :] = f_ref[4 * share : 4 * share + part, :].astype(full)
    go_out[part:, :] = f_ref[top + 4 * share : top + 4 * share + part, :].astype(full)
    vec_ref[...] = f_ref[top + 4 * share + part :, :].astype(full)
    for pair in range(4):
        at = slice(128 * pair, 128 * pair + 128)
        low, high = (w_ref[0, core, pair].astype(full) for core in range(2))
        gq_ref[:, at] = join(low[:, 0:128], half_roll(high[:, 0:128]))
        gk_out[:, at] = join(low[:, 128:256], half_roll(high[:, 128:256]))[:share]
        gv_ref[:, at] = join(half_roll(low[:, 0:128]), high[:, 0:128])
    for pair in range(2):
        at = slice(512 + 128 * pair, 640 + 128 * pair)
        low, high = (
            w_ref[1, 0, 2 * pair + i].astype(full) + w_ref[1, 1, 2 * pair + i].astype(full) for i in range(2)
        )
        gq_ref[:, at] = join(half_roll(low[:, 0:128]), high[:, 0:128])
        gk_out[:, at] = join(half_roll(low[:, 128:256]), high[:, 128:256])[:share]
        gv_ref[:, at] = join(low[:, 0:128], half_roll(high[:, 0:128]))
    gq_out[...] = gq_ref[:share, :]
    gv_out[...] = gv_ref[:share, :]

    def mine(rows):
        return pltpu.roll(rows, width - share * s, 1)[:, :share]

    short = mine(vec_ref[...])
    for row, ref in enumerate((gob_out, gfg_out, gfs_out, gub_out, gsg_out, gss_out)):
        ref[...] = short[row]
    gqb_out[...] = mine(gq_ref[share : share + 8, :])[0]
    gvb_out[...] = mine(gv_ref[share : share + 8, :])[0]
    row = vec_ref[pl.ds(6 + s // 2, 1), :]
    gib_out[...] = jnp.where(s % 2 == 1, row[:, 4 * share :], row[:, : 4 * share])[0]


def finish(reduced, w_all, output, grad, totals, head_count, inner_width):
    block, width = output.shape
    row_count = 8 * reduced.shape[3]
    share = width // 8
    low, full = jnp.bfloat16, jnp.float32
    vmem = pl.BlockSpec(memory_space=pltpu.VMEM)
    shape = jax.ShapeDtypeStruct
    square, vector = shape((share, width), full), shape((share,), full)
    out_shape = [
        shape((1, block, width), low),
        shape((1, block, width), low),
        square,
        vector,
        square,
        square,
        vector,
        square,
        vector,
        vector,
        vector,
        shape((share, inner_width), full),
        shape((inner_width // 8,), full),
        shape((inner_width // 8, width), full),
        vector,
        vector,
        vector,
        shape((2, head_count, 8), full),
    ]
    return pl.pallas_call(
        finish_kernel,
        out_shape=out_shape,
        in_specs=[vmem] * 5,
        out_specs=[vmem] * len(out_shape),
        scratch_shapes=[
            pltpu.VMEM((share + 16, width), full),
            pltpu.VMEM((share + 16, width), full),
            pltpu.VMEM((16, width), full),
        ],
        compiler_params=pltpu.CompilerParams(vmem_limit_bytes=40 << 20),
        name="finish",
    )(reduced.reshape(row_count, width), w_all, output, grad, totals)


def body(
    tokens,
    segments,
    orders,
    owners,
    query_weight,
    query_bias,
    key_weight,
    value_weight,
    value_bias,
    out_weight,
    out_bias,
    first_gain,
    first_shift,
    inner_weight,
    inner_bias,
    outer_weight,
    outer_bias,
    second_gain,
    second_shift,
    cotangent,
):
    seq_count = lax.axis_size("seq")
    groups = lax.axis_size("rep")
    own_index = lax.axis_index("seq")
    row_count = tokens.shape[1]
    model_width = tokens.shape[2]
    order_table = orders[0]
    owner_table = owners[0]
    head_count, group_tokens = order_table.shape
    cluster_count = owner_table.shape[1]
    cluster = group_tokens // cluster_count
    head_dim = model_width // head_count
    per_owner = row_count // cluster
    score_scale = head_dim ** (-0.5)
    flat_tokens = tokens[0]
    local_index = jnp.arange(row_count, dtype=jnp.int32)
    factor = 1
    for candidate in range(1, seq_count + 1):
        if seq_count % candidate == 0 and candidate * row_count <= 2048:
            factor = candidate
    block_count = seq_count // factor
    block_width = factor * row_count
    order_blocks = order_table.reshape(head_count, block_count, block_width).transpose(1, 0, 2)
    owner_blocks = (
        jnp.repeat(owner_table, cluster, axis=1)
        .reshape(head_count, block_count, block_width)
        .transpose(1, 0, 2)
    )

    def find_target(total, block_item):
        order_block, owner_block = block_item
        local = order_block - own_index * row_count
        hits = local[:, :, None] == local_index[None, None, :]
        return (total + jnp.sum(jnp.where(hits, owner_block[:, :, None], 0), axis=1), None)

    target, unused = lax.scan(
        find_target, jnp.zeros((head_count, row_count), jnp.int32), (order_blocks, owner_blocks)
    )
    send_matrix = rank_matrix(target * row_count + local_index[None, :])
    mine = (owner_table == own_index).astype(jnp.int32)
    before = jnp.cumsum(mine, axis=1) - mine
    slot_hot = (mine[:, None, :] == 1) & (
        before[:, None, :] == jnp.arange(per_owner, dtype=jnp.int32)[None, :, None]
    )
    order_grid = order_table.reshape(head_count, cluster_count, cluster)
    owned_tokens = jnp.sum(
        jnp.where(slot_hot[:, :, :, None], order_grid[:, None, :, :], 0), axis=2
    ).reshape(head_count, row_count)
    arrive_matrix = rank_matrix(owned_tokens)
    w_three = jnp.concatenate([query_weight, key_weight, value_weight], axis=1)
    bias_three = jnp.concatenate(
        [
            query_bias.astype(jnp.float32),
            jnp.zeros((model_width,), jnp.float32),
            value_bias.astype(jnp.float32),
        ]
    )
    projected = (
        jnp.dot(flat_tokens, w_three, preferred_element_type=jnp.float32) + bias_three
    ).astype(jnp.bfloat16)
    token_rows = (
        projected.reshape(row_count, 3, head_count, head_dim)
        .transpose(2, 0, 1, 3)
        .reshape(head_count, row_count, 3 * head_dim)
    )
    segment_rows = jnp.broadcast_to(
        segments[0].astype(jnp.bfloat16)[None, :, None], (head_count, row_count, 1)
    )
    send_values = scatter_rows(token_rows, send_matrix, seq_count)
    send_segments = scatter_rows(segment_rows, send_matrix, seq_count)
    arrived, arrived_segments = (
        lax.all_to_all(send_values, "seq", split_axis=0, concat_axis=0, tiled=True),
        lax.all_to_all(send_segments, "seq", split_axis=0, concat_axis=0, tiled=True),
    )
    cluster_rows = collect_rows(arrived, arrive_matrix, 3 * head_dim).reshape(
        head_count * per_owner, cluster, 3, head_dim
    )
    cluster_segments = collect_rows(arrived_segments, arrive_matrix, 1).reshape(
        head_count * per_owner, cluster
    )
    queries = cluster_rows[:, :, 0]
    keys_in = cluster_rows[:, :, 1]
    values = cluster_rows[:, :, 2]
    attended, log_total, entropy, occupied = cluster_forward(
        queries, keys_in, values, cluster_segments, score_scale
    )
    per_head = jnp.stack(
        [
            jnp.sum(entropy.reshape(head_count, -1), axis=1),
            jnp.sum(occupied.reshape(head_count, -1), axis=1) / cluster,
        ]
    ) / (groups * row_count)
    column = (jnp.arange(seq_count, dtype=jnp.int32) == own_index).astype(jnp.float32)
    cluster_stats = lax.psum(per_head[:, :, None] * column, ("seq", "rep"))
    leaving = scatter_rows(
        attended.reshape(head_count, row_count, head_dim), arrive_matrix, seq_count
    )
    returned = lax.all_to_all(leaving, "seq", split_axis=0, concat_axis=0, tiled=True)
    attended_rows = (
        collect_rows(returned, send_matrix, head_dim)
        .transpose(1, 0, 2)
        .reshape(row_count, model_width)
    )
    branch = jnp.dot(
        attended_rows, out_weight, preferred_element_type=jnp.float32
    ) + out_bias.astype(jnp.float32)
    first_out, normed_one, root_one = norm_forward(
        flat_tokens.astype(jnp.float32) + branch, first_gain, first_shift
    )
    first_low = first_out.astype(jnp.bfloat16)
    inner_sum = jnp.dot(
        first_low, inner_weight, preferred_element_type=jnp.float32
    ) + inner_bias.astype(jnp.float32)
    activated, gelu_pull = jax.vjp(exact_gelu, inner_sum)
    activated_low = activated.astype(jnp.bfloat16)
    second = jnp.dot(
        activated_low, outer_weight, preferred_element_type=jnp.float32
    ) + outer_bias.astype(jnp.float32)
    result, normed_two, root_two = norm_forward(first_out + second, second_gain, second_shift)
    output = result.astype(jnp.bfloat16)[None]
    upstream = cotangent[0].astype(jnp.float32)
    gradient_second_gain = jnp.sum(upstream * normed_two, axis=0)
    gradient_second_shift = jnp.sum(upstream, axis=0)
    delta_two = norm_backward(upstream, normed_two, root_two, second_gain)
    delta_second = delta_two.astype(jnp.bfloat16)
    gradient_outer_bias = jnp.sum(delta_second.astype(jnp.float32), axis=0)
    gradient_outer_weight = jnp.einsum(
        "tf,td->fd", activated_low, delta_second, preferred_element_type=jnp.float32
    )
    delta_activated = jnp.einsum(
        "td,fd->tf", delta_second, outer_weight, preferred_element_type=jnp.float32
    )
    delta_inner = gelu_pull(delta_activated)[0].astype(jnp.bfloat16)
    gradient_inner_bias = jnp.sum(delta_inner.astype(jnp.float32), axis=0)
    gradient_inner_weight = jnp.einsum(
        "td,tf->df", first_low, delta_inner, preferred_element_type=jnp.float32
    )
    delta_first = delta_two + jnp.einsum(
        "tf,df->td", delta_inner, inner_weight, preferred_element_type=jnp.float32
    )
    gradient_first_gain = jnp.sum(delta_first * normed_one, axis=0)
    gradient_first_shift = jnp.sum(delta_first, axis=0)
    delta_one = norm_backward(delta_first, normed_one, root_one, first_gain)
    delta_branch = delta_one.astype(jnp.bfloat16)
    gradient_out_bias = jnp.sum(delta_branch.astype(jnp.float32), axis=0)
    gradient_out_weight = jnp.einsum(
        "td,te->de", attended_rows, delta_branch, preferred_element_type=jnp.float32
    )
    delta_attended = jnp.einsum(
        "te,de->td", delta_branch, out_weight, preferred_element_type=jnp.float32
    ).astype(jnp.bfloat16)
    delta_rows = delta_attended.reshape(row_count, head_count, head_dim).transpose(1, 0, 2)
    send_grads = scatter_rows(delta_rows, send_matrix, seq_count)
    grad_arrived = lax.all_to_all(send_grads, "seq", split_axis=0, concat_axis=0, tiled=True)
    kept_queries, kept_keys, kept_values, kept_segments = (
        queries,
        keys_in,
        values,
        cluster_segments,
    )
    grad_cluster = collect_rows(grad_arrived, arrive_matrix, head_dim).reshape(
        head_count * per_owner, cluster, head_dim
    )
    three_grads = cluster_backward(
        kept_queries, kept_keys, kept_values, kept_segments, log_total, grad_cluster, score_scale
    )
    leaving_grads = scatter_rows(
        three_grads.reshape(head_count, row_count, 3 * head_dim), arrive_matrix, seq_count
    )
    returned_grads = lax.all_to_all(leaving_grads, "seq", split_axis=0, concat_axis=0, tiled=True)
    delta_three = (
        collect_rows(returned_grads, send_matrix, 3 * head_dim)
        .reshape(head_count, row_count, 3, head_dim)
        .transpose(1, 2, 0, 3)
        .reshape(row_count, 3 * model_width)
    )
    bias_grads = jnp.sum(delta_three.astype(jnp.float32), axis=0)
    weight_grads = jnp.einsum(
        "td,te->de", flat_tokens, delta_three, preferred_element_type=jnp.float32
    )
    gradient_tokens = (
        delta_one
        + jnp.einsum("te,de->td", delta_three, w_three, preferred_element_type=jnp.float32)
    ).astype(jnp.bfloat16)[None]
    gradient_query_weight = weight_grads[:, :model_width]
    gradient_key_weight = weight_grads[:, model_width : 2 * model_width]
    gradient_value_weight = weight_grads[:, 2 * model_width :]
    gradient_query_bias = bias_grads[:model_width]
    gradient_value_bias = bias_grads[2 * model_width :]
    pieces = (
        lax.psum_scatter(gradient_query_weight, "seq", scatter_dimension=0, tiled=True),
        lax.psum_scatter(gradient_query_bias, "seq", scatter_dimension=0, tiled=True),
        lax.psum_scatter(gradient_key_weight, "seq", scatter_dimension=0, tiled=True),
        lax.psum_scatter(gradient_value_weight, "seq", scatter_dimension=0, tiled=True),
        lax.psum_scatter(gradient_value_bias, "seq", scatter_dimension=0, tiled=True),
        lax.psum_scatter(gradient_out_weight, "seq", scatter_dimension=0, tiled=True),
        lax.psum_scatter(gradient_out_bias, "seq", scatter_dimension=0, tiled=True),
        lax.psum_scatter(gradient_first_gain, "seq", scatter_dimension=0, tiled=True),
        lax.psum_scatter(gradient_first_shift, "seq", scatter_dimension=0, tiled=True),
        lax.psum_scatter(gradient_inner_weight, "seq", scatter_dimension=0, tiled=True),
        lax.psum_scatter(gradient_inner_bias, "seq", scatter_dimension=0, tiled=True),
        lax.psum_scatter(gradient_outer_weight, "seq", scatter_dimension=0, tiled=True),
        lax.psum_scatter(gradient_outer_bias, "seq", scatter_dimension=0, tiled=True),
        lax.psum_scatter(gradient_second_gain, "seq", scatter_dimension=0, tiled=True),
        lax.psum_scatter(gradient_second_shift, "seq", scatter_dimension=0, tiled=True),
    )
    summed = (
        lax.psum(pieces[0].astype(jnp.bfloat16), "rep").astype(jnp.float32),
        lax.psum(pieces[1].astype(jnp.bfloat16), "rep").astype(jnp.float32),
        lax.psum(pieces[2].astype(jnp.bfloat16), "rep").astype(jnp.float32),
        lax.psum(pieces[3].astype(jnp.bfloat16), "rep").astype(jnp.float32),
        lax.psum(pieces[4].astype(jnp.bfloat16), "rep").astype(jnp.float32),
        lax.psum(pieces[5].astype(jnp.bfloat16), "rep").astype(jnp.float32),
        lax.psum(pieces[6].astype(jnp.bfloat16), "rep").astype(jnp.float32),
        lax.psum(pieces[7].astype(jnp.bfloat16), "rep").astype(jnp.float32),
        lax.psum(pieces[8].astype(jnp.bfloat16), "rep").astype(jnp.float32),
        lax.psum(pieces[9].astype(jnp.bfloat16), "rep").astype(jnp.float32),
        lax.psum(pieces[10].astype(jnp.bfloat16), "rep").astype(jnp.float32),
        lax.psum(pieces[11].astype(jnp.bfloat16), "rep").astype(jnp.float32),
        lax.psum(pieces[12].astype(jnp.bfloat16), "rep").astype(jnp.float32),
        lax.psum(pieces[13].astype(jnp.bfloat16), "rep").astype(jnp.float32),
        lax.psum(pieces[14].astype(jnp.bfloat16), "rep").astype(jnp.float32),
    )
    return (output, gradient_tokens) + tuple(summed) + (cluster_stats,)


def square_body(
    tokens,
    segments,
    orders,
    owners,
    query_weight,
    query_bias,
    key_weight,
    value_weight,
    value_bias,
    out_weight,
    out_bias,
    first_gain,
    first_shift,
    inner_weight,
    inner_bias,
    outer_weight,
    outer_bias,
    second_gain,
    second_shift,
    cotangent,
):
    model_width = tokens.shape[2]
    att, x_my, cot_my, wsel, order, stats, x_all, sorted_rows, prob = forward_attention(
        tokens[0],
        cotangent[0],
        segments,
        orders.transpose(1, 0, 2),
        owners.transpose(1, 0, 2),
        query_bias,
        value_bias,
        query_weight,
        key_weight,
        value_weight,
    )
    vectors = (out_bias, first_gain, first_shift, outer_bias, second_gain, second_shift, inner_bias)
    output, delta, datt, low_first, dsecond, dbranch, vector_grads, act, dinner = mlp(
        att, x_my, cot_my, vectors, out_weight, inner_weight, outer_weight, 2 * model_width
    )
    output, grad, reduced, w_all, totals = backward_attention(
        datt,
        order,
        output,
        stats,
        vector_grads,
        att,
        dbranch,
        low_first,
        dsecond,
        act,
        dinner,
        sorted_rows,
        prob,
        wsel,
        x_all,
        delta,
        3,
    )
    return tuple(
        finish(reduced, w_all, output, grad, totals, orders.shape[1], inner_weight.shape[1])
    )


def solution(mesh):
    square = mesh.shape["seq"] == 8 and mesh.shape["rep"] == 4
    placed = (
        P("rep", "seq", None),
        P("rep", "seq"),
        P("rep", None, None),
        P("rep", None, None),
        P(),
        P(),
        P(),
        P(),
        P(),
        P(),
        P(),
        P(),
        P(),
        P(),
        P(),
        P(),
        P(),
        P(),
        P(),
        P("rep", "seq", None),
    )
    return jax.shard_map(
        square_body if square else body,
        mesh=mesh,
        in_specs=placed,
        out_specs=(
            P("rep", "seq", None),
            P("rep", "seq", None),
            P("seq", None),
            P("seq"),
            P("seq", None),
            P("seq", None),
            P("seq"),
            P("seq", None),
            P("seq"),
            P("seq"),
            P("seq"),
            P("seq", None),
            P("seq"),
            P("seq", None),
            P("seq"),
            P("seq"),
            P("seq"),
            P(),
        ),
        check_vma=False,
    )
```

```python
import functools

import jax
import jax.numpy as jnp
from jax import lax
from jax.experimental import pallas as pl
from jax.experimental.pallas import tpu as pltpu
from jax.sharding import PartitionSpec as P

EPSILON = 1e-12
NEGATIVE = -1e30


def norm_forward(hidden, gain_vector, shift_vector):
    centre = hidden - jnp.mean(hidden, axis=-1, keepdims=True)
    root_inverse = lax.rsqrt(jnp.mean(centre * centre, axis=-1, keepdims=True) + EPSILON)
    normed = centre * root_inverse
    return (
        normed * gain_vector.astype(jnp.float32) + shift_vector.astype(jnp.float32),
        normed,
        root_inverse,
    )


def norm_backward(upstream, normed, root_inverse, gain_vector):
    scaled = upstream * gain_vector.astype(jnp.float32)
    return root_inverse * (
        scaled
        - jnp.mean(scaled, axis=-1, keepdims=True)
        - normed * jnp.mean(scaled * normed, axis=-1, keepdims=True)
    )


def exact_gelu(inner_sum):
    return jax.nn.gelu(inner_sum, approximate=False)


def rank_matrix(sort_keys):
    row_count = sort_keys.shape[1]
    ranks = jnp.sum((sort_keys[:, None, :] < sort_keys[:, :, None]).astype(jnp.int32), axis=2)
    return (ranks[:, None, :] == jnp.arange(row_count, dtype=jnp.int32)[None, :, None]).astype(
        jnp.bfloat16
    )


def scatter_rows(row_block, placing, seq_count):
    head_count, row_count, features = row_block.shape
    picked = jnp.einsum(
        "hri,hif->hrf", placing, row_block, preferred_element_type=jnp.float32
    ).astype(jnp.bfloat16)
    return picked.reshape(head_count, seq_count, row_count // seq_count * features).transpose(
        1, 0, 2
    )


def collect_rows(packed, placing, features):
    seq_count, head_count, flat_width = packed.shape
    row_block = packed.transpose(1, 0, 2).reshape(
        head_count, seq_count * flat_width // features, features
    )
    return jnp.einsum(
        "hri,hrf->hif", placing, row_block, preferred_element_type=jnp.float32
    ).astype(jnp.bfloat16)


def cluster_scores(queries, keys_in, segment_ids, score_scale):
    scores = (
        jnp.einsum("nqd,nkd->nqk", queries, keys_in, preferred_element_type=jnp.float32)
        * score_scale
    )
    allowed = segment_ids[:, :, None] == segment_ids[:, None, :]
    return (scores, allowed, jnp.where(allowed, scores, NEGATIVE))


def cluster_forward(queries, keys_in, values, segment_ids, score_scale):
    scores, allowed, masked = cluster_scores(queries, keys_in, segment_ids, score_scale)
    highest = jnp.max(masked, axis=-1, keepdims=True)
    raised = jnp.exp(masked - highest)
    totals = jnp.sum(raised, axis=-1, keepdims=True)
    weights = raised / totals
    attended = jnp.einsum(
        "nqk,nkd->nqd", weights.astype(jnp.bfloat16), values, preferred_element_type=jnp.float32
    ).astype(jnp.bfloat16)
    log_total = highest[:, :, 0] + jnp.log(totals[:, :, 0])
    entropy = log_total - jnp.sum(weights * jnp.where(allowed, scores, 0.0), axis=-1)
    occupied = jnp.sum(allowed.astype(jnp.float32), axis=-1)
    return (attended, log_total, entropy, occupied)


def cluster_backward(queries, keys_in, values, segment_ids, log_total, grad_out, score_scale):
    masked = cluster_scores(queries, keys_in, segment_ids, score_scale)[2]
    weights = jnp.exp(masked - log_total[:, :, None])
    weight_grads = jnp.einsum("nqd,nkd->nqk", grad_out, values, preferred_element_type=jnp.float32)
    value_grads = jnp.einsum(
        "nqk,nqd->nkd", weights.astype(jnp.bfloat16), grad_out, preferred_element_type=jnp.float32
    )
    score_grads = (
        weights * (weight_grads - jnp.sum(weights * weight_grads, axis=-1, keepdims=True))
    ).astype(jnp.bfloat16)
    query_grads = (
        jnp.einsum("nqk,nkd->nqd", score_grads, keys_in, preferred_element_type=jnp.float32)
        * score_scale
    )
    key_grads = (
        jnp.einsum("nqk,nqd->nkd", score_grads, queries, preferred_element_type=jnp.float32)
        * score_scale
    )
    return jnp.stack([query_grads, key_grads, value_grads], axis=2).astype(jnp.bfloat16)


MESH = pl.DeviceIdType.MESH


UNROLL = 8
PIECES = 4
FIRST = 1


def half_roll(block):
    return jnp.concatenate([block[:, 64:], block[:, :64]], axis=1)


def lanes(shape):
    return lax.broadcasted_iota(jnp.int32, shape, len(shape) - 1)


def bits(value, flip):
    return value + flip - 2 * value * flip


def coordinates():
    s, r = lax.axis_index("seq"), lax.axis_index("rep")
    return s // 4, (s // 2) % 2, s % 2, r // 2, r % 2


def device(zh, zl, x, y, c):
    return (4 * zh + 2 * zl + x, 2 * y + c)


def greet(peers):
    barrier = pltpu.get_barrier_semaphore()
    for peer in peers:
        pl.semaphore_signal(barrier, inc=1, device_id=peer, device_id_type=MESH)
    pl.semaphore_wait(barrier, len(peers))


def remote(src, dst, sems, index, peer):
    return pltpu.make_async_remote_copy(
        src_ref=src,
        dst_ref=dst,
        send_sem=sems[0].at[index],
        recv_sem=sems[1].at[index],
        device_id=peer,
        device_id_type=MESH,
    )


def dot(left, right, left_dim=1, right_dim=0):
    return lax.dot_general(
        left,
        right,
        (((left_dim,), (right_dim,)), ((), ())),
        preferred_element_type=jnp.float32,
    )


def hot(condition):
    return jnp.where(condition, 1.0, 0.0).astype(jnp.bfloat16)


def build_gather(order_ref, row, start, count, into):
    tokens = into.shape[1]

    def one(k, carry):
        at = pl.multiple_of(k * 128, 128)
        ids = order_ref[row : row + 1, pl.ds(pl.multiple_of(start + at, 128), 128)]
        column = jnp.broadcast_to(ids.astype(jnp.float32), (128, 128)).T
        lane = lanes((128, 128)).astype(jnp.float32)
        for t in range(tokens // 128):
            into[pl.ds(at, 128), t * 128 : (t + 1) * 128] = hot(column == lane + 128.0 * t)
        return carry

    lax.fori_loop(0, count // 128, one, 0)


def build_scatter(order_ref, row, start, count, into, base):
    def one(k, carry):
        at = pl.multiple_of(k * 128, 128)
        token = lax.broadcasted_iota(jnp.int32, (128, 128), 0) + at
        for p in range(count // 128):
            ids = order_ref[row : row + 1, pl.ds(pl.multiple_of(start + 128 * p, 128), 128)]
            into[pl.ds(at, 128), base + 128 * p : base + 128 * (p + 1)] = hot(ids == token)
        return carry

    lax.fori_loop(0, into.shape[0] // 128, one, 0)


def select_head(slab, half, place):
    return jnp.where(half == place, slab, half_roll(slab))


def join(low_lanes, high_lanes):
    return jnp.where(lanes(low_lanes.shape) < 64, low_lanes, high_lanes)


def pick_columns(pairs, j, c):
    (q_one, q_two), (k_one, k_two), (v_one, v_two) = pairs
    zero = jnp.zeros_like(q_one)
    q1, v1, k1 = select_head(q_one, c, 0), select_head(v_one, c, 1), select_head(k_one, c, 0)
    v2, q2, k2 = (
        select_head(v_two, j % 2, 0),
        select_head(q_two, j % 2, 1),
        select_head(k_two, j % 2, 1),
    )
    return join(q1, v1), join(k1, zero), join(v2, q2), join(zero, k2)


def forward_kernel(
    tokens_ref,
    cot_ref,
    seg_ref,
    orders_ref,
    owners_ref,
    query_bias_ref,
    value_bias_ref,
    wq_hbm,
    wk_hbm,
    wv_hbm,
    att_ref,
    x_my,
    cot_my,
    wsel_ref,
    order_ref,
    stats_ref,
    x_hbm,
    sorted_hbm,
    prob_hbm,
    gather_hbm,
    scatter_hbm,
    x_all,
    sorted_ref,
    prob_ref,
    weights,
    orders_in,
    owners_in,
    owner_pad,
    seg_src,
    seg_all,
    bias_rows,
    bias_sel,
    tok,
    partial,
    gather,
    scatter,
    att_sorted,
    att_send,
    att_in,
    ent_ref,
    cnt_ref,
    swap_send,
    swap_recv,
    ring_send,
    ring_recv,
    seg_send,
    seg_recv,
    back_send,
    back_recv,
    local_sem,
):
    zh, zl, x, y, c = coordinates()
    j = 2 * zl + x
    p = 4 * c + j
    block, width = tokens_ref.shape
    group = 8 * block
    scale = 0.125
    swap = (swap_send, swap_recv)
    ring = (ring_send, ring_recv)
    seg_sems = (seg_send, seg_recv)
    back = (back_send, back_recv)

    def member(flip):
        fc, fz, fx = flip // 4, (flip // 2) % 2, flip % 2
        mc, mz, mx = bits(c, fc), bits(zl, fz), bits(x, fx)
        return device(zh, mz, mx, y, mc), 4 * mc + 2 * mz + mx

    swap_peer = device(1 - zh, zl, x, y, 1 - c)
    peers = [member(flip)[0] for flip in range(1, 8)]
    sibling = peers[3]
    over_x, over_z = peers[0], peers[1]
    matched = c == zh

    slabs = [
        pltpu.make_async_copy(
            src.at[:, pl.ds(pl.multiple_of(index * 128, 128), 128)],
            weights.at[i, slot],
            local_sem.at[3 * slot + i],
        )
        for i, src in enumerate((wq_hbm, wk_hbm, wv_hbm))
        for slot, index in enumerate((j, 4 + j // 2))
    ]
    for copy in slabs:
        copy.start()
    greet(peers + [swap_peer])
    seg_src[...] = jnp.broadcast_to(seg_ref[...], seg_src.shape)
    table_copies = [
        remote(orders_ref, orders_in, swap, 0, sibling),
        remote(owners_ref, owners_in, swap, 1, sibling),
    ]
    for copy in table_copies:
        copy.start()
    p_swap = 4 * (1 - c) + j
    chunks = PIECES
    halves = [pl.ds(i * (block // chunks), block // chunks) for i in range(chunks)]
    pairs = [(tokens_ref.at[at], x_all.at[p_swap, at], x_all.at[p, at]) for at in halves]
    pairs.insert(0, (seg_src, seg_all.at[p_swap], seg_all.at[p]))
    pairs.append((cot_ref, cot_my, cot_my))
    swaps = [remote(src, dst, swap, 2 + i, swap_peer) for i, (src, dst, _) in enumerate(pairs)]
    locals_ = [
        pltpu.make_async_copy(src, own, swap_recv.at[4 + chunks + i]) for i, (src, _, own) in enumerate(pairs)
    ]

    px, pz, pd = member(1)[1], member(2)[1], member(3)[1]

    def share_block(index, position, i, peer):
        view = x_all.at[position, halves[i]]
        return remote(view, view, ring, index, peer)

    every = range(chunks)
    own_to_x = [share_block(i, p, i, over_x) for i in every]
    own_to_z = [share_block(chunks + i, p, i, over_z) for i in every]
    own_to_s = [share_block(2 * chunks + i, p, i, sibling) for i in every]
    x_to_s = [share_block(3 * chunks + i, px, i, sibling) for i in every]
    z_to_s = [share_block(4 * chunks + i, pz, i, sibling) for i in every]
    d_to_s = [share_block(5 * chunks + i, pd, i, sibling) for i in every]
    relays = [
        share_block(6 * chunks + i, px, i, over_z) if i < FIRST else share_block(6 * chunks + i, pz, i, over_x)
        for i in every
    ]
    seg_copies = [
        remote(seg_all.at[p], seg_all.at[p], seg_sems, flip - 1, peers[flip - 1]) for flip in range(1, 8)
    ]
    opposite = jnp.logical_not(matched)

    def own_half(i, arrivals):
        arrivals[1 + i].wait()
        own_to_x[i].start()
        own_to_z[i].start()
        own_to_s[i].start()

    def segments_out(arrivals):
        arrivals[0].wait()
        for copy in seg_copies:
            copy.start()

    def relay(i):
        own_to_x[i].wait()
        own_to_z[i].wait()
        relays[i].start()
        x_to_s[i].start()
        z_to_s[i].start()

    def relay_end(i):
        relays[i].wait()
        d_to_s[i].start()

    def wait_sibling():
        for copy in own_to_s + x_to_s + z_to_s + d_to_s:
            copy.wait_recv()

    @pl.when(matched)
    def _():
        for copy in locals_:
            copy.start()
        segments_out(locals_)
        for i in every:
            own_half(i, locals_)

    @pl.when(opposite)
    def _():
        for copy in swaps[: 1 + chunks]:
            copy.start()

    for copy in slabs:
        copy.wait()
    tiles = pick_columns([[weights[i, slot].astype(jnp.float32) for slot in range(2)] for i in range(3)], j, c)
    for i, tile in enumerate(tiles):
        wsel_ref[:, 128 * i : 128 * (i + 1)] = tile.astype(jnp.bfloat16)
    for i, ref in enumerate((query_bias_ref, None, value_bias_ref)):
        row = jnp.zeros((1, width), jnp.float32) if ref is None else ref[...].astype(jnp.float32).reshape(1, width)
        bias_rows[i : i + 1, :] = row
    bias_pairs = [
        [bias_rows[i : i + 1, pl.ds(pl.multiple_of(index * 128, 128), 128)] for index in (j, 4 + j // 2)]
        for i in range(3)
    ]
    for i, tile in enumerate(pick_columns(bias_pairs, j, c)):
        bias_sel[0:1, 128 * i : 128 * (i + 1)] = tile

    for copy in table_copies:
        copy.wait()
    h1, h2 = 2 * j + c, 8 + j
    for i, h in enumerate((h1, h2)):
        order_ref[i : i + 1, :] = jnp.where(matched, orders_ref[h], orders_in[h])
    half = 1024 * c

    build_gather(order_ref, 0, 0, group, gather.at[pl.ds(0, group)])

    @pl.when(matched)
    def _():
        for i in every:
            relay(i)

    @pl.when(opposite)
    def _():
        segments_out(swaps)
        for i in range(chunks // 2):
            own_half(i, swaps)

    build_gather(order_ref, 1, half, group // 2, gather.at[pl.ds(group, group // 2)])

    matrix_stores = [
        pltpu.make_async_copy(src, dst, local_sem.at[9 + i])
        for i, (src, dst) in enumerate(((gather, gather_hbm), (scatter, scatter_hbm)))
    ]

    @pl.when(matched)
    def _():
        for i in every:
            relay_end(i)

    @pl.when(opposite)
    def _():
        for i in range(chunks // 2, chunks):
            own_half(i, swaps)
        for i in range(chunks // 2):
            relay(i)

    def project(position):
        at = pl.ds(pl.multiple_of(position * block, block), block)
        out = dot(x_all[position], wsel_ref[...]) + bias_sel[0:1, :]
        ids = seg_all[position, 0:1, :].astype(jnp.float32)
        columns = [
            jnp.broadcast_to(ids[:, 128 * i : 128 * (i + 1)], (128, 128)).T for i in range(block // 128)
        ]
        lane = lanes((block, 128))
        seg_hot = hot(jnp.concatenate(columns, axis=0) == (lane % 64).astype(jnp.float32))
        low = out.astype(jnp.bfloat16)
        tok[at, 0:128] = low[:, 0:128]
        tok[at, 128:256] = jnp.where(lane < 64, low[:, 128:256], seg_hot)
        tok[at, 256:384] = low[:, 256:384]
        tok[at, 384:512] = jnp.where(lane < 64, seg_hot, low[:, 384:512])

    step = 512
    early, late = group // 2 * zh, group // 2 * (1 - zh)

    def gather_rows(start, add):
        tokens = pl.ds(pl.multiple_of(start, group // 2), group // 2)

        def one(first, columns):
            def body(k, carry):
                at = pl.ds(pl.multiple_of(k * step, step), step)
                rows = dot(gather[at, tokens], tok[tokens, columns])
                if add:
                    sorted_ref[at, :] = (rows + partial[at, :].astype(jnp.float32)).astype(jnp.bfloat16)
                else:
                    partial[at, :] = rows.astype(jnp.bfloat16)
                return carry

            return body

        lax.fori_loop(0, group // step, one(0, pl.ds(0, 256)), 0)
        lax.fori_loop(group // step, group * 3 // 2 // step, one(1, pl.ds(256, 256)), 0)

    for copy in seg_copies:
        copy.wait()
    pl.when(opposite)(wait_sibling)
    for k in range(4):
        project(4 * zh + k)

    @pl.when(opposite)
    def _():
        for i in range(chunks // 2, chunks):
            relay(i)
        for i in range(chunks // 2):
            relay_end(i)

    matrix_stores[0].start()
    gather_rows(early, False)

    @pl.when(opposite)
    def _():
        for i in range(chunks // 2, chunks):
            relay_end(i)

    build_scatter(order_ref, 0, 0, group, scatter, 0)
    build_scatter(order_ref, 1, half, group // 2, scatter, group)
    matrix_stores[1].start()
    pl.when(matched)(wait_sibling)
    for k in range(4):
        project(4 * (1 - zh) + k)
    stores = [
        pltpu.make_async_copy(src, dst, local_sem.at[6 + i])
        for i, (src, dst) in enumerate(((x_all, x_hbm), (sorted_ref, sorted_hbm), (prob_ref, prob_hbm)))
    ]
    stores[0].start()
    x_my[...] = x_all[p]


    @pl.when(opposite)
    def _():
        swaps[1 + chunks].start()

    gather_rows(late, True)
    def attend(first_lanes):
        def one(i, carry):
            at = pl.ds(pl.multiple_of(i * 128, 128), 128)
            tile_zero, tile_one = sorted_ref[at, 0:128], sorted_ref[at, 128:256]
            low_lanes = lanes((128, 128)) < 64
            query_lanes = low_lanes if first_lanes else jnp.logical_not(low_lanes)
            queries = jnp.where(query_lanes, tile_zero, jnp.zeros_like(tile_zero))
            ids = jnp.where(query_lanes, jnp.zeros_like(tile_one), tile_one)
            both = dot(jnp.concatenate([queries, ids], axis=0), tile_one, 1, 1)
            scores, allowed = both[:128] * scale, both[128:]
            masked = jnp.where(allowed > 0.5, scores, NEGATIVE)
            highest = jnp.max(masked, axis=1, keepdims=True)
            raised = jnp.exp(masked - highest)
            totals = jnp.sum(raised, axis=1, keepdims=True)
            weights = raised * (1.0 / totals)
            prob_ref[at, :] = weights
            mixed = dot(weights.astype(jnp.bfloat16), tile_zero)
            att_sorted[at, :] = jnp.where(query_lanes, 0.0, mixed).astype(jnp.bfloat16)
            log_total = highest + jnp.log(totals)
            entropy = jnp.where(lanes((128, 128)) == 0, log_total, 0.0) - weights * masked
            ent_ref[pl.ds(i, 1), :] = jnp.sum(entropy, axis=0, keepdims=True)
            cnt_ref[pl.ds(i, 1), :] = jnp.sum(allowed, axis=0, keepdims=True)
            return carry

        return one

    lax.fori_loop(0, 16, attend(True), 0, unroll=UNROLL)
    lax.fori_loop(16, 24, attend(False), 0, unroll=UNROLL)
    stores[1].start()
    stores[2].start()

    def place(position):
        at = pl.ds(pl.multiple_of(position * block, block), block)
        return dot(scatter[at, :], att_sorted[...]).astype(jnp.bfloat16)

    back_copies = []
    for flip in (3, 7, 1, 5, 2, 6, 4):
        peer, position = member(flip)
        att_send[flip] = place(position)
        copy = remote(att_send.at[flip], att_in.at[p], back, flip - 1, peer)
        copy.start()
        back_copies.append(copy)
    att_in[p] = place(p)

    stats_ref[...] = jnp.zeros_like(stats_ref)
    owner_pad[...] = jnp.full_like(owner_pad, -1.0)
    clusters = owners_ref.shape[2]
    for h, first, size, skip in ((h1, 0, clusters, 0), (h2, clusters, clusters // 2, c)):
        ids = jnp.where(matched, owners_ref[h], owners_in[h])
        owner_pad[0:1, 0:clusters] = ids.astype(jnp.float32)
        column = jnp.broadcast_to(owner_pad[0:1, :], (128, 128)).T
        column = jnp.where(skip == 1, column[clusters // 2 : clusters // 2 + size], column[0:size])
        owned = jnp.where(column == lanes((size, 128)).astype(jnp.float32), 1.0, 0.0)
        for kind, (lane_sums, divisor) in enumerate(((ent_ref, 4.0 * block), (cnt_ref, 4.0 * block * 128))):
            sums = jnp.sum(lane_sums[first : first + size, :], axis=1, keepdims=True) / divisor
            stats_ref[kind, pl.ds(h, 1), :] = jnp.sum(sums * owned, axis=0, keepdims=True)

    @pl.when(matched)
    def _():
        locals_[1 + chunks].wait()

    @pl.when(jnp.logical_not(matched))
    def _():
        swaps[1 + chunks].wait()

    for copy in back_copies:
        copy.wait()
    for copy in stores + matrix_stores:
        copy.wait()
    for copy in own_to_s + x_to_s + z_to_s + d_to_s:
        copy.wait_send()
    for pair in range(4):
        even, odd = att_in[pair], att_in[4 + pair]
        att_ref[:, 128 * pair : 128 * (pair + 1)] = join(half_roll(even), odd)
    for pair in range(2):
        low_half = att_in[2 * pair] + att_in[4 + 2 * pair]
        high_half = att_in[2 * pair + 1] + att_in[5 + 2 * pair]
        att_ref[:, 512 + 128 * pair : 640 + 128 * pair] = join(low_half, half_roll(high_half))


def forward_attention(
    tokens, cotangent, segments, orders, owners, query_bias, value_bias, wq, wk, wv
):
    block, width = tokens.shape
    group = 8 * block
    low, full = jnp.bfloat16, jnp.float32
    vmem = pl.BlockSpec(memory_space=pltpu.VMEM)
    hbm = pl.BlockSpec(memory_space=pl.ANY)
    dma = pltpu.SemaphoreType.DMA
    shape = jax.ShapeDtypeStruct
    rows = group * 3 // 2
    return pl.pallas_call(
        forward_kernel,
        out_shape=[
            shape((block, width), low),
            shape((block, width), low),
            shape((block, width), low),
            shape((width, 512), low),
            shape((8, group), jnp.int32),
            shape((2, 16, 128), full),
            shape((8, block, width), low),
            shape((rows, 256), low),
            shape((rows, 128), full),
            shape((rows, group), low),
            shape((group, rows), low),
        ],
        in_specs=[vmem] * 7 + [hbm] * 3,
        out_specs=[vmem] * 6 + [hbm] * 5,
        scratch_shapes=[
            pltpu.VMEM((8, block, width), low),
            pltpu.VMEM((rows, 256), low),
            pltpu.VMEM((rows, 128), full),
            pltpu.VMEM((3, 2, width, 128), low),
            pltpu.VMEM(orders.shape, jnp.int32),
            pltpu.VMEM(owners.shape, jnp.int32),
            pltpu.VMEM((8, 128), full),
            pltpu.VMEM((8, block), jnp.int32),
            pltpu.VMEM((8, 8, block), jnp.int32),
            pltpu.VMEM((8, width), full),
            pltpu.VMEM((8, 512), full),
            pltpu.VMEM((group, 512), low),
            pltpu.VMEM((rows, 256), low),
            pltpu.VMEM((rows, group), low),
            pltpu.VMEM((group, rows), low),
            pltpu.VMEM((rows, 128), low),
            pltpu.VMEM((8, block, 128), low),
            pltpu.VMEM((8, block, 128), low),
            pltpu.VMEM((24, 128), full),
            pltpu.VMEM((24, 128), full),
            dma((2 * PIECES + 6,)),
            dma((2 * PIECES + 6,)),
            dma((7 * PIECES,)),
            dma((7 * PIECES,)),
            dma((7,)),
            dma((7,)),
            dma((7,)),
            dma((7,)),
            dma((11,)),
        ],
        compiler_params=pltpu.CompilerParams(
            collective_id=1, has_side_effects=True, vmem_limit_bytes=60 << 20
        ),
        name="forward_attention",
    )(tokens, cotangent, segments, orders, owners, query_bias, value_bias, wq, wk, wv)


def normalize(hidden):
    centre = hidden - jnp.mean(hidden, axis=1, keepdims=True)
    root_inverse = lax.rsqrt(jnp.mean(centre * centre, axis=1, keepdims=True) + EPSILON)
    return centre * root_inverse, root_inverse


def normalize_back(scaled, normed, root_inverse):
    return root_inverse * (
        scaled
        - jnp.mean(scaled, axis=1, keepdims=True)
        - normed * jnp.mean(scaled * normed, axis=1, keepdims=True)
    )


def mlp_kernel(
    tile,
    att_ref,
    x_ref,
    cot_ref,
    out_bias_ref,
    first_gain_ref,
    first_shift_ref,
    outer_bias_ref,
    second_gain_ref,
    second_shift_ref,
    inner_bias_ref,
    out_w_hbm,
    inner_w_hbm,
    outer_w_hbm,
    output_ref,
    delta_ref,
    datt_ref,
    low_ref,
    dsecond_ref,
    dbranch_ref,
    vec_out,
    act_hbm,
    dinner_hbm,
    act_ref,
    dinner_ref,
    bias_ref,
    out_w,
    inner_w,
    outer_w,
    slope,
    total,
    normed_ref,
    first_ref,
    load_sem,
):
    width = x_ref.shape[1]
    inner_width = inner_w.shape[1]
    tiles = inner_width // tile
    parts = [slice(tile * t, tile * (t + 1)) for t in range(tiles)]
    loads = [pltpu.make_async_copy(out_w_hbm, out_w, load_sem.at[0])]
    for t, at in enumerate(parts):
        loads.append(
            pltpu.make_async_copy(inner_w_hbm.at[:, at], inner_w.at[:, at], load_sem.at[1 + 2 * t])
        )
        loads.append(pltpu.make_async_copy(outer_w_hbm.at[at], outer_w.at[at], load_sem.at[2 + 2 * t]))
    for copy in loads:
        copy.start()
    stores = [
        [
            pltpu.make_async_copy(src.at[:, at], dst.at[:, at], load_sem.at[1 + 2 * tiles + 2 * t + i])
            for i, (src, dst) in enumerate(((act_ref, act_hbm), (dinner_ref, dinner_hbm)))
        ]
        for t, at in enumerate(parts)
    ]
    bias_ref[0:1, :] = inner_bias_ref[...].astype(jnp.float32).reshape(1, inner_width)
    out_bias, first_gain, first_shift, outer_bias, second_gain, second_shift = (
        ref[...].astype(jnp.float32).reshape(1, width)
        for ref in (
            out_bias_ref,
            first_gain_ref,
            first_shift_ref,
            outer_bias_ref,
            second_gain_ref,
            second_shift_ref,
        )
    )
    loads[0].wait()
    branch = dot(att_ref[...], out_w[...]) + out_bias
    normed, root_one = normalize(x_ref[...].astype(jnp.float32) + branch)
    first = normed * first_gain + first_shift
    first_ref[...] = first
    normed_ref[...] = normed
    low_ref[...] = first.astype(jnp.bfloat16)
    total[...] = jnp.zeros_like(total)

    for t, at in enumerate(parts):
        loads[1 + 2 * t].wait()
        inner = dot(low_ref[...], inner_w[:, at]) + bias_ref[0:1, at]
        cumulative = 0.5 + 0.5 * lax.erf(inner * (0.5**0.5))
        density = jnp.exp(-0.5 * inner * inner) * 0.3989422804014327
        slope[:, at] = cumulative + inner * density
        act = (inner * cumulative).astype(jnp.bfloat16)
        act_ref[:, at] = act
        stores[t][0].start()
        loads[2 + 2 * t].wait()
        total[...] += dot(act, outer_w[at, :])
    normed_two, root_two = normalize(first_ref[...] + total[...] + outer_bias)
    output_ref[...] = (normed_two * second_gain + second_shift).astype(jnp.bfloat16)
    upstream = cot_ref[...].astype(jnp.float32)
    vec_out[4:5, :] = jnp.sum(upstream * normed_two, axis=0, keepdims=True)
    vec_out[5:6, :] = jnp.sum(upstream, axis=0, keepdims=True)
    delta_two = normalize_back(upstream * second_gain, normed_two, root_two)
    low_two = delta_two.astype(jnp.bfloat16)
    dsecond_ref[...] = low_two
    vec_out[3:4, :] = jnp.sum(low_two.astype(jnp.float32), axis=0, keepdims=True)
    total[...] = delta_two
    for t, at in enumerate(parts):
        dact = dot(dsecond_ref[...], outer_w[at, :], 1, 1)
        dinner = (dact * slope[:, at]).astype(jnp.bfloat16)
        dinner_ref[:, at] = dinner
        stores[t][1].start()
        bias_ref[0:1, at] = jnp.sum(dinner.astype(jnp.float32), axis=0, keepdims=True)
        total[...] += dot(dinner, inner_w[:, at], 1, 1)
    for i in range(inner_width // width):
        vec_out[6 + i : 7 + i, :] = bias_ref[0:1, width * i : width * (i + 1)]
    delta_first = total[...]
    normed = normed_ref[...]
    vec_out[1:2, :] = jnp.sum(delta_first * normed, axis=0, keepdims=True)
    vec_out[2:3, :] = jnp.sum(delta_first, axis=0, keepdims=True)
    delta_one = normalize_back(delta_first * first_gain, normed, root_one)
    delta_ref[...] = delta_one
    low_one = delta_one.astype(jnp.bfloat16)
    dbranch_ref[...] = low_one
    vec_out[0:1, :] = jnp.sum(low_one.astype(jnp.float32), axis=0, keepdims=True)
    vec_out[10:16, :] = jnp.zeros((6, width), jnp.float32)
    datt_ref[...] = dot(low_one, out_w[...], 1, 1).astype(jnp.bfloat16)
    for pair in stores:
        for copy in pair:
            copy.wait()


def mlp(att, x_my, cot_my, vectors, out_weight, inner_weight, outer_weight, tile):
    block, width = x_my.shape
    inner_width = inner_weight.shape[1]
    low, full = jnp.bfloat16, jnp.float32
    vmem = pl.BlockSpec(memory_space=pltpu.VMEM)
    hbm = pl.BlockSpec(memory_space=pl.ANY)
    shape = jax.ShapeDtypeStruct
    return pl.pallas_call(
        functools.partial(mlp_kernel, tile),
        out_shape=[
            shape((block, width), low),
            shape((block, width), full),
            shape((block, width), low),
            shape((block, width), low),
            shape((block, width), low),
            shape((block, width), low),
            shape((16, width), full),
            shape((block, inner_width), low),
            shape((block, inner_width), low),
        ],
        in_specs=[vmem] * 10 + [hbm] * 3,
        out_specs=[vmem] * 7 + [hbm] * 2,
        scratch_shapes=[
            pltpu.VMEM((block, inner_width), low),
            pltpu.VMEM((block, inner_width), low),
            pltpu.VMEM((8, inner_width), full),
            pltpu.VMEM(out_weight.shape, low),
            pltpu.VMEM(inner_weight.shape, low),
            pltpu.VMEM(outer_weight.shape, low),
            pltpu.VMEM((block, inner_width), full),
            pltpu.VMEM((block, width), full),
            pltpu.VMEM((block, width), full),
            pltpu.VMEM((block, width), full),
            pltpu.SemaphoreType.DMA((1 + 4 * (inner_width // tile),)),
        ],
        compiler_params=pltpu.CompilerParams(vmem_limit_bytes=60 << 20),
        name="mlp",
    )(att, x_my, cot_my, *vectors, out_weight, inner_weight, outer_weight)


def rows_of(start, q, size):
    return pl.ds(pl.multiple_of(start * q, 16), size * q)


def add_into(count, target, other):
    def one(i, carry):
        target(i)[...] = (
            target(i)[...].astype(jnp.float32) + other(i)[...].astype(jnp.float32)
        ).astype(jnp.bfloat16)
        return carry

    lax.fori_loop(0, count, one, 0)


def reduce_steps(parts, g_ref, f_ref, buffers, sems):
    core_in, a_one, b_one, ab_two, z_one, z_two = buffers
    zh, zl, x, y, c = coordinates()
    q = g_ref.shape[3] // 8
    width = g_ref.shape[4] // parts
    over_c, over_y = device(zh, zl, x, y, 1 - c), device(zh, zl, x, 1 - y, c)
    over_x, over_zl = device(zh, zl, 1 - x, y, c), device(zh, 1 - zl, x, y, c)
    over_zh = device(1 - zh, zl, x, y, c)
    flying = {}

    def send(name, k, src, dst, peer):
        copy = remote(src, dst, (sems[0].at[name], sems[1].at[name]), k, peer)
        copy.start()
        flying[name, k] = copy

    def arrive(name, k):
        flying.pop((name, k)).wait()

    def step(stage, k):
        cols = pl.ds(k * width, width)
        if stage == 0:
            send(
                0, k, g_ref.at[:, :, :, rows_of(4 * (1 - c), q, 4), cols], core_in.at[:, :, :, :, cols], over_c
            )
        if stage == 1:
            arrive(0, k)
            add_into(
                8,
                lambda i: core_in.at[i // 4, (i // 2) % 2, i % 2, :, cols],
                lambda i: g_ref.at[i // 4, (i // 2) % 2, i % 2, rows_of(4 * c, q, 4), cols],
            )
            send(1, k, core_in.at[:, :, 1 - x, pl.ds(0, 2 * q), cols], a_one.at[:, :, :, cols], over_x)
            send(2, k, core_in.at[:, :, :, rows_of(3 - y, q, 1), cols], b_one.at[:, :, :, :, cols], over_y)
        if stage == "2a":
            arrive(1, k)
            add_into(
                4,
                lambda i: a_one.at[i // 2, i % 2, :, cols],
                lambda i: core_in.at[i // 2, i % 2, x, pl.ds(0, 2 * q), cols],
            )
            send(3, k, a_one.at[:, :, rows_of(1 - y, q, 1), cols], ab_two.at[0, :, :, :, cols], over_y)
        if stage == "2b":
            arrive(2, k)
            add_into(
                8,
                lambda i: b_one.at[i // 4, (i // 2) % 2, i % 2, :, cols],
                lambda i: core_in.at[i // 4, (i // 2) % 2, i % 2, rows_of(2 + y, q, 1), cols],
            )
            send(4, k, b_one.at[:, :, 1 - x, :, cols], ab_two.at[1, :, :, :, cols], over_x)
        if stage == 3:
            arrive(3, k)
            add_into(
                4,
                lambda i: ab_two.at[0, i // 2, i % 2, :, cols],
                lambda i: a_one.at[i // 2, i % 2, rows_of(y, q, 1), cols],
            )
            arrive(4, k)
            add_into(
                4,
                lambda i: ab_two.at[1, i // 2, i % 2, :, cols],
                lambda i: b_one.at[i // 2, i % 2, x, :, cols],
            )
            send(5, k, ab_two.at[:, :, 1 - zl, :, cols], z_one.at[:, :, :, cols], over_zl)
        if stage == 4:
            arrive(5, k)
            add_into(
                4,
                lambda i: z_one.at[i // 2, i % 2, :, cols],
                lambda i: ab_two.at[i // 2, i % 2, zl, :, cols],
            )
            send(6, k, z_one.at[:, 1 - zh, :, cols], z_two.at[:, :, cols], over_zh)
        if stage == 5:
            arrive(6, k)
            for part in range(2):
                f_ref[c, part, y, :, cols] = (
                    z_two[part, :, cols].astype(jnp.float32) + z_one[part, zh, :, cols].astype(jnp.float32)
                ).astype(jnp.bfloat16)
            own_rows = f_ref.at[c, :, y, :, cols]
            send(7, k, own_rows, own_rows, over_y)
        if stage == 6:
            arrive(7, k)
            both = f_ref.at[c, :, :, :, cols]
            send(8, k, both, both, over_c)
        if stage == 7:
            arrive(8, k)

    return step


BACKWARD_ORDER = (
    "begin",
    "home0",
    "st:0",
    "datt",
    "g1",
    "S0",
    "g2",
    "st:1",
    "r1:0",
    "take:5",
    "take:2",
    "r1:1",
    "take:3",
    "take:1",
    "st:2",
    "hE0",
    "take:4",
    "take:0",
    "at:5",
    "st:3",
    "at:2",
    "r2b:0",
    "at:1",
    "r2a:0",
    "at:4",
    "r1:2",
    "r2b:1",
    "r1:3",
    "r2a:1",
    "at:0",
    "st:4",
    "r3:0",
    "at:3",
    "pl:0",
    "pl:1",
    "pl:2",
    "pl:3",
    "r2b:2",
    "r2a:2",
    "ph:1",
    "ph:2",
    "r4:0",
    "ph:0",
    "ph:3",
    "ab:1",
    "dw",
    "r3:1",
    "r2b:3",
    "stE",
    "ab:0",
    "r2a:3",
    "r5:0",
    "r1:4",
    "r1:5",
    "r3:2",
    "hb:1",
    "r4:1",
    "ha:1",
    "hb:0",
    "r4:2",
    "da",
    "ha:0",
    "r5:1",
    "r3:3",
    "r6:0",
    "r5:2",
    "r7:0",
    "r2a:4",
    "r2b:4",
    "r2a:5",
    "hm:1",
    "r4:3",
    "r2b:5",
    "r6:1",
    "hm:0",
    "r6:2",
    "r7:1",
    "wy",
    "r7:2",
    "hE:1",
    "r3:4",
    "r5:3",
    "r3:5",
    "r4:4",
    "hE:0",
    "wc",
    "r4:5",
    "r6:3",
    "r5:4",
    "wE",
    "r7:3",
    "r5:5",
    "r6:4",
    "r7:4",
    "r6:5",
    "r7:5",
)


def backward_kernel(
    parts,
    datt_ref,
    out_my,
    stats_ref,
    vec_ref,
    att_hbm,
    dbranch_hbm,
    low_hbm,
    dsecond_hbm,
    act_hbm,
    dinner_hbm,
    sorted_hbm,
    prob_hbm,
    wsel_hbm,
    x_hbm,
    delta_hbm,
    gather_hbm,
    scatter_hbm,
    out_home,
    grad_home,
    f_ref,
    w_all,
    stats_out,
    att_ref,
    dbranch_ref,
    low_ref,
    dsecond_ref,
    act_ref,
    dinner_ref,
    sorted_ref,
    prob_ref,
    wsel_ref,
    x_all,
    delta_ref,
    g_ref,
    datt_send,
    datt_in,
    gather,
    gathered,
    dsorted,
    scatter,
    dqkv,
    part_send,
    part_in,
    total,
    a_in,
    b_in,
    a_two,
    b_two,
    grad_my,
    dw,
    dw_y,
    dw_in,
    dw_all,
    stats_buf,
    stats_in,
    core_in,
    a_one,
    b_one,
    ab_two,
    z_one,
    z_two,
    datt_ssem,
    datt_rsem,
    part_ssem,
    part_rsem,
    swap_ssem,
    swap_rsem,
    dw_ssem,
    dw_rsem,
    stats_ssem,
    stats_rsem,
    red_ssem,
    red_rsem,
    load_sem,
    matrix_sem,
):
    zh, zl, x, y, c = coordinates()
    s = 4 * zh + 2 * zl + x
    j = 2 * zl + x
    p = 4 * c + j
    block, width = datt_ref.shape
    group = 8 * block
    scale = 0.125
    matched = c == zh
    datt_sems, part_sems = (datt_ssem, datt_rsem), (part_ssem, part_rsem)
    swap_sems, dw_sems, stats_sems = (swap_ssem, swap_rsem), (dw_ssem, dw_rsem), (stats_ssem, stats_rsem)

    def member(flip):
        fc, fz, fx = flip // 4, (flip // 2) % 2, flip % 2
        mc, mz, mx = bits(c, fc), bits(zl, fz), bits(x, fx)
        return device(zh, mz, mx, y, mc), mc, 2 * mz + mx

    peers = [member(flip)[0] for flip in range(1, 8)]
    sibling, over_x, over_z = peers[3], peers[0], peers[1]
    swap_peer = device(1 - zh, zl, x, y, 1 - c)
    over_y = device(zh, zl, x, 1 - y, c)
    across = [device(1 - zh, bits(zl, f // 2), bits(x, f % 2), y, c) for f in range(4)]
    loads = [
        pltpu.make_async_copy(src, dst, load_sem.at[i])
        for i, (src, dst) in enumerate(
            (
                (att_hbm, att_ref),
                (dbranch_hbm, dbranch_ref),
                (low_hbm, low_ref),
                (dsecond_hbm, dsecond_ref),
                (act_hbm, act_ref),
                (dinner_hbm, dinner_ref),
                (sorted_hbm, sorted_ref),
                (prob_hbm, prob_ref),
                (wsel_hbm, wsel_ref),
                (x_hbm, x_all),
                (delta_hbm, delta_ref),
            )
        )
    ]
    for copy in loads:
        copy.start()
    greet(peers + [swap_peer, over_y] + across)

    def home_copy(src, dst, index, start):
        away = remote(src, dst, swap_sems, index, swap_peer)
        here = pltpu.make_async_copy(src, dst, swap_rsem.at[3 + index])

        @pl.when(matched)
        def _():
            here.start() if start else here.wait()

        @pl.when(jnp.logical_not(matched))
        def _():
            away.start() if start else away.wait()

    def tile(mc, mj):
        first = datt_ref[:, pl.ds(pl.multiple_of(mj * 128, 128), 128)]
        other = datt_ref[:, pl.ds(pl.multiple_of((4 + mj // 2) * 128, 128), 128)]
        return join(
            select_head(other.astype(jnp.float32), mj % 2, 0), select_head(first.astype(jnp.float32), mc, 1)
        ).astype(jnp.bfloat16)

    datt_copies = []

    def datt_out():
        for flip in (3, 7, 1, 5, 2, 6, 4):
            peer, mc, mj = member(flip)
            datt_send[flip] = tile(mc, mj)
            copy = remote(datt_send.at[flip], datt_in.at[p], datt_sems, flip - 1, peer)
            copy.start()
            datt_copies.append(copy)
        datt_in[p] = tile(c, j)

    stats_peers = (sibling, over_x, over_z, across[0], over_y)
    stats_copies = [
        remote(stats_buf.at[k], stats_in.at[k], stats_sems, k, peer) for k, peer in enumerate(stats_peers)
    ]

    def stats_step(k):
        if k == 0:
            stats_buf[0] = stats_ref[...]
        else:
            stats_copies[k - 1].wait()
            stats_buf[k] = stats_buf[k - 1] + stats_in[k - 1]
        if k < len(stats_peers):
            stats_copies[k].start()
        else:
            stats_out[...] = stats_buf[k]

    share = width // 8
    q = g_ref.shape[3] // 8
    top = 4 * q

    def outer_grads():
        def one(d, carry):
            columns = pl.ds(pl.multiple_of(d * 4 * share, 128), 4 * share)
            g_ref[d // 4, (d // 2) % 2, d % 2, top : top + 4 * share, :] = dot(
                act_ref[:, columns], dsecond_ref[...], 0, 0
            ).astype(jnp.bfloat16)
            return carry

        lax.fori_loop(0, 8, one, 0)

    def inner_grads():
        def one(i, carry):
            z, n = i // 4, i % 4
            rows = pl.ds(pl.multiple_of(z * 4 * share, 128), 4 * share)
            columns = pl.ds(pl.multiple_of(n * width, 128), width)
            grads = dot(low_ref[:, rows], dinner_ref[:, columns], 0, 0).astype(jnp.bfloat16)
            for k in range(4):
                at = pl.ds(pl.multiple_of(n * share, 16), share)
                g_ref[z, k // 2, k % 2, at, :] = grads[share * k : share * (k + 1)]
            return carry

        lax.fori_loop(0, 8, one, 0)

    def grads_first():
        for copy in loads[:6]:
            copy.wait()
        vectors = vec_ref[...].astype(jnp.bfloat16)
        for z in range(2):
            columns = slice(4 * share * z, 4 * share * (z + 1))
            grads = dot(att_ref[:, columns], dbranch_ref[...], 0, 0).astype(jnp.bfloat16)
            for k in range(4):
                rows = grads[share * k : share * (k + 1)]
                g_ref[z, k // 2, k % 2, 4 * share : 4 * share + share // 2, :] = rows[: share // 2]
                g_ref[z, k // 2, k % 2, 4 * share + share // 2 : top, :] = jnp.zeros_like(vectors)
                g_ref[z, k // 2, k % 2, top + 4 * share : top + 4 * share + share // 2, :] = rows[share // 2 :]
                g_ref[z, k // 2, k % 2, top + 4 * share + share // 2 :, :] = vectors
        pl.when(c == 0)(outer_grads)
        pl.when(c == 1)(inner_grads)

    def grads_second():
        pl.when(c == 0)(inner_grads)
        pl.when(c == 1)(outer_grads)

    reduction = reduce_steps(
        parts,
        g_ref,
        f_ref,
        (core_in, a_one, b_one, ab_two, z_one, z_two),
        (red_ssem, red_rsem),
    )

    step = gather.shape[1]
    chunks = [int(name.partition(":")[2]) for name in BACKWARD_ORDER if name.startswith("take:")]
    blocks = [
        4 * (1 - c if name.startswith("pl:") else c) + int(name.partition(":")[2])
        for name in BACKWARD_ORDER
        if name.startswith("pl:") or name.startswith("ph:")
    ]
    gather_loads = [
        pltpu.make_async_copy(gather_hbm.at[pl.ds(k * step, step)], gather.at[i % 2], matrix_sem.at[0, i])
        for i, k in enumerate(chunks)
    ]
    scatter_loads = [
        pltpu.make_async_copy(
            scatter_hbm.at[pl.ds(pl.multiple_of(k * block, block), block)], scatter.at[i % 2], matrix_sem.at[1, i]
        )
        for i, k in enumerate(blocks)
    ]

    def begin():
        for copy in gather_loads[:2] + scatter_loads[:2]:
            copy.start()

    taken = []

    def take(k):
        if not taken:
            for copy in datt_copies:
                copy.wait()
        i = len(taken)
        taken.append(k)
        gather_loads[i].wait()
        gathered[k * step : (k + 1) * step, :] = dot(
            gather[i % 2], datt_in[...].reshape(group, 128)
        ).astype(jnp.bfloat16)
        if i + 2 < len(chunks):
            gather_loads[i + 2].start()

    def attend_back(first_lanes):
        def one(i, carry):
            at = pl.ds(pl.multiple_of(i * 128, 128), 128)
            tile_zero, tile_one = sorted_ref[at, 0:128], sorted_ref[at, 128:256]
            low_lanes = lanes((128, 128)) < 64
            query_lanes = low_lanes if first_lanes else jnp.logical_not(low_lanes)
            weights = prob_ref[at, :]
            taken = gathered[at, :]
            taken = jnp.where(query_lanes, jnp.zeros_like(taken), taken)
            weight_grads = dot(taken, tile_zero, 1, 1)
            inside = jnp.sum(weights * weight_grads, axis=1, keepdims=True)
            score_grads = weights * (weight_grads - inside)
            low_grads = score_grads.astype(jnp.bfloat16)
            query_grads = dot(low_grads, tile_one) * scale
            key_grads = dot(low_grads, tile_zero, 0, 0) * scale
            value_grads = dot(weights.astype(jnp.bfloat16), taken, 0, 0)
            dsorted[at, 0:128] = jnp.where(query_lanes, query_grads, value_grads).astype(jnp.bfloat16)
            dsorted[at, 128:256] = jnp.where(query_lanes, key_grads, 0.0).astype(jnp.bfloat16)
            return carry

        return one

    loaded = []

    def attend_some(i):
        if not loaded:
            for copy in loads[6:]:
                copy.wait()
            loaded.append(True)
        lax.fori_loop(4 * i, 4 * i + 4, attend_back(i < 4), 0, unroll=4)

    placed = []

    def place(position):
        i = len(placed)
        placed.append(position)
        scatter_loads[i].wait()
        matrix = scatter.at[i % 2]
        at = pl.ds(pl.multiple_of(position * block, block), block)
        dqkv[at, 0:256] = dot(matrix[:, 0:group], dsorted[0:group, :]).astype(jnp.bfloat16)
        dqkv[at, 256:512] = dot(matrix[:, group:], dsorted[group:, :]).astype(jnp.bfloat16)
        if i + 2 < len(blocks):
            scatter_loads[i + 2].start()
        return dot(dqkv[at, :], wsel_ref[...], 1, 1)

    part_copies = [remote(part_send.at[k], part_in.at[k], part_sems, k, sibling) for k in range(4)]

    def part_away(k):
        part_send[k] = place(4 * (1 - c) + k).astype(jnp.bfloat16)
        part_copies[k].start()

    def part_here(k):
        part = place(4 * c + k)
        part_copies[k].wait()
        total[k // 2, k % 2] = (part + part_in[k].astype(jnp.float32)).astype(jnp.bfloat16)

    upper, lower = pl.ds(0, block // 2), pl.ds(block // 2, block // 2)
    pieces = [pl.ds(i * (width // 2), width // 2) for i in range(2)]
    a_copies = [
        remote(total.at[:, 1 - x, upper, cols], a_in.at[:, :, cols], part_sems, 4 + i, over_x)
        for i, cols in enumerate(pieces)
    ]
    b_copies = [
        remote(total.at[1 - zl, :, lower, cols], b_in.at[:, :, cols], part_sems, 6 + i, over_z)
        for i, cols in enumerate(pieces)
    ]
    a_next = [
        remote(a_in.at[1 - zl, :, cols], a_two.at[:, cols], part_sems, 8 + i, over_z)
        for i, cols in enumerate(pieces)
    ]
    b_next = [
        remote(b_in.at[1 - x, :, cols], b_two.at[:, cols], part_sems, 10 + i, over_x)
        for i, cols in enumerate(pieces)
    ]

    def first_hops(i):
        a_copies[i].start()
        b_copies[i].start()

    def second_hop_a(i):
        cols = pieces[i]
        a_copies[i].wait()
        add_into(2, lambda k: a_in.at[k, :, cols], lambda k: total.at[k, x, upper, cols])
        a_next[i].start()

    def second_hop_b(i):
        cols = pieces[i]
        b_copies[i].wait()
        add_into(2, lambda k: b_in.at[k, :, cols], lambda k: total.at[zl, k, lower, cols])
        b_next[i].start()

    def grad_home_start(i):
        cols = pieces[i]
        a_next[i].wait()
        b_next[i].wait()
        for start, first, second, index in ((0, a_two, a_in, zl), (block // 2, b_two, b_in, x)):
            at = pl.ds(start, block // 2)
            grad_my[at, cols] = (
                delta_ref[at, cols]
                + first[:, cols].astype(jnp.float32)
                + second[index, :, cols].astype(jnp.float32)
            ).astype(jnp.bfloat16)
        home_copy(grad_my.at[:, cols], grad_home.at[:, cols], 1 + i, True)

    def grad_home_end(i):
        cols = pieces[i]
        home_copy(grad_my.at[:, cols], grad_home.at[:, cols], 1 + i, False)

    over_y_copy = remote(dw_y.at[1 - y], dw_in, dw_sems, 0, over_y)

    def projections():
        for k in range(width // 128):
            dw[128 * k : 128 * (k + 1), :] = dot(
                x_all[:, 128 * k : 128 * (k + 1)], dqkv[...], 0, 0
            ).astype(jnp.bfloat16)
        bias_row = jnp.broadcast_to(
            jnp.sum(dqkv[...].astype(jnp.float32), axis=0, keepdims=True), (16, 512)
        ).astype(jnp.bfloat16)
        for d in range(8):
            for h in range(2):
                dw_y[h, d, 0:share, :] = dw[share * d : share * (d + 1), 256 * h : 256 * (h + 1)]
                dw_y[h, d, share : share + 16, :] = bias_row[:, 256 * h : 256 * (h + 1)]
        over_y_copy.start()

    targets = across + [over_x, over_z, peers[2]]
    flips = [(1, f // 2, f % 2) for f in range(4)] + [(0, 0, 1), (0, 1, 0), (0, 1, 1)]
    dw_copies = []
    for i, (peer, (fh, fz, fx)) in enumerate(zip(targets, flips)):
        d = 4 * bits(zh, fh) + 2 * bits(zl, fz) + bits(x, fx)
        dw_copies.append(remote(dw_y.at[y, d], dw_all.at[s], dw_sems, 1 + i, peer))
    w_over_y = remote(w_all.at[y, c], w_all.at[y, c], dw_sems, 8, over_y)
    w_over_c = remote(w_all.at[:, c], w_all.at[:, c], dw_sems, 9, sibling)

    def dw_exchange():
        over_y_copy.wait()
        add_into(8, lambda i: dw_y.at[y, i], lambda i: dw_in.at[i])
        for copy in dw_copies:
            copy.start()
        dw_all[s] = dw_y[y, s]

    def dw_sum():
        for copy in dw_copies:
            copy.wait()
        for k in range(4):
            w_all[y, c, k] = (dw_all[k].astype(jnp.float32) + dw_all[4 + k].astype(jnp.float32)).astype(
                jnp.bfloat16
            )
        w_over_y.start()

    def dw_core():
        w_over_y.wait()
        w_over_c.start()

    def start_reduction():
        for k in range(parts):
            reduction(0, k)

    single = {
        "begin": begin,
        "datt": datt_out,
        "home0": lambda: home_copy(out_my, out_home, 0, True),
        "hE0": lambda: home_copy(out_my, out_home, 0, False),
        "g1": grads_first,
        "g2": grads_second,
        "S0": start_reduction,
        "dw": projections,
        "da": dw_exchange,
        "wy": dw_sum,
        "wc": dw_core,
        "wE": w_over_c.wait,
        "stE": lambda: stats_step(5),
    }
    indexed = {
        "take": take,
        "at": attend_some,
        "pl": part_away,
        "ph": part_here,
        "ab": first_hops,
        "ha": second_hop_a,
        "hb": second_hop_b,
        "hm": grad_home_start,
        "hE": grad_home_end,
        "st": stats_step,
    }
    for name in BACKWARD_ORDER:
        kind, _, index = name.partition(":")
        if kind in single:
            single[kind]()
        elif kind in indexed:
            indexed[kind](int(index))
        else:
            stage = kind[1:]
            reduction(stage if stage in ("2a", "2b") else int(stage), int(index))


def backward_attention(
    datt,
    output,
    stats,
    vectors,
    att,
    dbranch,
    low_first,
    dsecond,
    act,
    dinner,
    sorted_rows,
    prob,
    wsel,
    x_all,
    delta,
    gather,
    scatter,
    parts,
):
    block, width = datt.shape
    inner_width = act.shape[1]
    group = 8 * block
    rows = group * 3 // 2
    q = (9 * width // 8 + 32) // 8
    share = width // 8 + 16
    low, full = jnp.bfloat16, jnp.float32
    vmem = pl.BlockSpec(memory_space=pltpu.VMEM)
    hbm = pl.BlockSpec(memory_space=pl.ANY)
    dma = pltpu.SemaphoreType.DMA
    shape = jax.ShapeDtypeStruct
    return pl.pallas_call(
        functools.partial(backward_kernel, parts),
        out_shape=[
            shape((block, width), low),
            shape((block, width), low),
            shape((2, 2, 2, q, width), low),
            shape((2, 2, 4, share, 256), low),
            shape(stats.shape, full),
        ],
        in_specs=[vmem] * 4 + [hbm] * 13,
        out_specs=[vmem] * 5,
        scratch_shapes=[
            pltpu.VMEM((block, width), low),
            pltpu.VMEM((block, width), low),
            pltpu.VMEM((block, width), low),
            pltpu.VMEM((block, width), low),
            pltpu.VMEM((block, inner_width), low),
            pltpu.VMEM((block, inner_width), low),
            pltpu.VMEM((rows, 256), low),
            pltpu.VMEM((rows, 128), full),
            pltpu.VMEM((width, 512), low),
            pltpu.VMEM((group, width), low),
            pltpu.VMEM((block, width), full),
            pltpu.VMEM((2, 2, 2, 8 * q, width), low),
            pltpu.VMEM((8, block, 128), low),
            pltpu.VMEM((8, block, 128), low),
            pltpu.VMEM((2, 512, group), low),
            pltpu.VMEM((rows, 128), low),
            pltpu.VMEM((rows, 256), low),
            pltpu.VMEM((2, block, rows), low),
            pltpu.VMEM((group, 512), low),
            pltpu.VMEM((4, block, width), low),
            pltpu.VMEM((4, block, width), low),
            pltpu.VMEM((2, 2, block, width), low),
            pltpu.VMEM((2, block // 2, width), low),
            pltpu.VMEM((2, block // 2, width), low),
            pltpu.VMEM((block // 2, width), low),
            pltpu.VMEM((block // 2, width), low),
            pltpu.VMEM((block, width), low),
            pltpu.VMEM((width, 512), low),
            pltpu.VMEM((2, 8, share, 256), low),
            pltpu.VMEM((8, share, 256), low),
            pltpu.VMEM((8, share, 256), low),
            pltpu.VMEM((6,) + stats.shape, full),
            pltpu.VMEM((5,) + stats.shape, full),
            pltpu.VMEM((2, 2, 2, 4 * q, width), low),
            pltpu.VMEM((2, 2, 2 * q, width), low),
            pltpu.VMEM((2, 2, 2, q, width), low),
            pltpu.VMEM((2, 2, 2, q, width), low),
            pltpu.VMEM((2, 2, q, width), low),
            pltpu.VMEM((2, q, width), low),
            dma((7,)),
            dma((7,)),
            dma((12,)),
            dma((12,)),
            dma((6,)),
            dma((6,)),
            dma((10,)),
            dma((10,)),
            dma((5,)),
            dma((5,)),
            dma((9, parts)),
            dma((9, parts)),
            dma((11,)),
            dma((2, 8)),
        ],
        compiler_params=pltpu.CompilerParams(
            collective_id=2, has_side_effects=True, vmem_limit_bytes=62 << 20
        ),
        name="backward_attention",
    )(
        datt,
        output,
        stats,
        vectors,
        att,
        dbranch,
        low_first,
        dsecond,
        act,
        dinner,
        sorted_rows,
        prob,
        wsel,
        x_all.reshape(group, width),
        delta,
        gather,
        scatter,
    )


def finish_kernel(
    f_ref,
    w_ref,
    out_ref,
    grad_ref,
    stats_ref,
    output,
    grad_tokens,
    gq_out,
    gqb_out,
    gk_out,
    gv_out,
    gvb_out,
    go_out,
    gob_out,
    gfg_out,
    gfs_out,
    gi_out,
    gib_out,
    gu_out,
    gub_out,
    gsg_out,
    gss_out,
    stats_out,
    gq_ref,
    gv_ref,
    vec_ref,
):
    s = lax.axis_index("seq")
    output[0] = out_ref[...]
    grad_tokens[0] = grad_ref[...]
    stats_out[...] = stats_ref[:, : stats_out.shape[1], : stats_out.shape[2]]
    share, width = gk_out.shape
    top = f_ref.shape[0] // 2
    full = jnp.float32
    for n in range(gi_out.shape[1] // width):
        gi_out[:, n * width : (n + 1) * width] = f_ref[n * share : (n + 1) * share, :].astype(full)
    gu_out[...] = f_ref[top : top + 4 * share, :].astype(full)
    part = share // 2
    go_out[0:part, :] = f_ref[4 * share : 4 * share + part, :].astype(full)
    go_out[part:, :] = f_ref[top + 4 * share : top + 4 * share + part, :].astype(full)
    vec_ref[...] = f_ref[top + 4 * share + part :, :].astype(full)
    for pair in range(4):
        at = slice(128 * pair, 128 * pair + 128)
        low, high = (w_ref[0, core, pair].astype(full) for core in range(2))
        gq_ref[:, at] = join(low[:, 0:128], half_roll(high[:, 0:128]))
        gk_out[:, at] = join(low[:, 128:256], half_roll(high[:, 128:256]))[:share]
        gv_ref[:, at] = join(half_roll(low[:, 0:128]), high[:, 0:128])
    for pair in range(2):
        at = slice(512 + 128 * pair, 640 + 128 * pair)
        low, high = (
            w_ref[1, 0, 2 * pair + i].astype(full) + w_ref[1, 1, 2 * pair + i].astype(full) for i in range(2)
        )
        gq_ref[:, at] = join(half_roll(low[:, 0:128]), high[:, 0:128])
        gk_out[:, at] = join(half_roll(low[:, 128:256]), high[:, 128:256])[:share]
        gv_ref[:, at] = join(low[:, 0:128], half_roll(high[:, 0:128]))
    gq_out[...] = gq_ref[:share, :]
    gv_out[...] = gv_ref[:share, :]

    def mine(rows):
        return pltpu.roll(rows, width - share * s, 1)[:, :share]

    short = mine(vec_ref[...])
    for row, ref in enumerate((gob_out, gfg_out, gfs_out, gub_out, gsg_out, gss_out)):
        ref[...] = short[row]
    gqb_out[...] = mine(gq_ref[share : share + 8, :])[0]
    gvb_out[...] = mine(gv_ref[share : share + 8, :])[0]
    row = vec_ref[pl.ds(6 + s // 2, 1), :]
    gib_out[...] = jnp.where(s % 2 == 1, row[:, 4 * share :], row[:, : 4 * share])[0]


def finish(reduced, w_all, output, grad, totals, head_count, inner_width):
    block, width = output.shape
    row_count = 8 * reduced.shape[3]
    share = width // 8
    low, full = jnp.bfloat16, jnp.float32
    vmem = pl.BlockSpec(memory_space=pltpu.VMEM)
    shape = jax.ShapeDtypeStruct
    square, vector = shape((share, width), full), shape((share,), full)
    out_shape = [
        shape((1, block, width), low),
        shape((1, block, width), low),
        square,
        vector,
        square,
        square,
        vector,
        square,
        vector,
        vector,
        vector,
        shape((share, inner_width), full),
        shape((inner_width // 8,), full),
        shape((inner_width // 8, width), full),
        vector,
        vector,
        vector,
        shape((2, head_count, 8), full),
    ]
    return pl.pallas_call(
        finish_kernel,
        out_shape=out_shape,
        in_specs=[vmem] * 5,
        out_specs=[vmem] * len(out_shape),
        scratch_shapes=[
            pltpu.VMEM((share + 16, width), full),
            pltpu.VMEM((share + 16, width), full),
            pltpu.VMEM((16, width), full),
        ],
        compiler_params=pltpu.CompilerParams(vmem_limit_bytes=60 << 20),
        name="finish",
    )(reduced.reshape(row_count, width), w_all, output, grad, totals)


def body(
    tokens,
    segments,
    orders,
    owners,
    query_weight,
    query_bias,
    key_weight,
    value_weight,
    value_bias,
    out_weight,
    out_bias,
    first_gain,
    first_shift,
    inner_weight,
    inner_bias,
    outer_weight,
    outer_bias,
    second_gain,
    second_shift,
    cotangent,
):
    seq_count = lax.axis_size("seq")
    groups = lax.axis_size("rep")
    own_index = lax.axis_index("seq")
    row_count = tokens.shape[1]
    model_width = tokens.shape[2]
    order_table = orders[0]
    owner_table = owners[0]
    head_count, group_tokens = order_table.shape
    cluster_count = owner_table.shape[1]
    cluster = group_tokens // cluster_count
    head_dim = model_width // head_count
    per_owner = row_count // cluster
    score_scale = head_dim ** (-0.5)
    flat_tokens = tokens[0]
    local_index = jnp.arange(row_count, dtype=jnp.int32)
    factor = 1
    for candidate in range(1, seq_count + 1):
        if seq_count % candidate == 0 and candidate * row_count <= 2048:
            factor = candidate
    block_count = seq_count // factor
    block_width = factor * row_count
    order_blocks = order_table.reshape(head_count, block_count, block_width).transpose(1, 0, 2)
    owner_blocks = (
        jnp.repeat(owner_table, cluster, axis=1)
        .reshape(head_count, block_count, block_width)
        .transpose(1, 0, 2)
    )

    def find_target(total, block_item):
        order_block, owner_block = block_item
        local = order_block - own_index * row_count
        hits = local[:, :, None] == local_index[None, None, :]
        return (total + jnp.sum(jnp.where(hits, owner_block[:, :, None], 0), axis=1), None)

    target, unused = lax.scan(
        find_target, jnp.zeros((head_count, row_count), jnp.int32), (order_blocks, owner_blocks)
    )
    send_matrix = rank_matrix(target * row_count + local_index[None, :])
    mine = (owner_table == own_index).astype(jnp.int32)
    before = jnp.cumsum(mine, axis=1) - mine
    slot_hot = (mine[:, None, :] == 1) & (
        before[:, None, :] == jnp.arange(per_owner, dtype=jnp.int32)[None, :, None]
    )
    order_grid = order_table.reshape(head_count, cluster_count, cluster)
    owned_tokens = jnp.sum(
        jnp.where(slot_hot[:, :, :, None], order_grid[:, None, :, :], 0), axis=2
    ).reshape(head_count, row_count)
    arrive_matrix = rank_matrix(owned_tokens)
    w_three = jnp.concatenate([query_weight, key_weight, value_weight], axis=1)
    bias_three = jnp.concatenate(
        [
            query_bias.astype(jnp.float32),
            jnp.zeros((model_width,), jnp.float32),
            value_bias.astype(jnp.float32),
        ]
    )
    projected = (
        jnp.dot(flat_tokens, w_three, preferred_element_type=jnp.float32) + bias_three
    ).astype(jnp.bfloat16)
    token_rows = (
        projected.reshape(row_count, 3, head_count, head_dim)
        .transpose(2, 0, 1, 3)
        .reshape(head_count, row_count, 3 * head_dim)
    )
    segment_rows = jnp.broadcast_to(
        segments[0].astype(jnp.bfloat16)[None, :, None], (head_count, row_count, 1)
    )
    send_values = scatter_rows(token_rows, send_matrix, seq_count)
    send_segments = scatter_rows(segment_rows, send_matrix, seq_count)
    arrived, arrived_segments = (
        lax.all_to_all(send_values, "seq", split_axis=0, concat_axis=0, tiled=True),
        lax.all_to_all(send_segments, "seq", split_axis=0, concat_axis=0, tiled=True),
    )
    cluster_rows = collect_rows(arrived, arrive_matrix, 3 * head_dim).reshape(
        head_count * per_owner, cluster, 3, head_dim
    )
    cluster_segments = collect_rows(arrived_segments, arrive_matrix, 1).reshape(
        head_count * per_owner, cluster
    )
    queries = cluster_rows[:, :, 0]
    keys_in = cluster_rows[:, :, 1]
    values = cluster_rows[:, :, 2]
    attended, log_total, entropy, occupied = cluster_forward(
        queries, keys_in, values, cluster_segments, score_scale
    )
    per_head = jnp.stack(
        [
            jnp.sum(entropy.reshape(head_count, -1), axis=1),
            jnp.sum(occupied.reshape(head_count, -1), axis=1) / cluster,
        ]
    ) / (groups * row_count)
    column = (jnp.arange(seq_count, dtype=jnp.int32) == own_index).astype(jnp.float32)
    cluster_stats = lax.psum(per_head[:, :, None] * column, ("seq", "rep"))
    leaving = scatter_rows(
        attended.reshape(head_count, row_count, head_dim), arrive_matrix, seq_count
    )
    returned = lax.all_to_all(leaving, "seq", split_axis=0, concat_axis=0, tiled=True)
    attended_rows = (
        collect_rows(returned, send_matrix, head_dim)
        .transpose(1, 0, 2)
        .reshape(row_count, model_width)
    )
    branch = jnp.dot(
        attended_rows, out_weight, preferred_element_type=jnp.float32
    ) + out_bias.astype(jnp.float32)
    first_out, normed_one, root_one = norm_forward(
        flat_tokens.astype(jnp.float32) + branch, first_gain, first_shift
    )
    first_low = first_out.astype(jnp.bfloat16)
    inner_sum = jnp.dot(
        first_low, inner_weight, preferred_element_type=jnp.float32
    ) + inner_bias.astype(jnp.float32)
    activated, gelu_pull = jax.vjp(exact_gelu, inner_sum)
    activated_low = activated.astype(jnp.bfloat16)
    second = jnp.dot(
        activated_low, outer_weight, preferred_element_type=jnp.float32
    ) + outer_bias.astype(jnp.float32)
    result, normed_two, root_two = norm_forward(first_out + second, second_gain, second_shift)
    output = result.astype(jnp.bfloat16)[None]
    upstream = cotangent[0].astype(jnp.float32)
    gradient_second_gain = jnp.sum(upstream * normed_two, axis=0)
    gradient_second_shift = jnp.sum(upstream, axis=0)
    delta_two = norm_backward(upstream, normed_two, root_two, second_gain)
    delta_second = delta_two.astype(jnp.bfloat16)
    gradient_outer_bias = jnp.sum(delta_second.astype(jnp.float32), axis=0)
    gradient_outer_weight = jnp.einsum(
        "tf,td->fd", activated_low, delta_second, preferred_element_type=jnp.float32
    )
    delta_activated = jnp.einsum(
        "td,fd->tf", delta_second, outer_weight, preferred_element_type=jnp.float32
    )
    delta_inner = gelu_pull(delta_activated)[0].astype(jnp.bfloat16)
    gradient_inner_bias = jnp.sum(delta_inner.astype(jnp.float32), axis=0)
    gradient_inner_weight = jnp.einsum(
        "td,tf->df", first_low, delta_inner, preferred_element_type=jnp.float32
    )
    delta_first = delta_two + jnp.einsum(
        "tf,df->td", delta_inner, inner_weight, preferred_element_type=jnp.float32
    )
    gradient_first_gain = jnp.sum(delta_first * normed_one, axis=0)
    gradient_first_shift = jnp.sum(delta_first, axis=0)
    delta_one = norm_backward(delta_first, normed_one, root_one, first_gain)
    delta_branch = delta_one.astype(jnp.bfloat16)
    gradient_out_bias = jnp.sum(delta_branch.astype(jnp.float32), axis=0)
    gradient_out_weight = jnp.einsum(
        "td,te->de", attended_rows, delta_branch, preferred_element_type=jnp.float32
    )
    delta_attended = jnp.einsum(
        "te,de->td", delta_branch, out_weight, preferred_element_type=jnp.float32
    ).astype(jnp.bfloat16)
    delta_rows = delta_attended.reshape(row_count, head_count, head_dim).transpose(1, 0, 2)
    send_grads = scatter_rows(delta_rows, send_matrix, seq_count)
    grad_arrived = lax.all_to_all(send_grads, "seq", split_axis=0, concat_axis=0, tiled=True)
    kept_queries, kept_keys, kept_values, kept_segments = (
        queries,
        keys_in,
        values,
        cluster_segments,
    )
    grad_cluster = collect_rows(grad_arrived, arrive_matrix, head_dim).reshape(
        head_count * per_owner, cluster, head_dim
    )
    three_grads = cluster_backward(
        kept_queries, kept_keys, kept_values, kept_segments, log_total, grad_cluster, score_scale
    )
    leaving_grads = scatter_rows(
        three_grads.reshape(head_count, row_count, 3 * head_dim), arrive_matrix, seq_count
    )
    returned_grads = lax.all_to_all(leaving_grads, "seq", split_axis=0, concat_axis=0, tiled=True)
    delta_three = (
        collect_rows(returned_grads, send_matrix, 3 * head_dim)
        .reshape(head_count, row_count, 3, head_dim)
        .transpose(1, 2, 0, 3)
        .reshape(row_count, 3 * model_width)
    )
    bias_grads = jnp.sum(delta_three.astype(jnp.float32), axis=0)
    weight_grads = jnp.einsum(
        "td,te->de", flat_tokens, delta_three, preferred_element_type=jnp.float32
    )
    gradient_tokens = (
        delta_one
        + jnp.einsum("te,de->td", delta_three, w_three, preferred_element_type=jnp.float32)
    ).astype(jnp.bfloat16)[None]
    gradient_query_weight = weight_grads[:, :model_width]
    gradient_key_weight = weight_grads[:, model_width : 2 * model_width]
    gradient_value_weight = weight_grads[:, 2 * model_width :]
    gradient_query_bias = bias_grads[:model_width]
    gradient_value_bias = bias_grads[2 * model_width :]
    pieces = (
        lax.psum_scatter(gradient_query_weight, "seq", scatter_dimension=0, tiled=True),
        lax.psum_scatter(gradient_query_bias, "seq", scatter_dimension=0, tiled=True),
        lax.psum_scatter(gradient_key_weight, "seq", scatter_dimension=0, tiled=True),
        lax.psum_scatter(gradient_value_weight, "seq", scatter_dimension=0, tiled=True),
        lax.psum_scatter(gradient_value_bias, "seq", scatter_dimension=0, tiled=True),
        lax.psum_scatter(gradient_out_weight, "seq", scatter_dimension=0, tiled=True),
        lax.psum_scatter(gradient_out_bias, "seq", scatter_dimension=0, tiled=True),
        lax.psum_scatter(gradient_first_gain, "seq", scatter_dimension=0, tiled=True),
        lax.psum_scatter(gradient_first_shift, "seq", scatter_dimension=0, tiled=True),
        lax.psum_scatter(gradient_inner_weight, "seq", scatter_dimension=0, tiled=True),
        lax.psum_scatter(gradient_inner_bias, "seq", scatter_dimension=0, tiled=True),
        lax.psum_scatter(gradient_outer_weight, "seq", scatter_dimension=0, tiled=True),
        lax.psum_scatter(gradient_outer_bias, "seq", scatter_dimension=0, tiled=True),
        lax.psum_scatter(gradient_second_gain, "seq", scatter_dimension=0, tiled=True),
        lax.psum_scatter(gradient_second_shift, "seq", scatter_dimension=0, tiled=True),
    )
    summed = (
        lax.psum(pieces[0].astype(jnp.bfloat16), "rep").astype(jnp.float32),
        lax.psum(pieces[1].astype(jnp.bfloat16), "rep").astype(jnp.float32),
        lax.psum(pieces[2].astype(jnp.bfloat16), "rep").astype(jnp.float32),
        lax.psum(pieces[3].astype(jnp.bfloat16), "rep").astype(jnp.float32),
        lax.psum(pieces[4].astype(jnp.bfloat16), "rep").astype(jnp.float32),
        lax.psum(pieces[5].astype(jnp.bfloat16), "rep").astype(jnp.float32),
        lax.psum(pieces[6].astype(jnp.bfloat16), "rep").astype(jnp.float32),
        lax.psum(pieces[7].astype(jnp.bfloat16), "rep").astype(jnp.float32),
        lax.psum(pieces[8].astype(jnp.bfloat16), "rep").astype(jnp.float32),
        lax.psum(pieces[9].astype(jnp.bfloat16), "rep").astype(jnp.float32),
        lax.psum(pieces[10].astype(jnp.bfloat16), "rep").astype(jnp.float32),
        lax.psum(pieces[11].astype(jnp.bfloat16), "rep").astype(jnp.float32),
        lax.psum(pieces[12].astype(jnp.bfloat16), "rep").astype(jnp.float32),
        lax.psum(pieces[13].astype(jnp.bfloat16), "rep").astype(jnp.float32),
        lax.psum(pieces[14].astype(jnp.bfloat16), "rep").astype(jnp.float32),
    )
    return (output, gradient_tokens) + tuple(summed) + (cluster_stats,)


def square_body(
    tokens,
    segments,
    orders,
    owners,
    query_weight,
    query_bias,
    key_weight,
    value_weight,
    value_bias,
    out_weight,
    out_bias,
    first_gain,
    first_shift,
    inner_weight,
    inner_bias,
    outer_weight,
    outer_bias,
    second_gain,
    second_shift,
    cotangent,
):
    model_width = tokens.shape[2]
    att, x_my, cot_my, wsel, order, stats, x_all, sorted_rows, prob, gather, scatter = forward_attention(
        tokens[0],
        cotangent[0],
        segments,
        orders.transpose(1, 0, 2),
        owners.transpose(1, 0, 2),
        query_bias,
        value_bias,
        query_weight,
        key_weight,
        value_weight,
    )
    vectors = (out_bias, first_gain, first_shift, outer_bias, second_gain, second_shift, inner_bias)
    output, delta, datt, low_first, dsecond, dbranch, vector_grads, act, dinner = mlp(
        att, x_my, cot_my, vectors, out_weight, inner_weight, outer_weight, 2 * model_width
    )
    output, grad, reduced, w_all, totals = backward_attention(
        datt,
        output,
        stats,
        vector_grads,
        att,
        dbranch,
        low_first,
        dsecond,
        act,
        dinner,
        sorted_rows,
        prob,
        wsel,
        x_all,
        delta,
        gather,
        scatter,
        6,
    )
    return tuple(
        finish(reduced, w_all, output, grad, totals, orders.shape[1], inner_weight.shape[1])
    )


def solution(mesh):
    square = mesh.shape["seq"] == 8 and mesh.shape["rep"] == 4
    placed = (
        P("rep", "seq", None),
        P("rep", "seq"),
        P("rep", None, None),
        P("rep", None, None),
        P(),
        P(),
        P(),
        P(),
        P(),
        P(),
        P(),
        P(),
        P(),
        P(),
        P(),
        P(),
        P(),
        P(),
        P(),
        P("rep", "seq", None),
    )
    return jax.shard_map(
        square_body if square else body,
        mesh=mesh,
        in_specs=placed,
        out_specs=(
            P("rep", "seq", None),
            P("rep", "seq", None),
            P("seq", None),
            P("seq"),
            P("seq", None),
            P("seq", None),
            P("seq"),
            P("seq", None),
            P("seq"),
            P("seq"),
            P("seq"),
            P("seq", None),
            P("seq"),
            P("seq", None),
            P("seq"),
            P("seq"),
            P("seq"),
            P(),
        ),
        check_vma=False,
    )
```

```python
import functools

import jax
import jax.numpy as jnp
from jax import lax
from jax.experimental import pallas as pl
from jax.experimental.pallas import tpu as pltpu
from jax.sharding import PartitionSpec as P

EPSILON = 1e-12
NEGATIVE = -1e30


def norm_forward(hidden, gain_vector, shift_vector):
    centre = hidden - jnp.mean(hidden, axis=-1, keepdims=True)
    root_inverse = lax.rsqrt(jnp.mean(centre * centre, axis=-1, keepdims=True) + EPSILON)
    normed = centre * root_inverse
    return (
        normed * gain_vector.astype(jnp.float32) + shift_vector.astype(jnp.float32),
        normed,
        root_inverse,
    )


def norm_backward(upstream, normed, root_inverse, gain_vector):
    scaled = upstream * gain_vector.astype(jnp.float32)
    return root_inverse * (
        scaled
        - jnp.mean(scaled, axis=-1, keepdims=True)
        - normed * jnp.mean(scaled * normed, axis=-1, keepdims=True)
    )


def exact_gelu(inner_sum):
    return jax.nn.gelu(inner_sum, approximate=False)


def rank_matrix(sort_keys):
    row_count = sort_keys.shape[1]
    ranks = jnp.sum((sort_keys[:, None, :] < sort_keys[:, :, None]).astype(jnp.int32), axis=2)
    return (ranks[:, None, :] == jnp.arange(row_count, dtype=jnp.int32)[None, :, None]).astype(
        jnp.bfloat16
    )


def scatter_rows(row_block, placing, seq_count):
    head_count, row_count, features = row_block.shape
    picked = jnp.einsum(
        "hri,hif->hrf", placing, row_block, preferred_element_type=jnp.float32
    ).astype(jnp.bfloat16)
    return picked.reshape(head_count, seq_count, row_count // seq_count * features).transpose(
        1, 0, 2
    )


def collect_rows(packed, placing, features):
    seq_count, head_count, flat_width = packed.shape
    row_block = packed.transpose(1, 0, 2).reshape(
        head_count, seq_count * flat_width // features, features
    )
    return jnp.einsum(
        "hri,hrf->hif", placing, row_block, preferred_element_type=jnp.float32
    ).astype(jnp.bfloat16)


def cluster_scores(queries, keys_in, segment_ids, score_scale):
    scores = (
        jnp.einsum("nqd,nkd->nqk", queries, keys_in, preferred_element_type=jnp.float32)
        * score_scale
    )
    allowed = segment_ids[:, :, None] == segment_ids[:, None, :]
    return (scores, allowed, jnp.where(allowed, scores, NEGATIVE))


def cluster_forward(queries, keys_in, values, segment_ids, score_scale):
    scores, allowed, masked = cluster_scores(queries, keys_in, segment_ids, score_scale)
    highest = jnp.max(masked, axis=-1, keepdims=True)
    raised = jnp.exp(masked - highest)
    totals = jnp.sum(raised, axis=-1, keepdims=True)
    weights = raised / totals
    attended = jnp.einsum(
        "nqk,nkd->nqd", weights.astype(jnp.bfloat16), values, preferred_element_type=jnp.float32
    ).astype(jnp.bfloat16)
    log_total = highest[:, :, 0] + jnp.log(totals[:, :, 0])
    entropy = log_total - jnp.sum(weights * jnp.where(allowed, scores, 0.0), axis=-1)
    occupied = jnp.sum(allowed.astype(jnp.float32), axis=-1)
    return (attended, log_total, entropy, occupied)


def cluster_backward(queries, keys_in, values, segment_ids, log_total, grad_out, score_scale):
    masked = cluster_scores(queries, keys_in, segment_ids, score_scale)[2]
    weights = jnp.exp(masked - log_total[:, :, None])
    weight_grads = jnp.einsum("nqd,nkd->nqk", grad_out, values, preferred_element_type=jnp.float32)
    value_grads = jnp.einsum(
        "nqk,nqd->nkd", weights.astype(jnp.bfloat16), grad_out, preferred_element_type=jnp.float32
    )
    score_grads = (
        weights * (weight_grads - jnp.sum(weights * weight_grads, axis=-1, keepdims=True))
    ).astype(jnp.bfloat16)
    query_grads = (
        jnp.einsum("nqk,nkd->nqd", score_grads, keys_in, preferred_element_type=jnp.float32)
        * score_scale
    )
    key_grads = (
        jnp.einsum("nqk,nqd->nkd", score_grads, queries, preferred_element_type=jnp.float32)
        * score_scale
    )
    return jnp.stack([query_grads, key_grads, value_grads], axis=2).astype(jnp.bfloat16)


MESH = pl.DeviceIdType.MESH


UNROLL = 8
PIECES = 4
FIRST = 1


def half_roll(block):
    return jnp.concatenate([block[:, 64:], block[:, :64]], axis=1)


def lanes(shape):
    return lax.broadcasted_iota(jnp.int32, shape, len(shape) - 1)


def bits(value, flip):
    return value + flip - 2 * value * flip


def coordinates():
    s, r = lax.axis_index("seq"), lax.axis_index("rep")
    return s // 4, (s // 2) % 2, s % 2, r // 2, r % 2


def device(zh, zl, x, y, c):
    return (4 * zh + 2 * zl + x, 2 * y + c)


def greet(peers):
    barrier = pltpu.get_barrier_semaphore()
    for peer in peers:
        pl.semaphore_signal(barrier, inc=1, device_id=peer, device_id_type=MESH)
    pl.semaphore_wait(barrier, len(peers))


def remote(src, dst, sems, index, peer):
    return pltpu.make_async_remote_copy(
        src_ref=src,
        dst_ref=dst,
        send_sem=sems[0].at[index],
        recv_sem=sems[1].at[index],
        device_id=peer,
        device_id_type=MESH,
    )


def dot(left, right, left_dim=1, right_dim=0):
    return lax.dot_general(
        left,
        right,
        (((left_dim,), (right_dim,)), ((), ())),
        preferred_element_type=jnp.float32,
    )


def hot(condition):
    return jnp.where(condition, 1.0, 0.0).astype(jnp.bfloat16)


def build_gather(order_ref, row, start, count, into):
    tokens = into.shape[1]

    def one(k, carry):
        at = pl.multiple_of(k * 128, 128)
        ids = order_ref[row : row + 1, pl.ds(pl.multiple_of(start + at, 128), 128)]
        column = jnp.broadcast_to(ids.astype(jnp.float32), (128, 128)).T
        lane = lanes((128, 128)).astype(jnp.float32)
        for t in range(tokens // 128):
            into[pl.ds(at, 128), t * 128 : (t + 1) * 128] = hot(column == lane + 128.0 * t)
        return carry

    lax.fori_loop(0, count // 128, one, 0)


def build_scatter(order_ref, half, first_token, into):
    group = order_ref.shape[1]

    def one(k, carry):
        at = pl.multiple_of(k * 128, 128)
        token = lax.broadcasted_iota(jnp.int32, (128, 128), 0) + (first_token + at)
        for p in range(into.shape[1] // 128):
            row, start = (0, 128 * p) if 128 * p < group else (1, half + 128 * p - group)
            ids = order_ref[row : row + 1, pl.ds(pl.multiple_of(start, 128), 128)]
            into[pl.ds(at, 128), 128 * p : 128 * (p + 1)] = hot(ids == token)
        return carry

    lax.fori_loop(0, into.shape[0] // 128, one, 0)


def select_head(slab, half, place):
    return jnp.where(half == place, slab, half_roll(slab))


def join(low_lanes, high_lanes):
    return jnp.where(lanes(low_lanes.shape) < 64, low_lanes, high_lanes)


def pick_columns(pairs, j, c):
    (q_one, q_two), (k_one, k_two), (v_one, v_two) = pairs
    zero = jnp.zeros_like(q_one)
    q1, v1, k1 = select_head(q_one, c, 0), select_head(v_one, c, 1), select_head(k_one, c, 0)
    v2, q2, k2 = (
        select_head(v_two, j % 2, 0),
        select_head(q_two, j % 2, 1),
        select_head(k_two, j % 2, 1),
    )
    return join(q1, v1), join(k1, zero), join(v2, q2), join(zero, k2)


def normalize(hidden):
    centre = hidden - jnp.mean(hidden, axis=1, keepdims=True)
    root_inverse = lax.rsqrt(jnp.mean(centre * centre, axis=1, keepdims=True) + EPSILON)
    return centre * root_inverse, root_inverse


def normalize_back(scaled, normed, root_inverse):
    return root_inverse * (
        scaled
        - jnp.mean(scaled, axis=1, keepdims=True)
        - normed * jnp.mean(scaled * normed, axis=1, keepdims=True)
    )


def forward_kernel(
    tokens_ref,
    cot_ref,
    seg_ref,
    orders_ref,
    owners_ref,
    query_bias_ref,
    value_bias_ref,
    out_bias_ref,
    first_gain_ref,
    first_shift_ref,
    outer_bias_ref,
    second_gain_ref,
    second_shift_ref,
    inner_bias_ref,
    wq_hbm,
    wk_hbm,
    wv_hbm,
    out_w_hbm,
    inner_w_hbm,
    outer_w_hbm,
    wsel_hbm,
    order_hbm,
    stats_hbm,
    x_hbm,
    sorted_hbm,
    prob_hbm,
    att_hbm,
    low_hbm,
    act_hbm,
    output_hbm,
    dsecond_hbm,
    dinner_hbm,
    delta_hbm,
    dbranch_hbm,
    vec_hbm,
    datt_hbm,
    wsel_ref,
    order_ref,
    stats_ref,
    x_all,
    sorted_ref,
    prob_ref,
    att_ref,
    low_ref,
    act_ref,
    output_ref,
    dsecond_ref,
    dinner_ref,
    delta_ref,
    dbranch_ref,
    vec_out,
    datt_ref,
    cot_my,
    weights,
    orders_in,
    owners_in,
    owner_pad,
    seg_src,
    seg_all,
    bias_rows,
    bias_sel,
    tok,
    gather,
    scatter,
    att_sorted,
    att_send,
    att_in,
    ent_ref,
    cnt_ref,
    swap_send,
    swap_recv,
    ring_send,
    ring_recv,
    seg_send,
    seg_recv,
    back_send,
    back_recv,
    local_sem,
    out_w,
    inner_w,
    outer_w,
    slope,
    total,
    normed_ref,
    bias_ref,
    load_sem,
    store_sem,
):
    zh, zl, x, y, c = coordinates()
    j = 2 * zl + x
    p = 4 * c + j
    block, width = tokens_ref.shape
    group = 8 * block
    scale = 0.125
    swap = (swap_send, swap_recv)
    ring = (ring_send, ring_recv)
    seg_sems = (seg_send, seg_recv)
    back = (back_send, back_recv)

    def member(flip):
        fc, fz, fx = flip // 4, (flip // 2) % 2, flip % 2
        mc, mz, mx = bits(c, fc), bits(zl, fz), bits(x, fx)
        return device(zh, mz, mx, y, mc), 4 * mc + 2 * mz + mx

    swap_peer = device(1 - zh, zl, x, y, 1 - c)
    peers = [member(flip)[0] for flip in range(1, 8)]
    sibling = peers[3]
    over_x, over_z = peers[0], peers[1]
    matched = c == zh

    slabs = [
        pltpu.make_async_copy(
            src.at[:, pl.ds(pl.multiple_of(index * 128, 128), 128)],
            weights.at[i, slot],
            local_sem.at[3 * slot + i],
        )
        for i, src in enumerate((wq_hbm, wk_hbm, wv_hbm))
        for slot, index in enumerate((j, 4 + j // 2))
    ]
    for copy in slabs:
        copy.start()
    greet(peers + [swap_peer])
    width_inner = inner_w.shape[1]
    tile = 2 * width
    parts = [slice(tile * t, tile * (t + 1)) for t in range(width_inner // tile)]
    loads = [pltpu.make_async_copy(out_w_hbm, out_w, load_sem.at[0])]
    for t, at in enumerate(parts):
        loads.append(
            pltpu.make_async_copy(inner_w_hbm.at[:, at], inner_w.at[:, at], load_sem.at[1 + 2 * t])
        )
        loads.append(pltpu.make_async_copy(outer_w_hbm.at[at], outer_w.at[at], load_sem.at[2 + 2 * t]))
    kept = {
        "wsel": (wsel_ref, wsel_hbm),
        "order": (order_ref, order_hbm),
        "stats": (stats_ref, stats_hbm),
        "x": (x_all, x_hbm),
        "sorted": (sorted_ref, sorted_hbm),
        "prob": (prob_ref, prob_hbm),
        "att": (att_ref, att_hbm),
        "low": (low_ref, low_hbm),
        "act": (act_ref, act_hbm),
        "output": (output_ref, output_hbm),
        "dsecond": (dsecond_ref, dsecond_hbm),
        "dinner": (dinner_ref, dinner_hbm),
        "delta": (delta_ref, delta_hbm),
        "dbranch": (dbranch_ref, dbranch_hbm),
        "vec": (vec_out, vec_hbm),
        "datt": (datt_ref, datt_hbm),
    }
    stores = {
        name: pltpu.make_async_copy(src, dst, store_sem.at[i]) for i, (name, (src, dst)) in enumerate(kept.items())
    }

    seg_src[...] = jnp.broadcast_to(seg_ref[...], seg_src.shape)
    table_copies = [
        remote(orders_ref, orders_in, swap, 0, sibling),
        remote(owners_ref, owners_in, swap, 1, sibling),
    ]
    for copy in table_copies:
        copy.start()
    p_swap = 4 * (1 - c) + j
    chunks = PIECES
    halves = [pl.ds(i * (block // chunks), block // chunks) for i in range(chunks)]
    pairs = [(tokens_ref.at[at], x_all.at[p_swap, at], x_all.at[p, at]) for at in halves]
    pairs.insert(0, (seg_src, seg_all.at[p_swap], seg_all.at[p]))
    pairs.append((cot_ref, cot_my, cot_my))
    swaps = [remote(src, dst, swap, 2 + i, swap_peer) for i, (src, dst, _) in enumerate(pairs)]
    locals_ = [
        pltpu.make_async_copy(src, own, swap_recv.at[4 + chunks + i]) for i, (src, _, own) in enumerate(pairs)
    ]

    px, pz, pd = member(1)[1], member(2)[1], member(3)[1]

    def share_block(index, position, i, peer):
        view = x_all.at[position, halves[i]]
        return remote(view, view, ring, index, peer)

    every = range(chunks)
    own_to_x = [share_block(i, p, i, over_x) for i in every]
    own_to_z = [share_block(chunks + i, p, i, over_z) for i in every]
    own_to_s = [share_block(2 * chunks + i, p, i, sibling) for i in every]
    x_to_s = [share_block(3 * chunks + i, px, i, sibling) for i in every]
    z_to_s = [share_block(4 * chunks + i, pz, i, sibling) for i in every]
    d_to_s = [share_block(5 * chunks + i, pd, i, sibling) for i in every]
    relays = [
        share_block(6 * chunks + i, px, i, over_z) if i < FIRST else share_block(6 * chunks + i, pz, i, over_x)
        for i in every
    ]
    seg_copies = [
        remote(seg_all.at[p], seg_all.at[p], seg_sems, flip - 1, peers[flip - 1]) for flip in range(1, 8)
    ]
    opposite = jnp.logical_not(matched)

    def own_half(i, arrivals):
        arrivals[1 + i].wait()
        own_to_x[i].start()
        own_to_z[i].start()
        own_to_s[i].start()

    def segments_out(arrivals):
        arrivals[0].wait()
        for copy in seg_copies:
            copy.start()

    def relay(i):
        own_to_x[i].wait()
        own_to_z[i].wait()
        relays[i].start()
        x_to_s[i].start()
        z_to_s[i].start()

    def relay_end(i):
        relays[i].wait()
        d_to_s[i].start()

    def wait_sibling():
        for copy in own_to_s + x_to_s + z_to_s + d_to_s:
            copy.wait_recv()

    @pl.when(matched)
    def _():
        for copy in locals_:
            copy.start()
        segments_out(locals_)
        for i in every:
            own_half(i, locals_)

    @pl.when(opposite)
    def _():
        for copy in swaps[: 1 + chunks]:
            copy.start()

    for copy in slabs:
        copy.wait()
    tiles = pick_columns([[weights[i, slot].astype(jnp.float32) for slot in range(2)] for i in range(3)], j, c)
    for i, tile in enumerate(tiles):
        wsel_ref[:, 128 * i : 128 * (i + 1)] = tile.astype(jnp.bfloat16)
    for i, ref in enumerate((query_bias_ref, None, value_bias_ref)):
        row = jnp.zeros((1, width), jnp.float32) if ref is None else ref[...].astype(jnp.float32).reshape(1, width)
        bias_rows[i : i + 1, :] = row
    bias_pairs = [
        [bias_rows[i : i + 1, pl.ds(pl.multiple_of(index * 128, 128), 128)] for index in (j, 4 + j // 2)]
        for i in range(3)
    ]
    for i, tile in enumerate(pick_columns(bias_pairs, j, c)):
        bias_sel[0:1, 128 * i : 128 * (i + 1)] = tile

    for copy in table_copies:
        copy.wait()
    h1, h2 = 2 * j + c, 8 + j
    for i, h in enumerate((h1, h2)):
        order_ref[i : i + 1, :] = jnp.where(matched, orders_ref[h], orders_in[h])
    half = 1024 * c

    build_gather(order_ref, 0, 0, group, gather.at[pl.ds(0, group)])

    @pl.when(matched)
    def _():
        for i in every:
            relay(i)

    @pl.when(opposite)
    def _():
        segments_out(swaps)
        for i in range(chunks // 2):
            own_half(i, swaps)

    build_gather(order_ref, 1, half, group // 2, gather.at[pl.ds(group, group // 2)])

    @pl.when(matched)
    def _():
        for i in every:
            relay_end(i)

    @pl.when(opposite)
    def _():
        for i in range(chunks // 2, chunks):
            own_half(i, swaps)
        for i in range(chunks // 2):
            relay(i)

    def project(position):
        at = pl.ds(pl.multiple_of(position * block, block), block)
        out = dot(x_all[position], wsel_ref[...]) + bias_sel[0:1, :]
        ids = seg_all[position, 0:1, :].astype(jnp.float32)
        columns = [
            jnp.broadcast_to(ids[:, 128 * i : 128 * (i + 1)], (128, 128)).T for i in range(block // 128)
        ]
        lane = lanes((block, 128))
        seg_hot = hot(jnp.concatenate(columns, axis=0) == (lane % 64).astype(jnp.float32))
        low = out.astype(jnp.bfloat16)
        tok[at, 0:128] = low[:, 0:128]
        tok[at, 128:256] = jnp.where(lane < 64, low[:, 128:256], seg_hot)
        tok[at, 256:384] = low[:, 256:384]
        tok[at, 384:512] = jnp.where(lane < 64, seg_hot, low[:, 384:512])

    step = 512
    early, late = group // 2 * zh, group // 2 * (1 - zh)

    def gather_rows(start, add):
        tokens = pl.ds(pl.multiple_of(start, group // 2), group // 2)

        def one(first, columns):
            def body(k, carry):
                at = pl.ds(pl.multiple_of(k * step, step), step)
                rows = dot(gather[at, tokens], tok[tokens, columns])
                if add:
                    sorted_ref[at, :] = (rows + sorted_ref[at, :].astype(jnp.float32)).astype(jnp.bfloat16)
                else:
                    sorted_ref[at, :] = rows.astype(jnp.bfloat16)
                return carry

            return body

        lax.fori_loop(0, group // step, one(0, pl.ds(0, 256)), 0)
        lax.fori_loop(group // step, group * 3 // 2 // step, one(1, pl.ds(256, 256)), 0)

    for copy in seg_copies:
        copy.wait()
    pl.when(opposite)(wait_sibling)
    for k in range(4):
        project(4 * zh + k)

    @pl.when(opposite)
    def _():
        for i in range(chunks // 2, chunks):
            relay(i)
        for i in range(chunks // 2):
            relay_end(i)

    gather_rows(early, False)

    @pl.when(opposite)
    def _():
        for i in range(chunks // 2, chunks):
            relay_end(i)

    flips = (3, 7, 1, 5, 2, 6, 4, 0)
    for i in range(4):
        build_scatter(order_ref, half, member(flips[i])[1] * block, scatter.at[i])
    pl.when(matched)(wait_sibling)
    for k in range(4):
        project(4 * (1 - zh) + k)
    for name in ("x", "wsel", "order"):
        stores[name].start()
    for copy in loads:
        copy.start()


    @pl.when(opposite)
    def _():
        swaps[1 + chunks].start()

    gather_rows(late, True)
    def attend(first_lanes):
        def one(i, carry):
            at = pl.ds(pl.multiple_of(i * 128, 128), 128)
            tile_zero, tile_one = sorted_ref[at, 0:128], sorted_ref[at, 128:256]
            low_lanes = lanes((128, 128)) < 64
            query_lanes = low_lanes if first_lanes else jnp.logical_not(low_lanes)
            queries = jnp.where(query_lanes, tile_zero, jnp.zeros_like(tile_zero))
            ids = jnp.where(query_lanes, jnp.zeros_like(tile_one), tile_one)
            both = dot(jnp.concatenate([queries, ids], axis=0), tile_one, 1, 1)
            scores, allowed = both[:128] * scale, both[128:]
            masked = jnp.where(allowed > 0.5, scores, NEGATIVE)
            highest = jnp.max(masked, axis=1, keepdims=True)
            raised = jnp.exp(masked - highest)
            totals = jnp.sum(raised, axis=1, keepdims=True)
            weights = raised * (1.0 / totals)
            prob_ref[at, :] = weights
            mixed = dot(weights.astype(jnp.bfloat16), tile_zero)
            att_sorted[at, :] = jnp.where(query_lanes, 0.0, mixed).astype(jnp.bfloat16)
            log_total = highest + jnp.log(totals)
            entropy = jnp.where(lanes((128, 128)) == 0, log_total, 0.0) - weights * masked
            ent_ref[pl.ds(i, 1), :] = jnp.sum(entropy, axis=0, keepdims=True)
            cnt_ref[pl.ds(i, 1), :] = jnp.sum(allowed, axis=0, keepdims=True)
            return carry

        return one

    lax.fori_loop(0, 16, attend(True), 0, unroll=UNROLL)
    lax.fori_loop(16, 24, attend(False), 0, unroll=UNROLL)
    stores["sorted"].start()
    stores["prob"].start()

    back_copies = []
    for i, flip in enumerate(flips):
        peer, position = member(flip)
        rows = dot(scatter[i % 4], att_sorted[...]).astype(jnp.bfloat16)
        if i + 4 < len(flips):
            build_scatter(order_ref, half, member(flips[i + 4])[1] * block, scatter.at[i % 4])
        if flip == 0:
            att_in[p] = rows
        else:
            att_send[flip] = rows
            copy = remote(att_send.at[flip], att_in.at[p], back, flip - 1, peer)
            copy.start()
            back_copies.append(copy)

    stats_ref[...] = jnp.zeros_like(stats_ref)
    owner_pad[...] = jnp.full_like(owner_pad, -1.0)
    clusters = owners_ref.shape[2]
    for h, first, size, skip in ((h1, 0, clusters, 0), (h2, clusters, clusters // 2, c)):
        ids = jnp.where(matched, owners_ref[h], owners_in[h])
        owner_pad[0:1, 0:clusters] = ids.astype(jnp.float32)
        column = jnp.broadcast_to(owner_pad[0:1, :], (128, 128)).T
        column = jnp.where(skip == 1, column[clusters // 2 : clusters // 2 + size], column[0:size])
        owned = jnp.where(column == lanes((size, 128)).astype(jnp.float32), 1.0, 0.0)
        for kind, (lane_sums, divisor) in enumerate(((ent_ref, 4.0 * block), (cnt_ref, 4.0 * block * 128))):
            sums = jnp.sum(lane_sums[first : first + size, :], axis=1, keepdims=True) / divisor
            stats_ref[kind, pl.ds(h, 1), :] = jnp.sum(sums * owned, axis=0, keepdims=True)

    stores["stats"].start()
    bias_ref[0:1, :] = inner_bias_ref[...].astype(jnp.float32).reshape(1, width_inner)
    out_bias, first_gain, first_shift, outer_bias, second_gain, second_shift = (
        ref[...].astype(jnp.float32).reshape(1, width)
        for ref in (
            out_bias_ref,
            first_gain_ref,
            first_shift_ref,
            outer_bias_ref,
            second_gain_ref,
            second_shift_ref,
        )
    )
    for copy in back_copies:
        copy.wait()
    for pair in range(4):
        even, odd = att_in[pair], att_in[4 + pair]
        att_ref[:, 128 * pair : 128 * (pair + 1)] = join(half_roll(even), odd)
    for pair in range(2):
        low_half = att_in[2 * pair] + att_in[4 + 2 * pair]
        high_half = att_in[2 * pair + 1] + att_in[5 + 2 * pair]
        att_ref[:, 512 + 128 * pair : 640 + 128 * pair] = join(low_half, half_roll(high_half))
    stores["att"].start()

    loads[0].wait()
    branch = dot(att_ref[...], out_w[...]) + out_bias
    normed, root_one = normalize(x_all[p].astype(jnp.float32) + branch)
    first = normed * first_gain + first_shift
    normed_ref[...] = normed
    low_ref[...] = first.astype(jnp.bfloat16)
    stores["low"].start()
    total[...] = first + outer_bias
    for t, at in enumerate(parts):
        loads[1 + 2 * t].wait()
        inner = dot(low_ref[...], inner_w[:, at]) + bias_ref[0:1, at]
        cumulative = 0.5 + 0.5 * lax.erf(inner * (0.5**0.5))
        density = jnp.exp(-0.5 * inner * inner) * 0.3989422804014327
        slope[:, at] = cumulative + inner * density
        act = (inner * cumulative).astype(jnp.bfloat16)
        act_ref[:, at] = act
        loads[2 + 2 * t].wait()
        total[...] += dot(act, outer_w[at, :])
    stores["act"].start()

    @pl.when(matched)
    def _():
        locals_[1 + chunks].wait()

    @pl.when(opposite)
    def _():
        swaps[1 + chunks].wait()

    normed_two, root_two = normalize(total[...])
    output_ref[...] = (normed_two * second_gain + second_shift).astype(jnp.bfloat16)
    stores["output"].start()
    upstream = cot_my[...].astype(jnp.float32)
    vec_out[4:5, :] = jnp.sum(upstream * normed_two, axis=0, keepdims=True)
    vec_out[5:6, :] = jnp.sum(upstream, axis=0, keepdims=True)
    delta_two = normalize_back(upstream * second_gain, normed_two, root_two)
    low_two = delta_two.astype(jnp.bfloat16)
    dsecond_ref[...] = low_two
    stores["dsecond"].start()
    vec_out[3:4, :] = jnp.sum(low_two.astype(jnp.float32), axis=0, keepdims=True)
    total[...] = delta_two
    for t, at in enumerate(parts):
        dact = dot(dsecond_ref[...], outer_w[at, :], 1, 1)
        dinner = (dact * slope[:, at]).astype(jnp.bfloat16)
        dinner_ref[:, at] = dinner
        bias_ref[0:1, at] = jnp.sum(dinner.astype(jnp.float32), axis=0, keepdims=True)
        total[...] += dot(dinner, inner_w[:, at], 1, 1)
    stores["dinner"].start()
    for i in range(width_inner // width):
        vec_out[6 + i : 7 + i, :] = bias_ref[0:1, width * i : width * (i + 1)]
    delta_first = total[...]
    normed = normed_ref[...]
    vec_out[1:2, :] = jnp.sum(delta_first * normed, axis=0, keepdims=True)
    vec_out[2:3, :] = jnp.sum(delta_first, axis=0, keepdims=True)
    delta_one = normalize_back(delta_first * first_gain, normed, root_one)
    delta_ref[...] = delta_one
    stores["delta"].start()
    low_one = delta_one.astype(jnp.bfloat16)
    dbranch_ref[...] = low_one
    stores["dbranch"].start()
    vec_out[0:1, :] = jnp.sum(low_one.astype(jnp.float32), axis=0, keepdims=True)
    vec_out[10:16, :] = jnp.zeros((6, width), jnp.float32)
    stores["vec"].start()
    datt_ref[...] = dot(dbranch_ref[...], out_w[...], 1, 1).astype(jnp.bfloat16)
    stores["datt"].start()
    for copy in stores.values():
        copy.wait()
    for copy in own_to_s + x_to_s + z_to_s + d_to_s:
        copy.wait_send()


def forward_layer(tokens, cotangent, segments, orders, owners, vectors, weights):
    block, width = tokens.shape
    inner_width = weights[4].shape[1]
    group = 8 * block
    low, full = jnp.bfloat16, jnp.float32
    vmem = pl.BlockSpec(memory_space=pltpu.VMEM)
    hbm = pl.BlockSpec(memory_space=pl.ANY)
    dma = pltpu.SemaphoreType.DMA
    rows = group * 3 // 2
    kept = [
        ((width, 512), low),
        ((8, group), jnp.int32),
        ((2, 16, 128), full),
        ((8, block, width), low),
        ((rows, 256), low),
        ((rows, 128), full),
        ((block, width), low),
        ((block, width), low),
        ((block, inner_width), low),
        ((block, width), low),
        ((block, width), low),
        ((block, inner_width), low),
        ((block, width), full),
        ((block, width), low),
        ((16, width), full),
        ((block, width), low),
    ]
    return pl.pallas_call(
        forward_kernel,
        out_shape=[jax.ShapeDtypeStruct(*one) for one in kept],
        in_specs=[vmem] * 14 + [hbm] * 6,
        out_specs=[hbm] * len(kept),
        scratch_shapes=[pltpu.VMEM(*one) for one in kept]
        + [
            pltpu.VMEM((block, width), low),
            pltpu.VMEM((3, 2, width, 128), low),
            pltpu.VMEM(orders.shape, jnp.int32),
            pltpu.VMEM(owners.shape, jnp.int32),
            pltpu.VMEM((8, 128), full),
            pltpu.VMEM((8, block), jnp.int32),
            pltpu.VMEM((8, 8, block), jnp.int32),
            pltpu.VMEM((8, width), full),
            pltpu.VMEM((8, 512), full),
            pltpu.VMEM((group, 512), low),
            pltpu.VMEM((rows, group), low),
            pltpu.VMEM((4, block, rows), low),
            pltpu.VMEM((rows, 128), low),
            pltpu.VMEM((8, block, 128), low),
            pltpu.VMEM((8, block, 128), low),
            pltpu.VMEM((24, 128), full),
            pltpu.VMEM((24, 128), full),
            dma((2 * PIECES + 6,)),
            dma((2 * PIECES + 6,)),
            dma((7 * PIECES,)),
            dma((7 * PIECES,)),
            dma((7,)),
            dma((7,)),
            dma((7,)),
            dma((7,)),
            dma((6,)),
            pltpu.VMEM(weights[3].shape, low),
            pltpu.VMEM(weights[4].shape, low),
            pltpu.VMEM(weights[5].shape, low),
            pltpu.VMEM((block, inner_width), full),
            pltpu.VMEM((block, width), full),
            pltpu.VMEM((block, width), full),
            pltpu.VMEM((8, inner_width), full),
            dma((1 + inner_width // width,)),
            dma((len(kept),)),
        ],
        compiler_params=pltpu.CompilerParams(
            collective_id=1, has_side_effects=True, vmem_limit_bytes=62 << 20
        ),
        name="forward_layer",
    )(tokens, cotangent, segments, orders, owners, *vectors, *weights)


def rows_of(start, q, size):
    return pl.ds(pl.multiple_of(start * q, 16), size * q)


def add_into(count, target, other):
    def one(i, carry):
        target(i)[...] = (
            target(i)[...].astype(jnp.float32) + other(i)[...].astype(jnp.float32)
        ).astype(jnp.bfloat16)
        return carry

    lax.fori_loop(0, count, one, 0)


def reduce_steps(parts, g_ref, f_ref, buffers, sems):
    core_in, a_one, b_one, ab_two, z_one, z_two = buffers
    zh, zl, x, y, c = coordinates()
    q = g_ref.shape[3] // 8
    width = g_ref.shape[4] // parts
    over_c, over_y = device(zh, zl, x, y, 1 - c), device(zh, zl, x, 1 - y, c)
    over_x, over_zl = device(zh, zl, 1 - x, y, c), device(zh, 1 - zl, x, y, c)
    over_zh = device(1 - zh, zl, x, y, c)
    flying = {}

    def send(name, k, src, dst, peer):
        copy = remote(src, dst, (sems[0].at[name], sems[1].at[name]), k, peer)
        copy.start()
        flying[name, k] = copy

    def arrive(name, k):
        flying.pop((name, k)).wait()

    def step(stage, k):
        cols = pl.ds(k * width, width)
        if stage == 0:
            send(
                0, k, g_ref.at[:, :, :, rows_of(4 * (1 - c), q, 4), cols], core_in.at[:, :, :, :, cols], over_c
            )
        if stage == 1:
            arrive(0, k)
            add_into(
                8,
                lambda i: core_in.at[i // 4, (i // 2) % 2, i % 2, :, cols],
                lambda i: g_ref.at[i // 4, (i // 2) % 2, i % 2, rows_of(4 * c, q, 4), cols],
            )
            send(1, k, core_in.at[:, :, 1 - x, pl.ds(0, 2 * q), cols], a_one.at[:, :, :, cols], over_x)
            send(2, k, core_in.at[:, :, :, rows_of(3 - y, q, 1), cols], b_one.at[:, :, :, :, cols], over_y)
        if stage == "2a":
            arrive(1, k)
            add_into(
                4,
                lambda i: a_one.at[i // 2, i % 2, :, cols],
                lambda i: core_in.at[i // 2, i % 2, x, pl.ds(0, 2 * q), cols],
            )
            send(3, k, a_one.at[:, :, rows_of(1 - y, q, 1), cols], ab_two.at[0, :, :, :, cols], over_y)
        if stage == "2b":
            arrive(2, k)
            add_into(
                8,
                lambda i: b_one.at[i // 4, (i // 2) % 2, i % 2, :, cols],
                lambda i: core_in.at[i // 4, (i // 2) % 2, i % 2, rows_of(2 + y, q, 1), cols],
            )
            send(4, k, b_one.at[:, :, 1 - x, :, cols], ab_two.at[1, :, :, :, cols], over_x)
        if stage == 3:
            arrive(3, k)
            add_into(
                4,
                lambda i: ab_two.at[0, i // 2, i % 2, :, cols],
                lambda i: a_one.at[i // 2, i % 2, rows_of(y, q, 1), cols],
            )
            arrive(4, k)
            add_into(
                4,
                lambda i: ab_two.at[1, i // 2, i % 2, :, cols],
                lambda i: b_one.at[i // 2, i % 2, x, :, cols],
            )
            send(5, k, ab_two.at[:, :, 1 - zl, :, cols], z_one.at[:, :, :, cols], over_zl)
        if stage == 4:
            arrive(5, k)
            add_into(
                4,
                lambda i: z_one.at[i // 2, i % 2, :, cols],
                lambda i: ab_two.at[i // 2, i % 2, zl, :, cols],
            )
            send(6, k, z_one.at[:, 1 - zh, :, cols], z_two.at[:, :, cols], over_zh)
        if stage == 5:
            arrive(6, k)
            for part in range(2):
                f_ref[c, part, y, :, cols] = (
                    z_two[part, :, cols].astype(jnp.float32) + z_one[part, zh, :, cols].astype(jnp.float32)
                ).astype(jnp.bfloat16)
            own_rows = f_ref.at[c, :, y, :, cols]
            send(7, k, own_rows, own_rows, over_y)
        if stage == 6:
            arrive(7, k)
            both = f_ref.at[c, :, :, :, cols]
            send(8, k, both, both, over_c)
        if stage == 7:
            arrive(8, k)

    return step


BACKWARD_ORDER = (
    "begin",
    "datt",
    "home0",
    "g1",
    "S0",
    "g2",
    "bld:1",
    "r1:0",
    "bld:0",
    "take:0",
    "r1:1",
    "take:1",
    "r1:2",
    "bld:3",
    "take:3",
    "r1:3",
    "bld:5",
    "take:5",
    "hE0",
    "bld:2",
    "take:2",
    "bld:4",
    "take:4",
    "at:0",
    "r2a:0",
    "r2b:0",
    "at:1",
    "r2b:1",
    "r2a:1",
    "at:2",
    "at:3",
    "at:5",
    "r2b:2",
    "r2a:2",
    "at:4",
    "pl:1",
    "pl:3",
    "pl:0",
    "r2a:3",
    "r2b:3",
    "pl:2",
    "ph:1",
    "r3:0",
    "ph:0",
    "ph:2",
    "r3:1",
    "ph:3",
    "ab:0",
    "dw",
    "r4:0",
    "r3:3",
    "r4:1",
    "r3:2",
    "st:0",
    "r1:4",
    "r1:5",
    "ab:1",
    "st:1",
    "hb:0",
    "ha:0",
    "r5:0",
    "r4:3",
    "r5:1",
    "r2a:4",
    "r4:2",
    "da",
    "r2a:5",
    "hb:1",
    "r2b:4",
    "ha:1",
    "r5:3",
    "st:2",
    "r5:2",
    "hm:0",
    "r2b:5",
    "r6:0",
    "r6:1",
    "r7:0",
    "wy",
    "r7:1",
    "hm:1",
    "st:3",
    "r3:4",
    "hE:0",
    "r6:3",
    "r3:5",
    "r6:2",
    "r7:3",
    "r7:2",
    "hE:1",
    "st:4",
    "r4:4",
    "r4:5",
    "wc",
    "stE",
    "r5:4",
    "wE",
    "r5:5",
    "r6:4",
    "r7:4",
    "r6:5",
    "r7:5",
)


def backward_kernel(
    parts,
    datt_ref,
    order_ref,
    out_my,
    stats_ref,
    vec_ref,
    att_hbm,
    dbranch_hbm,
    low_hbm,
    dsecond_hbm,
    act_hbm,
    dinner_hbm,
    sorted_hbm,
    prob_hbm,
    wsel_hbm,
    x_hbm,
    delta_hbm,
    out_home,
    grad_home,
    f_ref,
    w_all,
    stats_out,
    att_ref,
    dbranch_ref,
    low_ref,
    dsecond_ref,
    act_ref,
    dinner_ref,
    sorted_ref,
    prob_ref,
    wsel_ref,
    x_all,
    delta_ref,
    g_ref,
    datt_send,
    datt_in,
    gather,
    gathered,
    dsorted,
    scatter,
    dqkv,
    part_send,
    part_in,
    total,
    a_in,
    b_in,
    a_two,
    b_two,
    grad_my,
    dw,
    dw_y,
    dw_in,
    dw_all,
    stats_buf,
    stats_in,
    core_in,
    a_one,
    b_one,
    ab_two,
    z_one,
    z_two,
    datt_ssem,
    datt_rsem,
    part_ssem,
    part_rsem,
    swap_ssem,
    swap_rsem,
    dw_ssem,
    dw_rsem,
    stats_ssem,
    stats_rsem,
    red_ssem,
    red_rsem,
    load_sem,
):
    zh, zl, x, y, c = coordinates()
    s = 4 * zh + 2 * zl + x
    j = 2 * zl + x
    p = 4 * c + j
    block, width = datt_ref.shape
    group = 8 * block
    scale = 0.125
    matched = c == zh
    datt_sems, part_sems = (datt_ssem, datt_rsem), (part_ssem, part_rsem)
    swap_sems, dw_sems, stats_sems = (swap_ssem, swap_rsem), (dw_ssem, dw_rsem), (stats_ssem, stats_rsem)

    def member(flip):
        fc, fz, fx = flip // 4, (flip // 2) % 2, flip % 2
        mc, mz, mx = bits(c, fc), bits(zl, fz), bits(x, fx)
        return device(zh, mz, mx, y, mc), mc, 2 * mz + mx

    peers = [member(flip)[0] for flip in range(1, 8)]
    sibling, over_x, over_z = peers[3], peers[0], peers[1]
    swap_peer = device(1 - zh, zl, x, y, 1 - c)
    over_y = device(zh, zl, x, 1 - y, c)
    across = [device(1 - zh, bits(zl, f // 2), bits(x, f % 2), y, c) for f in range(4)]
    loads = [
        pltpu.make_async_copy(src, dst, load_sem.at[i])
        for i, (src, dst) in enumerate(
            (
                (att_hbm, att_ref),
                (dbranch_hbm, dbranch_ref),
                (low_hbm, low_ref),
                (dsecond_hbm, dsecond_ref),
                (act_hbm, act_ref),
                (dinner_hbm, dinner_ref),
                (sorted_hbm, sorted_ref),
                (prob_hbm, prob_ref),
                (wsel_hbm, wsel_ref),
                (x_hbm, x_all),
                (delta_hbm, delta_ref),
            )
        )
    ]
    for copy in loads:
        copy.start()
    greet(peers + [swap_peer, over_y] + across)

    def home_copy(src, dst, index, start):
        away = remote(src, dst, swap_sems, index, swap_peer)
        here = pltpu.make_async_copy(src, dst, swap_rsem.at[3 + index])

        @pl.when(matched)
        def _():
            here.start() if start else here.wait()

        @pl.when(jnp.logical_not(matched))
        def _():
            away.start() if start else away.wait()

    def tile(mc, mj):
        first = datt_ref[:, pl.ds(pl.multiple_of(mj * 128, 128), 128)]
        other = datt_ref[:, pl.ds(pl.multiple_of((4 + mj // 2) * 128, 128), 128)]
        return join(
            select_head(other.astype(jnp.float32), mj % 2, 0), select_head(first.astype(jnp.float32), mc, 1)
        ).astype(jnp.bfloat16)

    datt_copies = []

    def datt_out():
        for flip in (3, 7, 1, 5, 2, 6, 4):
            peer, mc, mj = member(flip)
            datt_send[flip] = tile(mc, mj)
            copy = remote(datt_send.at[flip], datt_in.at[p], datt_sems, flip - 1, peer)
            copy.start()
            datt_copies.append(copy)
        datt_in[p] = tile(c, j)

    stats_peers = (sibling, over_x, over_z, across[0], over_y)
    stats_copies = [
        remote(stats_buf.at[k], stats_in.at[k], stats_sems, k, peer) for k, peer in enumerate(stats_peers)
    ]

    def stats_step(k):
        if k == 0:
            stats_buf[0] = stats_ref[...]
        else:
            stats_copies[k - 1].wait()
            stats_buf[k] = stats_buf[k - 1] + stats_in[k - 1]
        if k < len(stats_peers):
            stats_copies[k].start()
        else:
            stats_out[...] = stats_buf[k]

    share = width // 8
    q = g_ref.shape[3] // 8
    top = 4 * q

    def outer_grads():
        def one(d, carry):
            columns = pl.ds(pl.multiple_of(d * 4 * share, 128), 4 * share)
            g_ref[d // 4, (d // 2) % 2, d % 2, top : top + 4 * share, :] = dot(
                act_ref[:, columns], dsecond_ref[...], 0, 0
            ).astype(jnp.bfloat16)
            return carry

        lax.fori_loop(0, 8, one, 0)

    def inner_grads():
        def one(i, carry):
            z, n = i // 4, i % 4
            rows = pl.ds(pl.multiple_of(z * 4 * share, 128), 4 * share)
            columns = pl.ds(pl.multiple_of(n * width, 128), width)
            grads = dot(low_ref[:, rows], dinner_ref[:, columns], 0, 0).astype(jnp.bfloat16)
            for k in range(4):
                at = pl.ds(pl.multiple_of(n * share, 16), share)
                g_ref[z, k // 2, k % 2, at, :] = grads[share * k : share * (k + 1)]
            return carry

        lax.fori_loop(0, 8, one, 0)

    def grads_first():
        for copy in loads[:6]:
            copy.wait()
        vectors = vec_ref[...].astype(jnp.bfloat16)
        for z in range(2):
            columns = slice(4 * share * z, 4 * share * (z + 1))
            grads = dot(att_ref[:, columns], dbranch_ref[...], 0, 0).astype(jnp.bfloat16)
            for k in range(4):
                rows = grads[share * k : share * (k + 1)]
                g_ref[z, k // 2, k % 2, 4 * share : 4 * share + share // 2, :] = rows[: share // 2]
                g_ref[z, k // 2, k % 2, 4 * share + share // 2 : top, :] = jnp.zeros_like(vectors)
                g_ref[z, k // 2, k % 2, top + 4 * share : top + 4 * share + share // 2, :] = rows[share // 2 :]
                g_ref[z, k // 2, k % 2, top + 4 * share + share // 2 :, :] = vectors
        pl.when(c == 0)(outer_grads)
        pl.when(c == 1)(inner_grads)

    def grads_second():
        pl.when(c == 0)(inner_grads)
        pl.when(c == 1)(outer_grads)

    reduction = reduce_steps(
        parts,
        g_ref,
        f_ref,
        (core_in, a_one, b_one, ab_two, z_one, z_two),
        (red_ssem, red_rsem),
    )

    half = 1024 * c
    step = gather.shape[1]
    chunks = group * 3 // 2 // step

    def build(k):
        head, start = (0, k * step) if k * step < group else (1, half + k * step - group)
        build_gather(order_ref, head, start, step, gather.at[k % 2])

    arrivals = []

    def take(k):
        if not arrivals:
            for copy in datt_copies:
                copy.wait()
            arrivals.append(True)
        gathered[k * step : (k + 1) * step, :] = dot(
            gather[k % 2], datt_in[...].reshape(group, 128)
        ).astype(jnp.bfloat16)

    def attend_back(first_lanes):
        def one(i, carry):
            at = pl.ds(pl.multiple_of(i * 128, 128), 128)
            tile_zero, tile_one = sorted_ref[at, 0:128], sorted_ref[at, 128:256]
            low_lanes = lanes((128, 128)) < 64
            query_lanes = low_lanes if first_lanes else jnp.logical_not(low_lanes)
            weights = prob_ref[at, :]
            taken = gathered[at, :]
            taken = jnp.where(query_lanes, jnp.zeros_like(taken), taken)
            weight_grads = dot(taken, tile_zero, 1, 1)
            inside = jnp.sum(weights * weight_grads, axis=1, keepdims=True)
            score_grads = weights * (weight_grads - inside)
            low_grads = score_grads.astype(jnp.bfloat16)
            query_grads = dot(low_grads, tile_one) * scale
            key_grads = dot(low_grads, tile_zero, 0, 0) * scale
            value_grads = dot(weights.astype(jnp.bfloat16), taken, 0, 0)
            dsorted[at, 0:128] = jnp.where(query_lanes, query_grads, value_grads).astype(jnp.bfloat16)
            dsorted[at, 128:256] = jnp.where(query_lanes, key_grads, 0.0).astype(jnp.bfloat16)
            return carry

        return one

    loaded = []

    def attend_some(i):
        if not loaded:
            for copy in loads[6:]:
                copy.wait()
            loaded.append(True)
        lax.fori_loop(4 * i, 4 * i + 4, attend_back(i < 4), 0, unroll=4)

    def place(position):
        token = lax.broadcasted_iota(jnp.int32, (128, 128), 0) + position * block
        for t in range(block // 128):
            for head, start, count, base in ((0, 0, group, 0), (1, half, group // 2, group)):
                for k in range(count // 128):
                    ids = order_ref[head : head + 1, pl.ds(pl.multiple_of(start + 128 * k, 128), 128)]
                    scatter[128 * t : 128 * (t + 1), base + 128 * k : base + 128 * (k + 1)] = hot(
                        ids == token + 128 * t
                    )
        at = pl.ds(pl.multiple_of(position * block, block), block)
        dqkv[at, 0:256] = dot(scatter[:, 0:group], dsorted[0:group, :]).astype(jnp.bfloat16)
        dqkv[at, 256:512] = dot(scatter[:, group:], dsorted[group:, :]).astype(jnp.bfloat16)
        return dot(dqkv[at, :], wsel_ref[...], 1, 1)

    part_copies = [remote(part_send.at[k], part_in.at[k], part_sems, k, sibling) for k in range(4)]

    def part_away(k):
        part_send[k] = place(4 * (1 - c) + k).astype(jnp.bfloat16)
        part_copies[k].start()

    def part_here(k):
        part = place(4 * c + k)
        part_copies[k].wait()
        total[k // 2, k % 2] = (part + part_in[k].astype(jnp.float32)).astype(jnp.bfloat16)

    upper, lower = pl.ds(0, block // 2), pl.ds(block // 2, block // 2)
    pieces = [pl.ds(i * (width // 2), width // 2) for i in range(2)]
    a_copies = [
        remote(total.at[:, 1 - x, upper, cols], a_in.at[:, :, cols], part_sems, 4 + i, over_x)
        for i, cols in enumerate(pieces)
    ]
    b_copies = [
        remote(total.at[1 - zl, :, lower, cols], b_in.at[:, :, cols], part_sems, 6 + i, over_z)
        for i, cols in enumerate(pieces)
    ]
    a_next = [
        remote(a_in.at[1 - zl, :, cols], a_two.at[:, cols], part_sems, 8 + i, over_z)
        for i, cols in enumerate(pieces)
    ]
    b_next = [
        remote(b_in.at[1 - x, :, cols], b_two.at[:, cols], part_sems, 10 + i, over_x)
        for i, cols in enumerate(pieces)
    ]

    def first_hops(i):
        a_copies[i].start()
        b_copies[i].start()

    def second_hop_a(i):
        cols = pieces[i]
        a_copies[i].wait()
        add_into(2, lambda k: a_in.at[k, :, cols], lambda k: total.at[k, x, upper, cols])
        a_next[i].start()

    def second_hop_b(i):
        cols = pieces[i]
        b_copies[i].wait()
        add_into(2, lambda k: b_in.at[k, :, cols], lambda k: total.at[zl, k, lower, cols])
        b_next[i].start()

    def grad_home_start(i):
        cols = pieces[i]
        a_next[i].wait()
        b_next[i].wait()
        for start, first, second, index in ((0, a_two, a_in, zl), (block // 2, b_two, b_in, x)):
            at = pl.ds(start, block // 2)
            grad_my[at, cols] = (
                delta_ref[at, cols]
                + first[:, cols].astype(jnp.float32)
                + second[index, :, cols].astype(jnp.float32)
            ).astype(jnp.bfloat16)
        home_copy(grad_my.at[:, cols], grad_home.at[:, cols], 1 + i, True)

    def grad_home_end(i):
        cols = pieces[i]
        home_copy(grad_my.at[:, cols], grad_home.at[:, cols], 1 + i, False)

    over_y_copy = remote(dw_y.at[1 - y], dw_in, dw_sems, 0, over_y)

    def projections():
        for k in range(width // 128):
            dw[128 * k : 128 * (k + 1), :] = dot(
                x_all[:, 128 * k : 128 * (k + 1)], dqkv[...], 0, 0
            ).astype(jnp.bfloat16)
        bias_row = jnp.broadcast_to(
            jnp.sum(dqkv[...].astype(jnp.float32), axis=0, keepdims=True), (16, 512)
        ).astype(jnp.bfloat16)
        for d in range(8):
            for h in range(2):
                dw_y[h, d, 0:share, :] = dw[share * d : share * (d + 1), 256 * h : 256 * (h + 1)]
                dw_y[h, d, share : share + 16, :] = bias_row[:, 256 * h : 256 * (h + 1)]
        over_y_copy.start()

    targets = across + [over_x, over_z, peers[2]]
    flips = [(1, f // 2, f % 2) for f in range(4)] + [(0, 0, 1), (0, 1, 0), (0, 1, 1)]
    dw_copies = []
    for i, (peer, (fh, fz, fx)) in enumerate(zip(targets, flips)):
        d = 4 * bits(zh, fh) + 2 * bits(zl, fz) + bits(x, fx)
        dw_copies.append(remote(dw_y.at[y, d], dw_all.at[s], dw_sems, 1 + i, peer))
    w_over_y = remote(w_all.at[y, c], w_all.at[y, c], dw_sems, 8, over_y)
    w_over_c = remote(w_all.at[:, c], w_all.at[:, c], dw_sems, 9, sibling)

    def dw_exchange():
        over_y_copy.wait()
        add_into(8, lambda i: dw_y.at[y, i], lambda i: dw_in.at[i])
        for copy in dw_copies:
            copy.start()
        dw_all[s] = dw_y[y, s]

    def dw_sum():
        for copy in dw_copies:
            copy.wait()
        for k in range(4):
            w_all[y, c, k] = (dw_all[k].astype(jnp.float32) + dw_all[4 + k].astype(jnp.float32)).astype(
                jnp.bfloat16
            )
        w_over_y.start()

    def dw_core():
        w_over_y.wait()
        w_over_c.start()

    def start_reduction():
        for k in range(parts):
            reduction(0, k)

    single = {
        "begin": lambda: None,
        "datt": datt_out,
        "home0": lambda: home_copy(out_my, out_home, 0, True),
        "hE0": lambda: home_copy(out_my, out_home, 0, False),
        "g1": grads_first,
        "g2": grads_second,
        "S0": start_reduction,
        "dw": projections,
        "da": dw_exchange,
        "wy": dw_sum,
        "wc": dw_core,
        "wE": w_over_c.wait,
        "stE": lambda: stats_step(5),
    }
    indexed = {
        "bld": build,
        "take": take,
        "at": attend_some,
        "pl": part_away,
        "ph": part_here,
        "ab": first_hops,
        "ha": second_hop_a,
        "hb": second_hop_b,
        "hm": grad_home_start,
        "hE": grad_home_end,
        "st": stats_step,
    }
    for name in BACKWARD_ORDER:
        kind, _, index = name.partition(":")
        if kind in single:
            single[kind]()
        elif kind in indexed:
            indexed[kind](int(index))
        else:
            stage = kind[1:]
            reduction(stage if stage in ("2a", "2b") else int(stage), int(index))


def backward_attention(
    datt,
    order,
    output,
    stats,
    vectors,
    att,
    dbranch,
    low_first,
    dsecond,
    act,
    dinner,
    sorted_rows,
    prob,
    wsel,
    x_all,
    delta,
    parts,
):
    block, width = datt.shape
    inner_width = act.shape[1]
    group = 8 * block
    rows = group * 3 // 2
    q = (9 * width // 8 + 32) // 8
    share = width // 8 + 16
    low, full = jnp.bfloat16, jnp.float32
    vmem = pl.BlockSpec(memory_space=pltpu.VMEM)
    hbm = pl.BlockSpec(memory_space=pl.ANY)
    dma = pltpu.SemaphoreType.DMA
    shape = jax.ShapeDtypeStruct
    return pl.pallas_call(
        functools.partial(backward_kernel, parts),
        out_shape=[
            shape((block, width), low),
            shape((block, width), low),
            shape((2, 2, 2, q, width), low),
            shape((2, 2, 4, share, 256), low),
            shape(stats.shape, full),
        ],
        in_specs=[vmem] * 5 + [hbm] * 11,
        out_specs=[vmem] * 5,
        scratch_shapes=[
            pltpu.VMEM((block, width), low),
            pltpu.VMEM((block, width), low),
            pltpu.VMEM((block, width), low),
            pltpu.VMEM((block, width), low),
            pltpu.VMEM((block, inner_width), low),
            pltpu.VMEM((block, inner_width), low),
            pltpu.VMEM((rows, 256), low),
            pltpu.VMEM((rows, 128), full),
            pltpu.VMEM((width, 512), low),
            pltpu.VMEM((group, width), low),
            pltpu.VMEM((block, width), full),
            pltpu.VMEM((2, 2, 2, 8 * q, width), low),
            pltpu.VMEM((8, block, 128), low),
            pltpu.VMEM((8, block, 128), low),
            pltpu.VMEM((2, 512, group), low),
            pltpu.VMEM((rows, 128), low),
            pltpu.VMEM((rows, 256), low),
            pltpu.VMEM((block, rows), low),
            pltpu.VMEM((group, 512), low),
            pltpu.VMEM((4, block, width), low),
            pltpu.VMEM((4, block, width), low),
            pltpu.VMEM((2, 2, block, width), low),
            pltpu.VMEM((2, block // 2, width), low),
            pltpu.VMEM((2, block // 2, width), low),
            pltpu.VMEM((block // 2, width), low),
            pltpu.VMEM((block // 2, width), low),
            pltpu.VMEM((block, width), low),
            pltpu.VMEM((width, 512), low),
            pltpu.VMEM((2, 8, share, 256), low),
            pltpu.VMEM((8, share, 256), low),
            pltpu.VMEM((8, share, 256), low),
            pltpu.VMEM((6,) + stats.shape, full),
            pltpu.VMEM((5,) + stats.shape, full),
            pltpu.VMEM((2, 2, 2, 4 * q, width), low),
            pltpu.VMEM((2, 2, 2 * q, width), low),
            pltpu.VMEM((2, 2, 2, q, width), low),
            pltpu.VMEM((2, 2, 2, q, width), low),
            pltpu.VMEM((2, 2, q, width), low),
            pltpu.VMEM((2, q, width), low),
            dma((7,)),
            dma((7,)),
            dma((12,)),
            dma((12,)),
            dma((6,)),
            dma((6,)),
            dma((10,)),
            dma((10,)),
            dma((5,)),
            dma((5,)),
            dma((9, parts)),
            dma((9, parts)),
            dma((11,)),
        ],
        compiler_params=pltpu.CompilerParams(
            collective_id=2, has_side_effects=True, vmem_limit_bytes=62 << 20
        ),
        name="backward_attention",
    )(
        datt,
        order,
        output,
        stats,
        vectors,
        att,
        dbranch,
        low_first,
        dsecond,
        act,
        dinner,
        sorted_rows,
        prob,
        wsel,
        x_all.reshape(group, width),
        delta,
    )


def finish_kernel(
    f_ref,
    w_ref,
    out_ref,
    grad_ref,
    stats_ref,
    output,
    grad_tokens,
    gq_out,
    gqb_out,
    gk_out,
    gv_out,
    gvb_out,
    go_out,
    gob_out,
    gfg_out,
    gfs_out,
    gi_out,
    gib_out,
    gu_out,
    gub_out,
    gsg_out,
    gss_out,
    stats_out,
    gq_ref,
    gv_ref,
    vec_ref,
):
    s = lax.axis_index("seq")
    output[0] = out_ref[...]
    grad_tokens[0] = grad_ref[...]
    stats_out[...] = stats_ref[:, : stats_out.shape[1], : stats_out.shape[2]]
    share, width = gk_out.shape
    top = f_ref.shape[0] // 2
    full = jnp.float32
    for n in range(gi_out.shape[1] // width):
        gi_out[:, n * width : (n + 1) * width] = f_ref[n * share : (n + 1) * share, :].astype(full)
    gu_out[...] = f_ref[top : top + 4 * share, :].astype(full)
    part = share // 2
    go_out[0:part, :] = f_ref[4 * share : 4 * share + part, :].astype(full)
    go_out[part:, :] = f_ref[top + 4 * share : top + 4 * share + part, :].astype(full)
    vec_ref[...] = f_ref[top + 4 * share + part :, :].astype(full)
    for pair in range(4):
        at = slice(128 * pair, 128 * pair + 128)
        low, high = (w_ref[0, core, pair].astype(full) for core in range(2))
        gq_ref[:, at] = join(low[:, 0:128], half_roll(high[:, 0:128]))
        gk_out[:, at] = join(low[:, 128:256], half_roll(high[:, 128:256]))[:share]
        gv_ref[:, at] = join(half_roll(low[:, 0:128]), high[:, 0:128])
    for pair in range(2):
        at = slice(512 + 128 * pair, 640 + 128 * pair)
        low, high = (
            w_ref[1, 0, 2 * pair + i].astype(full) + w_ref[1, 1, 2 * pair + i].astype(full) for i in range(2)
        )
        gq_ref[:, at] = join(half_roll(low[:, 0:128]), high[:, 0:128])
        gk_out[:, at] = join(half_roll(low[:, 128:256]), high[:, 128:256])[:share]
        gv_ref[:, at] = join(low[:, 0:128], half_roll(high[:, 0:128]))
    gq_out[...] = gq_ref[:share, :]
    gv_out[...] = gv_ref[:share, :]

    def mine(rows):
        return pltpu.roll(rows, width - share * s, 1)[:, :share]

    short = mine(vec_ref[...])
    for row, ref in enumerate((gob_out, gfg_out, gfs_out, gub_out, gsg_out, gss_out)):
        ref[...] = short[row]
    gqb_out[...] = mine(gq_ref[share : share + 8, :])[0]
    gvb_out[...] = mine(gv_ref[share : share + 8, :])[0]
    row = vec_ref[pl.ds(6 + s // 2, 1), :]
    gib_out[...] = jnp.where(s % 2 == 1, row[:, 4 * share :], row[:, : 4 * share])[0]


def finish(reduced, w_all, output, grad, totals, head_count, inner_width):
    block, width = output.shape
    row_count = 8 * reduced.shape[3]
    share = width // 8
    low, full = jnp.bfloat16, jnp.float32
    vmem = pl.BlockSpec(memory_space=pltpu.VMEM)
    shape = jax.ShapeDtypeStruct
    square, vector = shape((share, width), full), shape((share,), full)
    out_shape = [
        shape((1, block, width), low),
        shape((1, block, width), low),
        square,
        vector,
        square,
        square,
        vector,
        square,
        vector,
        vector,
        vector,
        shape((share, inner_width), full),
        shape((inner_width // 8,), full),
        shape((inner_width // 8, width), full),
        vector,
        vector,
        vector,
        shape((2, head_count, 8), full),
    ]
    return pl.pallas_call(
        finish_kernel,
        out_shape=out_shape,
        in_specs=[vmem] * 5,
        out_specs=[vmem] * len(out_shape),
        scratch_shapes=[
            pltpu.VMEM((share + 16, width), full),
            pltpu.VMEM((share + 16, width), full),
            pltpu.VMEM((16, width), full),
        ],
        compiler_params=pltpu.CompilerParams(vmem_limit_bytes=60 << 20),
        name="finish",
    )(reduced.reshape(row_count, width), w_all, output, grad, totals)


def body(
    tokens,
    segments,
    orders,
    owners,
    query_weight,
    query_bias,
    key_weight,
    value_weight,
    value_bias,
    out_weight,
    out_bias,
    first_gain,
    first_shift,
    inner_weight,
    inner_bias,
    outer_weight,
    outer_bias,
    second_gain,
    second_shift,
    cotangent,
):
    seq_count = lax.axis_size("seq")
    groups = lax.axis_size("rep")
    own_index = lax.axis_index("seq")
    row_count = tokens.shape[1]
    model_width = tokens.shape[2]
    order_table = orders[0]
    owner_table = owners[0]
    head_count, group_tokens = order_table.shape
    cluster_count = owner_table.shape[1]
    cluster = group_tokens // cluster_count
    head_dim = model_width // head_count
    per_owner = row_count // cluster
    score_scale = head_dim ** (-0.5)
    flat_tokens = tokens[0]
    local_index = jnp.arange(row_count, dtype=jnp.int32)
    factor = 1
    for candidate in range(1, seq_count + 1):
        if seq_count % candidate == 0 and candidate * row_count <= 2048:
            factor = candidate
    block_count = seq_count // factor
    block_width = factor * row_count
    order_blocks = order_table.reshape(head_count, block_count, block_width).transpose(1, 0, 2)
    owner_blocks = (
        jnp.repeat(owner_table, cluster, axis=1)
        .reshape(head_count, block_count, block_width)
        .transpose(1, 0, 2)
    )

    def find_target(total, block_item):
        order_block, owner_block = block_item
        local = order_block - own_index * row_count
        hits = local[:, :, None] == local_index[None, None, :]
        return (total + jnp.sum(jnp.where(hits, owner_block[:, :, None], 0), axis=1), None)

    target, unused = lax.scan(
        find_target, jnp.zeros((head_count, row_count), jnp.int32), (order_blocks, owner_blocks)
    )
    send_matrix = rank_matrix(target * row_count + local_index[None, :])
    mine = (owner_table == own_index).astype(jnp.int32)
    before = jnp.cumsum(mine, axis=1) - mine
    slot_hot = (mine[:, None, :] == 1) & (
        before[:, None, :] == jnp.arange(per_owner, dtype=jnp.int32)[None, :, None]
    )
    order_grid = order_table.reshape(head_count, cluster_count, cluster)
    owned_tokens = jnp.sum(
        jnp.where(slot_hot[:, :, :, None], order_grid[:, None, :, :], 0), axis=2
    ).reshape(head_count, row_count)
    arrive_matrix = rank_matrix(owned_tokens)
    w_three = jnp.concatenate([query_weight, key_weight, value_weight], axis=1)
    bias_three = jnp.concatenate(
        [
            query_bias.astype(jnp.float32),
            jnp.zeros((model_width,), jnp.float32),
            value_bias.astype(jnp.float32),
        ]
    )
    projected = (
        jnp.dot(flat_tokens, w_three, preferred_element_type=jnp.float32) + bias_three
    ).astype(jnp.bfloat16)
    token_rows = (
        projected.reshape(row_count, 3, head_count, head_dim)
        .transpose(2, 0, 1, 3)
        .reshape(head_count, row_count, 3 * head_dim)
    )
    segment_rows = jnp.broadcast_to(
        segments[0].astype(jnp.bfloat16)[None, :, None], (head_count, row_count, 1)
    )
    send_values = scatter_rows(token_rows, send_matrix, seq_count)
    send_segments = scatter_rows(segment_rows, send_matrix, seq_count)
    arrived, arrived_segments = (
        lax.all_to_all(send_values, "seq", split_axis=0, concat_axis=0, tiled=True),
        lax.all_to_all(send_segments, "seq", split_axis=0, concat_axis=0, tiled=True),
    )
    cluster_rows = collect_rows(arrived, arrive_matrix, 3 * head_dim).reshape(
        head_count * per_owner, cluster, 3, head_dim
    )
    cluster_segments = collect_rows(arrived_segments, arrive_matrix, 1).reshape(
        head_count * per_owner, cluster
    )
    queries = cluster_rows[:, :, 0]
    keys_in = cluster_rows[:, :, 1]
    values = cluster_rows[:, :, 2]
    attended, log_total, entropy, occupied = cluster_forward(
        queries, keys_in, values, cluster_segments, score_scale
    )
    per_head = jnp.stack(
        [
            jnp.sum(entropy.reshape(head_count, -1), axis=1),
            jnp.sum(occupied.reshape(head_count, -1), axis=1) / cluster,
        ]
    ) / (groups * row_count)
    column = (jnp.arange(seq_count, dtype=jnp.int32) == own_index).astype(jnp.float32)
    cluster_stats = lax.psum(per_head[:, :, None] * column, ("seq", "rep"))
    leaving = scatter_rows(
        attended.reshape(head_count, row_count, head_dim), arrive_matrix, seq_count
    )
    returned = lax.all_to_all(leaving, "seq", split_axis=0, concat_axis=0, tiled=True)
    attended_rows = (
        collect_rows(returned, send_matrix, head_dim)
        .transpose(1, 0, 2)
        .reshape(row_count, model_width)
    )
    branch = jnp.dot(
        attended_rows, out_weight, preferred_element_type=jnp.float32
    ) + out_bias.astype(jnp.float32)
    first_out, normed_one, root_one = norm_forward(
        flat_tokens.astype(jnp.float32) + branch, first_gain, first_shift
    )
    first_low = first_out.astype(jnp.bfloat16)
    inner_sum = jnp.dot(
        first_low, inner_weight, preferred_element_type=jnp.float32
    ) + inner_bias.astype(jnp.float32)
    activated, gelu_pull = jax.vjp(exact_gelu, inner_sum)
    activated_low = activated.astype(jnp.bfloat16)
    second = jnp.dot(
        activated_low, outer_weight, preferred_element_type=jnp.float32
    ) + outer_bias.astype(jnp.float32)
    result, normed_two, root_two = norm_forward(first_out + second, second_gain, second_shift)
    output = result.astype(jnp.bfloat16)[None]
    upstream = cotangent[0].astype(jnp.float32)
    gradient_second_gain = jnp.sum(upstream * normed_two, axis=0)
    gradient_second_shift = jnp.sum(upstream, axis=0)
    delta_two = norm_backward(upstream, normed_two, root_two, second_gain)
    delta_second = delta_two.astype(jnp.bfloat16)
    gradient_outer_bias = jnp.sum(delta_second.astype(jnp.float32), axis=0)
    gradient_outer_weight = jnp.einsum(
        "tf,td->fd", activated_low, delta_second, preferred_element_type=jnp.float32
    )
    delta_activated = jnp.einsum(
        "td,fd->tf", delta_second, outer_weight, preferred_element_type=jnp.float32
    )
    delta_inner = gelu_pull(delta_activated)[0].astype(jnp.bfloat16)
    gradient_inner_bias = jnp.sum(delta_inner.astype(jnp.float32), axis=0)
    gradient_inner_weight = jnp.einsum(
        "td,tf->df", first_low, delta_inner, preferred_element_type=jnp.float32
    )
    delta_first = delta_two + jnp.einsum(
        "tf,df->td", delta_inner, inner_weight, preferred_element_type=jnp.float32
    )
    gradient_first_gain = jnp.sum(delta_first * normed_one, axis=0)
    gradient_first_shift = jnp.sum(delta_first, axis=0)
    delta_one = norm_backward(delta_first, normed_one, root_one, first_gain)
    delta_branch = delta_one.astype(jnp.bfloat16)
    gradient_out_bias = jnp.sum(delta_branch.astype(jnp.float32), axis=0)
    gradient_out_weight = jnp.einsum(
        "td,te->de", attended_rows, delta_branch, preferred_element_type=jnp.float32
    )
    delta_attended = jnp.einsum(
        "te,de->td", delta_branch, out_weight, preferred_element_type=jnp.float32
    ).astype(jnp.bfloat16)
    delta_rows = delta_attended.reshape(row_count, head_count, head_dim).transpose(1, 0, 2)
    send_grads = scatter_rows(delta_rows, send_matrix, seq_count)
    grad_arrived = lax.all_to_all(send_grads, "seq", split_axis=0, concat_axis=0, tiled=True)
    kept_queries, kept_keys, kept_values, kept_segments = (
        queries,
        keys_in,
        values,
        cluster_segments,
    )
    grad_cluster = collect_rows(grad_arrived, arrive_matrix, head_dim).reshape(
        head_count * per_owner, cluster, head_dim
    )
    three_grads = cluster_backward(
        kept_queries, kept_keys, kept_values, kept_segments, log_total, grad_cluster, score_scale
    )
    leaving_grads = scatter_rows(
        three_grads.reshape(head_count, row_count, 3 * head_dim), arrive_matrix, seq_count
    )
    returned_grads = lax.all_to_all(leaving_grads, "seq", split_axis=0, concat_axis=0, tiled=True)
    delta_three = (
        collect_rows(returned_grads, send_matrix, 3 * head_dim)
        .reshape(head_count, row_count, 3, head_dim)
        .transpose(1, 2, 0, 3)
        .reshape(row_count, 3 * model_width)
    )
    bias_grads = jnp.sum(delta_three.astype(jnp.float32), axis=0)
    weight_grads = jnp.einsum(
        "td,te->de", flat_tokens, delta_three, preferred_element_type=jnp.float32
    )
    gradient_tokens = (
        delta_one
        + jnp.einsum("te,de->td", delta_three, w_three, preferred_element_type=jnp.float32)
    ).astype(jnp.bfloat16)[None]
    gradient_query_weight = weight_grads[:, :model_width]
    gradient_key_weight = weight_grads[:, model_width : 2 * model_width]
    gradient_value_weight = weight_grads[:, 2 * model_width :]
    gradient_query_bias = bias_grads[:model_width]
    gradient_value_bias = bias_grads[2 * model_width :]
    pieces = (
        lax.psum_scatter(gradient_query_weight, "seq", scatter_dimension=0, tiled=True),
        lax.psum_scatter(gradient_query_bias, "seq", scatter_dimension=0, tiled=True),
        lax.psum_scatter(gradient_key_weight, "seq", scatter_dimension=0, tiled=True),
        lax.psum_scatter(gradient_value_weight, "seq", scatter_dimension=0, tiled=True),
        lax.psum_scatter(gradient_value_bias, "seq", scatter_dimension=0, tiled=True),
        lax.psum_scatter(gradient_out_weight, "seq", scatter_dimension=0, tiled=True),
        lax.psum_scatter(gradient_out_bias, "seq", scatter_dimension=0, tiled=True),
        lax.psum_scatter(gradient_first_gain, "seq", scatter_dimension=0, tiled=True),
        lax.psum_scatter(gradient_first_shift, "seq", scatter_dimension=0, tiled=True),
        lax.psum_scatter(gradient_inner_weight, "seq", scatter_dimension=0, tiled=True),
        lax.psum_scatter(gradient_inner_bias, "seq", scatter_dimension=0, tiled=True),
        lax.psum_scatter(gradient_outer_weight, "seq", scatter_dimension=0, tiled=True),
        lax.psum_scatter(gradient_outer_bias, "seq", scatter_dimension=0, tiled=True),
        lax.psum_scatter(gradient_second_gain, "seq", scatter_dimension=0, tiled=True),
        lax.psum_scatter(gradient_second_shift, "seq", scatter_dimension=0, tiled=True),
    )
    summed = (
        lax.psum(pieces[0].astype(jnp.bfloat16), "rep").astype(jnp.float32),
        lax.psum(pieces[1].astype(jnp.bfloat16), "rep").astype(jnp.float32),
        lax.psum(pieces[2].astype(jnp.bfloat16), "rep").astype(jnp.float32),
        lax.psum(pieces[3].astype(jnp.bfloat16), "rep").astype(jnp.float32),
        lax.psum(pieces[4].astype(jnp.bfloat16), "rep").astype(jnp.float32),
        lax.psum(pieces[5].astype(jnp.bfloat16), "rep").astype(jnp.float32),
        lax.psum(pieces[6].astype(jnp.bfloat16), "rep").astype(jnp.float32),
        lax.psum(pieces[7].astype(jnp.bfloat16), "rep").astype(jnp.float32),
        lax.psum(pieces[8].astype(jnp.bfloat16), "rep").astype(jnp.float32),
        lax.psum(pieces[9].astype(jnp.bfloat16), "rep").astype(jnp.float32),
        lax.psum(pieces[10].astype(jnp.bfloat16), "rep").astype(jnp.float32),
        lax.psum(pieces[11].astype(jnp.bfloat16), "rep").astype(jnp.float32),
        lax.psum(pieces[12].astype(jnp.bfloat16), "rep").astype(jnp.float32),
        lax.psum(pieces[13].astype(jnp.bfloat16), "rep").astype(jnp.float32),
        lax.psum(pieces[14].astype(jnp.bfloat16), "rep").astype(jnp.float32),
    )
    return (output, gradient_tokens) + tuple(summed) + (cluster_stats,)


def square_body(
    tokens,
    segments,
    orders,
    owners,
    query_weight,
    query_bias,
    key_weight,
    value_weight,
    value_bias,
    out_weight,
    out_bias,
    first_gain,
    first_shift,
    inner_weight,
    inner_bias,
    outer_weight,
    outer_bias,
    second_gain,
    second_shift,
    cotangent,
):
    (
        wsel,
        order,
        stats,
        x_all,
        sorted_rows,
        prob,
        att,
        low_first,
        act,
        output,
        dsecond,
        dinner,
        delta,
        dbranch,
        vector_grads,
        datt,
    ) = forward_layer(
        tokens[0],
        cotangent[0],
        segments,
        orders.transpose(1, 0, 2),
        owners.transpose(1, 0, 2),
        (
            query_bias,
            value_bias,
            out_bias,
            first_gain,
            first_shift,
            outer_bias,
            second_gain,
            second_shift,
            inner_bias,
        ),
        (query_weight, key_weight, value_weight, out_weight, inner_weight, outer_weight),
    )
    output, grad, reduced, w_all, totals = backward_attention(
        datt,
        order,
        output,
        stats,
        vector_grads,
        att,
        dbranch,
        low_first,
        dsecond,
        act,
        dinner,
        sorted_rows,
        prob,
        wsel,
        x_all,
        delta,
        6,
    )
    return tuple(
        finish(reduced, w_all, output, grad, totals, orders.shape[1], inner_weight.shape[1])
    )


def solution(mesh):
    square = mesh.shape["seq"] == 8 and mesh.shape["rep"] == 4
    placed = (
        P("rep", "seq", None),
        P("rep", "seq"),
        P("rep", None, None),
        P("rep", None, None),
        P(),
        P(),
        P(),
        P(),
        P(),
        P(),
        P(),
        P(),
        P(),
        P(),
        P(),
        P(),
        P(),
        P(),
        P(),
        P("rep", "seq", None),
    )
    return jax.shard_map(
        square_body if square else body,
        mesh=mesh,
        in_specs=placed,
        out_specs=(
            P("rep", "seq", None),
            P("rep", "seq", None),
            P("seq", None),
            P("seq"),
            P("seq", None),
            P("seq", None),
            P("seq"),
            P("seq", None),
            P("seq"),
            P("seq"),
            P("seq"),
            P("seq", None),
            P("seq"),
            P("seq", None),
            P("seq"),
            P("seq"),
            P("seq"),
            P(),
        ),
        check_vma=False,
    )
```

```python
import functools

import jax
import jax.numpy as jnp
from jax import lax
from jax.experimental import pallas as pl
from jax.experimental.pallas import tpu as pltpu
from jax.sharding import PartitionSpec as P

EPSILON = 1e-12
NEGATIVE = -1e30


def norm_forward(hidden, gain_vector, shift_vector):
    centre = hidden - jnp.mean(hidden, axis=-1, keepdims=True)
    root_inverse = lax.rsqrt(jnp.mean(centre * centre, axis=-1, keepdims=True) + EPSILON)
    normed = centre * root_inverse
    return (
        normed * gain_vector.astype(jnp.float32) + shift_vector.astype(jnp.float32),
        normed,
        root_inverse,
    )


def norm_backward(upstream, normed, root_inverse, gain_vector):
    scaled = upstream * gain_vector.astype(jnp.float32)
    return root_inverse * (
        scaled
        - jnp.mean(scaled, axis=-1, keepdims=True)
        - normed * jnp.mean(scaled * normed, axis=-1, keepdims=True)
    )


def exact_gelu(inner_sum):
    return jax.nn.gelu(inner_sum, approximate=False)


def rank_matrix(sort_keys):
    row_count = sort_keys.shape[1]
    ranks = jnp.sum((sort_keys[:, None, :] < sort_keys[:, :, None]).astype(jnp.int32), axis=2)
    return (ranks[:, None, :] == jnp.arange(row_count, dtype=jnp.int32)[None, :, None]).astype(
        jnp.bfloat16
    )


def scatter_rows(row_block, placing, seq_count):
    head_count, row_count, features = row_block.shape
    picked = jnp.einsum(
        "hri,hif->hrf", placing, row_block, preferred_element_type=jnp.float32
    ).astype(jnp.bfloat16)
    return picked.reshape(head_count, seq_count, row_count // seq_count * features).transpose(
        1, 0, 2
    )


def collect_rows(packed, placing, features):
    seq_count, head_count, flat_width = packed.shape
    row_block = packed.transpose(1, 0, 2).reshape(
        head_count, seq_count * flat_width // features, features
    )
    return jnp.einsum(
        "hri,hrf->hif", placing, row_block, preferred_element_type=jnp.float32
    ).astype(jnp.bfloat16)


def cluster_scores(queries, keys_in, segment_ids, score_scale):
    scores = (
        jnp.einsum("nqd,nkd->nqk", queries, keys_in, preferred_element_type=jnp.float32)
        * score_scale
    )
    allowed = segment_ids[:, :, None] == segment_ids[:, None, :]
    return (scores, allowed, jnp.where(allowed, scores, NEGATIVE))


def cluster_forward(queries, keys_in, values, segment_ids, score_scale):
    scores, allowed, masked = cluster_scores(queries, keys_in, segment_ids, score_scale)
    highest = jnp.max(masked, axis=-1, keepdims=True)
    raised = jnp.exp(masked - highest)
    totals = jnp.sum(raised, axis=-1, keepdims=True)
    weights = raised / totals
    attended = jnp.einsum(
        "nqk,nkd->nqd", weights.astype(jnp.bfloat16), values, preferred_element_type=jnp.float32
    ).astype(jnp.bfloat16)
    log_total = highest[:, :, 0] + jnp.log(totals[:, :, 0])
    entropy = log_total - jnp.sum(weights * jnp.where(allowed, scores, 0.0), axis=-1)
    occupied = jnp.sum(allowed.astype(jnp.float32), axis=-1)
    return (attended, log_total, entropy, occupied)


def cluster_backward(queries, keys_in, values, segment_ids, log_total, grad_out, score_scale):
    masked = cluster_scores(queries, keys_in, segment_ids, score_scale)[2]
    weights = jnp.exp(masked - log_total[:, :, None])
    weight_grads = jnp.einsum("nqd,nkd->nqk", grad_out, values, preferred_element_type=jnp.float32)
    value_grads = jnp.einsum(
        "nqk,nqd->nkd", weights.astype(jnp.bfloat16), grad_out, preferred_element_type=jnp.float32
    )
    score_grads = (
        weights * (weight_grads - jnp.sum(weights * weight_grads, axis=-1, keepdims=True))
    ).astype(jnp.bfloat16)
    query_grads = (
        jnp.einsum("nqk,nkd->nqd", score_grads, keys_in, preferred_element_type=jnp.float32)
        * score_scale
    )
    key_grads = (
        jnp.einsum("nqk,nqd->nkd", score_grads, queries, preferred_element_type=jnp.float32)
        * score_scale
    )
    return jnp.stack([query_grads, key_grads, value_grads], axis=2).astype(jnp.bfloat16)


MESH = pl.DeviceIdType.MESH


UNROLL = 8
PIECES = 4
FIRST = 1


def half_roll(block):
    return jnp.concatenate([block[:, 64:], block[:, :64]], axis=1)


def lanes(shape):
    return lax.broadcasted_iota(jnp.int32, shape, len(shape) - 1)


def bits(value, flip):
    return value + flip - 2 * value * flip


def coordinates():
    s, r = lax.axis_index("seq"), lax.axis_index("rep")
    return s // 4, (s // 2) % 2, s % 2, r // 2, r % 2


def device(zh, zl, x, y, c):
    return (4 * zh + 2 * zl + x, 2 * y + c)


def greet(peers):
    barrier = pltpu.get_barrier_semaphore()
    for peer in peers:
        pl.semaphore_signal(barrier, inc=1, device_id=peer, device_id_type=MESH)
    pl.semaphore_wait(barrier, len(peers))


def remote(src, dst, sems, index, peer):
    return pltpu.make_async_remote_copy(
        src_ref=src,
        dst_ref=dst,
        send_sem=sems[0].at[index],
        recv_sem=sems[1].at[index],
        device_id=peer,
        device_id_type=MESH,
    )


def dot(left, right, left_dim=1, right_dim=0):
    return lax.dot_general(
        left,
        right,
        (((left_dim,), (right_dim,)), ((), ())),
        preferred_element_type=jnp.float32,
    )


def hot(condition):
    return jnp.where(condition, 1.0, 0.0).astype(jnp.bfloat16)


def build_gather(order_ref, row, start, count, into):
    tokens = into.shape[1]

    def one(k, carry):
        at = pl.multiple_of(k * 128, 128)
        ids = order_ref[row : row + 1, pl.ds(pl.multiple_of(start + at, 128), 128)]
        column = jnp.broadcast_to(ids.astype(jnp.float32), (128, 128)).T
        lane = lanes((128, 128)).astype(jnp.float32)
        for t in range(tokens // 128):
            into[pl.ds(at, 128), t * 128 : (t + 1) * 128] = hot(column == lane + 128.0 * t)
        return carry

    lax.fori_loop(0, count // 128, one, 0)


def build_scatter(order_ref, half, first_token, into):
    group = order_ref.shape[1]

    def one(k, carry):
        at = pl.multiple_of(k * 128, 128)
        token = lax.broadcasted_iota(jnp.int32, (128, 128), 0) + (first_token + at)
        for p in range(into.shape[1] // 128):
            row, start = (0, 128 * p) if 128 * p < group else (1, half + 128 * p - group)
            ids = order_ref[row : row + 1, pl.ds(pl.multiple_of(start, 128), 128)]
            into[pl.ds(at, 128), 128 * p : 128 * (p + 1)] = hot(ids == token)
        return carry

    lax.fori_loop(0, into.shape[0] // 128, one, 0)


def select_head(slab, half, place):
    return jnp.where(half == place, slab, half_roll(slab))


def join(low_lanes, high_lanes):
    return jnp.where(lanes(low_lanes.shape) < 64, low_lanes, high_lanes)


def pick_columns(pairs, j, c):
    (q_one, q_two), (k_one, k_two), (v_one, v_two) = pairs
    zero = jnp.zeros_like(q_one)
    q1, v1, k1 = select_head(q_one, c, 0), select_head(v_one, c, 1), select_head(k_one, c, 0)
    v2, q2, k2 = (
        select_head(v_two, j % 2, 0),
        select_head(q_two, j % 2, 1),
        select_head(k_two, j % 2, 1),
    )
    return join(q1, v1), join(k1, zero), join(v2, q2), join(zero, k2)


def normalize(hidden):
    centre = hidden - jnp.mean(hidden, axis=1, keepdims=True)
    root_inverse = lax.rsqrt(jnp.mean(centre * centre, axis=1, keepdims=True) + EPSILON)
    return centre * root_inverse, root_inverse


def normalize_back(scaled, normed, root_inverse):
    return root_inverse * (
        scaled
        - jnp.mean(scaled, axis=1, keepdims=True)
        - normed * jnp.mean(scaled * normed, axis=1, keepdims=True)
    )


def forward_kernel(
    tokens_ref,
    cot_ref,
    seg_ref,
    orders_ref,
    owners_ref,
    query_bias_ref,
    value_bias_ref,
    out_bias_ref,
    first_gain_ref,
    first_shift_ref,
    outer_bias_ref,
    second_gain_ref,
    second_shift_ref,
    inner_bias_ref,
    wq_hbm,
    wk_hbm,
    wv_hbm,
    out_w_hbm,
    inner_w_hbm,
    outer_w_hbm,
    wsel_hbm,
    order_hbm,
    stats_hbm,
    x_hbm,
    sorted_hbm,
    prob_hbm,
    att_hbm,
    low_hbm,
    act_hbm,
    output_hbm,
    dsecond_hbm,
    dinner_hbm,
    delta_hbm,
    dbranch_hbm,
    vec_hbm,
    datt_hbm,
    wsel_ref,
    order_ref,
    stats_ref,
    x_all,
    sorted_ref,
    prob_ref,
    att_ref,
    low_ref,
    act_ref,
    output_ref,
    dsecond_ref,
    dinner_ref,
    delta_ref,
    dbranch_ref,
    vec_out,
    datt_ref,
    cot_my,
    weights,
    orders_in,
    owners_in,
    owner_pad,
    seg_src,
    seg_all,
    bias_rows,
    bias_sel,
    tok,
    gather,
    scatter,
    att_sorted,
    att_send,
    att_in,
    ent_ref,
    cnt_ref,
    swap_send,
    swap_recv,
    ring_send,
    ring_recv,
    seg_send,
    seg_recv,
    back_send,
    back_recv,
    local_sem,
    out_w,
    inner_w,
    outer_w,
    slope,
    total,
    normed_ref,
    bias_ref,
    load_sem,
    store_sem,
):
    zh, zl, x, y, c = coordinates()
    j = 2 * zl + x
    p = 4 * c + j
    block, width = tokens_ref.shape
    group = 8 * block
    scale = 0.125
    swap = (swap_send, swap_recv)
    ring = (ring_send, ring_recv)
    seg_sems = (seg_send, seg_recv)
    back = (back_send, back_recv)

    def member(flip):
        fc, fz, fx = flip // 4, (flip // 2) % 2, flip % 2
        mc, mz, mx = bits(c, fc), bits(zl, fz), bits(x, fx)
        return device(zh, mz, mx, y, mc), 4 * mc + 2 * mz + mx

    swap_peer = device(1 - zh, zl, x, y, 1 - c)
    peers = [member(flip)[0] for flip in range(1, 8)]
    sibling = peers[3]
    over_x, over_z = peers[0], peers[1]
    matched = c == zh

    slabs = [
        pltpu.make_async_copy(
            src.at[:, pl.ds(pl.multiple_of(index * 128, 128), 128)],
            weights.at[i, slot],
            local_sem.at[3 * slot + i],
        )
        for i, src in enumerate((wq_hbm, wk_hbm, wv_hbm))
        for slot, index in enumerate((j, 4 + j // 2))
    ]
    for copy in slabs:
        copy.start()
    greet(peers + [swap_peer])
    width_inner = inner_w.shape[1]
    dense_tile = 2 * width
    parts = [slice(dense_tile * t, dense_tile * (t + 1)) for t in range(width_inner // dense_tile)]
    loads = [pltpu.make_async_copy(out_w_hbm, out_w, load_sem.at[0])]
    for t, at in enumerate(parts):
        loads.append(
            pltpu.make_async_copy(inner_w_hbm.at[:, at], inner_w.at[:, at], load_sem.at[1 + 2 * t])
        )
        loads.append(pltpu.make_async_copy(outer_w_hbm.at[at], outer_w.at[at], load_sem.at[2 + 2 * t]))
    kept = {
        "wsel": (wsel_ref, wsel_hbm),
        "order": (order_ref, order_hbm),
        "stats": (stats_ref, stats_hbm),
        "x": (x_all, x_hbm),
        "sorted": (sorted_ref, sorted_hbm),
        "prob": (prob_ref, prob_hbm),
        "att": (att_ref, att_hbm),
        "low": (low_ref, low_hbm),
        "act": (act_ref, act_hbm),
        "output": (output_ref, output_hbm),
        "dsecond": (dsecond_ref, dsecond_hbm),
        "dinner": (dinner_ref, dinner_hbm),
        "delta": (delta_ref, delta_hbm),
        "dbranch": (dbranch_ref, dbranch_hbm),
        "vec": (vec_out, vec_hbm),
        "datt": (datt_ref, datt_hbm),
    }
    stores = {
        name: pltpu.make_async_copy(src, dst, store_sem.at[i]) for i, (name, (src, dst)) in enumerate(kept.items())
    }

    seg_src[...] = jnp.broadcast_to(seg_ref[...], seg_src.shape)
    table_copies = [
        remote(orders_ref, orders_in, swap, 0, sibling),
        remote(owners_ref, owners_in, swap, 1, sibling),
    ]
    for copy in table_copies:
        copy.start()
    p_swap = 4 * (1 - c) + j
    chunks = PIECES
    halves = [pl.ds(i * (block // chunks), block // chunks) for i in range(chunks)]
    pairs = [(tokens_ref.at[at], x_all.at[p_swap, at], x_all.at[p, at]) for at in halves]
    pairs.insert(0, (seg_src, seg_all.at[p_swap], seg_all.at[p]))
    pairs.append((cot_ref, cot_my, cot_my))
    swaps = [remote(src, dst, swap, 2 + i, swap_peer) for i, (src, dst, _) in enumerate(pairs)]
    locals_ = [
        pltpu.make_async_copy(src, own, swap_recv.at[4 + chunks + i]) for i, (src, _, own) in enumerate(pairs)
    ]

    px, pz, pd = member(1)[1], member(2)[1], member(3)[1]

    def share_block(index, position, i, peer):
        view = x_all.at[position, halves[i]]
        return remote(view, view, ring, index, peer)

    every = range(chunks)
    own_to_x = [share_block(i, p, i, over_x) for i in every]
    own_to_z = [share_block(chunks + i, p, i, over_z) for i in every]
    own_to_s = [share_block(2 * chunks + i, p, i, sibling) for i in every]
    x_to_s = [share_block(3 * chunks + i, px, i, sibling) for i in every]
    z_to_s = [share_block(4 * chunks + i, pz, i, sibling) for i in every]
    d_to_s = [share_block(5 * chunks + i, pd, i, sibling) for i in every]
    relays = [
        share_block(6 * chunks + i, px, i, over_z) if i < FIRST else share_block(6 * chunks + i, pz, i, over_x)
        for i in every
    ]
    seg_copies = [
        remote(seg_all.at[p], seg_all.at[p], seg_sems, flip - 1, peers[flip - 1]) for flip in range(1, 8)
    ]
    opposite = jnp.logical_not(matched)

    def own_half(i, arrivals):
        arrivals[1 + i].wait()
        own_to_x[i].start()
        own_to_z[i].start()
        own_to_s[i].start()

    def segments_out(arrivals):
        arrivals[0].wait()
        for copy in seg_copies:
            copy.start()

    def relay(i):
        own_to_x[i].wait()
        own_to_z[i].wait()
        relays[i].start()
        x_to_s[i].start()
        z_to_s[i].start()

    def relay_end(i):
        relays[i].wait()
        d_to_s[i].start()

    def wait_sibling():
        for copy in own_to_s + x_to_s + z_to_s + d_to_s:
            copy.wait_recv()

    @pl.when(matched)
    def _():
        for copy in locals_:
            copy.start()
        segments_out(locals_)
        for i in every:
            own_half(i, locals_)

    @pl.when(opposite)
    def _():
        for copy in swaps[: 1 + chunks]:
            copy.start()

    for copy in slabs:
        copy.wait()
    tiles = pick_columns([[weights[i, slot].astype(jnp.float32) for slot in range(2)] for i in range(3)], j, c)
    for i, tile in enumerate(tiles):
        wsel_ref[:, 128 * i : 128 * (i + 1)] = tile.astype(jnp.bfloat16)
    for i, ref in enumerate((query_bias_ref, None, value_bias_ref)):
        row = jnp.zeros((1, width), jnp.float32) if ref is None else ref[...].astype(jnp.float32).reshape(1, width)
        bias_rows[i : i + 1, :] = row
    bias_pairs = [
        [bias_rows[i : i + 1, pl.ds(pl.multiple_of(index * 128, 128), 128)] for index in (j, 4 + j // 2)]
        for i in range(3)
    ]
    for i, tile in enumerate(pick_columns(bias_pairs, j, c)):
        bias_sel[0:1, 128 * i : 128 * (i + 1)] = tile

    for copy in table_copies:
        copy.wait()
    h1, h2 = 2 * j + c, 8 + j
    for i, h in enumerate((h1, h2)):
        order_ref[i : i + 1, :] = jnp.where(matched, orders_ref[h], orders_in[h])
    half = 1024 * c

    build_gather(order_ref, 0, 0, group, gather.at[pl.ds(0, group)])

    @pl.when(matched)
    def _():
        for i in every:
            relay(i)

    @pl.when(opposite)
    def _():
        segments_out(swaps)
        for i in range(chunks // 2):
            own_half(i, swaps)

    build_gather(order_ref, 1, half, group // 2, gather.at[pl.ds(group, group // 2)])

    @pl.when(matched)
    def _():
        for i in every:
            relay_end(i)

    @pl.when(opposite)
    def _():
        for i in range(chunks // 2, chunks):
            own_half(i, swaps)
        for i in range(chunks // 2):
            relay(i)

    def project(position):
        at = pl.ds(pl.multiple_of(position * block, block), block)
        out = dot(x_all[position], wsel_ref[...]) + bias_sel[0:1, :]
        ids = seg_all[position, 0:1, :].astype(jnp.float32)
        columns = [
            jnp.broadcast_to(ids[:, 128 * i : 128 * (i + 1)], (128, 128)).T for i in range(block // 128)
        ]
        lane = lanes((block, 128))
        seg_hot = hot(jnp.concatenate(columns, axis=0) == (lane % 64).astype(jnp.float32))
        low = out.astype(jnp.bfloat16)
        tok[at, 0:128] = low[:, 0:128]
        tok[at, 128:256] = jnp.where(lane < 64, low[:, 128:256], seg_hot)
        tok[at, 256:384] = low[:, 256:384]
        tok[at, 384:512] = jnp.where(lane < 64, seg_hot, low[:, 384:512])

    step = 512
    early, late = group // 2 * zh, group // 2 * (1 - zh)

    def gather_rows(start, add):
        tokens = pl.ds(pl.multiple_of(start, group // 2), group // 2)

        def one(first, columns):
            def body(k, carry):
                at = pl.ds(pl.multiple_of(k * step, step), step)
                rows = dot(gather[at, tokens], tok[tokens, columns])
                if add:
                    sorted_ref[at, :] = (rows + sorted_ref[at, :].astype(jnp.float32)).astype(jnp.bfloat16)
                else:
                    sorted_ref[at, :] = rows.astype(jnp.bfloat16)
                return carry

            return body

        lax.fori_loop(0, group // step, one(0, pl.ds(0, 256)), 0)
        lax.fori_loop(group // step, group * 3 // 2 // step, one(1, pl.ds(256, 256)), 0)

    for copy in seg_copies:
        copy.wait()
    pl.when(opposite)(wait_sibling)
    for k in range(4):
        project(4 * zh + k)

    @pl.when(opposite)
    def _():
        for i in range(chunks // 2, chunks):
            relay(i)
        for i in range(chunks // 2):
            relay_end(i)

    gather_rows(early, False)

    @pl.when(opposite)
    def _():
        for i in range(chunks // 2, chunks):
            relay_end(i)

    def build_block(i, carry):
        build_scatter(order_ref, half, member(7 - i)[1] * block, scatter.at[i % 4])
        return carry

    lax.fori_loop(0, 4, build_block, 0)
    pl.when(matched)(wait_sibling)
    for k in range(4):
        project(4 * (1 - zh) + k)
    for name in ("x", "wsel", "order"):
        stores[name].start()
    for copy in loads:
        copy.start()


    @pl.when(opposite)
    def _():
        swaps[1 + chunks].start()

    gather_rows(late, True)
    def attend(first_lanes):
        def one(i, carry):
            at = pl.ds(pl.multiple_of(i * 128, 128), 128)
            tile_zero, tile_one = sorted_ref[at, 0:128], sorted_ref[at, 128:256]
            low_lanes = lanes((128, 128)) < 64
            query_lanes = low_lanes if first_lanes else jnp.logical_not(low_lanes)
            queries = jnp.where(query_lanes, tile_zero, jnp.zeros_like(tile_zero))
            ids = jnp.where(query_lanes, jnp.zeros_like(tile_one), tile_one)
            both = dot(jnp.concatenate([queries, ids], axis=0), tile_one, 1, 1)
            scores, allowed = both[:128] * scale, both[128:]
            masked = jnp.where(allowed > 0.5, scores, NEGATIVE)
            highest = jnp.max(masked, axis=1, keepdims=True)
            raised = jnp.exp(masked - highest)
            totals = jnp.sum(raised, axis=1, keepdims=True)
            weights = raised * (1.0 / totals)
            prob_ref[at, :] = weights
            mixed = dot(weights.astype(jnp.bfloat16), tile_zero)
            att_sorted[at, :] = jnp.where(query_lanes, 0.0, mixed).astype(jnp.bfloat16)
            log_total = highest + jnp.log(totals)
            entropy = jnp.where(lanes((128, 128)) == 0, log_total, 0.0) - weights * masked
            ent_ref[pl.ds(i, 1), :] = jnp.sum(entropy, axis=0, keepdims=True)
            cnt_ref[pl.ds(i, 1), :] = jnp.sum(allowed, axis=0, keepdims=True)
            return carry

        return one

    lax.fori_loop(0, 16, attend(True), 0, unroll=UNROLL)
    lax.fori_loop(16, 24, attend(False), 0, unroll=UNROLL)
    stores["sorted"].start()
    stores["prob"].start()

    def send_back(i, carry):
        flip = 7 - i
        peer = member(flip)[0]
        att_send[flip] = dot(scatter[i % 4], att_sorted[...]).astype(jnp.bfloat16)

        @pl.when(i < 7)
        def _():
            remote(att_send.at[flip], att_in.at[p], back, flip, peer).start()

        @pl.when(i < 4)
        def _():
            build_block(i + 4, 0)

        return carry

    lax.fori_loop(0, 8, send_back, 0)
    back_copies = [remote(att_send.at[flip], att_in.at[p], back, flip, peers[flip - 1]) for flip in range(1, 8)]
    att_in[p] = att_send[0]

    stats_ref[...] = jnp.zeros_like(stats_ref)
    owner_pad[...] = jnp.full_like(owner_pad, -1.0)
    clusters = owners_ref.shape[2]
    for h, first, size, skip in ((h1, 0, clusters, 0), (h2, clusters, clusters // 2, c)):
        ids = jnp.where(matched, owners_ref[h], owners_in[h])
        owner_pad[0:1, 0:clusters] = ids.astype(jnp.float32)
        column = jnp.broadcast_to(owner_pad[0:1, :], (128, 128)).T
        column = jnp.where(skip == 1, column[clusters // 2 : clusters // 2 + size], column[0:size])
        owned = jnp.where(column == lanes((size, 128)).astype(jnp.float32), 1.0, 0.0)
        for kind, (lane_sums, divisor) in enumerate(((ent_ref, 4.0 * block), (cnt_ref, 4.0 * block * 128))):
            sums = jnp.sum(lane_sums[first : first + size, :], axis=1, keepdims=True) / divisor
            stats_ref[kind, pl.ds(h, 1), :] = jnp.sum(sums * owned, axis=0, keepdims=True)

    stores["stats"].start()
    bias_ref[0:1, :] = inner_bias_ref[...].astype(jnp.float32).reshape(1, width_inner)
    out_bias, first_gain, first_shift, outer_bias, second_gain, second_shift = (
        ref[...].astype(jnp.float32).reshape(1, width)
        for ref in (
            out_bias_ref,
            first_gain_ref,
            first_shift_ref,
            outer_bias_ref,
            second_gain_ref,
            second_shift_ref,
        )
    )
    for copy in back_copies:
        copy.wait()
    for pair in range(4):
        even, odd = att_in[pair], att_in[4 + pair]
        att_ref[:, 128 * pair : 128 * (pair + 1)] = join(half_roll(even), odd)
    for pair in range(2):
        low_half = att_in[2 * pair] + att_in[4 + 2 * pair]
        high_half = att_in[2 * pair + 1] + att_in[5 + 2 * pair]
        att_ref[:, 512 + 128 * pair : 640 + 128 * pair] = join(low_half, half_roll(high_half))
    stores["att"].start()

    loads[0].wait()
    branch = dot(att_ref[...], out_w[...]) + out_bias
    normed, root_one = normalize(x_all[p].astype(jnp.float32) + branch)
    first = normed * first_gain + first_shift
    normed_ref[...] = normed
    low_ref[...] = first.astype(jnp.bfloat16)
    stores["low"].start()
    total[...] = first + outer_bias
    for copy in loads[1:]:
        copy.wait()

    def dense_forward(t, carry):
        at = pl.ds(pl.multiple_of(t * dense_tile, dense_tile), dense_tile)
        inner = dot(low_ref[...], inner_w[:, at]) + bias_ref[0:1, at]
        cumulative = 0.5 + 0.5 * lax.erf(inner * (0.5**0.5))
        density = jnp.exp(-0.5 * inner * inner) * 0.3989422804014327
        slope[:, at] = cumulative + inner * density
        act = (inner * cumulative).astype(jnp.bfloat16)
        act_ref[:, at] = act
        total[...] += dot(act, outer_w[at, :])
        return carry

    lax.fori_loop(0, len(parts), dense_forward, 0)
    stores["act"].start()

    @pl.when(matched)
    def _():
        locals_[1 + chunks].wait()

    @pl.when(opposite)
    def _():
        swaps[1 + chunks].wait()

    normed_two, root_two = normalize(total[...])
    output_ref[...] = (normed_two * second_gain + second_shift).astype(jnp.bfloat16)
    stores["output"].start()
    upstream = cot_my[...].astype(jnp.float32)
    vec_out[4:5, :] = jnp.sum(upstream * normed_two, axis=0, keepdims=True)
    vec_out[5:6, :] = jnp.sum(upstream, axis=0, keepdims=True)
    delta_two = normalize_back(upstream * second_gain, normed_two, root_two)
    low_two = delta_two.astype(jnp.bfloat16)
    dsecond_ref[...] = low_two
    stores["dsecond"].start()
    vec_out[3:4, :] = jnp.sum(low_two.astype(jnp.float32), axis=0, keepdims=True)
    total[...] = delta_two

    def dense_back(t, carry):
        at = pl.ds(pl.multiple_of(t * dense_tile, dense_tile), dense_tile)
        dact = dot(dsecond_ref[...], outer_w[at, :], 1, 1)
        dinner = (dact * slope[:, at]).astype(jnp.bfloat16)
        dinner_ref[:, at] = dinner
        bias_ref[0:1, at] = jnp.sum(dinner.astype(jnp.float32), axis=0, keepdims=True)
        total[...] += dot(dinner, inner_w[:, at], 1, 1)
        return carry

    lax.fori_loop(0, len(parts), dense_back, 0)
    stores["dinner"].start()
    for i in range(width_inner // width):
        vec_out[6 + i : 7 + i, :] = bias_ref[0:1, width * i : width * (i + 1)]
    delta_first = total[...]
    normed = normed_ref[...]
    vec_out[1:2, :] = jnp.sum(delta_first * normed, axis=0, keepdims=True)
    vec_out[2:3, :] = jnp.sum(delta_first, axis=0, keepdims=True)
    delta_one = normalize_back(delta_first * first_gain, normed, root_one)
    delta_ref[...] = delta_one
    stores["delta"].start()
    low_one = delta_one.astype(jnp.bfloat16)
    dbranch_ref[...] = low_one
    stores["dbranch"].start()
    vec_out[0:1, :] = jnp.sum(low_one.astype(jnp.float32), axis=0, keepdims=True)
    vec_out[10:16, :] = jnp.zeros((6, width), jnp.float32)
    stores["vec"].start()
    datt_ref[...] = dot(dbranch_ref[...], out_w[...], 1, 1).astype(jnp.bfloat16)
    stores["datt"].start()
    for copy in stores.values():
        copy.wait()
    for copy in own_to_s + x_to_s + z_to_s + d_to_s:
        copy.wait_send()


def forward_layer(tokens, cotangent, segments, orders, owners, vectors, weights):
    block, width = tokens.shape
    inner_width = weights[4].shape[1]
    group = 8 * block
    low, full = jnp.bfloat16, jnp.float32
    vmem = pl.BlockSpec(memory_space=pltpu.VMEM)
    hbm = pl.BlockSpec(memory_space=pl.ANY)
    dma = pltpu.SemaphoreType.DMA
    rows = group * 3 // 2
    kept = [
        ((width, 512), low),
        ((8, group), jnp.int32),
        ((2, 16, 128), full),
        ((8, block, width), low),
        ((rows, 256), low),
        ((rows, 128), full),
        ((block, width), low),
        ((block, width), low),
        ((block, inner_width), low),
        ((block, width), low),
        ((block, width), low),
        ((block, inner_width), low),
        ((block, width), full),
        ((block, width), low),
        ((16, width), full),
        ((block, width), low),
    ]
    return pl.pallas_call(
        forward_kernel,
        out_shape=[jax.ShapeDtypeStruct(*one) for one in kept],
        in_specs=[vmem] * 14 + [hbm] * 6,
        out_specs=[hbm] * len(kept),
        scratch_shapes=[pltpu.VMEM(*one) for one in kept]
        + [
            pltpu.VMEM((block, width), low),
            pltpu.VMEM((3, 2, width, 128), low),
            pltpu.VMEM(orders.shape, jnp.int32),
            pltpu.VMEM(owners.shape, jnp.int32),
            pltpu.VMEM((8, 128), full),
            pltpu.VMEM((8, block), jnp.int32),
            pltpu.VMEM((8, 8, block), jnp.int32),
            pltpu.VMEM((8, width), full),
            pltpu.VMEM((8, 512), full),
            pltpu.VMEM((group, 512), low),
            pltpu.VMEM((rows, group), low),
            pltpu.VMEM((4, block, rows), low),
            pltpu.VMEM((rows, 128), low),
            pltpu.VMEM((8, block, 128), low),
            pltpu.VMEM((8, block, 128), low),
            pltpu.VMEM((24, 128), full),
            pltpu.VMEM((24, 128), full),
            dma((2 * PIECES + 6,)),
            dma((2 * PIECES + 6,)),
            dma((7 * PIECES,)),
            dma((7 * PIECES,)),
            dma((7,)),
            dma((7,)),
            dma((8,)),
            dma((8,)),
            dma((6,)),
            pltpu.VMEM(weights[3].shape, low),
            pltpu.VMEM(weights[4].shape, low),
            pltpu.VMEM(weights[5].shape, low),
            pltpu.VMEM((block, inner_width), full),
            pltpu.VMEM((block, width), full),
            pltpu.VMEM((block, width), full),
            pltpu.VMEM((8, inner_width), full),
            dma((1 + inner_width // width,)),
            dma((len(kept),)),
        ],
        compiler_params=pltpu.CompilerParams(
            collective_id=1, has_side_effects=True, vmem_limit_bytes=62 << 20
        ),
        name="forward_layer",
    )(tokens, cotangent, segments, orders, owners, *vectors, *weights)


def rows_of(start, q, size):
    return pl.ds(pl.multiple_of(start * q, 16), size * q)


def add_into(count, target, other):
    def one(i, carry):
        target(i)[...] = (
            target(i)[...].astype(jnp.float32) + other(i)[...].astype(jnp.float32)
        ).astype(jnp.bfloat16)
        return carry

    lax.fori_loop(0, count, one, 0)


def reduce_steps(parts, g_ref, f_ref, buffers, sems):
    core_in, a_one, a_two, a_three, a_four, b_one, b_two, b_three, b_four = buffers
    zh, zl, x, y, c = coordinates()
    q = g_ref.shape[3] // 8
    width = g_ref.shape[4] // parts
    over_c, over_y = device(zh, zl, x, y, 1 - c), device(zh, zl, x, 1 - y, c)
    over_x, over_zl = device(zh, zl, 1 - x, y, c), device(zh, 1 - zl, x, y, c)
    over_zh = device(1 - zh, zl, x, y, c)
    flying = {}

    def send(name, k, src, dst, peer):
        copy = remote(src, dst, (sems[0].at[name], sems[1].at[name]), k, peer)
        copy.start()
        flying[name, k] = copy

    def arrive(name, k):
        flying.pop((name, k)).wait()

    def step(stage, k):
        cols = pl.ds(k * width, width)
        if stage == "0":
            send(
                0, k, g_ref.at[:, :, :, rows_of(4 * (1 - c), q, 4), cols], core_in.at[:, :, :, :, cols], over_c
            )
        if stage == "1":
            arrive(0, k)
            add_into(
                8,
                lambda i: core_in.at[i // 4, (i // 2) % 2, i % 2, :, cols],
                lambda i: g_ref.at[i // 4, (i // 2) % 2, i % 2, rows_of(4 * c, q, 4), cols],
            )
            send(1, k, core_in.at[:, :, 1 - x, pl.ds(0, 2 * q), cols], a_one.at[:, :, :, cols], over_x)
            send(2, k, core_in.at[:, :, :, rows_of(3 - y, q, 1), cols], b_one.at[:, :, :, :, cols], over_y)
        if stage == "2a":
            arrive(1, k)
            add_into(
                4,
                lambda i: a_one.at[i // 2, i % 2, :, cols],
                lambda i: core_in.at[i // 2, i % 2, x, pl.ds(0, 2 * q), cols],
            )
            send(3, k, a_one.at[:, 1 - zl, :, cols], a_two.at[:, :, cols], over_zl)
        if stage == "3a":
            arrive(3, k)
            add_into(2, lambda i: a_two.at[i, :, cols], lambda i: a_one.at[i, zl, :, cols])
            send(4, k, a_two.at[1 - zh, :, cols], a_three.at[:, cols], over_zh)
        if stage == "4a":
            arrive(4, k)
            add_into(1, lambda i: a_three.at[:, cols], lambda i: a_two.at[zh, :, cols])
            send(5, k, a_three.at[:, cols], a_four.at[:, cols], over_y)
        if stage == "2b":
            arrive(2, k)
            add_into(
                8,
                lambda i: b_one.at[i // 4, (i // 2) % 2, i % 2, :, cols],
                lambda i: core_in.at[i // 4, (i // 2) % 2, i % 2, rows_of(2 + y, q, 1), cols],
            )
            send(6, k, b_one.at[:, :, 1 - x, :, cols], b_two.at[:, :, :, cols], over_x)
        if stage == "3":
            arrive(6, k)
            add_into(
                4,
                lambda i: b_two.at[i // 2, i % 2, :, cols],
                lambda i: b_one.at[i // 2, i % 2, x, :, cols],
            )
            send(7, k, b_two.at[:, 1 - zl, :, cols], b_three.at[:, :, cols], over_zl)
        if stage == "4":
            arrive(7, k)
            add_into(2, lambda i: b_three.at[i, :, cols], lambda i: b_two.at[i, zl, :, cols])
            send(8, k, b_three.at[1 - zh, :, cols], b_four.at[:, cols], over_zh)
        if stage == "5":
            arrive(8, k)
            f_ref[c, 1, y, :, cols] = (
                b_four[:, cols].astype(jnp.float32) + b_three[zh, :, cols].astype(jnp.float32)
            ).astype(jnp.bfloat16)
            own_rows = f_ref.at[c, 1, y, :, cols]
            send(9, k, own_rows, own_rows, over_y)
        if stage == "6":
            arrive(5, k)
            for half in range(2):
                at = pl.ds(half * q, q)
                f_ref[c, 0, half, :, cols] = (
                    a_three[at, cols].astype(jnp.float32) + a_four[at, cols].astype(jnp.float32)
                ).astype(jnp.bfloat16)
            arrive(9, k)
            both = f_ref.at[c, :, :, :, cols]
            send(10, k, both, both, over_c)
        if stage == "7":
            arrive(10, k)

    return step


BACKWARD_ORDER = (
    "begin",
    "st:0",
    "datt",
    "g1",
    "S0",
    "g2",
    "bld:1",
    "r1:0",
    "bld:0",
    "r1:1",
    "take:0",
    "r1:2",
    "home0",
    "st:1",
    "bld:2",
    "take:2",
    "bld:4",
    "r1:3",
    "r2a:0",
    "r2b:0",
    "r1:4",
    "r1:5",
    "take:1",
    "take:4",
    "bld:3",
    "take:3",
    "r2a:1",
    "r3a:0",
    "bld:5",
    "take:5",
    "at:1",
    "r2a:2",
    "r3a:1",
    "at:0",
    "r4a:0",
    "at:2",
    "r2a:3",
    "r3a:2",
    "pl",
    "r3a:3",
    "r4a:1",
    "r3:0",
    "r2b:3",
    "r4a:2",
    "r2b:4",
    "r2b:1",
    "r2a:4",
    "hE0",
    "st:2",
    "r2b:2",
    "ph",
    "r2a:5",
    "dw",
    "r4:0",
    "r4a:3",
    "r3a:4",
    "r2b:5",
    "r3:4",
    "ab:0",
    "ab:1",
    "r3a:5",
    "r3:3",
    "st:3",
    "r3:1",
    "r5:0",
    "r4:4",
    "r3:2",
    "r4a:4",
    "r3:5",
    "st:4",
    "hb:0",
    "da",
    "ha:0",
    "hb:1",
    "r6:0",
    "r4a:5",
    "stE",
    "r4:3",
    "r7:0",
    "ha:1",
    "r4:1",
    "r5:4",
    "r4:2",
    "r4:5",
    "r6:4",
    "r7:4",
    "wy",
    "hm:0",
    "r5:3",
    "hm:1",
    "r5:1",
    "r5:2",
    "r5:5",
    "wc",
    "r6:3",
    "r6:1",
    "hE:0",
    "r6:2",
    "r6:5",
    "wE",
    "r7:3",
    "r7:1",
    "r7:2",
    "r7:5",
    "hE:1",
)


def backward_kernel(
    parts,
    datt_ref,
    order_ref,
    out_my,
    stats_ref,
    vec_ref,
    att_hbm,
    dbranch_hbm,
    low_hbm,
    dsecond_hbm,
    act_hbm,
    dinner_hbm,
    sorted_hbm,
    prob_hbm,
    wsel_hbm,
    x_hbm,
    delta_hbm,
    out_home,
    grad_home,
    f_ref,
    w_all,
    stats_out,
    att_ref,
    dbranch_ref,
    low_ref,
    dsecond_ref,
    act_ref,
    dinner_ref,
    sorted_ref,
    prob_ref,
    wsel_ref,
    x_all,
    delta_ref,
    g_ref,
    datt_send,
    datt_in,
    gather,
    gathered,
    dsorted,
    scatter,
    dqkv,
    part_send,
    part_in,
    total,
    a_in,
    b_in,
    a_two,
    b_two,
    grad_my,
    dw,
    dw_y,
    dw_in,
    dw_all,
    stats_buf,
    stats_in,
    core_in,
    r_a_one,
    r_a_two,
    r_a_three,
    r_a_four,
    r_b_one,
    r_b_two,
    r_b_three,
    r_b_four,
    datt_ssem,
    datt_rsem,
    part_ssem,
    part_rsem,
    swap_ssem,
    swap_rsem,
    dw_ssem,
    dw_rsem,
    stats_ssem,
    stats_rsem,
    red_ssem,
    red_rsem,
    load_sem,
):
    zh, zl, x, y, c = coordinates()
    s = 4 * zh + 2 * zl + x
    j = 2 * zl + x
    p = 4 * c + j
    block, width = datt_ref.shape
    group = 8 * block
    scale = 0.125
    matched = c == zh
    datt_sems, part_sems = (datt_ssem, datt_rsem), (part_ssem, part_rsem)
    swap_sems, dw_sems, stats_sems = (swap_ssem, swap_rsem), (dw_ssem, dw_rsem), (stats_ssem, stats_rsem)

    def member(flip):
        fc, fz, fx = flip // 4, (flip // 2) % 2, flip % 2
        mc, mz, mx = bits(c, fc), bits(zl, fz), bits(x, fx)
        return device(zh, mz, mx, y, mc), mc, 2 * mz + mx

    peers = [member(flip)[0] for flip in range(1, 8)]
    sibling, over_x, over_z = peers[3], peers[0], peers[1]
    swap_peer = device(1 - zh, zl, x, y, 1 - c)
    over_y = device(zh, zl, x, 1 - y, c)
    across = [device(1 - zh, bits(zl, f // 2), bits(x, f % 2), y, c) for f in range(4)]
    loads = [
        pltpu.make_async_copy(src, dst, load_sem.at[i])
        for i, (src, dst) in enumerate(
            (
                (att_hbm, att_ref),
                (dbranch_hbm, dbranch_ref),
                (low_hbm, low_ref),
                (dsecond_hbm, dsecond_ref),
                (act_hbm, act_ref),
                (dinner_hbm, dinner_ref),
                (sorted_hbm, sorted_ref),
                (prob_hbm, prob_ref),
                (wsel_hbm, wsel_ref),
                (x_hbm, x_all),
                (delta_hbm, delta_ref),
            )
        )
    ]
    for copy in loads:
        copy.start()
    greet(peers + [swap_peer, over_y] + across)

    def home_copy(src, dst, index, start):
        away = remote(src, dst, swap_sems, index, swap_peer)
        here = pltpu.make_async_copy(src, dst, swap_rsem.at[3 + index])

        @pl.when(matched)
        def _():
            here.start() if start else here.wait()

        @pl.when(jnp.logical_not(matched))
        def _():
            away.start() if start else away.wait()

    def tile(mc, mj):
        first = datt_ref[:, pl.ds(pl.multiple_of(mj * 128, 128), 128)]
        other = datt_ref[:, pl.ds(pl.multiple_of((4 + mj // 2) * 128, 128), 128)]
        return join(
            select_head(other.astype(jnp.float32), mj % 2, 0), select_head(first.astype(jnp.float32), mc, 1)
        ).astype(jnp.bfloat16)

    datt_copies = []

    def datt_out():
        for flip in (3, 7, 1, 5, 2, 6, 4):
            peer, mc, mj = member(flip)
            datt_send[flip] = tile(mc, mj)
            copy = remote(datt_send.at[flip], datt_in.at[p], datt_sems, flip - 1, peer)
            copy.start()
            datt_copies.append(copy)
        datt_in[p] = tile(c, j)

    stats_peers = (sibling, over_x, over_z, across[0], over_y)
    stats_copies = [
        remote(stats_buf.at[k], stats_in.at[k], stats_sems, k, peer) for k, peer in enumerate(stats_peers)
    ]

    def stats_step(k):
        if k == 0:
            stats_buf[0] = stats_ref[...]
        else:
            stats_copies[k - 1].wait()
            stats_buf[k] = stats_buf[k - 1] + stats_in[k - 1]
        if k < len(stats_peers):
            stats_copies[k].start()
        else:
            stats_out[...] = stats_buf[k]

    share = width // 8
    q = g_ref.shape[3] // 8
    top = 4 * q

    def outer_grads():
        def one(d, carry):
            columns = pl.ds(pl.multiple_of(d * 4 * share, 128), 4 * share)
            g_ref[d // 4, (d // 2) % 2, d % 2, top : top + 4 * share, :] = dot(
                act_ref[:, columns], dsecond_ref[...], 0, 0
            ).astype(jnp.bfloat16)
            return carry

        lax.fori_loop(0, 8, one, 0)

    def inner_grads():
        def one(i, carry):
            z, n = i // 4, i % 4
            rows = pl.ds(pl.multiple_of(z * 4 * share, 128), 4 * share)
            columns = pl.ds(pl.multiple_of(n * width, 128), width)
            grads = dot(low_ref[:, rows], dinner_ref[:, columns], 0, 0).astype(jnp.bfloat16)
            for k in range(4):
                at = pl.ds(pl.multiple_of(n * share, 16), share)
                g_ref[z, k // 2, k % 2, at, :] = grads[share * k : share * (k + 1)]
            return carry

        lax.fori_loop(0, 8, one, 0)

    def grads_first():
        for copy in loads[:6]:
            copy.wait()
        vectors = vec_ref[...].astype(jnp.bfloat16)
        for z in range(2):
            columns = slice(4 * share * z, 4 * share * (z + 1))
            grads = dot(att_ref[:, columns], dbranch_ref[...], 0, 0).astype(jnp.bfloat16)
            for k in range(4):
                rows = grads[share * k : share * (k + 1)]
                g_ref[z, k // 2, k % 2, 4 * share : 4 * share + share // 2, :] = rows[: share // 2]
                g_ref[z, k // 2, k % 2, 4 * share + share // 2 : top, :] = jnp.zeros_like(vectors)
                g_ref[z, k // 2, k % 2, top + 4 * share : top + 4 * share + share // 2, :] = rows[share // 2 :]
                g_ref[z, k // 2, k % 2, top + 4 * share + share // 2 :, :] = vectors
        pl.when(c == 0)(outer_grads)
        pl.when(c == 1)(inner_grads)

    def grads_second():
        pl.when(c == 0)(inner_grads)
        pl.when(c == 1)(outer_grads)

    reduction = reduce_steps(
        parts,
        g_ref,
        f_ref,
        (core_in, r_a_one, r_a_two, r_a_three, r_a_four, r_b_one, r_b_two, r_b_three, r_b_four),
        (red_ssem, red_rsem),
    )

    half = 1024 * c
    step = gather.shape[1]
    chunks = group * 3 // 2 // step

    def build(k):
        head, start = (0, k * step) if k * step < group else (1, half + k * step - group)
        build_gather(order_ref, head, start, step, gather.at[k % 2])

    arrivals = []

    def take(k):
        if not arrivals:
            for copy in datt_copies:
                copy.wait()
            arrivals.append(True)
        gathered[k * step : (k + 1) * step, :] = dot(
            gather[k % 2], datt_in[...].reshape(group, 128)
        ).astype(jnp.bfloat16)

    def attend_back(first_lanes):
        def one(i, carry):
            at = pl.ds(pl.multiple_of(i * 128, 128), 128)
            tile_zero, tile_one = sorted_ref[at, 0:128], sorted_ref[at, 128:256]
            low_lanes = lanes((128, 128)) < 64
            query_lanes = low_lanes if first_lanes else jnp.logical_not(low_lanes)
            weights = prob_ref[at, :]
            taken = gathered[at, :]
            taken = jnp.where(query_lanes, jnp.zeros_like(taken), taken)
            weight_grads = dot(taken, tile_zero, 1, 1)
            inside = jnp.sum(weights * weight_grads, axis=1, keepdims=True)
            score_grads = weights * (weight_grads - inside)
            low_grads = score_grads.astype(jnp.bfloat16)
            query_grads = dot(low_grads, tile_one) * scale
            key_grads = dot(low_grads, tile_zero, 0, 0) * scale
            value_grads = dot(weights.astype(jnp.bfloat16), taken, 0, 0)
            dsorted[at, 0:128] = jnp.where(query_lanes, query_grads, value_grads).astype(jnp.bfloat16)
            dsorted[at, 128:256] = jnp.where(query_lanes, key_grads, 0.0).astype(jnp.bfloat16)
            return carry

        return one

    loaded = []

    def attend_some(i):
        if not loaded:
            for copy in loads[6:]:
                copy.wait()
            loaded.append(True)
        lax.fori_loop(8 * i, 8 * i + 8, attend_back(i < 2), 0, unroll=4)

    def place(position):
        token = lax.broadcasted_iota(jnp.int32, (128, 128), 0) + position * block
        for t in range(block // 128):
            for head, start, count, base in ((0, 0, group, 0), (1, half, group // 2, group)):
                for k in range(count // 128):
                    ids = order_ref[head : head + 1, pl.ds(pl.multiple_of(start + 128 * k, 128), 128)]
                    scatter[128 * t : 128 * (t + 1), base + 128 * k : base + 128 * (k + 1)] = hot(
                        ids == token + 128 * t
                    )
        at = pl.ds(pl.multiple_of(position * block, block), block)
        dqkv[at, 0:256] = dot(scatter[:, 0:group], dsorted[0:group, :]).astype(jnp.bfloat16)
        dqkv[at, 256:512] = dot(scatter[:, group:], dsorted[group:, :]).astype(jnp.bfloat16)
        return dot(dqkv[at, :], wsel_ref[...], 1, 1)

    def part_copy(k):
        return remote(part_send.at[k], part_in.at[k], part_sems, k, sibling)

    def parts_away():
        def one(k, carry):
            part_send[k] = place(4 * (1 - c) + k).astype(jnp.bfloat16)
            part_copy(k).start()
            return carry

        lax.fori_loop(0, 4, one, 0)

    def parts_here():
        def one(k, carry):
            part = place(4 * c + k)
            part_copy(k).wait()
            total[k // 2, k % 2] = (part + part_in[k].astype(jnp.float32)).astype(jnp.bfloat16)
            return carry

        lax.fori_loop(0, 4, one, 0)

    upper, lower = pl.ds(0, block // 2), pl.ds(block // 2, block // 2)
    pieces = [pl.ds(i * (width // 2), width // 2) for i in range(2)]
    a_copies = [
        remote(total.at[:, 1 - x, upper, cols], a_in.at[:, :, cols], part_sems, 4 + i, over_x)
        for i, cols in enumerate(pieces)
    ]
    b_copies = [
        remote(total.at[1 - zl, :, lower, cols], b_in.at[:, :, cols], part_sems, 6 + i, over_z)
        for i, cols in enumerate(pieces)
    ]
    a_next = [
        remote(a_in.at[1 - zl, :, cols], a_two.at[:, cols], part_sems, 8 + i, over_z)
        for i, cols in enumerate(pieces)
    ]
    b_next = [
        remote(b_in.at[1 - x, :, cols], b_two.at[:, cols], part_sems, 10 + i, over_x)
        for i, cols in enumerate(pieces)
    ]

    def first_hops(i):
        a_copies[i].start()
        b_copies[i].start()

    def second_hop_a(i):
        cols = pieces[i]
        a_copies[i].wait()
        add_into(2, lambda k: a_in.at[k, :, cols], lambda k: total.at[k, x, upper, cols])
        a_next[i].start()

    def second_hop_b(i):
        cols = pieces[i]
        b_copies[i].wait()
        add_into(2, lambda k: b_in.at[k, :, cols], lambda k: total.at[zl, k, lower, cols])
        b_next[i].start()

    def grad_home_start(i):
        cols = pieces[i]
        a_next[i].wait()
        b_next[i].wait()
        for start, first, second, index in ((0, a_two, a_in, zl), (block // 2, b_two, b_in, x)):
            at = pl.ds(start, block // 2)
            grad_my[at, cols] = (
                delta_ref[at, cols]
                + first[:, cols].astype(jnp.float32)
                + second[index, :, cols].astype(jnp.float32)
            ).astype(jnp.bfloat16)
        home_copy(grad_my.at[:, cols], grad_home.at[:, cols], 1 + i, True)

    def grad_home_end(i):
        cols = pieces[i]
        home_copy(grad_my.at[:, cols], grad_home.at[:, cols], 1 + i, False)

    over_y_copy = remote(dw_y.at[1 - y], dw_in, dw_sems, 0, over_y)

    def projections():
        for k in range(width // 128):
            dw[128 * k : 128 * (k + 1), :] = dot(
                x_all[:, 128 * k : 128 * (k + 1)], dqkv[...], 0, 0
            ).astype(jnp.bfloat16)
        bias_row = jnp.broadcast_to(
            jnp.sum(dqkv[...].astype(jnp.float32), axis=0, keepdims=True), (16, 512)
        ).astype(jnp.bfloat16)
        for d in range(8):
            for h in range(2):
                dw_y[h, d, 0:share, :] = dw[share * d : share * (d + 1), 256 * h : 256 * (h + 1)]
                dw_y[h, d, share : share + 16, :] = bias_row[:, 256 * h : 256 * (h + 1)]
        over_y_copy.start()

    targets = across + [over_x, over_z, peers[2]]
    flips = [(1, f // 2, f % 2) for f in range(4)] + [(0, 0, 1), (0, 1, 0), (0, 1, 1)]
    dw_copies = []
    for i, (peer, (fh, fz, fx)) in enumerate(zip(targets, flips)):
        d = 4 * bits(zh, fh) + 2 * bits(zl, fz) + bits(x, fx)
        dw_copies.append(remote(dw_y.at[y, d], dw_all.at[s], dw_sems, 1 + i, peer))
    w_over_y = remote(w_all.at[y, c], w_all.at[y, c], dw_sems, 8, over_y)
    w_over_c = remote(w_all.at[:, c], w_all.at[:, c], dw_sems, 9, sibling)

    def dw_exchange():
        over_y_copy.wait()
        add_into(8, lambda i: dw_y.at[y, i], lambda i: dw_in.at[i])
        for copy in dw_copies:
            copy.start()
        dw_all[s] = dw_y[y, s]

    def dw_sum():
        for copy in dw_copies:
            copy.wait()
        for k in range(4):
            w_all[y, c, k] = (dw_all[k].astype(jnp.float32) + dw_all[4 + k].astype(jnp.float32)).astype(
                jnp.bfloat16
            )
        w_over_y.start()

    def dw_core():
        w_over_y.wait()
        w_over_c.start()

    def start_reduction():
        for k in range(parts):
            reduction("0", k)

    single = {
        "begin": lambda: None,
        "datt": datt_out,
        "home0": lambda: home_copy(out_my, out_home, 0, True),
        "hE0": lambda: home_copy(out_my, out_home, 0, False),
        "g1": grads_first,
        "g2": grads_second,
        "S0": start_reduction,
        "pl": parts_away,
        "ph": parts_here,
        "dw": projections,
        "da": dw_exchange,
        "wy": dw_sum,
        "wc": dw_core,
        "wE": w_over_c.wait,
        "stE": lambda: stats_step(5),
    }
    indexed = {
        "bld": build,
        "take": take,
        "at": attend_some,
        "ab": first_hops,
        "ha": second_hop_a,
        "hb": second_hop_b,
        "hm": grad_home_start,
        "hE": grad_home_end,
        "st": stats_step,
    }
    for name in BACKWARD_ORDER:
        kind, _, index = name.partition(":")
        if kind in single:
            single[kind]()
        elif kind in indexed:
            indexed[kind](int(index))
        else:
            reduction(kind[1:], int(index))


def backward_attention(
    datt,
    order,
    output,
    stats,
    vectors,
    att,
    dbranch,
    low_first,
    dsecond,
    act,
    dinner,
    sorted_rows,
    prob,
    wsel,
    x_all,
    delta,
    parts,
):
    block, width = datt.shape
    inner_width = act.shape[1]
    group = 8 * block
    rows = group * 3 // 2
    q = (9 * width // 8 + 32) // 8
    share = width // 8 + 16
    low, full = jnp.bfloat16, jnp.float32
    vmem = pl.BlockSpec(memory_space=pltpu.VMEM)
    hbm = pl.BlockSpec(memory_space=pl.ANY)
    dma = pltpu.SemaphoreType.DMA
    shape = jax.ShapeDtypeStruct
    return pl.pallas_call(
        functools.partial(backward_kernel, parts),
        out_shape=[
            shape((block, width), low),
            shape((block, width), low),
            shape((2, 2, 2, q, width), low),
            shape((2, 2, 4, share, 256), low),
            shape(stats.shape, full),
        ],
        in_specs=[vmem] * 5 + [hbm] * 11,
        out_specs=[vmem] * 5,
        scratch_shapes=[
            pltpu.VMEM((block, width), low),
            pltpu.VMEM((block, width), low),
            pltpu.VMEM((block, width), low),
            pltpu.VMEM((block, width), low),
            pltpu.VMEM((block, inner_width), low),
            pltpu.VMEM((block, inner_width), low),
            pltpu.VMEM((rows, 256), low),
            pltpu.VMEM((rows, 128), full),
            pltpu.VMEM((width, 512), low),
            pltpu.VMEM((group, width), low),
            pltpu.VMEM((block, width), full),
            pltpu.VMEM((2, 2, 2, 8 * q, width), low),
            pltpu.VMEM((8, block, 128), low),
            pltpu.VMEM((8, block, 128), low),
            pltpu.VMEM((2, 512, group), low),
            pltpu.VMEM((rows, 128), low),
            pltpu.VMEM((rows, 256), low),
            pltpu.VMEM((block, rows), low),
            pltpu.VMEM((group, 512), low),
            pltpu.VMEM((4, block, width), low),
            pltpu.VMEM((4, block, width), low),
            pltpu.VMEM((2, 2, block, width), low),
            pltpu.VMEM((2, block // 2, width), low),
            pltpu.VMEM((2, block // 2, width), low),
            pltpu.VMEM((block // 2, width), low),
            pltpu.VMEM((block // 2, width), low),
            pltpu.VMEM((block, width), low),
            pltpu.VMEM((width, 512), low),
            pltpu.VMEM((2, 8, share, 256), low),
            pltpu.VMEM((8, share, 256), low),
            pltpu.VMEM((8, share, 256), low),
            pltpu.VMEM((6,) + stats.shape, full),
            pltpu.VMEM((5,) + stats.shape, full),
            pltpu.VMEM((2, 2, 2, 4 * q, width), low),
            pltpu.VMEM((2, 2, 2 * q, width), low),
            pltpu.VMEM((2, 2 * q, width), low),
            pltpu.VMEM((2 * q, width), low),
            pltpu.VMEM((2 * q, width), low),
            pltpu.VMEM((2, 2, 2, q, width), low),
            pltpu.VMEM((2, 2, q, width), low),
            pltpu.VMEM((2, q, width), low),
            pltpu.VMEM((q, width), low),
            dma((7,)),
            dma((7,)),
            dma((12,)),
            dma((12,)),
            dma((6,)),
            dma((6,)),
            dma((10,)),
            dma((10,)),
            dma((5,)),
            dma((5,)),
            dma((11, parts)),
            dma((11, parts)),
            dma((11,)),
        ],
        compiler_params=pltpu.CompilerParams(
            collective_id=2, has_side_effects=True, vmem_limit_bytes=62 << 20
        ),
        name="backward_attention",
    )(
        datt,
        order,
        output,
        stats,
        vectors,
        att,
        dbranch,
        low_first,
        dsecond,
        act,
        dinner,
        sorted_rows,
        prob,
        wsel,
        x_all.reshape(group, width),
        delta,
    )


def finish_kernel(
    f_ref,
    w_ref,
    out_ref,
    grad_ref,
    stats_ref,
    output,
    grad_tokens,
    gq_out,
    gqb_out,
    gk_out,
    gv_out,
    gvb_out,
    go_out,
    gob_out,
    gfg_out,
    gfs_out,
    gi_out,
    gib_out,
    gu_out,
    gub_out,
    gsg_out,
    gss_out,
    stats_out,
    gq_ref,
    gv_ref,
    vec_ref,
    square,
):
    s = lax.axis_index("seq")
    output[0] = out_ref[...]
    grad_tokens[0] = grad_ref[...]
    for kind in range(2):
        square[0:16, :] = stats_ref[kind]
        stats_out[kind] = square[...].T[: stats_out.shape[1], : stats_out.shape[2]]
    share, width = gk_out.shape
    top = f_ref.shape[0] // 2
    full = jnp.float32
    for n in range(gi_out.shape[1] // width):
        gi_out[:, n * width : (n + 1) * width] = f_ref[n * share : (n + 1) * share, :].astype(full)
    gu_out[...] = f_ref[top : top + 4 * share, :].astype(full)
    part = share // 2
    go_out[0:part, :] = f_ref[4 * share : 4 * share + part, :].astype(full)
    go_out[part:, :] = f_ref[top + 4 * share : top + 4 * share + part, :].astype(full)
    vec_ref[...] = f_ref[top + 4 * share + part :, :].astype(full)
    for pair in range(4):
        at = slice(128 * pair, 128 * pair + 128)
        low, high = (w_ref[0, core, pair].astype(full) for core in range(2))
        gq_ref[:, at] = join(low[:, 0:128], half_roll(high[:, 0:128]))
        gk_out[:, at] = join(low[:, 128:256], half_roll(high[:, 128:256]))[:share]
        gv_ref[:, at] = join(half_roll(low[:, 0:128]), high[:, 0:128])
    for pair in range(2):
        at = slice(512 + 128 * pair, 640 + 128 * pair)
        low, high = (
            w_ref[1, 0, 2 * pair + i].astype(full) + w_ref[1, 1, 2 * pair + i].astype(full) for i in range(2)
        )
        gq_ref[:, at] = join(half_roll(low[:, 0:128]), high[:, 0:128])
        gk_out[:, at] = join(half_roll(low[:, 128:256]), high[:, 128:256])[:share]
        gv_ref[:, at] = join(low[:, 0:128], half_roll(high[:, 0:128]))
    gq_out[...] = gq_ref[:share, :]
    gv_out[...] = gv_ref[:share, :]

    def mine(rows):
        return pltpu.roll(rows, width - share * s, 1)[:, :share]

    short = mine(vec_ref[...])
    for row, ref in enumerate((gob_out, gfg_out, gfs_out, gub_out, gsg_out, gss_out)):
        ref[...] = short[row]
    gqb_out[...] = mine(gq_ref[share : share + 8, :])[0]
    gvb_out[...] = mine(gv_ref[share : share + 8, :])[0]
    row = vec_ref[pl.ds(6 + s // 2, 1), :]
    gib_out[...] = jnp.where(s % 2 == 1, row[:, 4 * share :], row[:, : 4 * share])[0]


def finish(reduced, w_all, output, grad, totals, head_count, inner_width):
    block, width = output.shape
    row_count = 8 * reduced.shape[3]
    share = width // 8
    low, full = jnp.bfloat16, jnp.float32
    vmem = pl.BlockSpec(memory_space=pltpu.VMEM)
    shape = jax.ShapeDtypeStruct
    square, vector = shape((share, width), full), shape((share,), full)
    out_shape = [
        shape((1, block, width), low),
        shape((1, block, width), low),
        square,
        vector,
        square,
        square,
        vector,
        square,
        vector,
        vector,
        vector,
        shape((share, inner_width), full),
        shape((inner_width // 8,), full),
        shape((inner_width // 8, width), full),
        vector,
        vector,
        vector,
        shape((2, 8, head_count), full),
    ]
    outs = pl.pallas_call(
        finish_kernel,
        out_shape=out_shape,
        in_specs=[vmem] * 5,
        out_specs=[vmem] * len(out_shape),
        scratch_shapes=[
            pltpu.VMEM((share + 16, width), full),
            pltpu.VMEM((share + 16, width), full),
            pltpu.VMEM((16, width), full),
            pltpu.VMEM((128, 128), full),
        ],
        compiler_params=pltpu.CompilerParams(vmem_limit_bytes=60 << 20),
        name="finish",
    )(reduced.reshape(row_count, width), w_all, output, grad, totals)
    return (*outs[:-1], outs[-1].transpose(0, 2, 1))


def body(
    tokens,
    segments,
    orders,
    owners,
    query_weight,
    query_bias,
    key_weight,
    value_weight,
    value_bias,
    out_weight,
    out_bias,
    first_gain,
    first_shift,
    inner_weight,
    inner_bias,
    outer_weight,
    outer_bias,
    second_gain,
    second_shift,
    cotangent,
):
    seq_count = lax.axis_size("seq")
    groups = lax.axis_size("rep")
    own_index = lax.axis_index("seq")
    row_count = tokens.shape[1]
    model_width = tokens.shape[2]
    order_table = orders[0]
    owner_table = owners[0]
    head_count, group_tokens = order_table.shape
    cluster_count = owner_table.shape[1]
    cluster = group_tokens // cluster_count
    head_dim = model_width // head_count
    per_owner = row_count // cluster
    score_scale = head_dim ** (-0.5)
    flat_tokens = tokens[0]
    local_index = jnp.arange(row_count, dtype=jnp.int32)
    factor = 1
    for candidate in range(1, seq_count + 1):
        if seq_count % candidate == 0 and candidate * row_count <= 2048:
            factor = candidate
    block_count = seq_count // factor
    block_width = factor * row_count
    order_blocks = order_table.reshape(head_count, block_count, block_width).transpose(1, 0, 2)
    owner_blocks = (
        jnp.repeat(owner_table, cluster, axis=1)
        .reshape(head_count, block_count, block_width)
        .transpose(1, 0, 2)
    )

    def find_target(total, block_item):
        order_block, owner_block = block_item
        local = order_block - own_index * row_count
        hits = local[:, :, None] == local_index[None, None, :]
        return (total + jnp.sum(jnp.where(hits, owner_block[:, :, None], 0), axis=1), None)

    target, unused = lax.scan(
        find_target, jnp.zeros((head_count, row_count), jnp.int32), (order_blocks, owner_blocks)
    )
    send_matrix = rank_matrix(target * row_count + local_index[None, :])
    mine = (owner_table == own_index).astype(jnp.int32)
    before = jnp.cumsum(mine, axis=1) - mine
    slot_hot = (mine[:, None, :] == 1) & (
        before[:, None, :] == jnp.arange(per_owner, dtype=jnp.int32)[None, :, None]
    )
    order_grid = order_table.reshape(head_count, cluster_count, cluster)
    owned_tokens = jnp.sum(
        jnp.where(slot_hot[:, :, :, None], order_grid[:, None, :, :], 0), axis=2
    ).reshape(head_count, row_count)
    arrive_matrix = rank_matrix(owned_tokens)
    w_three = jnp.concatenate([query_weight, key_weight, value_weight], axis=1)
    bias_three = jnp.concatenate(
        [
            query_bias.astype(jnp.float32),
            jnp.zeros((model_width,), jnp.float32),
            value_bias.astype(jnp.float32),
        ]
    )
    projected = (
        jnp.dot(flat_tokens, w_three, preferred_element_type=jnp.float32) + bias_three
    ).astype(jnp.bfloat16)
    token_rows = (
        projected.reshape(row_count, 3, head_count, head_dim)
        .transpose(2, 0, 1, 3)
        .reshape(head_count, row_count, 3 * head_dim)
    )
    segment_rows = jnp.broadcast_to(
        segments[0].astype(jnp.bfloat16)[None, :, None], (head_count, row_count, 1)
    )
    send_values = scatter_rows(token_rows, send_matrix, seq_count)
    send_segments = scatter_rows(segment_rows, send_matrix, seq_count)
    arrived, arrived_segments = (
        lax.all_to_all(send_values, "seq", split_axis=0, concat_axis=0, tiled=True),
        lax.all_to_all(send_segments, "seq", split_axis=0, concat_axis=0, tiled=True),
    )
    cluster_rows = collect_rows(arrived, arrive_matrix, 3 * head_dim).reshape(
        head_count * per_owner, cluster, 3, head_dim
    )
    cluster_segments = collect_rows(arrived_segments, arrive_matrix, 1).reshape(
        head_count * per_owner, cluster
    )
    queries = cluster_rows[:, :, 0]
    keys_in = cluster_rows[:, :, 1]
    values = cluster_rows[:, :, 2]
    attended, log_total, entropy, occupied = cluster_forward(
        queries, keys_in, values, cluster_segments, score_scale
    )
    per_head = jnp.stack(
        [
            jnp.sum(entropy.reshape(head_count, -1), axis=1),
            jnp.sum(occupied.reshape(head_count, -1), axis=1) / cluster,
        ]
    ) / (groups * row_count)
    column = (jnp.arange(seq_count, dtype=jnp.int32) == own_index).astype(jnp.float32)
    cluster_stats = lax.psum(per_head[:, :, None] * column, ("seq", "rep"))
    leaving = scatter_rows(
        attended.reshape(head_count, row_count, head_dim), arrive_matrix, seq_count
    )
    returned = lax.all_to_all(leaving, "seq", split_axis=0, concat_axis=0, tiled=True)
    attended_rows = (
        collect_rows(returned, send_matrix, head_dim)
        .transpose(1, 0, 2)
        .reshape(row_count, model_width)
    )
    branch = jnp.dot(
        attended_rows, out_weight, preferred_element_type=jnp.float32
    ) + out_bias.astype(jnp.float32)
    first_out, normed_one, root_one = norm_forward(
        flat_tokens.astype(jnp.float32) + branch, first_gain, first_shift
    )
    first_low = first_out.astype(jnp.bfloat16)
    inner_sum = jnp.dot(
        first_low, inner_weight, preferred_element_type=jnp.float32
    ) + inner_bias.astype(jnp.float32)
    activated, gelu_pull = jax.vjp(exact_gelu, inner_sum)
    activated_low = activated.astype(jnp.bfloat16)
    second = jnp.dot(
        activated_low, outer_weight, preferred_element_type=jnp.float32
    ) + outer_bias.astype(jnp.float32)
    result, normed_two, root_two = norm_forward(first_out + second, second_gain, second_shift)
    output = result.astype(jnp.bfloat16)[None]
    upstream = cotangent[0].astype(jnp.float32)
    gradient_second_gain = jnp.sum(upstream * normed_two, axis=0)
    gradient_second_shift = jnp.sum(upstream, axis=0)
    delta_two = norm_backward(upstream, normed_two, root_two, second_gain)
    delta_second = delta_two.astype(jnp.bfloat16)
    gradient_outer_bias = jnp.sum(delta_second.astype(jnp.float32), axis=0)
    gradient_outer_weight = jnp.einsum(
        "tf,td->fd", activated_low, delta_second, preferred_element_type=jnp.float32
    )
    delta_activated = jnp.einsum(
        "td,fd->tf", delta_second, outer_weight, preferred_element_type=jnp.float32
    )
    delta_inner = gelu_pull(delta_activated)[0].astype(jnp.bfloat16)
    gradient_inner_bias = jnp.sum(delta_inner.astype(jnp.float32), axis=0)
    gradient_inner_weight = jnp.einsum(
        "td,tf->df", first_low, delta_inner, preferred_element_type=jnp.float32
    )
    delta_first = delta_two + jnp.einsum(
        "tf,df->td", delta_inner, inner_weight, preferred_element_type=jnp.float32
    )
    gradient_first_gain = jnp.sum(delta_first * normed_one, axis=0)
    gradient_first_shift = jnp.sum(delta_first, axis=0)
    delta_one = norm_backward(delta_first, normed_one, root_one, first_gain)
    delta_branch = delta_one.astype(jnp.bfloat16)
    gradient_out_bias = jnp.sum(delta_branch.astype(jnp.float32), axis=0)
    gradient_out_weight = jnp.einsum(
        "td,te->de", attended_rows, delta_branch, preferred_element_type=jnp.float32
    )
    delta_attended = jnp.einsum(
        "te,de->td", delta_branch, out_weight, preferred_element_type=jnp.float32
    ).astype(jnp.bfloat16)
    delta_rows = delta_attended.reshape(row_count, head_count, head_dim).transpose(1, 0, 2)
    send_grads = scatter_rows(delta_rows, send_matrix, seq_count)
    grad_arrived = lax.all_to_all(send_grads, "seq", split_axis=0, concat_axis=0, tiled=True)
    kept_queries, kept_keys, kept_values, kept_segments = (
        queries,
        keys_in,
        values,
        cluster_segments,
    )
    grad_cluster = collect_rows(grad_arrived, arrive_matrix, head_dim).reshape(
        head_count * per_owner, cluster, head_dim
    )
    three_grads = cluster_backward(
        kept_queries, kept_keys, kept_values, kept_segments, log_total, grad_cluster, score_scale
    )
    leaving_grads = scatter_rows(
        three_grads.reshape(head_count, row_count, 3 * head_dim), arrive_matrix, seq_count
    )
    returned_grads = lax.all_to_all(leaving_grads, "seq", split_axis=0, concat_axis=0, tiled=True)
    delta_three = (
        collect_rows(returned_grads, send_matrix, 3 * head_dim)
        .reshape(head_count, row_count, 3, head_dim)
        .transpose(1, 2, 0, 3)
        .reshape(row_count, 3 * model_width)
    )
    bias_grads = jnp.sum(delta_three.astype(jnp.float32), axis=0)
    weight_grads = jnp.einsum(
        "td,te->de", flat_tokens, delta_three, preferred_element_type=jnp.float32
    )
    gradient_tokens = (
        delta_one
        + jnp.einsum("te,de->td", delta_three, w_three, preferred_element_type=jnp.float32)
    ).astype(jnp.bfloat16)[None]
    gradient_query_weight = weight_grads[:, :model_width]
    gradient_key_weight = weight_grads[:, model_width : 2 * model_width]
    gradient_value_weight = weight_grads[:, 2 * model_width :]
    gradient_query_bias = bias_grads[:model_width]
    gradient_value_bias = bias_grads[2 * model_width :]
    pieces = (
        lax.psum_scatter(gradient_query_weight, "seq", scatter_dimension=0, tiled=True),
        lax.psum_scatter(gradient_query_bias, "seq", scatter_dimension=0, tiled=True),
        lax.psum_scatter(gradient_key_weight, "seq", scatter_dimension=0, tiled=True),
        lax.psum_scatter(gradient_value_weight, "seq", scatter_dimension=0, tiled=True),
        lax.psum_scatter(gradient_value_bias, "seq", scatter_dimension=0, tiled=True),
        lax.psum_scatter(gradient_out_weight, "seq", scatter_dimension=0, tiled=True),
        lax.psum_scatter(gradient_out_bias, "seq", scatter_dimension=0, tiled=True),
        lax.psum_scatter(gradient_first_gain, "seq", scatter_dimension=0, tiled=True),
        lax.psum_scatter(gradient_first_shift, "seq", scatter_dimension=0, tiled=True),
        lax.psum_scatter(gradient_inner_weight, "seq", scatter_dimension=0, tiled=True),
        lax.psum_scatter(gradient_inner_bias, "seq", scatter_dimension=0, tiled=True),
        lax.psum_scatter(gradient_outer_weight, "seq", scatter_dimension=0, tiled=True),
        lax.psum_scatter(gradient_outer_bias, "seq", scatter_dimension=0, tiled=True),
        lax.psum_scatter(gradient_second_gain, "seq", scatter_dimension=0, tiled=True),
        lax.psum_scatter(gradient_second_shift, "seq", scatter_dimension=0, tiled=True),
    )
    summed = (
        lax.psum(pieces[0].astype(jnp.bfloat16), "rep").astype(jnp.float32),
        lax.psum(pieces[1].astype(jnp.bfloat16), "rep").astype(jnp.float32),
        lax.psum(pieces[2].astype(jnp.bfloat16), "rep").astype(jnp.float32),
        lax.psum(pieces[3].astype(jnp.bfloat16), "rep").astype(jnp.float32),
        lax.psum(pieces[4].astype(jnp.bfloat16), "rep").astype(jnp.float32),
        lax.psum(pieces[5].astype(jnp.bfloat16), "rep").astype(jnp.float32),
        lax.psum(pieces[6].astype(jnp.bfloat16), "rep").astype(jnp.float32),
        lax.psum(pieces[7].astype(jnp.bfloat16), "rep").astype(jnp.float32),
        lax.psum(pieces[8].astype(jnp.bfloat16), "rep").astype(jnp.float32),
        lax.psum(pieces[9].astype(jnp.bfloat16), "rep").astype(jnp.float32),
        lax.psum(pieces[10].astype(jnp.bfloat16), "rep").astype(jnp.float32),
        lax.psum(pieces[11].astype(jnp.bfloat16), "rep").astype(jnp.float32),
        lax.psum(pieces[12].astype(jnp.bfloat16), "rep").astype(jnp.float32),
        lax.psum(pieces[13].astype(jnp.bfloat16), "rep").astype(jnp.float32),
        lax.psum(pieces[14].astype(jnp.bfloat16), "rep").astype(jnp.float32),
    )
    return (output, gradient_tokens) + tuple(summed) + (cluster_stats,)


def square_body(
    tokens,
    segments,
    orders,
    owners,
    query_weight,
    query_bias,
    key_weight,
    value_weight,
    value_bias,
    out_weight,
    out_bias,
    first_gain,
    first_shift,
    inner_weight,
    inner_bias,
    outer_weight,
    outer_bias,
    second_gain,
    second_shift,
    cotangent,
):
    (
        wsel,
        order,
        stats,
        x_all,
        sorted_rows,
        prob,
        att,
        low_first,
        act,
        output,
        dsecond,
        dinner,
        delta,
        dbranch,
        vector_grads,
        datt,
    ) = forward_layer(
        tokens[0],
        cotangent[0],
        segments,
        orders.transpose(1, 0, 2),
        owners.transpose(1, 0, 2),
        (
            query_bias,
            value_bias,
            out_bias,
            first_gain,
            first_shift,
            outer_bias,
            second_gain,
            second_shift,
            inner_bias,
        ),
        (query_weight, key_weight, value_weight, out_weight, inner_weight, outer_weight),
    )
    output, grad, reduced, w_all, totals = backward_attention(
        datt,
        order,
        output,
        stats,
        vector_grads,
        att,
        dbranch,
        low_first,
        dsecond,
        act,
        dinner,
        sorted_rows,
        prob,
        wsel,
        x_all,
        delta,
        6,
    )
    return finish(reduced, w_all, output, grad, totals, orders.shape[1], inner_weight.shape[1])


def solution(mesh):
    square = mesh.shape["seq"] == 8 and mesh.shape["rep"] == 4
    placed = (
        P("rep", "seq", None),
        P("rep", "seq"),
        P("rep", None, None),
        P("rep", None, None),
        P(),
        P(),
        P(),
        P(),
        P(),
        P(),
        P(),
        P(),
        P(),
        P(),
        P(),
        P(),
        P(),
        P(),
        P(),
        P("rep", "seq", None),
    )
    return jax.shard_map(
        square_body if square else body,
        mesh=mesh,
        in_specs=placed,
        out_specs=(
            P("rep", "seq", None),
            P("rep", "seq", None),
            P("seq", None),
            P("seq"),
            P("seq", None),
            P("seq", None),
            P("seq"),
            P("seq", None),
            P("seq"),
            P("seq"),
            P("seq"),
            P("seq", None),
            P("seq"),
            P("seq", None),
            P("seq"),
            P("seq"),
            P("seq"),
            P(),
        ),
        check_vma=False,
    )
```

```python
import functools

import jax
import jax.numpy as jnp
from jax import lax
from jax.experimental import pallas as pl
from jax.experimental.pallas import tpu as pltpu
from jax.sharding import PartitionSpec as P

EPSILON = 1e-12
NEGATIVE = -1e30


def norm_forward(hidden, gain_vector, shift_vector):
    centre = hidden - jnp.mean(hidden, axis=-1, keepdims=True)
    root_inverse = lax.rsqrt(jnp.mean(centre * centre, axis=-1, keepdims=True) + EPSILON)
    normed = centre * root_inverse
    return (
        normed * gain_vector.astype(jnp.float32) + shift_vector.astype(jnp.float32),
        normed,
        root_inverse,
    )


def norm_backward(upstream, normed, root_inverse, gain_vector):
    scaled = upstream * gain_vector.astype(jnp.float32)
    return root_inverse * (
        scaled
        - jnp.mean(scaled, axis=-1, keepdims=True)
        - normed * jnp.mean(scaled * normed, axis=-1, keepdims=True)
    )


def exact_gelu(inner_sum):
    return jax.nn.gelu(inner_sum, approximate=False)


def rank_matrix(sort_keys):
    row_count = sort_keys.shape[1]
    ranks = jnp.sum((sort_keys[:, None, :] < sort_keys[:, :, None]).astype(jnp.int32), axis=2)
    return (ranks[:, None, :] == jnp.arange(row_count, dtype=jnp.int32)[None, :, None]).astype(
        jnp.bfloat16
    )


def scatter_rows(row_block, placing, seq_count):
    head_count, row_count, features = row_block.shape
    picked = jnp.einsum(
        "hri,hif->hrf", placing, row_block, preferred_element_type=jnp.float32
    ).astype(jnp.bfloat16)
    return picked.reshape(head_count, seq_count, row_count // seq_count * features).transpose(
        1, 0, 2
    )


def collect_rows(packed, placing, features):
    seq_count, head_count, flat_width = packed.shape
    row_block = packed.transpose(1, 0, 2).reshape(
        head_count, seq_count * flat_width // features, features
    )
    return jnp.einsum(
        "hri,hrf->hif", placing, row_block, preferred_element_type=jnp.float32
    ).astype(jnp.bfloat16)


def cluster_scores(queries, keys_in, segment_ids, score_scale):
    scores = (
        jnp.einsum("nqd,nkd->nqk", queries, keys_in, preferred_element_type=jnp.float32)
        * score_scale
    )
    allowed = segment_ids[:, :, None] == segment_ids[:, None, :]
    return (scores, allowed, jnp.where(allowed, scores, NEGATIVE))


def cluster_forward(queries, keys_in, values, segment_ids, score_scale):
    scores, allowed, masked = cluster_scores(queries, keys_in, segment_ids, score_scale)
    highest = jnp.max(masked, axis=-1, keepdims=True)
    raised = jnp.exp(masked - highest)
    totals = jnp.sum(raised, axis=-1, keepdims=True)
    weights = raised / totals
    attended = jnp.einsum(
        "nqk,nkd->nqd", weights.astype(jnp.bfloat16), values, preferred_element_type=jnp.float32
    ).astype(jnp.bfloat16)
    log_total = highest[:, :, 0] + jnp.log(totals[:, :, 0])
    entropy = log_total - jnp.sum(weights * jnp.where(allowed, scores, 0.0), axis=-1)
    occupied = jnp.sum(allowed.astype(jnp.float32), axis=-1)
    return (attended, log_total, entropy, occupied)


def cluster_backward(queries, keys_in, values, segment_ids, log_total, grad_out, score_scale):
    masked = cluster_scores(queries, keys_in, segment_ids, score_scale)[2]
    weights = jnp.exp(masked - log_total[:, :, None])
    weight_grads = jnp.einsum("nqd,nkd->nqk", grad_out, values, preferred_element_type=jnp.float32)
    value_grads = jnp.einsum(
        "nqk,nqd->nkd", weights.astype(jnp.bfloat16), grad_out, preferred_element_type=jnp.float32
    )
    score_grads = (
        weights * (weight_grads - jnp.sum(weights * weight_grads, axis=-1, keepdims=True))
    ).astype(jnp.bfloat16)
    query_grads = (
        jnp.einsum("nqk,nkd->nqd", score_grads, keys_in, preferred_element_type=jnp.float32)
        * score_scale
    )
    key_grads = (
        jnp.einsum("nqk,nqd->nkd", score_grads, queries, preferred_element_type=jnp.float32)
        * score_scale
    )
    return jnp.stack([query_grads, key_grads, value_grads], axis=2).astype(jnp.bfloat16)


MESH = pl.DeviceIdType.MESH


UNROLL = 8
PIECES = 4
FIRST = 1


def half_roll(block):
    return jnp.concatenate([block[:, 64:], block[:, :64]], axis=1)


def lanes(shape):
    return lax.broadcasted_iota(jnp.int32, shape, len(shape) - 1)


def bits(value, flip):
    return value + flip - 2 * value * flip


def coordinates():
    s, r = lax.axis_index("seq"), lax.axis_index("rep")
    return s // 4, (s // 2) % 2, s % 2, r // 2, r % 2


def device(zh, zl, x, y, c):
    return (4 * zh + 2 * zl + x, 2 * y + c)


def greet(peers):
    barrier = pltpu.get_barrier_semaphore()
    for peer in peers:
        pl.semaphore_signal(barrier, inc=1, device_id=peer, device_id_type=MESH)
    pl.semaphore_wait(barrier, len(peers))


def remote(src, dst, sems, index, peer):
    return pltpu.make_async_remote_copy(
        src_ref=src,
        dst_ref=dst,
        send_sem=sems[0].at[index],
        recv_sem=sems[1].at[index],
        device_id=peer,
        device_id_type=MESH,
    )


def dot(left, right, left_dim=1, right_dim=0):
    return lax.dot_general(
        left,
        right,
        (((left_dim,), (right_dim,)), ((), ())),
        preferred_element_type=jnp.float32,
    )


def hot(condition):
    return jnp.where(condition, 1.0, 0.0).astype(jnp.bfloat16)


def build_gather(order_ref, row, start, count, into):
    tokens = into.shape[1]

    def one(k, carry):
        at = pl.multiple_of(k * 128, 128)
        ids = order_ref[row : row + 1, pl.ds(pl.multiple_of(start + at, 128), 128)]
        column = jnp.broadcast_to(ids.astype(jnp.float32), (128, 128)).T
        lane = lanes((128, 128)).astype(jnp.float32)
        for t in range(tokens // 128):
            into[pl.ds(at, 128), t * 128 : (t + 1) * 128] = hot(column == lane + 128.0 * t)
        return carry

    lax.fori_loop(0, count // 128, one, 0)


def build_scatter(order_ref, half, first_token, into):
    group = order_ref.shape[1]

    def one(k, carry):
        at = pl.multiple_of(k * 128, 128)
        token = lax.broadcasted_iota(jnp.int32, (128, 128), 0) + (first_token + at)
        for p in range(into.shape[1] // 128):
            row, start = (0, 128 * p) if 128 * p < group else (1, half + 128 * p - group)
            ids = order_ref[row : row + 1, pl.ds(pl.multiple_of(start, 128), 128)]
            into[pl.ds(at, 128), 128 * p : 128 * (p + 1)] = hot(ids == token)
        return carry

    lax.fori_loop(0, into.shape[0] // 128, one, 0)


def select_head(slab, half, place):
    return jnp.where(half == place, slab, half_roll(slab))


def join(low_lanes, high_lanes):
    return jnp.where(lanes(low_lanes.shape) < 64, low_lanes, high_lanes)


def pick_columns(pairs, j, c):
    (q_one, q_two), (k_one, k_two), (v_one, v_two) = pairs
    zero = jnp.zeros_like(q_one)
    q1, v1, k1 = select_head(q_one, c, 0), select_head(v_one, c, 1), select_head(k_one, c, 0)
    v2, q2, k2 = (
        select_head(v_two, j % 2, 0),
        select_head(q_two, j % 2, 1),
        select_head(k_two, j % 2, 1),
    )
    return join(q1, v1), join(k1, zero), join(v2, q2), join(zero, k2)


def normalize(hidden):
    centre = hidden - jnp.mean(hidden, axis=1, keepdims=True)
    root_inverse = lax.rsqrt(jnp.mean(centre * centre, axis=1, keepdims=True) + EPSILON)
    return centre * root_inverse, root_inverse


def normalize_back(scaled, normed, root_inverse):
    return root_inverse * (
        scaled
        - jnp.mean(scaled, axis=1, keepdims=True)
        - normed * jnp.mean(scaled * normed, axis=1, keepdims=True)
    )


def forward_kernel(
    tokens_ref,
    cot_ref,
    seg_ref,
    orders_ref,
    owners_ref,
    query_bias_ref,
    value_bias_ref,
    out_bias_ref,
    first_gain_ref,
    first_shift_ref,
    outer_bias_ref,
    second_gain_ref,
    second_shift_ref,
    inner_bias_ref,
    wq_hbm,
    wk_hbm,
    wv_hbm,
    out_w_hbm,
    inner_w_hbm,
    outer_w_hbm,
    wsel_hbm,
    order_hbm,
    stats_hbm,
    x_hbm,
    sorted_hbm,
    prob_hbm,
    att_hbm,
    low_hbm,
    act_hbm,
    output_hbm,
    dsecond_hbm,
    dinner_hbm,
    delta_hbm,
    dbranch_hbm,
    vec_hbm,
    datt_hbm,
    wsel_ref,
    order_ref,
    stats_ref,
    x_all,
    sorted_ref,
    prob_ref,
    att_ref,
    low_ref,
    act_ref,
    output_ref,
    dsecond_ref,
    dinner_ref,
    delta_ref,
    dbranch_ref,
    vec_out,
    datt_ref,
    cot_my,
    weights,
    orders_in,
    owners_in,
    owner_pad,
    seg_src,
    seg_all,
    bias_rows,
    bias_sel,
    tok,
    gather,
    scatter,
    att_sorted,
    att_send,
    att_in,
    ent_ref,
    cnt_ref,
    swap_send,
    swap_recv,
    ring_send,
    ring_recv,
    seg_send,
    seg_recv,
    back_send,
    back_recv,
    local_sem,
    out_w,
    inner_w,
    outer_w,
    slope,
    total,
    normed_ref,
    bias_ref,
    load_sem,
    store_sem,
):
    zh, zl, x, y, c = coordinates()
    j = 2 * zl + x
    p = 4 * c + j
    block, width = tokens_ref.shape
    group = 8 * block
    scale = 0.125
    swap = (swap_send, swap_recv)
    ring = (ring_send, ring_recv)
    seg_sems = (seg_send, seg_recv)
    back = (back_send, back_recv)

    def member(flip):
        fc, fz, fx = flip // 4, (flip // 2) % 2, flip % 2
        mc, mz, mx = bits(c, fc), bits(zl, fz), bits(x, fx)
        return device(zh, mz, mx, y, mc), 4 * mc + 2 * mz + mx

    swap_peer = device(1 - zh, zl, x, y, 1 - c)
    peers = [member(flip)[0] for flip in range(1, 8)]
    sibling = peers[3]
    over_x, over_z = peers[0], peers[1]
    matched = c == zh

    slabs = [
        pltpu.make_async_copy(
            src.at[:, pl.ds(pl.multiple_of(index * 128, 128), 128)],
            weights.at[i, slot],
            local_sem.at[3 * slot + i],
        )
        for i, src in enumerate((wq_hbm, wk_hbm, wv_hbm))
        for slot, index in enumerate((j, 4 + j // 2))
    ]
    for copy in slabs:
        copy.start()
    greet(peers + [swap_peer])
    width_inner = inner_w.shape[1]
    dense_tile = 2 * width
    parts = [slice(dense_tile * t, dense_tile * (t + 1)) for t in range(width_inner // dense_tile)]
    loads = [pltpu.make_async_copy(out_w_hbm, out_w, load_sem.at[0])]
    for t, at in enumerate(parts):
        loads.append(
            pltpu.make_async_copy(inner_w_hbm.at[:, at], inner_w.at[:, at], load_sem.at[1 + 2 * t])
        )
        loads.append(pltpu.make_async_copy(outer_w_hbm.at[at], outer_w.at[at], load_sem.at[2 + 2 * t]))
    kept = {
        "wsel": (wsel_ref, wsel_hbm),
        "order": (order_ref, order_hbm),
        "stats": (stats_ref, stats_hbm),
        "x": (x_all, x_hbm),
        "sorted": (sorted_ref, sorted_hbm),
        "prob": (prob_ref, prob_hbm),
        "att": (att_ref, att_hbm),
        "low": (low_ref, low_hbm),
        "act": (act_ref, act_hbm),
        "output": (output_ref, output_hbm),
        "dsecond": (dsecond_ref, dsecond_hbm),
        "dinner": (dinner_ref, dinner_hbm),
        "delta": (delta_ref, delta_hbm),
        "dbranch": (dbranch_ref, dbranch_hbm),
        "vec": (vec_out, vec_hbm),
        "datt": (datt_ref, datt_hbm),
    }
    stores = {
        name: pltpu.make_async_copy(src, dst, store_sem.at[i]) for i, (name, (src, dst)) in enumerate(kept.items())
    }

    seg_src[...] = jnp.broadcast_to(seg_ref[...], seg_src.shape)
    table_copies = [
        remote(orders_ref, orders_in, swap, 0, sibling),
        remote(owners_ref, owners_in, swap, 1, sibling),
    ]
    for copy in table_copies:
        copy.start()
    p_swap = 4 * (1 - c) + j
    chunks = PIECES
    halves = [pl.ds(i * (block // chunks), block // chunks) for i in range(chunks)]
    pairs = [(tokens_ref.at[at], x_all.at[p_swap, at], x_all.at[p, at]) for at in halves]
    pairs.insert(0, (seg_src, seg_all.at[p_swap], seg_all.at[p]))
    pairs.append((cot_ref, cot_my, cot_my))
    swaps = [remote(src, dst, swap, 2 + i, swap_peer) for i, (src, dst, _) in enumerate(pairs)]
    locals_ = [
        pltpu.make_async_copy(src, own, swap_recv.at[4 + chunks + i]) for i, (src, _, own) in enumerate(pairs)
    ]

    px, pz, pd = member(1)[1], member(2)[1], member(3)[1]

    def share_block(index, position, i, peer):
        view = x_all.at[position, halves[i]]
        return remote(view, view, ring, index, peer)

    every = range(chunks)
    own_to_x = [share_block(i, p, i, over_x) for i in every]
    own_to_z = [share_block(chunks + i, p, i, over_z) for i in every]
    own_to_s = [share_block(2 * chunks + i, p, i, sibling) for i in every]
    x_to_s = [share_block(3 * chunks + i, px, i, sibling) for i in every]
    z_to_s = [share_block(4 * chunks + i, pz, i, sibling) for i in every]
    d_to_s = [share_block(5 * chunks + i, pd, i, sibling) for i in every]
    relays = [
        share_block(6 * chunks + i, px, i, over_z) if i < FIRST else share_block(6 * chunks + i, pz, i, over_x)
        for i in every
    ]
    seg_copies = [
        remote(seg_all.at[p], seg_all.at[p], seg_sems, flip - 1, peers[flip - 1]) for flip in range(1, 8)
    ]
    opposite = jnp.logical_not(matched)

    def own_half(i, arrivals):
        arrivals[1 + i].wait()
        own_to_x[i].start()
        own_to_z[i].start()
        own_to_s[i].start()

    def segments_out(arrivals):
        arrivals[0].wait()
        for copy in seg_copies:
            copy.start()

    def relay(i):
        own_to_x[i].wait()
        own_to_z[i].wait()
        relays[i].start()
        x_to_s[i].start()
        z_to_s[i].start()

    def relay_end(i):
        relays[i].wait()
        d_to_s[i].start()

    def wait_sibling():
        for copy in own_to_s + x_to_s + z_to_s + d_to_s:
            copy.wait_recv()

    @pl.when(matched)
    def _():
        for copy in locals_:
            copy.start()
        segments_out(locals_)
        for i in every:
            own_half(i, locals_)

    @pl.when(opposite)
    def _():
        for copy in swaps[: 1 + chunks]:
            copy.start()

    for copy in slabs:
        copy.wait()
    tiles = pick_columns([[weights[i, slot].astype(jnp.float32) for slot in range(2)] for i in range(3)], j, c)
    for i, tile in enumerate(tiles):
        wsel_ref[:, 128 * i : 128 * (i + 1)] = tile.astype(jnp.bfloat16)
    for i, ref in enumerate((query_bias_ref, None, value_bias_ref)):
        row = jnp.zeros((1, width), jnp.float32) if ref is None else ref[...].astype(jnp.float32).reshape(1, width)
        bias_rows[i : i + 1, :] = row
    bias_pairs = [
        [bias_rows[i : i + 1, pl.ds(pl.multiple_of(index * 128, 128), 128)] for index in (j, 4 + j // 2)]
        for i in range(3)
    ]
    for i, tile in enumerate(pick_columns(bias_pairs, j, c)):
        bias_sel[0:1, 128 * i : 128 * (i + 1)] = tile

    for copy in table_copies:
        copy.wait()
    h1, h2 = 2 * j + c, 8 + j
    for i, h in enumerate((h1, h2)):
        order_ref[i : i + 1, :] = jnp.where(matched, orders_ref[h], orders_in[h])
    half = 1024 * c

    build_gather(order_ref, 0, 0, group, gather.at[pl.ds(0, group)])

    @pl.when(matched)
    def _():
        for i in every:
            relay(i)

    @pl.when(opposite)
    def _():
        segments_out(swaps)
        for i in range(chunks // 2):
            own_half(i, swaps)

    build_gather(order_ref, 1, half, group // 2, gather.at[pl.ds(group, group // 2)])

    @pl.when(matched)
    def _():
        for i in every:
            relay_end(i)

    @pl.when(opposite)
    def _():
        for i in range(chunks // 2, chunks):
            own_half(i, swaps)
        for i in range(chunks // 2):
            relay(i)

    def project(position):
        at = pl.ds(pl.multiple_of(position * block, block), block)
        out = dot(x_all[position], wsel_ref[...]) + bias_sel[0:1, :]
        ids = seg_all[position, 0:1, :].astype(jnp.float32)
        columns = [
            jnp.broadcast_to(ids[:, 128 * i : 128 * (i + 1)], (128, 128)).T for i in range(block // 128)
        ]
        lane = lanes((block, 128))
        seg_hot = hot(jnp.concatenate(columns, axis=0) == (lane % 64).astype(jnp.float32))
        low = out.astype(jnp.bfloat16)
        tok[at, 0:128] = low[:, 0:128]
        tok[at, 128:256] = jnp.where(lane < 64, low[:, 128:256], seg_hot)
        tok[at, 256:384] = low[:, 256:384]
        tok[at, 384:512] = jnp.where(lane < 64, seg_hot, low[:, 384:512])

    step = 512
    early, late = group // 2 * zh, group // 2 * (1 - zh)

    def gather_rows(start, add):
        tokens = pl.ds(pl.multiple_of(start, group // 2), group // 2)

        def one(first, columns):
            def body(k, carry):
                at = pl.ds(pl.multiple_of(k * step, step), step)
                rows = dot(gather[at, tokens], tok[tokens, columns])
                if add:
                    sorted_ref[at, :] = (rows + sorted_ref[at, :].astype(jnp.float32)).astype(jnp.bfloat16)
                else:
                    sorted_ref[at, :] = rows.astype(jnp.bfloat16)
                return carry

            return body

        lax.fori_loop(0, group // step, one(0, pl.ds(0, 256)), 0)
        lax.fori_loop(group // step, group * 3 // 2 // step, one(1, pl.ds(256, 256)), 0)

    for copy in seg_copies:
        copy.wait()
    pl.when(opposite)(wait_sibling)
    for k in range(4):
        project(4 * zh + k)

    @pl.when(opposite)
    def _():
        for i in range(chunks // 2, chunks):
            relay(i)
        for i in range(chunks // 2):
            relay_end(i)

    gather_rows(early, False)

    @pl.when(opposite)
    def _():
        for i in range(chunks // 2, chunks):
            relay_end(i)

    def build_block(i, carry):
        build_scatter(order_ref, half, member(7 - i)[1] * block, scatter.at[i % 4])
        return carry

    lax.fori_loop(0, 4, build_block, 0)
    pl.when(matched)(wait_sibling)
    for k in range(4):
        project(4 * (1 - zh) + k)
    for name in ("x", "wsel", "order"):
        stores[name].start()
    for copy in loads:
        copy.start()


    @pl.when(opposite)
    def _():
        swaps[1 + chunks].start()

    gather_rows(late, True)
    def attend(first_lanes):
        def one(i, carry):
            at = pl.ds(pl.multiple_of(i * 128, 128), 128)
            tile_zero, tile_one = sorted_ref[at, 0:128], sorted_ref[at, 128:256]
            low_lanes = lanes((128, 128)) < 64
            query_lanes = low_lanes if first_lanes else jnp.logical_not(low_lanes)
            queries = jnp.where(query_lanes, tile_zero, jnp.zeros_like(tile_zero))
            ids = jnp.where(query_lanes, jnp.zeros_like(tile_one), tile_one)
            both = dot(jnp.concatenate([queries, ids], axis=0), tile_one, 1, 1)
            scores, allowed = both[:128] * scale, both[128:]
            masked = jnp.where(allowed > 0.5, scores, NEGATIVE)
            highest = jnp.max(masked, axis=1, keepdims=True)
            raised = jnp.exp(masked - highest)
            totals = jnp.sum(raised, axis=1, keepdims=True)
            weights = raised * (1.0 / totals)
            prob_ref[at, :] = weights
            mixed = dot(weights.astype(jnp.bfloat16), tile_zero)
            att_sorted[at, :] = jnp.where(query_lanes, 0.0, mixed).astype(jnp.bfloat16)
            log_total = highest + jnp.log(totals)
            entropy = jnp.where(lanes((128, 128)) == 0, log_total, 0.0) - weights * masked
            ent_ref[pl.ds(i, 1), :] = jnp.sum(entropy, axis=0, keepdims=True)
            cnt_ref[pl.ds(i, 1), :] = jnp.sum(allowed, axis=0, keepdims=True)
            return carry

        return one

    lax.fori_loop(0, 16, attend(True), 0, unroll=UNROLL)
    lax.fori_loop(16, 24, attend(False), 0, unroll=UNROLL)
    stores["sorted"].start()
    stores["prob"].start()

    def send_back(i, carry):
        flip = 7 - i
        peer = member(flip)[0]
        att_send[flip] = dot(scatter[i % 4], att_sorted[...]).astype(jnp.bfloat16)

        @pl.when(i < 7)
        def _():
            remote(att_send.at[flip], att_in.at[p], back, flip, peer).start()

        @pl.when(i < 4)
        def _():
            build_block(i + 4, 0)

        return carry

    lax.fori_loop(0, 8, send_back, 0)
    back_copies = [remote(att_send.at[flip], att_in.at[p], back, flip, peers[flip - 1]) for flip in range(1, 8)]
    att_in[p] = att_send[0]

    stats_ref[...] = jnp.zeros_like(stats_ref)
    owner_pad[...] = jnp.full_like(owner_pad, -1.0)
    clusters = owners_ref.shape[2]
    for h, first, size, skip in ((h1, 0, clusters, 0), (h2, clusters, clusters // 2, c)):
        ids = jnp.where(matched, owners_ref[h], owners_in[h])
        owner_pad[0:1, 0:clusters] = ids.astype(jnp.float32)
        column = jnp.broadcast_to(owner_pad[0:1, :], (128, 128)).T
        column = jnp.where(skip == 1, column[clusters // 2 : clusters // 2 + size], column[0:size])
        owned = jnp.where(column == lanes((size, 128)).astype(jnp.float32), 1.0, 0.0)
        for kind, (lane_sums, divisor) in enumerate(((ent_ref, 4.0 * block), (cnt_ref, 4.0 * block * 128))):
            sums = jnp.sum(lane_sums[first : first + size, :], axis=1, keepdims=True) / divisor
            stats_ref[kind, pl.ds(h, 1), :] = jnp.sum(sums * owned, axis=0, keepdims=True)

    stores["stats"].start()
    bias_ref[0:1, :] = inner_bias_ref[...].astype(jnp.float32).reshape(1, width_inner)
    out_bias, first_gain, first_shift, outer_bias, second_gain, second_shift = (
        ref[...].astype(jnp.float32).reshape(1, width)
        for ref in (
            out_bias_ref,
            first_gain_ref,
            first_shift_ref,
            outer_bias_ref,
            second_gain_ref,
            second_shift_ref,
        )
    )
    for copy in back_copies:
        copy.wait()
    for pair in range(4):
        even, odd = att_in[pair], att_in[4 + pair]
        att_ref[:, 128 * pair : 128 * (pair + 1)] = join(half_roll(even), odd)
    for pair in range(2):
        low_half = att_in[2 * pair] + att_in[4 + 2 * pair]
        high_half = att_in[2 * pair + 1] + att_in[5 + 2 * pair]
        att_ref[:, 512 + 128 * pair : 640 + 128 * pair] = join(low_half, half_roll(high_half))
    stores["att"].start()

    loads[0].wait()
    branch = dot(att_ref[...], out_w[...]) + out_bias
    normed, root_one = normalize(x_all[p].astype(jnp.float32) + branch)
    first = normed * first_gain + first_shift
    normed_ref[...] = normed
    low_ref[...] = first.astype(jnp.bfloat16)
    stores["low"].start()
    total[...] = first + outer_bias
    for copy in loads[1:]:
        copy.wait()

    def dense_forward(t, carry):
        at = pl.ds(pl.multiple_of(t * dense_tile, dense_tile), dense_tile)
        inner = dot(low_ref[...], inner_w[:, at]) + bias_ref[0:1, at]
        cumulative = 0.5 + 0.5 * lax.erf(inner * (0.5**0.5))
        density = jnp.exp(-0.5 * inner * inner) * 0.3989422804014327
        slope[:, at] = cumulative + inner * density
        act = (inner * cumulative).astype(jnp.bfloat16)
        act_ref[:, at] = act
        total[...] += dot(act, outer_w[at, :])
        return carry

    lax.fori_loop(0, len(parts), dense_forward, 0)
    stores["act"].start()

    @pl.when(matched)
    def _():
        locals_[1 + chunks].wait()

    @pl.when(opposite)
    def _():
        swaps[1 + chunks].wait()

    normed_two, root_two = normalize(total[...])
    output_ref[...] = (normed_two * second_gain + second_shift).astype(jnp.bfloat16)
    stores["output"].start()
    upstream = cot_my[...].astype(jnp.float32)
    vec_out[4:5, :] = jnp.sum(upstream * normed_two, axis=0, keepdims=True)
    vec_out[5:6, :] = jnp.sum(upstream, axis=0, keepdims=True)
    delta_two = normalize_back(upstream * second_gain, normed_two, root_two)
    low_two = delta_two.astype(jnp.bfloat16)
    dsecond_ref[...] = low_two
    stores["dsecond"].start()
    vec_out[3:4, :] = jnp.sum(low_two.astype(jnp.float32), axis=0, keepdims=True)
    total[...] = delta_two

    def dense_back(t, carry):
        at = pl.ds(pl.multiple_of(t * dense_tile, dense_tile), dense_tile)
        dact = dot(dsecond_ref[...], outer_w[at, :], 1, 1)
        dinner = (dact * slope[:, at]).astype(jnp.bfloat16)
        dinner_ref[:, at] = dinner
        bias_ref[0:1, at] = jnp.sum(dinner.astype(jnp.float32), axis=0, keepdims=True)
        total[...] += dot(dinner, inner_w[:, at], 1, 1)
        return carry

    lax.fori_loop(0, len(parts), dense_back, 0)
    stores["dinner"].start()
    for i in range(width_inner // width):
        vec_out[6 + i : 7 + i, :] = bias_ref[0:1, width * i : width * (i + 1)]
    delta_first = total[...]
    normed = normed_ref[...]
    vec_out[1:2, :] = jnp.sum(delta_first * normed, axis=0, keepdims=True)
    vec_out[2:3, :] = jnp.sum(delta_first, axis=0, keepdims=True)
    delta_one = normalize_back(delta_first * first_gain, normed, root_one)
    delta_ref[...] = delta_one
    stores["delta"].start()
    low_one = delta_one.astype(jnp.bfloat16)
    dbranch_ref[...] = low_one
    stores["dbranch"].start()
    vec_out[0:1, :] = jnp.sum(low_one.astype(jnp.float32), axis=0, keepdims=True)
    vec_out[10:16, :] = jnp.zeros((6, width), jnp.float32)
    stores["vec"].start()
    datt_ref[...] = dot(dbranch_ref[...], out_w[...], 1, 1).astype(jnp.bfloat16)
    stores["datt"].start()
    for copy in stores.values():
        copy.wait()
    for copy in own_to_s + x_to_s + z_to_s + d_to_s:
        copy.wait_send()


def forward_layer(tokens, cotangent, segments, orders, owners, vectors, weights):
    block, width = tokens.shape
    inner_width = weights[4].shape[1]
    group = 8 * block
    low, full = jnp.bfloat16, jnp.float32
    vmem = pl.BlockSpec(memory_space=pltpu.VMEM)
    hbm = pl.BlockSpec(memory_space=pl.ANY)
    dma = pltpu.SemaphoreType.DMA
    rows = group * 3 // 2
    kept = [
        ((width, 512), low),
        ((8, group), jnp.int32),
        ((2, 16, 128), full),
        ((8, block, width), low),
        ((rows, 256), low),
        ((rows, 128), full),
        ((block, width), low),
        ((block, width), low),
        ((block, inner_width), low),
        ((block, width), low),
        ((block, width), low),
        ((block, inner_width), low),
        ((block, width), full),
        ((block, width), low),
        ((16, width), full),
        ((block, width), low),
    ]
    return pl.pallas_call(
        forward_kernel,
        out_shape=[jax.ShapeDtypeStruct(*one) for one in kept],
        in_specs=[vmem] * 14 + [hbm] * 6,
        out_specs=[hbm] * len(kept),
        scratch_shapes=[pltpu.VMEM(*one) for one in kept]
        + [
            pltpu.VMEM((block, width), low),
            pltpu.VMEM((3, 2, width, 128), low),
            pltpu.VMEM(orders.shape, jnp.int32),
            pltpu.VMEM(owners.shape, jnp.int32),
            pltpu.VMEM((8, 128), full),
            pltpu.VMEM((8, block), jnp.int32),
            pltpu.VMEM((8, 8, block), jnp.int32),
            pltpu.VMEM((8, width), full),
            pltpu.VMEM((8, 512), full),
            pltpu.VMEM((group, 512), low),
            pltpu.VMEM((rows, group), low),
            pltpu.VMEM((4, block, rows), low),
            pltpu.VMEM((rows, 128), low),
            pltpu.VMEM((8, block, 128), low),
            pltpu.VMEM((8, block, 128), low),
            pltpu.VMEM((24, 128), full),
            pltpu.VMEM((24, 128), full),
            dma((2 * PIECES + 6,)),
            dma((2 * PIECES + 6,)),
            dma((7 * PIECES,)),
            dma((7 * PIECES,)),
            dma((7,)),
            dma((7,)),
            dma((8,)),
            dma((8,)),
            dma((6,)),
            pltpu.VMEM(weights[3].shape, low),
            pltpu.VMEM(weights[4].shape, low),
            pltpu.VMEM(weights[5].shape, low),
            pltpu.VMEM((block, inner_width), full),
            pltpu.VMEM((block, width), full),
            pltpu.VMEM((block, width), full),
            pltpu.VMEM((8, inner_width), full),
            dma((1 + inner_width // width,)),
            dma((len(kept),)),
        ],
        compiler_params=pltpu.CompilerParams(
            collective_id=1, has_side_effects=True, vmem_limit_bytes=62 << 20
        ),
        name="forward_layer",
    )(tokens, cotangent, segments, orders, owners, *vectors, *weights)


def rows_of(start, q, size):
    return pl.ds(pl.multiple_of(start * q, 16), size * q)


def add_into(count, target, other):
    def one(i, carry):
        target(i)[...] = (
            target(i)[...].astype(jnp.float32) + other(i)[...].astype(jnp.float32)
        ).astype(jnp.bfloat16)
        return carry

    lax.fori_loop(0, count, one, 0)


def reduce_steps(parts, g_ref, f_ref, f_hbm, buffers, sems, out_sem):
    core_in, a_one, a_two, a_three, a_four, b_one, b_two, b_three, b_four = buffers
    zh, zl, x, y, c = coordinates()
    q = g_ref.shape[3] // 8
    width = g_ref.shape[4] // parts
    over_c, over_y = device(zh, zl, x, y, 1 - c), device(zh, zl, x, 1 - y, c)
    over_x, over_zl = device(zh, zl, 1 - x, y, c), device(zh, 1 - zl, x, y, c)
    over_zh = device(1 - zh, zl, x, y, c)
    flying, outward = {}, []

    def send(name, k, src, dst, peer):
        copy = remote(src, dst, (sems[0].at[name], sems[1].at[name]), k, peer)
        copy.start()
        flying[name, k] = copy

    def arrive(name, k):
        flying.pop((name, k)).wait()

    def step(stage, k):
        cols = pl.ds(k * width, width)
        if stage == "0":
            send(
                0, k, g_ref.at[:, :, :, rows_of(4 * (1 - c), q, 4), cols], core_in.at[:, :, :, :, cols], over_c
            )
        if stage == "1":
            arrive(0, k)
            add_into(
                8,
                lambda i: core_in.at[i // 4, (i // 2) % 2, i % 2, :, cols],
                lambda i: g_ref.at[i // 4, (i // 2) % 2, i % 2, rows_of(4 * c, q, 4), cols],
            )
            send(1, k, core_in.at[:, :, 1 - x, pl.ds(0, 2 * q), cols], a_one.at[:, :, :, cols], over_x)
            send(2, k, core_in.at[:, :, :, rows_of(3 - y, q, 1), cols], b_one.at[:, :, :, :, cols], over_y)
        if stage == "2a":
            arrive(1, k)
            add_into(
                4,
                lambda i: a_one.at[i // 2, i % 2, :, cols],
                lambda i: core_in.at[i // 2, i % 2, x, pl.ds(0, 2 * q), cols],
            )
            send(3, k, a_one.at[:, 1 - zl, :, cols], a_two.at[:, :, cols], over_zl)
        if stage == "3a":
            arrive(3, k)
            add_into(2, lambda i: a_two.at[i, :, cols], lambda i: a_one.at[i, zl, :, cols])
            send(4, k, a_two.at[1 - zh, :, cols], a_three.at[:, cols], over_zh)
        if stage == "4a":
            arrive(4, k)
            add_into(1, lambda i: a_three.at[:, cols], lambda i: a_two.at[zh, :, cols])
            send(5, k, a_three.at[:, cols], a_four.at[:, cols], over_y)
        if stage == "2b":
            arrive(2, k)
            add_into(
                8,
                lambda i: b_one.at[i // 4, (i // 2) % 2, i % 2, :, cols],
                lambda i: core_in.at[i // 4, (i // 2) % 2, i % 2, rows_of(2 + y, q, 1), cols],
            )
            send(6, k, b_one.at[:, :, 1 - x, :, cols], b_two.at[:, :, :, cols], over_x)
        if stage == "3":
            arrive(6, k)
            add_into(
                4,
                lambda i: b_two.at[i // 2, i % 2, :, cols],
                lambda i: b_one.at[i // 2, i % 2, x, :, cols],
            )
            send(7, k, b_two.at[:, 1 - zl, :, cols], b_three.at[:, :, cols], over_zl)
        if stage == "4":
            arrive(7, k)
            add_into(2, lambda i: b_three.at[i, :, cols], lambda i: b_two.at[i, zl, :, cols])
            send(8, k, b_three.at[1 - zh, :, cols], b_four.at[:, cols], over_zh)
        if stage == "5":
            arrive(8, k)
            f_ref[c, 1, y, :, cols] = (
                b_four[:, cols].astype(jnp.float32) + b_three[zh, :, cols].astype(jnp.float32)
            ).astype(jnp.bfloat16)
            own_rows = f_ref.at[c, 1, y, :, cols]
            send(9, k, own_rows, own_rows, over_y)
        if stage == "6":
            arrive(5, k)
            for half in range(2):
                at = pl.ds(half * q, q)
                f_ref[c, 0, half, :, cols] = (
                    a_three[at, cols].astype(jnp.float32) + a_four[at, cols].astype(jnp.float32)
                ).astype(jnp.bfloat16)
            arrive(9, k)
            both = f_ref.at[c, :, :, :, cols]
            send(10, k, both, both, over_c)
        if stage == "7":
            arrive(10, k)
            copy = pltpu.make_async_copy(f_ref.at[:, :, :, :, cols], f_hbm.at[:, :, :, :, cols], out_sem.at[k])
            copy.start()
            outward.append(copy)

    return step, outward


BACKWARD_ORDER = (
    "begin",
    "home0",
    "datt",
    "g1",
    "S0",
    "g2",
    "bld:0",
    "r1:0",
    "st:0",
    "bld:1",
    "take:0",
    "r1:1",
    "r1:2",
    "hE0",
    "bld:2",
    "take:2",
    "r1:3",
    "r1:4",
    "take:1",
    "r2b:0",
    "r1:5",
    "st:1",
    "r2a:0",
    "bld:4",
    "take:4",
    "bld:3",
    "r2b:1",
    "r2a:1",
    "take:3",
    "bld:5",
    "take:5",
    "at:1",
    "at:0",
    "r2a:2",
    "r2b:2",
    "at:2",
    "r2a:3",
    "r3a:0",
    "pl",
    "r3a:2",
    "r2b:4",
    "r2a:4",
    "r3a:1",
    "r2b:3",
    "r3a:3",
    "r4a:0",
    "r3:0",
    "ph",
    "r4a:2",
    "st:2",
    "r3a:4",
    "r2b:5",
    "ab:0",
    "dw",
    "r4a:3",
    "st:3",
    "r4:0",
    "r3:2",
    "r3:1",
    "r2a:5",
    "ab:1",
    "r4a:4",
    "r4a:1",
    "st:4",
    "r3:4",
    "hb:0",
    "r5:0",
    "r4:2",
    "r3:3",
    "r4:1",
    "r3:5",
    "r3a:5",
    "da",
    "ha:0",
    "hb:1",
    "r4:4",
    "r5:2",
    "stE",
    "r6:0",
    "r4:3",
    "ha:1",
    "r5:1",
    "r6:2",
    "r7:0",
    "r4:5",
    "r6:1",
    "r7:2",
    "r4a:5",
    "r7:1",
    "wy",
    "hm:0",
    "r5:4",
    "r5:3",
    "hm:1",
    "r5:5",
    "wc",
    "r6:4",
    "r6:3",
    "hE:0",
    "r6:5",
    "wE",
    "r7:4",
    "r7:3",
    "r7:5",
    "hE:1",
)


def backward_kernel(
    parts,
    datt_hbm,
    order_hbm,
    out_my,
    stats_hbm,
    vec_hbm,
    att_hbm,
    dbranch_hbm,
    low_hbm,
    dsecond_hbm,
    act_hbm,
    dinner_hbm,
    sorted_hbm,
    prob_hbm,
    wsel_hbm,
    x_hbm,
    delta_hbm,
    out_home,
    grad_home,
    f_hbm,
    w_hbm,
    stats_out,
    datt_ref,
    att_ref,
    dbranch_ref,
    vec_ref,
    low_ref,
    dsecond_ref,
    act_ref,
    dinner_ref,
    order_ref,
    stats_ref,
    sorted_ref,
    prob_ref,
    wsel_ref,
    x_all,
    delta_ref,
    f_ref,
    w_all,
    g_ref,
    datt_send,
    datt_in,
    gather,
    gathered,
    dsorted,
    scatter,
    dqkv,
    part_send,
    part_in,
    total,
    a_in,
    b_in,
    a_two,
    b_two,
    grad_my,
    dw,
    dw_y,
    dw_in,
    dw_all,
    stats_buf,
    stats_in,
    core_in,
    r_a_one,
    r_a_two,
    r_a_three,
    r_a_four,
    r_b_one,
    r_b_two,
    r_b_three,
    r_b_four,
    datt_ssem,
    datt_rsem,
    part_ssem,
    part_rsem,
    swap_ssem,
    swap_rsem,
    dw_ssem,
    dw_rsem,
    stats_ssem,
    stats_rsem,
    red_ssem,
    red_rsem,
    load_sem,
    out_sem,
):
    zh, zl, x, y, c = coordinates()
    s = 4 * zh + 2 * zl + x
    j = 2 * zl + x
    p = 4 * c + j
    block, width = datt_ref.shape
    group = 8 * block
    scale = 0.125
    matched = c == zh
    datt_sems, part_sems = (datt_ssem, datt_rsem), (part_ssem, part_rsem)
    swap_sems, dw_sems, stats_sems = (swap_ssem, swap_rsem), (dw_ssem, dw_rsem), (stats_ssem, stats_rsem)

    def member(flip):
        fc, fz, fx = flip // 4, (flip // 2) % 2, flip % 2
        mc, mz, mx = bits(c, fc), bits(zl, fz), bits(x, fx)
        return device(zh, mz, mx, y, mc), mc, 2 * mz + mx

    peers = [member(flip)[0] for flip in range(1, 8)]
    sibling, over_x, over_z = peers[3], peers[0], peers[1]
    swap_peer = device(1 - zh, zl, x, y, 1 - c)
    over_y = device(zh, zl, x, 1 - y, c)
    across = [device(1 - zh, bits(zl, f // 2), bits(x, f % 2), y, c) for f in range(4)]
    everyone = peers + [swap_peer, over_y] + across
    barrier = pltpu.get_barrier_semaphore()
    for peer in everyone:
        pl.semaphore_signal(barrier, inc=1, device_id=peer, device_id_type=MESH)
    loads = [
        pltpu.make_async_copy(src, dst, load_sem.at[i])
        for i, (src, dst) in enumerate(
            (
                (datt_hbm, datt_ref),
                (att_hbm, att_ref),
                (dbranch_hbm, dbranch_ref),
                (vec_hbm, vec_ref),
                (low_hbm, low_ref),
                (dsecond_hbm, dsecond_ref),
                (act_hbm, act_ref),
                (dinner_hbm, dinner_ref),
                (order_hbm, order_ref),
                (stats_hbm, stats_ref),
                (sorted_hbm, sorted_ref),
                (prob_hbm, prob_ref),
                (wsel_hbm, wsel_ref),
                (x_hbm, x_all),
                (delta_hbm, delta_ref),
            )
        )
    ]
    for copy in loads:
        copy.start()

    def home_copy(src, dst, index, start):
        away = remote(src, dst, swap_sems, index, swap_peer)
        here = pltpu.make_async_copy(src, dst, swap_rsem.at[3 + index])

        @pl.when(matched)
        def _():
            here.start() if start else here.wait()

        @pl.when(jnp.logical_not(matched))
        def _():
            away.start() if start else away.wait()

    def tile(mc, mj):
        first = datt_ref[:, pl.ds(pl.multiple_of(mj * 128, 128), 128)]
        other = datt_ref[:, pl.ds(pl.multiple_of((4 + mj // 2) * 128, 128), 128)]
        return join(
            select_head(other.astype(jnp.float32), mj % 2, 0), select_head(first.astype(jnp.float32), mc, 1)
        ).astype(jnp.bfloat16)

    datt_copies = []

    def datt_tiles():
        loads[0].wait()
        for flip in range(1, 8):
            peer, mc, mj = member(flip)
            datt_send[flip] = tile(mc, mj)
            datt_copies.append(remote(datt_send.at[flip], datt_in.at[p], datt_sems, flip - 1, peer))
        datt_in[p] = tile(c, j)

    def datt_out():
        for flip in (3, 7, 1, 5, 2, 6, 4):
            datt_copies[flip - 1].start()

    stats_peers = (sibling, over_x, over_z, across[0], over_y)
    stats_copies = [
        remote(stats_buf.at[k], stats_in.at[k], stats_sems, k, peer) for k, peer in enumerate(stats_peers)
    ]

    def stats_step(k):
        if k == 0:
            loads[9].wait()
            stats_buf[0] = stats_ref[...]
        else:
            stats_copies[k - 1].wait()
            stats_buf[k] = stats_buf[k - 1] + stats_in[k - 1]
        if k < len(stats_peers):
            stats_copies[k].start()
        else:
            copy = pltpu.make_async_copy(stats_buf.at[k], stats_out, out_sem.at[parts])
            copy.start()
            outward.append(copy)

    share = width // 8
    q = g_ref.shape[3] // 8
    top = 4 * q

    def outer_grads():
        def one(d, carry):
            columns = pl.ds(pl.multiple_of(d * 4 * share, 128), 4 * share)
            g_ref[d // 4, (d // 2) % 2, d % 2, top : top + 4 * share, :] = dot(
                act_ref[:, columns], dsecond_ref[...], 0, 0
            ).astype(jnp.bfloat16)
            return carry

        lax.fori_loop(0, 8, one, 0)

    def inner_grads():
        def one(i, carry):
            z, n = i // 4, i % 4
            rows = pl.ds(pl.multiple_of(z * 4 * share, 128), 4 * share)
            columns = pl.ds(pl.multiple_of(n * width, 128), width)
            grads = dot(low_ref[:, rows], dinner_ref[:, columns], 0, 0).astype(jnp.bfloat16)
            for k in range(4):
                at = pl.ds(pl.multiple_of(n * share, 16), share)
                g_ref[z, k // 2, k % 2, at, :] = grads[share * k : share * (k + 1)]
            return carry

        lax.fori_loop(0, 8, one, 0)

    def out_grads():
        for copy in loads[1:4]:
            copy.wait()
        vectors = vec_ref[...].astype(jnp.bfloat16)
        for z in range(2):
            columns = slice(4 * share * z, 4 * share * (z + 1))
            grads = dot(att_ref[:, columns], dbranch_ref[...], 0, 0).astype(jnp.bfloat16)
            for k in range(4):
                rows = grads[share * k : share * (k + 1)]
                g_ref[z, k // 2, k % 2, 4 * share : 4 * share + share // 2, :] = rows[: share // 2]
                g_ref[z, k // 2, k % 2, 4 * share + share // 2 : top, :] = jnp.zeros_like(vectors)
                g_ref[z, k // 2, k % 2, top + 4 * share : top + 4 * share + share // 2, :] = rows[share // 2 :]
                g_ref[z, k // 2, k % 2, top + 4 * share + share // 2 :, :] = vectors

    def grads_first():
        for copy in loads[4:9]:
            copy.wait()
        pl.when(c == 0)(outer_grads)
        pl.when(c == 1)(inner_grads)

    def grads_second():
        pl.when(c == 0)(inner_grads)
        pl.when(c == 1)(outer_grads)

    reduction, outward = reduce_steps(
        parts,
        g_ref,
        f_ref,
        f_hbm,
        (core_in, r_a_one, r_a_two, r_a_three, r_a_four, r_b_one, r_b_two, r_b_three, r_b_four),
        (red_ssem, red_rsem),
        out_sem,
    )

    half = 1024 * c
    step = gather.shape[1]
    chunks = group * 3 // 2 // step

    def build(k):
        head, start = (0, k * step) if k * step < group else (1, half + k * step - group)
        build_gather(order_ref, head, start, step, gather.at[k % 2])

    arrivals = []

    def take(k):
        if not arrivals:
            for copy in datt_copies:
                copy.wait()
            arrivals.append(True)
        gathered[k * step : (k + 1) * step, :] = dot(
            gather[k % 2], datt_in[...].reshape(group, 128)
        ).astype(jnp.bfloat16)

    def attend_back(first_lanes):
        def one(i, carry):
            at = pl.ds(pl.multiple_of(i * 128, 128), 128)
            tile_zero, tile_one = sorted_ref[at, 0:128], sorted_ref[at, 128:256]
            low_lanes = lanes((128, 128)) < 64
            query_lanes = low_lanes if first_lanes else jnp.logical_not(low_lanes)
            weights = prob_ref[at, :]
            taken = gathered[at, :]
            taken = jnp.where(query_lanes, jnp.zeros_like(taken), taken)
            weight_grads = dot(taken, tile_zero, 1, 1)
            inside = jnp.sum(weights * weight_grads, axis=1, keepdims=True)
            score_grads = weights * (weight_grads - inside)
            low_grads = score_grads.astype(jnp.bfloat16)
            query_grads = dot(low_grads, tile_one) * scale
            key_grads = dot(low_grads, tile_zero, 0, 0) * scale
            value_grads = dot(weights.astype(jnp.bfloat16), taken, 0, 0)
            dsorted[at, 0:128] = jnp.where(query_lanes, query_grads, value_grads).astype(jnp.bfloat16)
            dsorted[at, 128:256] = jnp.where(query_lanes, key_grads, 0.0).astype(jnp.bfloat16)
            return carry

        return one

    loaded = []

    def attend_some(i):
        if not loaded:
            for copy in loads[10:]:
                copy.wait()
            loaded.append(True)
        lax.fori_loop(8 * i, 8 * i + 8, attend_back(i < 2), 0, unroll=4)

    def place(position):
        token = lax.broadcasted_iota(jnp.int32, (128, 128), 0) + position * block
        for t in range(block // 128):
            for head, start, count, base in ((0, 0, group, 0), (1, half, group // 2, group)):
                for k in range(count // 128):
                    ids = order_ref[head : head + 1, pl.ds(pl.multiple_of(start + 128 * k, 128), 128)]
                    scatter[128 * t : 128 * (t + 1), base + 128 * k : base + 128 * (k + 1)] = hot(
                        ids == token + 128 * t
                    )
        at = pl.ds(pl.multiple_of(position * block, block), block)
        dqkv[at, 0:256] = dot(scatter[:, 0:group], dsorted[0:group, :]).astype(jnp.bfloat16)
        dqkv[at, 256:512] = dot(scatter[:, group:], dsorted[group:, :]).astype(jnp.bfloat16)
        return dot(dqkv[at, :], wsel_ref[...], 1, 1)

    def part_copy(k):
        return remote(part_send.at[k], part_in.at[k], part_sems, k, sibling)

    def parts_away():
        def one(k, carry):
            part_send[k] = place(4 * (1 - c) + k).astype(jnp.bfloat16)
            part_copy(k).start()
            return carry

        lax.fori_loop(0, 4, one, 0)

    def parts_here():
        def one(k, carry):
            part = place(4 * c + k)
            part_copy(k).wait()
            total[k // 2, k % 2] = (part + part_in[k].astype(jnp.float32)).astype(jnp.bfloat16)
            return carry

        lax.fori_loop(0, 4, one, 0)

    upper, lower = pl.ds(0, block // 2), pl.ds(block // 2, block // 2)
    pieces = [pl.ds(i * (width // 2), width // 2) for i in range(2)]
    a_copies = [
        remote(total.at[:, 1 - x, upper, cols], a_in.at[:, :, cols], part_sems, 4 + i, over_x)
        for i, cols in enumerate(pieces)
    ]
    b_copies = [
        remote(total.at[1 - zl, :, lower, cols], b_in.at[:, :, cols], part_sems, 6 + i, over_z)
        for i, cols in enumerate(pieces)
    ]
    a_next = [
        remote(a_in.at[1 - zl, :, cols], a_two.at[:, cols], part_sems, 8 + i, over_z)
        for i, cols in enumerate(pieces)
    ]
    b_next = [
        remote(b_in.at[1 - x, :, cols], b_two.at[:, cols], part_sems, 10 + i, over_x)
        for i, cols in enumerate(pieces)
    ]

    def first_hops(i):
        a_copies[i].start()
        b_copies[i].start()

    def second_hop_a(i):
        cols = pieces[i]
        a_copies[i].wait()
        add_into(2, lambda k: a_in.at[k, :, cols], lambda k: total.at[k, x, upper, cols])
        a_next[i].start()

    def second_hop_b(i):
        cols = pieces[i]
        b_copies[i].wait()
        add_into(2, lambda k: b_in.at[k, :, cols], lambda k: total.at[zl, k, lower, cols])
        b_next[i].start()

    def grad_home_start(i):
        cols = pieces[i]
        a_next[i].wait()
        b_next[i].wait()
        for start, first, second, index in ((0, a_two, a_in, zl), (block // 2, b_two, b_in, x)):
            at = pl.ds(start, block // 2)
            grad_my[at, cols] = (
                delta_ref[at, cols]
                + first[:, cols].astype(jnp.float32)
                + second[index, :, cols].astype(jnp.float32)
            ).astype(jnp.bfloat16)
        home_copy(grad_my.at[:, cols], grad_home.at[:, cols], 1 + i, True)

    def grad_home_end(i):
        cols = pieces[i]
        home_copy(grad_my.at[:, cols], grad_home.at[:, cols], 1 + i, False)

    over_y_copy = remote(dw_y.at[1 - y], dw_in, dw_sems, 0, over_y)

    def projections():
        for k in range(width // 128):
            dw[128 * k : 128 * (k + 1), :] = dot(
                x_all[:, 128 * k : 128 * (k + 1)], dqkv[...], 0, 0
            ).astype(jnp.bfloat16)
        bias_row = jnp.broadcast_to(
            jnp.sum(dqkv[...].astype(jnp.float32), axis=0, keepdims=True), (16, 512)
        ).astype(jnp.bfloat16)
        for d in range(8):
            for h in range(2):
                dw_y[h, d, 0:share, :] = dw[share * d : share * (d + 1), 256 * h : 256 * (h + 1)]
                dw_y[h, d, share : share + 16, :] = bias_row[:, 256 * h : 256 * (h + 1)]
        over_y_copy.start()

    targets = across + [over_x, over_z, peers[2]]
    flips = [(1, f // 2, f % 2) for f in range(4)] + [(0, 0, 1), (0, 1, 0), (0, 1, 1)]
    dw_copies = []
    for i, (peer, (fh, fz, fx)) in enumerate(zip(targets, flips)):
        d = 4 * bits(zh, fh) + 2 * bits(zl, fz) + bits(x, fx)
        dw_copies.append(remote(dw_y.at[y, d], dw_all.at[s], dw_sems, 1 + i, peer))
    w_over_y = remote(w_all.at[y, c], w_all.at[y, c], dw_sems, 8, over_y)
    w_over_c = remote(w_all.at[:, c], w_all.at[:, c], dw_sems, 9, sibling)

    def dw_exchange():
        over_y_copy.wait()
        add_into(8, lambda i: dw_y.at[y, i], lambda i: dw_in.at[i])
        for copy in dw_copies:
            copy.start()
        dw_all[s] = dw_y[y, s]

    def dw_sum():
        for copy in dw_copies:
            copy.wait()
        for k in range(4):
            w_all[y, c, k] = (dw_all[k].astype(jnp.float32) + dw_all[4 + k].astype(jnp.float32)).astype(
                jnp.bfloat16
            )
        w_over_y.start()

    def dw_core():
        w_over_y.wait()
        w_over_c.start()

    def dw_end():
        w_over_c.wait()
        copy = pltpu.make_async_copy(w_all, w_hbm, out_sem.at[parts + 1])
        copy.start()
        outward.append(copy)

    def begin():
        datt_tiles()
        out_grads()
        pl.semaphore_wait(barrier, len(everyone))

    def start_reduction():
        for k in range(parts):
            reduction("0", k)

    single = {
        "begin": begin,
        "datt": datt_out,
        "home0": lambda: home_copy(out_my, out_home, 0, True),
        "hE0": lambda: home_copy(out_my, out_home, 0, False),
        "g1": grads_first,
        "g2": grads_second,
        "S0": start_reduction,
        "pl": parts_away,
        "ph": parts_here,
        "dw": projections,
        "da": dw_exchange,
        "wy": dw_sum,
        "wc": dw_core,
        "wE": dw_end,
        "stE": lambda: stats_step(5),
    }
    indexed = {
        "bld": build,
        "take": take,
        "at": attend_some,
        "ab": first_hops,
        "ha": second_hop_a,
        "hb": second_hop_b,
        "hm": grad_home_start,
        "hE": grad_home_end,
        "st": stats_step,
    }
    for name in BACKWARD_ORDER:
        kind, _, index = name.partition(":")
        if kind in single:
            single[kind]()
        elif kind in indexed:
            indexed[kind](int(index))
        else:
            reduction(kind[1:], int(index))
    for copy in outward:
        copy.wait()


def backward_attention(
    datt,
    order,
    output,
    stats,
    vectors,
    att,
    dbranch,
    low_first,
    dsecond,
    act,
    dinner,
    sorted_rows,
    prob,
    wsel,
    x_all,
    delta,
    parts,
):
    block, width = datt.shape
    inner_width = act.shape[1]
    group = 8 * block
    rows = group * 3 // 2
    q = (9 * width // 8 + 32) // 8
    share = width // 8 + 16
    low, full = jnp.bfloat16, jnp.float32
    vmem = pl.BlockSpec(memory_space=pltpu.VMEM)
    hbm = pl.BlockSpec(memory_space=pl.ANY)
    dma = pltpu.SemaphoreType.DMA
    shape = jax.ShapeDtypeStruct
    return pl.pallas_call(
        functools.partial(backward_kernel, parts),
        out_shape=[
            shape((block, width), low),
            shape((block, width), low),
            shape((2, 2, 2, q, width), low),
            shape((2, 2, 4, share, 256), low),
            shape(stats.shape, full),
        ],
        in_specs=[hbm] * 16,
        out_specs=[hbm] * 5,
        scratch_shapes=[
            pltpu.VMEM((block, width), low),
            pltpu.VMEM((block, width), low),
            pltpu.VMEM((block, width), low),
            pltpu.VMEM(vectors.shape, full),
            pltpu.VMEM((block, width), low),
            pltpu.VMEM((block, width), low),
            pltpu.VMEM((block, inner_width), low),
            pltpu.VMEM((block, inner_width), low),
            pltpu.VMEM(order.shape, order.dtype),
            pltpu.VMEM(stats.shape, full),
            pltpu.VMEM((rows, 256), low),
            pltpu.VMEM((rows, 128), full),
            pltpu.VMEM((width, 512), low),
            pltpu.VMEM((group, width), low),
            pltpu.VMEM((block, width), full),
            pltpu.VMEM((2, 2, 2, q, width), low),
            pltpu.VMEM((2, 2, 4, share, 256), low),
            pltpu.VMEM((2, 2, 2, 8 * q, width), low),
            pltpu.VMEM((8, block, 128), low),
            pltpu.VMEM((8, block, 128), low),
            pltpu.VMEM((2, 512, group), low),
            pltpu.VMEM((rows, 128), low),
            pltpu.VMEM((rows, 256), low),
            pltpu.VMEM((block, rows), low),
            pltpu.VMEM((group, 512), low),
            pltpu.VMEM((4, block, width), low),
            pltpu.VMEM((4, block, width), low),
            pltpu.VMEM((2, 2, block, width), low),
            pltpu.VMEM((2, block // 2, width), low),
            pltpu.VMEM((2, block // 2, width), low),
            pltpu.VMEM((block // 2, width), low),
            pltpu.VMEM((block // 2, width), low),
            pltpu.VMEM((block, width), low),
            pltpu.VMEM((width, 512), low),
            pltpu.VMEM((2, 8, share, 256), low),
            pltpu.VMEM((8, share, 256), low),
            pltpu.VMEM((8, share, 256), low),
            pltpu.VMEM((6,) + stats.shape, full),
            pltpu.VMEM((5,) + stats.shape, full),
            pltpu.VMEM((2, 2, 2, 4 * q, width), low),
            pltpu.VMEM((2, 2, 2 * q, width), low),
            pltpu.VMEM((2, 2 * q, width), low),
            pltpu.VMEM((2 * q, width), low),
            pltpu.VMEM((2 * q, width), low),
            pltpu.VMEM((2, 2, 2, q, width), low),
            pltpu.VMEM((2, 2, q, width), low),
            pltpu.VMEM((2, q, width), low),
            pltpu.VMEM((q, width), low),
            dma((7,)),
            dma((7,)),
            dma((12,)),
            dma((12,)),
            dma((6,)),
            dma((6,)),
            dma((10,)),
            dma((10,)),
            dma((5,)),
            dma((5,)),
            dma((11, parts)),
            dma((11, parts)),
            dma((15,)),
            dma((parts + 2,)),
        ],
        compiler_params=pltpu.CompilerParams(
            collective_id=2, has_side_effects=True, vmem_limit_bytes=62 << 20
        ),
        name="backward_attention",
    )(
        datt,
        order,
        output,
        stats,
        vectors,
        att,
        dbranch,
        low_first,
        dsecond,
        act,
        dinner,
        sorted_rows,
        prob,
        wsel,
        x_all.reshape(group, width),
        delta,
    )


def finish_kernel(
    f_ref,
    w_ref,
    out_ref,
    grad_ref,
    stats_ref,
    output,
    grad_tokens,
    gq_out,
    gqb_out,
    gk_out,
    gv_out,
    gvb_out,
    go_out,
    gob_out,
    gfg_out,
    gfs_out,
    gi_out,
    gib_out,
    gu_out,
    gub_out,
    gsg_out,
    gss_out,
    stats_out,
    gq_ref,
    gv_ref,
    vec_ref,
    square,
):
    s = lax.axis_index("seq")
    output[0] = out_ref[...]
    grad_tokens[0] = grad_ref[...]
    for kind in range(2):
        square[0:16, :] = stats_ref[kind]
        stats_out[kind] = square[...].T[: stats_out.shape[1], : stats_out.shape[2]]
    share, width = gk_out.shape
    top = f_ref.shape[0] // 2
    full = jnp.float32
    for n in range(gi_out.shape[1] // width):
        gi_out[:, n * width : (n + 1) * width] = f_ref[n * share : (n + 1) * share, :].astype(full)
    gu_out[...] = f_ref[top : top + 4 * share, :].astype(full)
    part = share // 2
    go_out[0:part, :] = f_ref[4 * share : 4 * share + part, :].astype(full)
    go_out[part:, :] = f_ref[top + 4 * share : top + 4 * share + part, :].astype(full)
    vec_ref[...] = f_ref[top + 4 * share + part :, :].astype(full)
    for pair in range(4):
        at = slice(128 * pair, 128 * pair + 128)
        low, high = (w_ref[0, core, pair].astype(full) for core in range(2))
        gq_ref[:, at] = join(low[:, 0:128], half_roll(high[:, 0:128]))
        gk_out[:, at] = join(low[:, 128:256], half_roll(high[:, 128:256]))[:share]
        gv_ref[:, at] = join(half_roll(low[:, 0:128]), high[:, 0:128])
    for pair in range(2):
        at = slice(512 + 128 * pair, 640 + 128 * pair)
        low, high = (
            w_ref[1, 0, 2 * pair + i].astype(full) + w_ref[1, 1, 2 * pair + i].astype(full) for i in range(2)
        )
        gq_ref[:, at] = join(half_roll(low[:, 0:128]), high[:, 0:128])
        gk_out[:, at] = join(half_roll(low[:, 128:256]), high[:, 128:256])[:share]
        gv_ref[:, at] = join(low[:, 0:128], half_roll(high[:, 0:128]))
    gq_out[...] = gq_ref[:share, :]
    gv_out[...] = gv_ref[:share, :]

    def mine(rows):
        return pltpu.roll(rows, width - share * s, 1)[:, :share]

    short = mine(vec_ref[...])
    for row, ref in enumerate((gob_out, gfg_out, gfs_out, gub_out, gsg_out, gss_out)):
        ref[...] = short[row]
    gqb_out[...] = mine(gq_ref[share : share + 8, :])[0]
    gvb_out[...] = mine(gv_ref[share : share + 8, :])[0]
    row = vec_ref[pl.ds(6 + s // 2, 1), :]
    gib_out[...] = jnp.where(s % 2 == 1, row[:, 4 * share :], row[:, : 4 * share])[0]


def finish(reduced, w_all, output, grad, totals, head_count, inner_width):
    block, width = output.shape
    row_count = 8 * reduced.shape[3]
    share = width // 8
    low, full = jnp.bfloat16, jnp.float32
    vmem = pl.BlockSpec(memory_space=pltpu.VMEM)
    shape = jax.ShapeDtypeStruct
    square, vector = shape((share, width), full), shape((share,), full)
    out_shape = [
        shape((1, block, width), low),
        shape((1, block, width), low),
        square,
        vector,
        square,
        square,
        vector,
        square,
        vector,
        vector,
        vector,
        shape((share, inner_width), full),
        shape((inner_width // 8,), full),
        shape((inner_width // 8, width), full),
        vector,
        vector,
        vector,
        shape((2, 8, head_count), full),
    ]
    outs = pl.pallas_call(
        finish_kernel,
        out_shape=out_shape,
        in_specs=[vmem] * 5,
        out_specs=[vmem] * len(out_shape),
        scratch_shapes=[
            pltpu.VMEM((share + 16, width), full),
            pltpu.VMEM((share + 16, width), full),
            pltpu.VMEM((16, width), full),
            pltpu.VMEM((128, 128), full),
        ],
        compiler_params=pltpu.CompilerParams(vmem_limit_bytes=60 << 20),
        name="finish",
    )(reduced.reshape(row_count, width), w_all, output, grad, totals)
    return (*outs[:-1], outs[-1].transpose(0, 2, 1))


def body(
    tokens,
    segments,
    orders,
    owners,
    query_weight,
    query_bias,
    key_weight,
    value_weight,
    value_bias,
    out_weight,
    out_bias,
    first_gain,
    first_shift,
    inner_weight,
    inner_bias,
    outer_weight,
    outer_bias,
    second_gain,
    second_shift,
    cotangent,
):
    seq_count = lax.axis_size("seq")
    groups = lax.axis_size("rep")
    own_index = lax.axis_index("seq")
    row_count = tokens.shape[1]
    model_width = tokens.shape[2]
    order_table = orders[0]
    owner_table = owners[0]
    head_count, group_tokens = order_table.shape
    cluster_count = owner_table.shape[1]
    cluster = group_tokens // cluster_count
    head_dim = model_width // head_count
    per_owner = row_count // cluster
    score_scale = head_dim ** (-0.5)
    flat_tokens = tokens[0]
    local_index = jnp.arange(row_count, dtype=jnp.int32)
    factor = 1
    for candidate in range(1, seq_count + 1):
        if seq_count % candidate == 0 and candidate * row_count <= 2048:
            factor = candidate
    block_count = seq_count // factor
    block_width = factor * row_count
    order_blocks = order_table.reshape(head_count, block_count, block_width).transpose(1, 0, 2)
    owner_blocks = (
        jnp.repeat(owner_table, cluster, axis=1)
        .reshape(head_count, block_count, block_width)
        .transpose(1, 0, 2)
    )

    def find_target(total, block_item):
        order_block, owner_block = block_item
        local = order_block - own_index * row_count
        hits = local[:, :, None] == local_index[None, None, :]
        return (total + jnp.sum(jnp.where(hits, owner_block[:, :, None], 0), axis=1), None)

    target, unused = lax.scan(
        find_target, jnp.zeros((head_count, row_count), jnp.int32), (order_blocks, owner_blocks)
    )
    send_matrix = rank_matrix(target * row_count + local_index[None, :])
    mine = (owner_table == own_index).astype(jnp.int32)
    before = jnp.cumsum(mine, axis=1) - mine
    slot_hot = (mine[:, None, :] == 1) & (
        before[:, None, :] == jnp.arange(per_owner, dtype=jnp.int32)[None, :, None]
    )
    order_grid = order_table.reshape(head_count, cluster_count, cluster)
    owned_tokens = jnp.sum(
        jnp.where(slot_hot[:, :, :, None], order_grid[:, None, :, :], 0), axis=2
    ).reshape(head_count, row_count)
    arrive_matrix = rank_matrix(owned_tokens)
    w_three = jnp.concatenate([query_weight, key_weight, value_weight], axis=1)
    bias_three = jnp.concatenate(
        [
            query_bias.astype(jnp.float32),
            jnp.zeros((model_width,), jnp.float32),
            value_bias.astype(jnp.float32),
        ]
    )
    projected = (
        jnp.dot(flat_tokens, w_three, preferred_element_type=jnp.float32) + bias_three
    ).astype(jnp.bfloat16)
    token_rows = (
        projected.reshape(row_count, 3, head_count, head_dim)
        .transpose(2, 0, 1, 3)
        .reshape(head_count, row_count, 3 * head_dim)
    )
    segment_rows = jnp.broadcast_to(
        segments[0].astype(jnp.bfloat16)[None, :, None], (head_count, row_count, 1)
    )
    send_values = scatter_rows(token_rows, send_matrix, seq_count)
    send_segments = scatter_rows(segment_rows, send_matrix, seq_count)
    arrived, arrived_segments = (
        lax.all_to_all(send_values, "seq", split_axis=0, concat_axis=0, tiled=True),
        lax.all_to_all(send_segments, "seq", split_axis=0, concat_axis=0, tiled=True),
    )
    cluster_rows = collect_rows(arrived, arrive_matrix, 3 * head_dim).reshape(
        head_count * per_owner, cluster, 3, head_dim
    )
    cluster_segments = collect_rows(arrived_segments, arrive_matrix, 1).reshape(
        head_count * per_owner, cluster
    )
    queries = cluster_rows[:, :, 0]
    keys_in = cluster_rows[:, :, 1]
    values = cluster_rows[:, :, 2]
    attended, log_total, entropy, occupied = cluster_forward(
        queries, keys_in, values, cluster_segments, score_scale
    )
    per_head = jnp.stack(
        [
            jnp.sum(entropy.reshape(head_count, -1), axis=1),
            jnp.sum(occupied.reshape(head_count, -1), axis=1) / cluster,
        ]
    ) / (groups * row_count)
    column = (jnp.arange(seq_count, dtype=jnp.int32) == own_index).astype(jnp.float32)
    cluster_stats = lax.psum(per_head[:, :, None] * column, ("seq", "rep"))
    leaving = scatter_rows(
        attended.reshape(head_count, row_count, head_dim), arrive_matrix, seq_count
    )
    returned = lax.all_to_all(leaving, "seq", split_axis=0, concat_axis=0, tiled=True)
    attended_rows = (
        collect_rows(returned, send_matrix, head_dim)
        .transpose(1, 0, 2)
        .reshape(row_count, model_width)
    )
    branch = jnp.dot(
        attended_rows, out_weight, preferred_element_type=jnp.float32
    ) + out_bias.astype(jnp.float32)
    first_out, normed_one, root_one = norm_forward(
        flat_tokens.astype(jnp.float32) + branch, first_gain, first_shift
    )
    first_low = first_out.astype(jnp.bfloat16)
    inner_sum = jnp.dot(
        first_low, inner_weight, preferred_element_type=jnp.float32
    ) + inner_bias.astype(jnp.float32)
    activated, gelu_pull = jax.vjp(exact_gelu, inner_sum)
    activated_low = activated.astype(jnp.bfloat16)
    second = jnp.dot(
        activated_low, outer_weight, preferred_element_type=jnp.float32
    ) + outer_bias.astype(jnp.float32)
    result, normed_two, root_two = norm_forward(first_out + second, second_gain, second_shift)
    output = result.astype(jnp.bfloat16)[None]
    upstream = cotangent[0].astype(jnp.float32)
    gradient_second_gain = jnp.sum(upstream * normed_two, axis=0)
    gradient_second_shift = jnp.sum(upstream, axis=0)
    delta_two = norm_backward(upstream, normed_two, root_two, second_gain)
    delta_second = delta_two.astype(jnp.bfloat16)
    gradient_outer_bias = jnp.sum(delta_second.astype(jnp.float32), axis=0)
    gradient_outer_weight = jnp.einsum(
        "tf,td->fd", activated_low, delta_second, preferred_element_type=jnp.float32
    )
    delta_activated = jnp.einsum(
        "td,fd->tf", delta_second, outer_weight, preferred_element_type=jnp.float32
    )
    delta_inner = gelu_pull(delta_activated)[0].astype(jnp.bfloat16)
    gradient_inner_bias = jnp.sum(delta_inner.astype(jnp.float32), axis=0)
    gradient_inner_weight = jnp.einsum(
        "td,tf->df", first_low, delta_inner, preferred_element_type=jnp.float32
    )
    delta_first = delta_two + jnp.einsum(
        "tf,df->td", delta_inner, inner_weight, preferred_element_type=jnp.float32
    )
    gradient_first_gain = jnp.sum(delta_first * normed_one, axis=0)
    gradient_first_shift = jnp.sum(delta_first, axis=0)
    delta_one = norm_backward(delta_first, normed_one, root_one, first_gain)
    delta_branch = delta_one.astype(jnp.bfloat16)
    gradient_out_bias = jnp.sum(delta_branch.astype(jnp.float32), axis=0)
    gradient_out_weight = jnp.einsum(
        "td,te->de", attended_rows, delta_branch, preferred_element_type=jnp.float32
    )
    delta_attended = jnp.einsum(
        "te,de->td", delta_branch, out_weight, preferred_element_type=jnp.float32
    ).astype(jnp.bfloat16)
    delta_rows = delta_attended.reshape(row_count, head_count, head_dim).transpose(1, 0, 2)
    send_grads = scatter_rows(delta_rows, send_matrix, seq_count)
    grad_arrived = lax.all_to_all(send_grads, "seq", split_axis=0, concat_axis=0, tiled=True)
    kept_queries, kept_keys, kept_values, kept_segments = (
        queries,
        keys_in,
        values,
        cluster_segments,
    )
    grad_cluster = collect_rows(grad_arrived, arrive_matrix, head_dim).reshape(
        head_count * per_owner, cluster, head_dim
    )
    three_grads = cluster_backward(
        kept_queries, kept_keys, kept_values, kept_segments, log_total, grad_cluster, score_scale
    )
    leaving_grads = scatter_rows(
        three_grads.reshape(head_count, row_count, 3 * head_dim), arrive_matrix, seq_count
    )
    returned_grads = lax.all_to_all(leaving_grads, "seq", split_axis=0, concat_axis=0, tiled=True)
    delta_three = (
        collect_rows(returned_grads, send_matrix, 3 * head_dim)
        .reshape(head_count, row_count, 3, head_dim)
        .transpose(1, 2, 0, 3)
        .reshape(row_count, 3 * model_width)
    )
    bias_grads = jnp.sum(delta_three.astype(jnp.float32), axis=0)
    weight_grads = jnp.einsum(
        "td,te->de", flat_tokens, delta_three, preferred_element_type=jnp.float32
    )
    gradient_tokens = (
        delta_one
        + jnp.einsum("te,de->td", delta_three, w_three, preferred_element_type=jnp.float32)
    ).astype(jnp.bfloat16)[None]
    gradient_query_weight = weight_grads[:, :model_width]
    gradient_key_weight = weight_grads[:, model_width : 2 * model_width]
    gradient_value_weight = weight_grads[:, 2 * model_width :]
    gradient_query_bias = bias_grads[:model_width]
    gradient_value_bias = bias_grads[2 * model_width :]
    pieces = (
        lax.psum_scatter(gradient_query_weight, "seq", scatter_dimension=0, tiled=True),
        lax.psum_scatter(gradient_query_bias, "seq", scatter_dimension=0, tiled=True),
        lax.psum_scatter(gradient_key_weight, "seq", scatter_dimension=0, tiled=True),
        lax.psum_scatter(gradient_value_weight, "seq", scatter_dimension=0, tiled=True),
        lax.psum_scatter(gradient_value_bias, "seq", scatter_dimension=0, tiled=True),
        lax.psum_scatter(gradient_out_weight, "seq", scatter_dimension=0, tiled=True),
        lax.psum_scatter(gradient_out_bias, "seq", scatter_dimension=0, tiled=True),
        lax.psum_scatter(gradient_first_gain, "seq", scatter_dimension=0, tiled=True),
        lax.psum_scatter(gradient_first_shift, "seq", scatter_dimension=0, tiled=True),
        lax.psum_scatter(gradient_inner_weight, "seq", scatter_dimension=0, tiled=True),
        lax.psum_scatter(gradient_inner_bias, "seq", scatter_dimension=0, tiled=True),
        lax.psum_scatter(gradient_outer_weight, "seq", scatter_dimension=0, tiled=True),
        lax.psum_scatter(gradient_outer_bias, "seq", scatter_dimension=0, tiled=True),
        lax.psum_scatter(gradient_second_gain, "seq", scatter_dimension=0, tiled=True),
        lax.psum_scatter(gradient_second_shift, "seq", scatter_dimension=0, tiled=True),
    )
    summed = (
        lax.psum(pieces[0].astype(jnp.bfloat16), "rep").astype(jnp.float32),
        lax.psum(pieces[1].astype(jnp.bfloat16), "rep").astype(jnp.float32),
        lax.psum(pieces[2].astype(jnp.bfloat16), "rep").astype(jnp.float32),
        lax.psum(pieces[3].astype(jnp.bfloat16), "rep").astype(jnp.float32),
        lax.psum(pieces[4].astype(jnp.bfloat16), "rep").astype(jnp.float32),
        lax.psum(pieces[5].astype(jnp.bfloat16), "rep").astype(jnp.float32),
        lax.psum(pieces[6].astype(jnp.bfloat16), "rep").astype(jnp.float32),
        lax.psum(pieces[7].astype(jnp.bfloat16), "rep").astype(jnp.float32),
        lax.psum(pieces[8].astype(jnp.bfloat16), "rep").astype(jnp.float32),
        lax.psum(pieces[9].astype(jnp.bfloat16), "rep").astype(jnp.float32),
        lax.psum(pieces[10].astype(jnp.bfloat16), "rep").astype(jnp.float32),
        lax.psum(pieces[11].astype(jnp.bfloat16), "rep").astype(jnp.float32),
        lax.psum(pieces[12].astype(jnp.bfloat16), "rep").astype(jnp.float32),
        lax.psum(pieces[13].astype(jnp.bfloat16), "rep").astype(jnp.float32),
        lax.psum(pieces[14].astype(jnp.bfloat16), "rep").astype(jnp.float32),
    )
    return (output, gradient_tokens) + tuple(summed) + (cluster_stats,)


def square_body(
    tokens,
    segments,
    orders,
    owners,
    query_weight,
    query_bias,
    key_weight,
    value_weight,
    value_bias,
    out_weight,
    out_bias,
    first_gain,
    first_shift,
    inner_weight,
    inner_bias,
    outer_weight,
    outer_bias,
    second_gain,
    second_shift,
    cotangent,
):
    (
        wsel,
        order,
        stats,
        x_all,
        sorted_rows,
        prob,
        att,
        low_first,
        act,
        output,
        dsecond,
        dinner,
        delta,
        dbranch,
        vector_grads,
        datt,
    ) = forward_layer(
        tokens[0],
        cotangent[0],
        segments,
        orders.transpose(1, 0, 2),
        owners.transpose(1, 0, 2),
        (
            query_bias,
            value_bias,
            out_bias,
            first_gain,
            first_shift,
            outer_bias,
            second_gain,
            second_shift,
            inner_bias,
        ),
        (query_weight, key_weight, value_weight, out_weight, inner_weight, outer_weight),
    )
    output, grad, reduced, w_all, totals = backward_attention(
        datt,
        order,
        output,
        stats,
        vector_grads,
        att,
        dbranch,
        low_first,
        dsecond,
        act,
        dinner,
        sorted_rows,
        prob,
        wsel,
        x_all,
        delta,
        6,
    )
    return finish(reduced, w_all, output, grad, totals, orders.shape[1], inner_weight.shape[1])


def solution(mesh):
    square = mesh.shape["seq"] == 8 and mesh.shape["rep"] == 4
    placed = (
        P("rep", "seq", None),
        P("rep", "seq"),
        P("rep", None, None),
        P("rep", None, None),
        P(),
        P(),
        P(),
        P(),
        P(),
        P(),
        P(),
        P(),
        P(),
        P(),
        P(),
        P(),
        P(),
        P(),
        P(),
        P("rep", "seq", None),
    )
    return jax.shard_map(
        square_body if square else body,
        mesh=mesh,
        in_specs=placed,
        out_specs=(
            P("rep", "seq", None),
            P("rep", "seq", None),
            P("seq", None),
            P("seq"),
            P("seq", None),
            P("seq", None),
            P("seq"),
            P("seq", None),
            P("seq"),
            P("seq"),
            P("seq"),
            P("seq", None),
            P("seq"),
            P("seq", None),
            P("seq"),
            P("seq"),
            P("seq"),
            P(),
        ),
        check_vma=False,
    )
```

```python
import functools

import jax
import jax.numpy as jnp
from jax import lax
from jax.experimental import pallas as pl
from jax.experimental.pallas import tpu as pltpu
from jax.sharding import PartitionSpec as P

EPSILON = 1e-12
NEGATIVE = -1e30


def norm_forward(hidden, gain_vector, shift_vector):
    centre = hidden - jnp.mean(hidden, axis=-1, keepdims=True)
    root_inverse = lax.rsqrt(jnp.mean(centre * centre, axis=-1, keepdims=True) + EPSILON)
    normed = centre * root_inverse
    return (
        normed * gain_vector.astype(jnp.float32) + shift_vector.astype(jnp.float32),
        normed,
        root_inverse,
    )


def norm_backward(upstream, normed, root_inverse, gain_vector):
    scaled = upstream * gain_vector.astype(jnp.float32)
    return root_inverse * (
        scaled
        - jnp.mean(scaled, axis=-1, keepdims=True)
        - normed * jnp.mean(scaled * normed, axis=-1, keepdims=True)
    )


def exact_gelu(inner_sum):
    return jax.nn.gelu(inner_sum, approximate=False)


def rank_matrix(sort_keys):
    row_count = sort_keys.shape[1]
    ranks = jnp.sum((sort_keys[:, None, :] < sort_keys[:, :, None]).astype(jnp.int32), axis=2)
    return (ranks[:, None, :] == jnp.arange(row_count, dtype=jnp.int32)[None, :, None]).astype(
        jnp.bfloat16
    )


def scatter_rows(row_block, placing, seq_count):
    head_count, row_count, features = row_block.shape
    picked = jnp.einsum(
        "hri,hif->hrf", placing, row_block, preferred_element_type=jnp.float32
    ).astype(jnp.bfloat16)
    return picked.reshape(head_count, seq_count, row_count // seq_count * features).transpose(
        1, 0, 2
    )


def collect_rows(packed, placing, features):
    seq_count, head_count, flat_width = packed.shape
    row_block = packed.transpose(1, 0, 2).reshape(
        head_count, seq_count * flat_width // features, features
    )
    return jnp.einsum(
        "hri,hrf->hif", placing, row_block, preferred_element_type=jnp.float32
    ).astype(jnp.bfloat16)


def cluster_scores(queries, keys_in, segment_ids, score_scale):
    scores = (
        jnp.einsum("nqd,nkd->nqk", queries, keys_in, preferred_element_type=jnp.float32)
        * score_scale
    )
    allowed = segment_ids[:, :, None] == segment_ids[:, None, :]
    return (scores, allowed, jnp.where(allowed, scores, NEGATIVE))


def cluster_forward(queries, keys_in, values, segment_ids, score_scale):
    scores, allowed, masked = cluster_scores(queries, keys_in, segment_ids, score_scale)
    highest = jnp.max(masked, axis=-1, keepdims=True)
    raised = jnp.exp(masked - highest)
    totals = jnp.sum(raised, axis=-1, keepdims=True)
    weights = raised / totals
    attended = jnp.einsum(
        "nqk,nkd->nqd", weights.astype(jnp.bfloat16), values, preferred_element_type=jnp.float32
    ).astype(jnp.bfloat16)
    log_total = highest[:, :, 0] + jnp.log(totals[:, :, 0])
    entropy = log_total - jnp.sum(weights * jnp.where(allowed, scores, 0.0), axis=-1)
    occupied = jnp.sum(allowed.astype(jnp.float32), axis=-1)
    return (attended, log_total, entropy, occupied)


def cluster_backward(queries, keys_in, values, segment_ids, log_total, grad_out, score_scale):
    masked = cluster_scores(queries, keys_in, segment_ids, score_scale)[2]
    weights = jnp.exp(masked - log_total[:, :, None])
    weight_grads = jnp.einsum("nqd,nkd->nqk", grad_out, values, preferred_element_type=jnp.float32)
    value_grads = jnp.einsum(
        "nqk,nqd->nkd", weights.astype(jnp.bfloat16), grad_out, preferred_element_type=jnp.float32
    )
    score_grads = (
        weights * (weight_grads - jnp.sum(weights * weight_grads, axis=-1, keepdims=True))
    ).astype(jnp.bfloat16)
    query_grads = (
        jnp.einsum("nqk,nkd->nqd", score_grads, keys_in, preferred_element_type=jnp.float32)
        * score_scale
    )
    key_grads = (
        jnp.einsum("nqk,nqd->nkd", score_grads, queries, preferred_element_type=jnp.float32)
        * score_scale
    )
    return jnp.stack([query_grads, key_grads, value_grads], axis=2).astype(jnp.bfloat16)


MESH = pl.DeviceIdType.MESH


UNROLL = 8
PIECES = 4
FIRST = 1


def half_roll(block):
    return jnp.concatenate([block[:, 64:], block[:, :64]], axis=1)


def lanes(shape):
    return lax.broadcasted_iota(jnp.int32, shape, len(shape) - 1)


def bits(value, flip):
    return value + flip - 2 * value * flip


def coordinates():
    s, r = lax.axis_index("seq"), lax.axis_index("rep")
    return s // 4, (s // 2) % 2, s % 2, r // 2, r % 2


def device(zh, zl, x, y, c):
    return (4 * zh + 2 * zl + x, 2 * y + c)


def greet(peers):
    barrier = pltpu.get_barrier_semaphore()
    for peer in peers:
        pl.semaphore_signal(barrier, inc=1, device_id=peer, device_id_type=MESH)
    pl.semaphore_wait(barrier, len(peers))


def remote(src, dst, sems, index, peer):
    return pltpu.make_async_remote_copy(
        src_ref=src,
        dst_ref=dst,
        send_sem=sems[0].at[index],
        recv_sem=sems[1].at[index],
        device_id=peer,
        device_id_type=MESH,
    )


def dot(left, right, left_dim=1, right_dim=0):
    return lax.dot_general(
        left,
        right,
        (((left_dim,), (right_dim,)), ((), ())),
        preferred_element_type=jnp.float32,
    )


def hot(condition):
    return jnp.where(condition, 1.0, 0.0).astype(jnp.bfloat16)


def build_gather(order_ref, row, start, count, into):
    tokens = into.shape[1]

    def one(k, carry):
        at = pl.multiple_of(k * 128, 128)
        ids = order_ref[row : row + 1, pl.ds(pl.multiple_of(start + at, 128), 128)]
        column = jnp.broadcast_to(ids.astype(jnp.float32), (128, 128)).T
        lane = lanes((128, 128)).astype(jnp.float32)
        for t in range(tokens // 128):
            into[pl.ds(at, 128), t * 128 : (t + 1) * 128] = hot(column == lane + 128.0 * t)
        return carry

    lax.fori_loop(0, count // 128, one, 0)


def build_scatter(order_ref, half, first_token, into):
    group = order_ref.shape[1]

    def one(k, carry):
        at = pl.multiple_of(k * 128, 128)
        token = lax.broadcasted_iota(jnp.int32, (128, 128), 0) + (first_token + at)
        for p in range(into.shape[1] // 128):
            row, start = (0, 128 * p) if 128 * p < group else (1, half + 128 * p - group)
            ids = order_ref[row : row + 1, pl.ds(pl.multiple_of(start, 128), 128)]
            into[pl.ds(at, 128), 128 * p : 128 * (p + 1)] = hot(ids == token)
        return carry

    lax.fori_loop(0, into.shape[0] // 128, one, 0)


def select_head(slab, half, place):
    return jnp.where(half == place, slab, half_roll(slab))


def join(low_lanes, high_lanes):
    return jnp.where(lanes(low_lanes.shape) < 64, low_lanes, high_lanes)


def pick_columns(pairs, j, c):
    (q_one, q_two), (k_one, k_two), (v_one, v_two) = pairs
    zero = jnp.zeros_like(q_one)
    q1, v1, k1 = select_head(q_one, c, 0), select_head(v_one, c, 1), select_head(k_one, c, 0)
    v2, q2, k2 = (
        select_head(v_two, j % 2, 0),
        select_head(q_two, j % 2, 1),
        select_head(k_two, j % 2, 1),
    )
    return join(q1, v1), join(k1, zero), join(v2, q2), join(zero, k2)


def normalize(hidden):
    centre = hidden - jnp.mean(hidden, axis=1, keepdims=True)
    root_inverse = lax.rsqrt(jnp.mean(centre * centre, axis=1, keepdims=True) + EPSILON)
    return centre * root_inverse, root_inverse


def normalize_back(scaled, normed, root_inverse):
    return root_inverse * (
        scaled
        - jnp.mean(scaled, axis=1, keepdims=True)
        - normed * jnp.mean(scaled * normed, axis=1, keepdims=True)
    )


def forward_kernel(
    tokens_ref,
    cot_ref,
    seg_ref,
    orders_ref,
    owners_ref,
    query_bias_ref,
    value_bias_ref,
    out_bias_ref,
    first_gain_ref,
    first_shift_ref,
    outer_bias_ref,
    second_gain_ref,
    second_shift_ref,
    inner_bias_ref,
    wq_hbm,
    wk_hbm,
    wv_hbm,
    out_w_hbm,
    inner_w_hbm,
    outer_w_hbm,
    wsel_hbm,
    order_hbm,
    stats_hbm,
    x_hbm,
    sorted_hbm,
    prob_hbm,
    att_hbm,
    low_hbm,
    act_hbm,
    output_hbm,
    dsecond_hbm,
    dinner_hbm,
    delta_hbm,
    dbranch_hbm,
    vec_hbm,
    datt_hbm,
    wsel_ref,
    order_ref,
    stats_ref,
    x_all,
    sorted_ref,
    prob_ref,
    att_ref,
    low_ref,
    act_ref,
    output_ref,
    dsecond_ref,
    dinner_ref,
    delta_ref,
    dbranch_ref,
    vec_out,
    datt_ref,
    cot_my,
    weights,
    orders_in,
    owners_in,
    owner_pad,
    seg_src,
    seg_all,
    bias_rows,
    bias_sel,
    tok,
    gather,
    scatter,
    att_sorted,
    att_send,
    att_in,
    ent_ref,
    cnt_ref,
    swap_send,
    swap_recv,
    ring_send,
    ring_recv,
    seg_send,
    seg_recv,
    back_send,
    back_recv,
    local_sem,
    out_w,
    inner_w,
    outer_w,
    slope,
    total,
    normed_ref,
    bias_ref,
    load_sem,
    store_sem,
):
    zh, zl, x, y, c = coordinates()
    j = 2 * zl + x
    p = 4 * c + j
    block, width = tokens_ref.shape
    group = 8 * block
    scale = 0.125
    swap = (swap_send, swap_recv)
    ring = (ring_send, ring_recv)
    seg_sems = (seg_send, seg_recv)
    back = (back_send, back_recv)

    def member(flip):
        fc, fz, fx = flip // 4, (flip // 2) % 2, flip % 2
        mc, mz, mx = bits(c, fc), bits(zl, fz), bits(x, fx)
        return device(zh, mz, mx, y, mc), 4 * mc + 2 * mz + mx

    swap_peer = device(1 - zh, zl, x, y, 1 - c)
    peers = [member(flip)[0] for flip in range(1, 8)]
    sibling = peers[3]
    over_x, over_z = peers[0], peers[1]
    matched = c == zh

    slabs = [
        pltpu.make_async_copy(
            src.at[:, pl.ds(pl.multiple_of(index * 128, 128), 128)],
            weights.at[i, slot],
            local_sem.at[3 * slot + i],
        )
        for i, src in enumerate((wq_hbm, wk_hbm, wv_hbm))
        for slot, index in enumerate((j, 4 + j // 2))
    ]
    greet(peers + [swap_peer])
    for copy in slabs:
        copy.start()
    width_inner = inner_w.shape[1]
    dense_tile = 2 * width
    parts = [slice(dense_tile * t, dense_tile * (t + 1)) for t in range(width_inner // dense_tile)]
    loads = [pltpu.make_async_copy(out_w_hbm, out_w, load_sem.at[0])]
    for t, at in enumerate(parts):
        loads.append(
            pltpu.make_async_copy(inner_w_hbm.at[:, at], inner_w.at[:, at], load_sem.at[1 + 2 * t])
        )
        loads.append(pltpu.make_async_copy(outer_w_hbm.at[at], outer_w.at[at], load_sem.at[2 + 2 * t]))
    kept = {
        "wsel": (wsel_ref, wsel_hbm),
        "order": (order_ref, order_hbm),
        "stats": (stats_ref, stats_hbm),
        "x": (x_all, x_hbm),
        "sorted": (sorted_ref, sorted_hbm),
        "prob": (prob_ref, prob_hbm),
        "att": (att_ref, att_hbm),
        "low": (low_ref, low_hbm),
        "act": (act_ref, act_hbm),
        "output": (output_ref, output_hbm),
        "dsecond": (dsecond_ref, dsecond_hbm),
        "dinner": (dinner_ref, dinner_hbm),
        "delta": (delta_ref, delta_hbm),
        "dbranch": (dbranch_ref, dbranch_hbm),
        "vec": (vec_out, vec_hbm),
        "datt": (datt_ref, datt_hbm),
    }
    stores = {
        name: pltpu.make_async_copy(src, dst, store_sem.at[i]) for i, (name, (src, dst)) in enumerate(kept.items())
    }

    seg_src[...] = jnp.broadcast_to(seg_ref[...], seg_src.shape)
    table_copies = [
        remote(orders_ref, orders_in, swap, 0, sibling),
        remote(owners_ref, owners_in, swap, 1, sibling),
    ]
    for copy in table_copies:
        copy.start()
    p_swap = 4 * (1 - c) + j
    chunks = PIECES
    halves = [pl.ds(i * (block // chunks), block // chunks) for i in range(chunks)]
    pairs = [(tokens_ref.at[at], x_all.at[p_swap, at], x_all.at[p, at]) for at in halves]
    pairs.insert(0, (seg_src, seg_all.at[p_swap], seg_all.at[p]))
    pairs.append((cot_ref, cot_my, cot_my))
    swaps = [remote(src, dst, swap, 2 + i, swap_peer) for i, (src, dst, _) in enumerate(pairs)]
    locals_ = [
        pltpu.make_async_copy(src, own, swap_recv.at[4 + chunks + i]) for i, (src, _, own) in enumerate(pairs)
    ]

    px, pz, pd = member(1)[1], member(2)[1], member(3)[1]

    def share_block(index, position, i, peer):
        view = x_all.at[position, halves[i]]
        return remote(view, view, ring, index, peer)

    every = range(chunks)
    own_to_x = [share_block(i, p, i, over_x) for i in every]
    own_to_z = [share_block(chunks + i, p, i, over_z) for i in every]
    own_to_s = [share_block(2 * chunks + i, p, i, sibling) for i in every]
    x_to_s = [share_block(3 * chunks + i, px, i, sibling) for i in every]
    z_to_s = [share_block(4 * chunks + i, pz, i, sibling) for i in every]
    d_to_s = [share_block(5 * chunks + i, pd, i, sibling) for i in every]
    relays = [
        share_block(6 * chunks + i, px, i, over_z) if i < FIRST else share_block(6 * chunks + i, pz, i, over_x)
        for i in every
    ]
    seg_copies = [
        remote(seg_all.at[p], seg_all.at[p], seg_sems, flip - 1, peers[flip - 1]) for flip in range(1, 8)
    ]
    opposite = jnp.logical_not(matched)

    def own_half(i, arrivals):
        arrivals[1 + i].wait()
        own_to_x[i].start()
        own_to_z[i].start()
        own_to_s[i].start()

    def segments_out(arrivals):
        arrivals[0].wait()
        for copy in seg_copies:
            copy.start()

    def relay(i):
        own_to_x[i].wait()
        own_to_z[i].wait()
        relays[i].start()
        x_to_s[i].start()
        z_to_s[i].start()

    def relay_end(i):
        relays[i].wait()
        d_to_s[i].start()

    def wait_sibling():
        for copy in own_to_s + x_to_s + z_to_s + d_to_s:
            copy.wait_recv()

    @pl.when(matched)
    def _():
        for copy in locals_:
            copy.start()
        segments_out(locals_)
        for i in every:
            own_half(i, locals_)

    @pl.when(opposite)
    def _():
        for copy in swaps[: 1 + chunks]:
            copy.start()

    for copy in slabs:
        copy.wait()
    tiles = pick_columns([[weights[i, slot].astype(jnp.float32) for slot in range(2)] for i in range(3)], j, c)
    for i, tile in enumerate(tiles):
        wsel_ref[:, 128 * i : 128 * (i + 1)] = tile.astype(jnp.bfloat16)
    for i, ref in enumerate((query_bias_ref, None, value_bias_ref)):
        row = jnp.zeros((1, width), jnp.float32) if ref is None else ref[...].astype(jnp.float32).reshape(1, width)
        bias_rows[i : i + 1, :] = row
    bias_pairs = [
        [bias_rows[i : i + 1, pl.ds(pl.multiple_of(index * 128, 128), 128)] for index in (j, 4 + j // 2)]
        for i in range(3)
    ]
    for i, tile in enumerate(pick_columns(bias_pairs, j, c)):
        bias_sel[0:1, 128 * i : 128 * (i + 1)] = tile

    for copy in table_copies:
        copy.wait()
    h1, h2 = 2 * j + c, 8 + j
    for i, h in enumerate((h1, h2)):
        order_ref[i : i + 1, :] = jnp.where(matched, orders_ref[h], orders_in[h])
    half = 1024 * c

    build_gather(order_ref, 0, 0, group, gather.at[pl.ds(0, group)])

    @pl.when(matched)
    def _():
        for i in every:
            relay(i)

    @pl.when(opposite)
    def _():
        segments_out(swaps)
        for i in range(chunks // 2):
            own_half(i, swaps)

    build_gather(order_ref, 1, half, group // 2, gather.at[pl.ds(group, group // 2)])

    @pl.when(matched)
    def _():
        for i in every:
            relay_end(i)

    @pl.when(opposite)
    def _():
        for i in range(chunks // 2, chunks):
            own_half(i, swaps)
        for i in range(chunks // 2):
            relay(i)

    def project(position):
        at = pl.ds(pl.multiple_of(position * block, block), block)
        out = dot(x_all[position], wsel_ref[...]) + bias_sel[0:1, :]
        ids = seg_all[position, 0:1, :].astype(jnp.float32)
        columns = [
            jnp.broadcast_to(ids[:, 128 * i : 128 * (i + 1)], (128, 128)).T for i in range(block // 128)
        ]
        lane = lanes((block, 128))
        seg_hot = hot(jnp.concatenate(columns, axis=0) == (lane % 64).astype(jnp.float32))
        low = out.astype(jnp.bfloat16)
        tok[at, 0:128] = low[:, 0:128]
        tok[at, 128:256] = jnp.where(lane < 64, low[:, 128:256], seg_hot)
        tok[at, 256:384] = low[:, 256:384]
        tok[at, 384:512] = jnp.where(lane < 64, seg_hot, low[:, 384:512])

    step = 512
    early, late = group // 2 * zh, group // 2 * (1 - zh)

    def gather_rows(start, add):
        tokens = pl.ds(pl.multiple_of(start, group // 2), group // 2)

        def one(first, columns):
            def body(k, carry):
                at = pl.ds(pl.multiple_of(k * step, step), step)
                rows = dot(gather[at, tokens], tok[tokens, columns])
                if add:
                    sorted_ref[at, :] = (rows + sorted_ref[at, :].astype(jnp.float32)).astype(jnp.bfloat16)
                else:
                    sorted_ref[at, :] = rows.astype(jnp.bfloat16)
                return carry

            return body

        lax.fori_loop(0, group // step, one(0, pl.ds(0, 256)), 0)
        lax.fori_loop(group // step, group * 3 // 2 // step, one(1, pl.ds(256, 256)), 0)

    for copy in seg_copies:
        copy.wait()
    pl.when(opposite)(wait_sibling)
    for k in range(4):
        project(4 * zh + k)

    @pl.when(opposite)
    def _():
        for i in range(chunks // 2, chunks):
            relay(i)
        for i in range(chunks // 2):
            relay_end(i)

    gather_rows(early, False)

    @pl.when(opposite)
    def _():
        for i in range(chunks // 2, chunks):
            relay_end(i)

    def build_block(i, carry):
        build_scatter(order_ref, half, member(7 - i)[1] * block, scatter.at[i % 4])
        return carry

    lax.fori_loop(0, 4, build_block, 0)
    pl.when(matched)(wait_sibling)
    for k in range(4):
        project(4 * (1 - zh) + k)
    for name in ("x", "wsel", "order"):
        stores[name].start()
    for copy in loads:
        copy.start()


    @pl.when(opposite)
    def _():
        swaps[1 + chunks].start()

    gather_rows(late, True)
    def attend(first_lanes):
        def one(i, carry):
            at = pl.ds(pl.multiple_of(i * 128, 128), 128)
            tile_zero, tile_one = sorted_ref[at, 0:128], sorted_ref[at, 128:256]
            low_lanes = lanes((128, 128)) < 64
            query_lanes = low_lanes if first_lanes else jnp.logical_not(low_lanes)
            queries = jnp.where(query_lanes, tile_zero, jnp.zeros_like(tile_zero))
            ids = jnp.where(query_lanes, jnp.zeros_like(tile_one), tile_one)
            both = dot(jnp.concatenate([queries, ids], axis=0), tile_one, 1, 1)
            scores, allowed = both[:128] * scale, both[128:]
            masked = jnp.where(allowed > 0.5, scores, NEGATIVE)
            highest = jnp.max(masked, axis=1, keepdims=True)
            raised = jnp.exp(masked - highest)
            totals = jnp.sum(raised, axis=1, keepdims=True)
            weights = raised * (1.0 / totals)
            prob_ref[at, :] = weights
            mixed = dot(weights.astype(jnp.bfloat16), tile_zero)
            att_sorted[at, :] = jnp.where(query_lanes, 0.0, mixed).astype(jnp.bfloat16)
            log_total = highest + jnp.log(totals)
            entropy = jnp.where(lanes((128, 128)) == 0, log_total, 0.0) - weights * masked
            ent_ref[pl.ds(i, 1), :] = jnp.sum(entropy, axis=0, keepdims=True)
            cnt_ref[pl.ds(i, 1), :] = jnp.sum(allowed, axis=0, keepdims=True)
            return carry

        return one

    lax.fori_loop(0, 16, attend(True), 0, unroll=UNROLL)
    lax.fori_loop(16, 24, attend(False), 0, unroll=UNROLL)
    stores["sorted"].start()
    stores["prob"].start()

    def send_back(i, carry):
        flip = 7 - i
        peer = member(flip)[0]
        att_send[flip] = dot(scatter[i % 4], att_sorted[...]).astype(jnp.bfloat16)

        @pl.when(i < 7)
        def _():
            remote(att_send.at[flip], att_in.at[p], back, flip, peer).start()

        @pl.when(i < 4)
        def _():
            build_block(i + 4, 0)

        return carry

    lax.fori_loop(0, 8, send_back, 0)
    back_copies = [remote(att_send.at[flip], att_in.at[p], back, flip, peers[flip - 1]) for flip in range(1, 8)]
    att_in[p] = att_send[0]

    stats_ref[...] = jnp.zeros_like(stats_ref)
    owner_pad[...] = jnp.full_like(owner_pad, -1.0)
    clusters = owners_ref.shape[2]
    for h, first, size, skip in ((h1, 0, clusters, 0), (h2, clusters, clusters // 2, c)):
        ids = jnp.where(matched, owners_ref[h], owners_in[h])
        owner_pad[0:1, 0:clusters] = ids.astype(jnp.float32)
        column = jnp.broadcast_to(owner_pad[0:1, :], (128, 128)).T
        column = jnp.where(skip == 1, column[clusters // 2 : clusters // 2 + size], column[0:size])
        owned = jnp.where(column == lanes((size, 128)).astype(jnp.float32), 1.0, 0.0)
        for kind, (lane_sums, divisor) in enumerate(((ent_ref, 4.0 * block), (cnt_ref, 4.0 * block * 128))):
            sums = jnp.sum(lane_sums[first : first + size, :], axis=1, keepdims=True) / divisor
            stats_ref[kind, pl.ds(h, 1), :] = jnp.sum(sums * owned, axis=0, keepdims=True)

    stores["stats"].start()
    bias_ref[0:1, :] = inner_bias_ref[...].astype(jnp.float32).reshape(1, width_inner)
    out_bias, first_gain, first_shift, outer_bias, second_gain, second_shift = (
        ref[...].astype(jnp.float32).reshape(1, width)
        for ref in (
            out_bias_ref,
            first_gain_ref,
            first_shift_ref,
            outer_bias_ref,
            second_gain_ref,
            second_shift_ref,
        )
    )
    for copy in back_copies:
        copy.wait()
    for pair in range(4):
        even, odd = att_in[pair], att_in[4 + pair]
        att_ref[:, 128 * pair : 128 * (pair + 1)] = join(half_roll(even), odd)
    for pair in range(2):
        low_half = att_in[2 * pair] + att_in[4 + 2 * pair]
        high_half = att_in[2 * pair + 1] + att_in[5 + 2 * pair]
        att_ref[:, 512 + 128 * pair : 640 + 128 * pair] = join(low_half, half_roll(high_half))
    stores["att"].start()

    loads[0].wait()
    branch = dot(att_ref[...], out_w[...]) + out_bias
    normed, root_one = normalize(x_all[p].astype(jnp.float32) + branch)
    first = normed * first_gain + first_shift
    normed_ref[...] = normed
    low_ref[...] = first.astype(jnp.bfloat16)
    stores["low"].start()
    total[...] = first + outer_bias
    for copy in loads[1:]:
        copy.wait()

    def dense_forward(t, carry):
        at = pl.ds(pl.multiple_of(t * dense_tile, dense_tile), dense_tile)
        inner = dot(low_ref[...], inner_w[:, at]) + bias_ref[0:1, at]
        cumulative = 0.5 + 0.5 * lax.erf(inner * (0.5**0.5))
        density = jnp.exp(-0.5 * inner * inner) * 0.3989422804014327
        slope[:, at] = cumulative + inner * density
        act = (inner * cumulative).astype(jnp.bfloat16)
        act_ref[:, at] = act
        total[...] += dot(act, outer_w[at, :])
        return carry

    lax.fori_loop(0, len(parts), dense_forward, 0)
    stores["act"].start()

    @pl.when(matched)
    def _():
        locals_[1 + chunks].wait()

    @pl.when(opposite)
    def _():
        swaps[1 + chunks].wait()

    normed_two, root_two = normalize(total[...])
    output_ref[...] = (normed_two * second_gain + second_shift).astype(jnp.bfloat16)
    stores["output"].start()
    upstream = cot_my[...].astype(jnp.float32)
    vec_out[4:5, :] = jnp.sum(upstream * normed_two, axis=0, keepdims=True)
    vec_out[5:6, :] = jnp.sum(upstream, axis=0, keepdims=True)
    delta_two = normalize_back(upstream * second_gain, normed_two, root_two)
    low_two = delta_two.astype(jnp.bfloat16)
    dsecond_ref[...] = low_two
    stores["dsecond"].start()
    vec_out[3:4, :] = jnp.sum(low_two.astype(jnp.float32), axis=0, keepdims=True)
    total[...] = delta_two

    def dense_back(t, carry):
        at = pl.ds(pl.multiple_of(t * dense_tile, dense_tile), dense_tile)
        dact = dot(dsecond_ref[...], outer_w[at, :], 1, 1)
        dinner = (dact * slope[:, at]).astype(jnp.bfloat16)
        dinner_ref[:, at] = dinner
        bias_ref[0:1, at] = jnp.sum(dinner.astype(jnp.float32), axis=0, keepdims=True)
        total[...] += dot(dinner, inner_w[:, at], 1, 1)
        return carry

    lax.fori_loop(0, len(parts), dense_back, 0)
    stores["dinner"].start()
    for i in range(width_inner // width):
        vec_out[6 + i : 7 + i, :] = bias_ref[0:1, width * i : width * (i + 1)]
    delta_first = total[...]
    normed = normed_ref[...]
    vec_out[1:2, :] = jnp.sum(delta_first * normed, axis=0, keepdims=True)
    vec_out[2:3, :] = jnp.sum(delta_first, axis=0, keepdims=True)
    delta_one = normalize_back(delta_first * first_gain, normed, root_one)
    delta_ref[...] = delta_one
    stores["delta"].start()
    low_one = delta_one.astype(jnp.bfloat16)
    dbranch_ref[...] = low_one
    stores["dbranch"].start()
    vec_out[0:1, :] = jnp.sum(low_one.astype(jnp.float32), axis=0, keepdims=True)
    vec_out[10:16, :] = jnp.zeros((6, width), jnp.float32)
    stores["vec"].start()
    datt_ref[...] = dot(dbranch_ref[...], out_w[...], 1, 1).astype(jnp.bfloat16)
    stores["datt"].start()
    for copy in stores.values():
        copy.wait()
    for copy in own_to_s + x_to_s + z_to_s + d_to_s:
        copy.wait_send()


def forward_layer(tokens, cotangent, segments, orders, owners, vectors, weights):
    block, width = tokens.shape
    inner_width = weights[4].shape[1]
    group = 8 * block
    low, full = jnp.bfloat16, jnp.float32
    vmem = pl.BlockSpec(memory_space=pltpu.VMEM)
    hbm = pl.BlockSpec(memory_space=pl.ANY)
    dma = pltpu.SemaphoreType.DMA
    rows = group * 3 // 2
    kept = [
        ((width, 512), low),
        ((8, group), jnp.int32),
        ((2, 16, 128), full),
        ((8, block, width), low),
        ((rows, 256), low),
        ((rows, 128), full),
        ((block, width), low),
        ((block, width), low),
        ((block, inner_width), low),
        ((block, width), low),
        ((block, width), low),
        ((block, inner_width), low),
        ((block, width), full),
        ((block, width), low),
        ((16, width), full),
        ((block, width), low),
    ]
    return pl.pallas_call(
        forward_kernel,
        out_shape=[jax.ShapeDtypeStruct(*one) for one in kept],
        in_specs=[vmem] * 14 + [hbm] * 6,
        out_specs=[hbm] * len(kept),
        scratch_shapes=[pltpu.VMEM(*one) for one in kept]
        + [
            pltpu.VMEM((block, width), low),
            pltpu.VMEM((3, 2, width, 128), low),
            pltpu.VMEM(orders.shape, jnp.int32),
            pltpu.VMEM(owners.shape, jnp.int32),
            pltpu.VMEM((8, 128), full),
            pltpu.VMEM((8, block), jnp.int32),
            pltpu.VMEM((8, 8, block), jnp.int32),
            pltpu.VMEM((8, width), full),
            pltpu.VMEM((8, 512), full),
            pltpu.VMEM((group, 512), low),
            pltpu.VMEM((rows, group), low),
            pltpu.VMEM((4, block, rows), low),
            pltpu.VMEM((rows, 128), low),
            pltpu.VMEM((8, block, 128), low),
            pltpu.VMEM((8, block, 128), low),
            pltpu.VMEM((24, 128), full),
            pltpu.VMEM((24, 128), full),
            dma((2 * PIECES + 6,)),
            dma((2 * PIECES + 6,)),
            dma((7 * PIECES,)),
            dma((7 * PIECES,)),
            dma((7,)),
            dma((7,)),
            dma((8,)),
            dma((8,)),
            dma((6,)),
            pltpu.VMEM(weights[3].shape, low),
            pltpu.VMEM(weights[4].shape, low),
            pltpu.VMEM(weights[5].shape, low),
            pltpu.VMEM((block, inner_width), full),
            pltpu.VMEM((block, width), full),
            pltpu.VMEM((block, width), full),
            pltpu.VMEM((8, inner_width), full),
            dma((1 + inner_width // width,)),
            dma((len(kept),)),
        ],
        compiler_params=pltpu.CompilerParams(
            collective_id=1, has_side_effects=True, vmem_limit_bytes=62 << 20
        ),
        name="forward_layer",
    )(tokens, cotangent, segments, orders, owners, *vectors, *weights)


def rows_of(start, q, size):
    return pl.ds(pl.multiple_of(start * q, 16), size * q)


def add_into(count, target, other):
    def one(i, carry):
        target(i)[...] = (
            target(i)[...].astype(jnp.float32) + other(i)[...].astype(jnp.float32)
        ).astype(jnp.bfloat16)
        return carry

    lax.fori_loop(0, count, one, 0)


def reduce_steps(parts, g_ref, f_ref, f_hbm, buffers, sems, out_sem):
    core_in, a_one, a_two, a_three, a_four, b_one, b_two, b_three, b_four = buffers
    zh, zl, x, y, c = coordinates()
    q = g_ref.shape[3] // 8
    width = g_ref.shape[4] // parts
    over_c, over_y = device(zh, zl, x, y, 1 - c), device(zh, zl, x, 1 - y, c)
    over_x, over_zl = device(zh, zl, 1 - x, y, c), device(zh, 1 - zl, x, y, c)
    over_zh = device(1 - zh, zl, x, y, c)
    flying, outward = {}, []

    def send(name, k, src, dst, peer):
        copy = remote(src, dst, (sems[0].at[name], sems[1].at[name]), k, peer)
        copy.start()
        flying[name, k] = copy

    def arrive(name, k):
        flying.pop((name, k)).wait()

    def step(stage, k):
        cols = pl.ds(k * width, width)
        if stage == "0":
            send(
                0, k, g_ref.at[:, :, :, rows_of(4 * (1 - c), q, 4), cols], core_in.at[:, :, :, :, cols], over_c
            )
        if stage == "1":
            arrive(0, k)
            add_into(
                8,
                lambda i: core_in.at[i // 4, (i // 2) % 2, i % 2, :, cols],
                lambda i: g_ref.at[i // 4, (i // 2) % 2, i % 2, rows_of(4 * c, q, 4), cols],
            )
            send(1, k, core_in.at[:, :, 1 - x, pl.ds(0, 2 * q), cols], a_one.at[:, :, :, cols], over_x)
            send(2, k, core_in.at[:, :, :, rows_of(3 - y, q, 1), cols], b_one.at[:, :, :, :, cols], over_y)
        if stage == "2a":
            arrive(1, k)
            add_into(
                4,
                lambda i: a_one.at[i // 2, i % 2, :, cols],
                lambda i: core_in.at[i // 2, i % 2, x, pl.ds(0, 2 * q), cols],
            )
            send(3, k, a_one.at[:, 1 - zl, :, cols], a_two.at[:, :, cols], over_zl)
        if stage == "3a":
            arrive(3, k)
            add_into(2, lambda i: a_two.at[i, :, cols], lambda i: a_one.at[i, zl, :, cols])
            send(4, k, a_two.at[1 - zh, :, cols], a_three.at[:, cols], over_zh)
        if stage == "4a":
            arrive(4, k)
            add_into(1, lambda i: a_three.at[:, cols], lambda i: a_two.at[zh, :, cols])
            send(5, k, a_three.at[:, cols], a_four.at[:, cols], over_y)
        if stage == "2b":
            arrive(2, k)
            add_into(
                8,
                lambda i: b_one.at[i // 4, (i // 2) % 2, i % 2, :, cols],
                lambda i: core_in.at[i // 4, (i // 2) % 2, i % 2, rows_of(2 + y, q, 1), cols],
            )
            send(6, k, b_one.at[:, :, 1 - x, :, cols], b_two.at[:, :, :, cols], over_x)
        if stage == "3":
            arrive(6, k)
            add_into(
                4,
                lambda i: b_two.at[i // 2, i % 2, :, cols],
                lambda i: b_one.at[i // 2, i % 2, x, :, cols],
            )
            send(7, k, b_two.at[:, 1 - zl, :, cols], b_three.at[:, :, cols], over_zl)
        if stage == "4":
            arrive(7, k)
            add_into(2, lambda i: b_three.at[i, :, cols], lambda i: b_two.at[i, zl, :, cols])
            send(8, k, b_three.at[1 - zh, :, cols], b_four.at[:, cols], over_zh)
        if stage == "5":
            arrive(8, k)
            f_ref[c, 1, y, :, cols] = (
                b_four[:, cols].astype(jnp.float32) + b_three[zh, :, cols].astype(jnp.float32)
            ).astype(jnp.bfloat16)
            own_rows = f_ref.at[c, 1, y, :, cols]
            send(9, k, own_rows, own_rows, over_y)
        if stage == "6":
            arrive(5, k)
            for half in range(2):
                at = pl.ds(half * q, q)
                f_ref[c, 0, half, :, cols] = (
                    a_three[at, cols].astype(jnp.float32) + a_four[at, cols].astype(jnp.float32)
                ).astype(jnp.bfloat16)
            arrive(9, k)
            both = f_ref.at[c, :, :, :, cols]
            send(10, k, both, both, over_c)
        if stage == "7":
            arrive(10, k)
            copy = pltpu.make_async_copy(f_ref.at[:, :, :, :, cols], f_hbm.at[:, :, :, :, cols], out_sem.at[k])
            copy.start()
            outward.append(copy)

    return step, outward


BACKWARD_ORDER = (
    "begin",
    "home0",
    "datt",
    "g1",
    "S0",
    "g2",
    "bld:0",
    "r1:0",
    "st:0",
    "bld:1",
    "take:0",
    "r1:1",
    "r1:2",
    "hE0",
    "bld:2",
    "take:2",
    "r1:3",
    "r1:4",
    "take:1",
    "r2b:0",
    "r1:5",
    "st:1",
    "r2a:0",
    "bld:4",
    "take:4",
    "bld:3",
    "r2b:1",
    "r2a:1",
    "take:3",
    "bld:5",
    "take:5",
    "at:1",
    "at:0",
    "r2a:2",
    "r2b:2",
    "at:2",
    "r2a:3",
    "r3a:0",
    "pl",
    "r3a:2",
    "r2b:4",
    "r2a:4",
    "r3a:1",
    "r2b:3",
    "r3a:3",
    "r4a:0",
    "r3:0",
    "ph",
    "r4a:2",
    "st:2",
    "r3a:4",
    "r2b:5",
    "ab:0",
    "dw",
    "r4a:3",
    "st:3",
    "r4:0",
    "r3:2",
    "r3:1",
    "r2a:5",
    "ab:1",
    "r4a:4",
    "r4a:1",
    "st:4",
    "r3:4",
    "hb:0",
    "r5:0",
    "r4:2",
    "r3:3",
    "r4:1",
    "r3:5",
    "r3a:5",
    "da",
    "ha:0",
    "hb:1",
    "r4:4",
    "r5:2",
    "stE",
    "r6:0",
    "r4:3",
    "ha:1",
    "r5:1",
    "r6:2",
    "r7:0",
    "r4:5",
    "r6:1",
    "r7:2",
    "r4a:5",
    "r7:1",
    "wy",
    "hm:0",
    "r5:4",
    "r5:3",
    "hm:1",
    "r5:5",
    "wc",
    "r6:4",
    "r6:3",
    "hE:0",
    "r6:5",
    "wE",
    "r7:4",
    "r7:3",
    "r7:5",
    "hE:1",
)


def backward_kernel(
    parts,
    datt_hbm,
    order_hbm,
    out_my,
    stats_hbm,
    vec_hbm,
    att_hbm,
    dbranch_hbm,
    low_hbm,
    dsecond_hbm,
    act_hbm,
    dinner_hbm,
    sorted_hbm,
    prob_hbm,
    wsel_hbm,
    x_hbm,
    delta_hbm,
    out_home,
    grad_home,
    f_hbm,
    w_hbm,
    stats_out,
    datt_ref,
    att_ref,
    dbranch_ref,
    vec_ref,
    low_ref,
    dsecond_ref,
    act_ref,
    dinner_ref,
    order_ref,
    stats_ref,
    sorted_ref,
    prob_ref,
    wsel_ref,
    x_all,
    delta_ref,
    f_ref,
    w_all,
    g_ref,
    datt_send,
    datt_in,
    gather,
    gathered,
    dsorted,
    scatter,
    dqkv,
    part_send,
    part_in,
    total,
    a_in,
    b_in,
    a_two,
    b_two,
    grad_my,
    dw,
    dw_y,
    dw_in,
    dw_all,
    stats_buf,
    stats_in,
    core_in,
    r_a_one,
    r_a_two,
    r_a_three,
    r_a_four,
    r_b_one,
    r_b_two,
    r_b_three,
    r_b_four,
    datt_ssem,
    datt_rsem,
    part_ssem,
    part_rsem,
    swap_ssem,
    swap_rsem,
    dw_ssem,
    dw_rsem,
    stats_ssem,
    stats_rsem,
    red_ssem,
    red_rsem,
    load_sem,
    out_sem,
):
    zh, zl, x, y, c = coordinates()
    s = 4 * zh + 2 * zl + x
    j = 2 * zl + x
    p = 4 * c + j
    block, width = datt_ref.shape
    group = 8 * block
    scale = 0.125
    matched = c == zh
    datt_sems, part_sems = (datt_ssem, datt_rsem), (part_ssem, part_rsem)
    swap_sems, dw_sems, stats_sems = (swap_ssem, swap_rsem), (dw_ssem, dw_rsem), (stats_ssem, stats_rsem)

    def member(flip):
        fc, fz, fx = flip // 4, (flip // 2) % 2, flip % 2
        mc, mz, mx = bits(c, fc), bits(zl, fz), bits(x, fx)
        return device(zh, mz, mx, y, mc), mc, 2 * mz + mx

    peers = [member(flip)[0] for flip in range(1, 8)]
    sibling, over_x, over_z = peers[3], peers[0], peers[1]
    swap_peer = device(1 - zh, zl, x, y, 1 - c)
    over_y = device(zh, zl, x, 1 - y, c)
    across = [device(1 - zh, bits(zl, f // 2), bits(x, f % 2), y, c) for f in range(4)]
    everyone = peers + [swap_peer, over_y] + across
    barrier = pltpu.get_barrier_semaphore()
    for peer in everyone:
        pl.semaphore_signal(barrier, inc=1, device_id=peer, device_id_type=MESH)
    loads = [
        pltpu.make_async_copy(src, dst, load_sem.at[i])
        for i, (src, dst) in enumerate(
            (
                (datt_hbm, datt_ref),
                (att_hbm, att_ref),
                (dbranch_hbm, dbranch_ref),
                (vec_hbm, vec_ref),
                (low_hbm, low_ref),
                (dsecond_hbm, dsecond_ref),
                (act_hbm, act_ref),
                (dinner_hbm, dinner_ref),
                (order_hbm, order_ref),
                (stats_hbm, stats_ref),
                (sorted_hbm, sorted_ref),
                (prob_hbm, prob_ref),
                (wsel_hbm, wsel_ref),
                (x_hbm, x_all),
                (delta_hbm, delta_ref),
            )
        )
    ]
    for copy in loads:
        copy.start()

    def home_copy(src, dst, index, start):
        away = remote(src, dst, swap_sems, index, swap_peer)
        here = pltpu.make_async_copy(src, dst, swap_rsem.at[3 + index])

        @pl.when(matched)
        def _():
            here.start() if start else here.wait()

        @pl.when(jnp.logical_not(matched))
        def _():
            away.start() if start else away.wait()

    def tile(mc, mj):
        first = datt_ref[:, pl.ds(pl.multiple_of(mj * 128, 128), 128)]
        other = datt_ref[:, pl.ds(pl.multiple_of((4 + mj // 2) * 128, 128), 128)]
        return join(
            select_head(other.astype(jnp.float32), mj % 2, 0), select_head(first.astype(jnp.float32), mc, 1)
        ).astype(jnp.bfloat16)

    datt_copies = []

    def datt_tiles():
        loads[0].wait()
        for flip in range(1, 8):
            peer, mc, mj = member(flip)
            datt_send[flip] = tile(mc, mj)
            datt_copies.append(remote(datt_send.at[flip], datt_in.at[p], datt_sems, flip - 1, peer))
        datt_in[p] = tile(c, j)

    def datt_out():
        for flip in (3, 7, 1, 5, 2, 6, 4):
            datt_copies[flip - 1].start()

    stats_peers = (sibling, over_x, over_z, across[0], over_y)
    stats_copies = [
        remote(stats_buf.at[k], stats_in.at[k], stats_sems, k, peer) for k, peer in enumerate(stats_peers)
    ]

    def stats_step(k):
        if k == 0:
            loads[9].wait()
            stats_buf[0] = stats_ref[...]
        else:
            stats_copies[k - 1].wait()
            stats_buf[k] = stats_buf[k - 1] + stats_in[k - 1]
        if k < len(stats_peers):
            stats_copies[k].start()
        else:
            copy = pltpu.make_async_copy(stats_buf.at[k], stats_out, out_sem.at[parts])
            copy.start()
            outward.append(copy)

    share = width // 8
    q = g_ref.shape[3] // 8
    top = 4 * q

    def outer_grads():
        def one(d, carry):
            columns = pl.ds(pl.multiple_of(d * 4 * share, 128), 4 * share)
            g_ref[d // 4, (d // 2) % 2, d % 2, top : top + 4 * share, :] = dot(
                act_ref[:, columns], dsecond_ref[...], 0, 0
            ).astype(jnp.bfloat16)
            return carry

        lax.fori_loop(0, 8, one, 0)

    def inner_grads():
        def one(i, carry):
            z, n = i // 4, i % 4
            rows = pl.ds(pl.multiple_of(z * 4 * share, 128), 4 * share)
            columns = pl.ds(pl.multiple_of(n * width, 128), width)
            grads = dot(low_ref[:, rows], dinner_ref[:, columns], 0, 0).astype(jnp.bfloat16)
            for k in range(4):
                at = pl.ds(pl.multiple_of(n * share, 16), share)
                g_ref[z, k // 2, k % 2, at, :] = grads[share * k : share * (k + 1)]
            return carry

        lax.fori_loop(0, 8, one, 0)

    def out_grads():
        for copy in loads[1:4]:
            copy.wait()
        vectors = vec_ref[...].astype(jnp.bfloat16)
        for z in range(2):
            columns = slice(4 * share * z, 4 * share * (z + 1))
            grads = dot(att_ref[:, columns], dbranch_ref[...], 0, 0).astype(jnp.bfloat16)
            for k in range(4):
                rows = grads[share * k : share * (k + 1)]
                g_ref[z, k // 2, k % 2, 4 * share : 4 * share + share // 2, :] = rows[: share // 2]
                g_ref[z, k // 2, k % 2, 4 * share + share // 2 : top, :] = jnp.zeros_like(vectors)
                g_ref[z, k // 2, k % 2, top + 4 * share : top + 4 * share + share // 2, :] = rows[share // 2 :]
                g_ref[z, k // 2, k % 2, top + 4 * share + share // 2 :, :] = vectors

    def grads_first():
        for copy in loads[4:9]:
            copy.wait()
        pl.when(c == 0)(outer_grads)
        pl.when(c == 1)(inner_grads)

    def grads_second():
        pl.when(c == 0)(inner_grads)
        pl.when(c == 1)(outer_grads)

    reduction, outward = reduce_steps(
        parts,
        g_ref,
        f_ref,
        f_hbm,
        (core_in, r_a_one, r_a_two, r_a_three, r_a_four, r_b_one, r_b_two, r_b_three, r_b_four),
        (red_ssem, red_rsem),
        out_sem,
    )

    half = 1024 * c
    step = gather.shape[1]
    chunks = group * 3 // 2 // step

    def build(k):
        head, start = (0, k * step) if k * step < group else (1, half + k * step - group)
        build_gather(order_ref, head, start, step, gather.at[k % 2])

    arrivals = []

    def take(k):
        if not arrivals:
            for copy in datt_copies:
                copy.wait()
            arrivals.append(True)
        gathered[k * step : (k + 1) * step, :] = dot(
            gather[k % 2], datt_in[...].reshape(group, 128)
        ).astype(jnp.bfloat16)

    def attend_back(first_lanes):
        def one(i, carry):
            at = pl.ds(pl.multiple_of(i * 128, 128), 128)
            tile_zero, tile_one = sorted_ref[at, 0:128], sorted_ref[at, 128:256]
            low_lanes = lanes((128, 128)) < 64
            query_lanes = low_lanes if first_lanes else jnp.logical_not(low_lanes)
            weights = prob_ref[at, :]
            taken = gathered[at, :]
            taken = jnp.where(query_lanes, jnp.zeros_like(taken), taken)
            weight_grads = dot(taken, tile_zero, 1, 1)
            inside = jnp.sum(weights * weight_grads, axis=1, keepdims=True)
            score_grads = weights * (weight_grads - inside)
            low_grads = score_grads.astype(jnp.bfloat16)
            query_grads = dot(low_grads, tile_one) * scale
            key_grads = dot(low_grads, tile_zero, 0, 0) * scale
            value_grads = dot(weights.astype(jnp.bfloat16), taken, 0, 0)
            dsorted[at, 0:128] = jnp.where(query_lanes, query_grads, value_grads).astype(jnp.bfloat16)
            dsorted[at, 128:256] = jnp.where(query_lanes, key_grads, 0.0).astype(jnp.bfloat16)
            return carry

        return one

    loaded = []

    def attend_some(i):
        if not loaded:
            for copy in loads[10:]:
                copy.wait()
            loaded.append(True)
        lax.fori_loop(8 * i, 8 * i + 8, attend_back(i < 2), 0, unroll=4)

    def place(position):
        token = lax.broadcasted_iota(jnp.int32, (128, 128), 0) + position * block
        for t in range(block // 128):
            for head, start, count, base in ((0, 0, group, 0), (1, half, group // 2, group)):
                for k in range(count // 128):
                    ids = order_ref[head : head + 1, pl.ds(pl.multiple_of(start + 128 * k, 128), 128)]
                    scatter[128 * t : 128 * (t + 1), base + 128 * k : base + 128 * (k + 1)] = hot(
                        ids == token + 128 * t
                    )
        at = pl.ds(pl.multiple_of(position * block, block), block)
        dqkv[at, 0:256] = dot(scatter[:, 0:group], dsorted[0:group, :]).astype(jnp.bfloat16)
        dqkv[at, 256:512] = dot(scatter[:, group:], dsorted[group:, :]).astype(jnp.bfloat16)
        return dot(dqkv[at, :], wsel_ref[...], 1, 1)

    def part_copy(k):
        return remote(part_send.at[k], part_in.at[k], part_sems, k, sibling)

    def parts_away():
        def one(k, carry):
            part_send[k] = place(4 * (1 - c) + k).astype(jnp.bfloat16)
            part_copy(k).start()
            return carry

        lax.fori_loop(0, 4, one, 0)

    def parts_here():
        def one(k, carry):
            part = place(4 * c + k)
            part_copy(k).wait()
            total[k // 2, k % 2] = (part + part_in[k].astype(jnp.float32)).astype(jnp.bfloat16)
            return carry

        lax.fori_loop(0, 4, one, 0)

    upper, lower = pl.ds(0, block // 2), pl.ds(block // 2, block // 2)
    pieces = [pl.ds(i * (width // 2), width // 2) for i in range(2)]
    a_copies = [
        remote(total.at[:, 1 - x, upper, cols], a_in.at[:, :, cols], part_sems, 4 + i, over_x)
        for i, cols in enumerate(pieces)
    ]
    b_copies = [
        remote(total.at[1 - zl, :, lower, cols], b_in.at[:, :, cols], part_sems, 6 + i, over_z)
        for i, cols in enumerate(pieces)
    ]
    a_next = [
        remote(a_in.at[1 - zl, :, cols], a_two.at[:, cols], part_sems, 8 + i, over_z)
        for i, cols in enumerate(pieces)
    ]
    b_next = [
        remote(b_in.at[1 - x, :, cols], b_two.at[:, cols], part_sems, 10 + i, over_x)
        for i, cols in enumerate(pieces)
    ]

    def first_hops(i):
        a_copies[i].start()
        b_copies[i].start()

    def second_hop_a(i):
        cols = pieces[i]
        a_copies[i].wait()
        add_into(2, lambda k: a_in.at[k, :, cols], lambda k: total.at[k, x, upper, cols])
        a_next[i].start()

    def second_hop_b(i):
        cols = pieces[i]
        b_copies[i].wait()
        add_into(2, lambda k: b_in.at[k, :, cols], lambda k: total.at[zl, k, lower, cols])
        b_next[i].start()

    def grad_home_start(i):
        cols = pieces[i]
        a_next[i].wait()
        b_next[i].wait()
        for start, first, second, index in ((0, a_two, a_in, zl), (block // 2, b_two, b_in, x)):
            at = pl.ds(start, block // 2)
            grad_my[at, cols] = (
                delta_ref[at, cols]
                + first[:, cols].astype(jnp.float32)
                + second[index, :, cols].astype(jnp.float32)
            ).astype(jnp.bfloat16)
        home_copy(grad_my.at[:, cols], grad_home.at[:, cols], 1 + i, True)

    def grad_home_end(i):
        cols = pieces[i]
        home_copy(grad_my.at[:, cols], grad_home.at[:, cols], 1 + i, False)

    over_y_copy = remote(dw_y.at[1 - y], dw_in, dw_sems, 0, over_y)

    def projections():
        for k in range(width // 128):
            dw[128 * k : 128 * (k + 1), :] = dot(
                x_all[:, 128 * k : 128 * (k + 1)], dqkv[...], 0, 0
            ).astype(jnp.bfloat16)
        bias_row = jnp.broadcast_to(
            jnp.sum(dqkv[...].astype(jnp.float32), axis=0, keepdims=True), (16, 512)
        ).astype(jnp.bfloat16)
        for d in range(8):
            for h in range(2):
                dw_y[h, d, 0:share, :] = dw[share * d : share * (d + 1), 256 * h : 256 * (h + 1)]
                dw_y[h, d, share : share + 16, :] = bias_row[:, 256 * h : 256 * (h + 1)]
        over_y_copy.start()

    targets = across + [over_x, over_z, peers[2]]
    flips = [(1, f // 2, f % 2) for f in range(4)] + [(0, 0, 1), (0, 1, 0), (0, 1, 1)]
    dw_copies = []
    for i, (peer, (fh, fz, fx)) in enumerate(zip(targets, flips)):
        d = 4 * bits(zh, fh) + 2 * bits(zl, fz) + bits(x, fx)
        dw_copies.append(remote(dw_y.at[y, d], dw_all.at[s], dw_sems, 1 + i, peer))
    w_over_y = remote(w_all.at[y, c], w_all.at[y, c], dw_sems, 8, over_y)
    w_over_c = remote(w_all.at[:, c], w_all.at[:, c], dw_sems, 9, sibling)

    def dw_exchange():
        over_y_copy.wait()
        add_into(8, lambda i: dw_y.at[y, i], lambda i: dw_in.at[i])
        for copy in dw_copies:
            copy.start()
        dw_all[s] = dw_y[y, s]

    def dw_sum():
        for copy in dw_copies:
            copy.wait()
        for k in range(4):
            w_all[y, c, k] = (dw_all[k].astype(jnp.float32) + dw_all[4 + k].astype(jnp.float32)).astype(
                jnp.bfloat16
            )
        w_over_y.start()

    def dw_core():
        w_over_y.wait()
        w_over_c.start()

    def dw_end():
        w_over_c.wait()
        copy = pltpu.make_async_copy(w_all, w_hbm, out_sem.at[parts + 1])
        copy.start()
        outward.append(copy)

    def begin():
        datt_tiles()
        out_grads()
        pl.semaphore_wait(barrier, len(everyone))

    def start_reduction():
        for k in range(parts):
            reduction("0", k)

    single = {
        "begin": begin,
        "datt": datt_out,
        "home0": lambda: home_copy(out_my, out_home, 0, True),
        "hE0": lambda: home_copy(out_my, out_home, 0, False),
        "g1": grads_first,
        "g2": grads_second,
        "S0": start_reduction,
        "pl": parts_away,
        "ph": parts_here,
        "dw": projections,
        "da": dw_exchange,
        "wy": dw_sum,
        "wc": dw_core,
        "wE": dw_end,
        "stE": lambda: stats_step(5),
    }
    indexed = {
        "bld": build,
        "take": take,
        "at": attend_some,
        "ab": first_hops,
        "ha": second_hop_a,
        "hb": second_hop_b,
        "hm": grad_home_start,
        "hE": grad_home_end,
        "st": stats_step,
    }
    for name in BACKWARD_ORDER:
        kind, _, index = name.partition(":")
        if kind in single:
            single[kind]()
        elif kind in indexed:
            indexed[kind](int(index))
        else:
            reduction(kind[1:], int(index))
    for copy in outward:
        copy.wait()


def backward_attention(
    datt,
    order,
    output,
    stats,
    vectors,
    att,
    dbranch,
    low_first,
    dsecond,
    act,
    dinner,
    sorted_rows,
    prob,
    wsel,
    x_all,
    delta,
    parts,
):
    block, width = datt.shape
    inner_width = act.shape[1]
    group = 8 * block
    rows = group * 3 // 2
    q = (9 * width // 8 + 32) // 8
    share = width // 8 + 16
    low, full = jnp.bfloat16, jnp.float32
    vmem = pl.BlockSpec(memory_space=pltpu.VMEM)
    hbm = pl.BlockSpec(memory_space=pl.ANY)
    dma = pltpu.SemaphoreType.DMA
    shape = jax.ShapeDtypeStruct
    return pl.pallas_call(
        functools.partial(backward_kernel, parts),
        out_shape=[
            shape((block, width), low),
            shape((block, width), low),
            shape((2, 2, 2, q, width), low),
            shape((2, 2, 4, share, 256), low),
            shape(stats.shape, full),
        ],
        in_specs=[hbm] * 16,
        out_specs=[hbm] * 5,
        scratch_shapes=[
            pltpu.VMEM((block, width), low),
            pltpu.VMEM((block, width), low),
            pltpu.VMEM((block, width), low),
            pltpu.VMEM(vectors.shape, full),
            pltpu.VMEM((block, width), low),
            pltpu.VMEM((block, width), low),
            pltpu.VMEM((block, inner_width), low),
            pltpu.VMEM((block, inner_width), low),
            pltpu.VMEM(order.shape, order.dtype),
            pltpu.VMEM(stats.shape, full),
            pltpu.VMEM((rows, 256), low),
            pltpu.VMEM((rows, 128), full),
            pltpu.VMEM((width, 512), low),
            pltpu.VMEM((group, width), low),
            pltpu.VMEM((block, width), full),
            pltpu.VMEM((2, 2, 2, q, width), low),
            pltpu.VMEM((2, 2, 4, share, 256), low),
            pltpu.VMEM((2, 2, 2, 8 * q, width), low),
            pltpu.VMEM((8, block, 128), low),
            pltpu.VMEM((8, block, 128), low),
            pltpu.VMEM((2, 512, group), low),
            pltpu.VMEM((rows, 128), low),
            pltpu.VMEM((rows, 256), low),
            pltpu.VMEM((block, rows), low),
            pltpu.VMEM((group, 512), low),
            pltpu.VMEM((4, block, width), low),
            pltpu.VMEM((4, block, width), low),
            pltpu.VMEM((2, 2, block, width), low),
            pltpu.VMEM((2, block // 2, width), low),
            pltpu.VMEM((2, block // 2, width), low),
            pltpu.VMEM((block // 2, width), low),
            pltpu.VMEM((block // 2, width), low),
            pltpu.VMEM((block, width), low),
            pltpu.VMEM((width, 512), low),
            pltpu.VMEM((2, 8, share, 256), low),
            pltpu.VMEM((8, share, 256), low),
            pltpu.VMEM((8, share, 256), low),
            pltpu.VMEM((6,) + stats.shape, full),
            pltpu.VMEM((5,) + stats.shape, full),
            pltpu.VMEM((2, 2, 2, 4 * q, width), low),
            pltpu.VMEM((2, 2, 2 * q, width), low),
            pltpu.VMEM((2, 2 * q, width), low),
            pltpu.VMEM((2 * q, width), low),
            pltpu.VMEM((2 * q, width), low),
            pltpu.VMEM((2, 2, 2, q, width), low),
            pltpu.VMEM((2, 2, q, width), low),
            pltpu.VMEM((2, q, width), low),
            pltpu.VMEM((q, width), low),
            dma((7,)),
            dma((7,)),
            dma((12,)),
            dma((12,)),
            dma((6,)),
            dma((6,)),
            dma((10,)),
            dma((10,)),
            dma((5,)),
            dma((5,)),
            dma((11, parts)),
            dma((11, parts)),
            dma((15,)),
            dma((parts + 2,)),
        ],
        compiler_params=pltpu.CompilerParams(
            collective_id=2, has_side_effects=True, vmem_limit_bytes=62 << 20
        ),
        name="backward_attention",
    )(
        datt,
        order,
        output,
        stats,
        vectors,
        att,
        dbranch,
        low_first,
        dsecond,
        act,
        dinner,
        sorted_rows,
        prob,
        wsel,
        x_all.reshape(group, width),
        delta,
    )


def finish_kernel(
    f_ref,
    w_ref,
    out_ref,
    grad_ref,
    stats_ref,
    output,
    grad_tokens,
    gq_out,
    gqb_out,
    gk_out,
    gv_out,
    gvb_out,
    go_out,
    gob_out,
    gfg_out,
    gfs_out,
    gi_out,
    gib_out,
    gu_out,
    gub_out,
    gsg_out,
    gss_out,
    stats_out,
    gq_ref,
    gv_ref,
    vec_ref,
    square,
):
    s = lax.axis_index("seq")
    output[0] = out_ref[...]
    grad_tokens[0] = grad_ref[...]
    for kind in range(2):
        square[0:16, :] = stats_ref[kind]
        stats_out[kind] = square[...].T[: stats_out.shape[1], : stats_out.shape[2]]
    share, width = gk_out.shape
    top = f_ref.shape[0] // 2
    full = jnp.float32
    for n in range(gi_out.shape[1] // width):
        gi_out[:, n * width : (n + 1) * width] = f_ref[n * share : (n + 1) * share, :].astype(full)
    gu_out[...] = f_ref[top : top + 4 * share, :].astype(full)
    part = share // 2
    go_out[0:part, :] = f_ref[4 * share : 4 * share + part, :].astype(full)
    go_out[part:, :] = f_ref[top + 4 * share : top + 4 * share + part, :].astype(full)
    vec_ref[...] = f_ref[top + 4 * share + part :, :].astype(full)
    for pair in range(4):
        at = slice(128 * pair, 128 * pair + 128)
        low, high = (w_ref[0, core, pair].astype(full) for core in range(2))
        gq_ref[:, at] = join(low[:, 0:128], half_roll(high[:, 0:128]))
        gk_out[:, at] = join(low[:, 128:256], half_roll(high[:, 128:256]))[:share]
        gv_ref[:, at] = join(half_roll(low[:, 0:128]), high[:, 0:128])
    for pair in range(2):
        at = slice(512 + 128 * pair, 640 + 128 * pair)
        low, high = (
            w_ref[1, 0, 2 * pair + i].astype(full) + w_ref[1, 1, 2 * pair + i].astype(full) for i in range(2)
        )
        gq_ref[:, at] = join(half_roll(low[:, 0:128]), high[:, 0:128])
        gk_out[:, at] = join(half_roll(low[:, 128:256]), high[:, 128:256])[:share]
        gv_ref[:, at] = join(low[:, 0:128], half_roll(high[:, 0:128]))
    gq_out[...] = gq_ref[:share, :]
    gv_out[...] = gv_ref[:share, :]

    def mine(rows):
        return pltpu.roll(rows, width - share * s, 1)[:, :share]

    short = mine(vec_ref[...])
    for row, ref in enumerate((gob_out, gfg_out, gfs_out, gub_out, gsg_out, gss_out)):
        ref[...] = short[row]
    gqb_out[...] = mine(gq_ref[share : share + 8, :])[0]
    gvb_out[...] = mine(gv_ref[share : share + 8, :])[0]
    row = vec_ref[pl.ds(6 + s // 2, 1), :]
    gib_out[...] = jnp.where(s % 2 == 1, row[:, 4 * share :], row[:, : 4 * share])[0]


def finish(reduced, w_all, output, grad, totals, head_count, inner_width):
    block, width = output.shape
    row_count = 8 * reduced.shape[3]
    share = width // 8
    low, full = jnp.bfloat16, jnp.float32
    vmem = pl.BlockSpec(memory_space=pltpu.VMEM)
    shape = jax.ShapeDtypeStruct
    square, vector = shape((share, width), full), shape((share,), full)
    out_shape = [
        shape((1, block, width), low),
        shape((1, block, width), low),
        square,
        vector,
        square,
        square,
        vector,
        square,
        vector,
        vector,
        vector,
        shape((share, inner_width), full),
        shape((inner_width // 8,), full),
        shape((inner_width // 8, width), full),
        vector,
        vector,
        vector,
        shape((2, 8, head_count), full),
    ]
    outs = pl.pallas_call(
        finish_kernel,
        out_shape=out_shape,
        in_specs=[vmem] * 5,
        out_specs=[vmem] * len(out_shape),
        scratch_shapes=[
            pltpu.VMEM((share + 16, width), full),
            pltpu.VMEM((share + 16, width), full),
            pltpu.VMEM((16, width), full),
            pltpu.VMEM((128, 128), full),
        ],
        compiler_params=pltpu.CompilerParams(vmem_limit_bytes=60 << 20),
        name="finish",
    )(reduced.reshape(row_count, width), w_all, output, grad, totals)
    return (*outs[:-1], outs[-1].transpose(0, 2, 1))


def body(
    tokens,
    segments,
    orders,
    owners,
    query_weight,
    query_bias,
    key_weight,
    value_weight,
    value_bias,
    out_weight,
    out_bias,
    first_gain,
    first_shift,
    inner_weight,
    inner_bias,
    outer_weight,
    outer_bias,
    second_gain,
    second_shift,
    cotangent,
):
    seq_count = lax.axis_size("seq")
    groups = lax.axis_size("rep")
    own_index = lax.axis_index("seq")
    row_count = tokens.shape[1]
    model_width = tokens.shape[2]
    order_table = orders[0]
    owner_table = owners[0]
    head_count, group_tokens = order_table.shape
    cluster_count = owner_table.shape[1]
    cluster = group_tokens // cluster_count
    head_dim = model_width // head_count
    per_owner = row_count // cluster
    score_scale = head_dim ** (-0.5)
    flat_tokens = tokens[0]
    local_index = jnp.arange(row_count, dtype=jnp.int32)
    factor = 1
    for candidate in range(1, seq_count + 1):
        if seq_count % candidate == 0 and candidate * row_count <= 2048:
            factor = candidate
    block_count = seq_count // factor
    block_width = factor * row_count
    order_blocks = order_table.reshape(head_count, block_count, block_width).transpose(1, 0, 2)
    owner_blocks = (
        jnp.repeat(owner_table, cluster, axis=1)
        .reshape(head_count, block_count, block_width)
        .transpose(1, 0, 2)
    )

    def find_target(total, block_item):
        order_block, owner_block = block_item
        local = order_block - own_index * row_count
        hits = local[:, :, None] == local_index[None, None, :]
        return (total + jnp.sum(jnp.where(hits, owner_block[:, :, None], 0), axis=1), None)

    target, unused = lax.scan(
        find_target, jnp.zeros((head_count, row_count), jnp.int32), (order_blocks, owner_blocks)
    )
    send_matrix = rank_matrix(target * row_count + local_index[None, :])
    mine = (owner_table == own_index).astype(jnp.int32)
    before = jnp.cumsum(mine, axis=1) - mine
    slot_hot = (mine[:, None, :] == 1) & (
        before[:, None, :] == jnp.arange(per_owner, dtype=jnp.int32)[None, :, None]
    )
    order_grid = order_table.reshape(head_count, cluster_count, cluster)
    owned_tokens = jnp.sum(
        jnp.where(slot_hot[:, :, :, None], order_grid[:, None, :, :], 0), axis=2
    ).reshape(head_count, row_count)
    arrive_matrix = rank_matrix(owned_tokens)
    w_three = jnp.concatenate([query_weight, key_weight, value_weight], axis=1)
    bias_three = jnp.concatenate(
        [
            query_bias.astype(jnp.float32),
            jnp.zeros((model_width,), jnp.float32),
            value_bias.astype(jnp.float32),
        ]
    )
    projected = (
        jnp.dot(flat_tokens, w_three, preferred_element_type=jnp.float32) + bias_three
    ).astype(jnp.bfloat16)
    token_rows = (
        projected.reshape(row_count, 3, head_count, head_dim)
        .transpose(2, 0, 1, 3)
        .reshape(head_count, row_count, 3 * head_dim)
    )
    segment_rows = jnp.broadcast_to(
        segments[0].astype(jnp.bfloat16)[None, :, None], (head_count, row_count, 1)
    )
    send_values = scatter_rows(token_rows, send_matrix, seq_count)
    send_segments = scatter_rows(segment_rows, send_matrix, seq_count)
    arrived, arrived_segments = (
        lax.all_to_all(send_values, "seq", split_axis=0, concat_axis=0, tiled=True),
        lax.all_to_all(send_segments, "seq", split_axis=0, concat_axis=0, tiled=True),
    )
    cluster_rows = collect_rows(arrived, arrive_matrix, 3 * head_dim).reshape(
        head_count * per_owner, cluster, 3, head_dim
    )
    cluster_segments = collect_rows(arrived_segments, arrive_matrix, 1).reshape(
        head_count * per_owner, cluster
    )
    queries = cluster_rows[:, :, 0]
    keys_in = cluster_rows[:, :, 1]
    values = cluster_rows[:, :, 2]
    attended, log_total, entropy, occupied = cluster_forward(
        queries, keys_in, values, cluster_segments, score_scale
    )
    per_head = jnp.stack(
        [
            jnp.sum(entropy.reshape(head_count, -1), axis=1),
            jnp.sum(occupied.reshape(head_count, -1), axis=1) / cluster,
        ]
    ) / (groups * row_count)
    column = (jnp.arange(seq_count, dtype=jnp.int32) == own_index).astype(jnp.float32)
    cluster_stats = lax.psum(per_head[:, :, None] * column, ("seq", "rep"))
    leaving = scatter_rows(
        attended.reshape(head_count, row_count, head_dim), arrive_matrix, seq_count
    )
    returned = lax.all_to_all(leaving, "seq", split_axis=0, concat_axis=0, tiled=True)
    attended_rows = (
        collect_rows(returned, send_matrix, head_dim)
        .transpose(1, 0, 2)
        .reshape(row_count, model_width)
    )
    branch = jnp.dot(
        attended_rows, out_weight, preferred_element_type=jnp.float32
    ) + out_bias.astype(jnp.float32)
    first_out, normed_one, root_one = norm_forward(
        flat_tokens.astype(jnp.float32) + branch, first_gain, first_shift
    )
    first_low = first_out.astype(jnp.bfloat16)
    inner_sum = jnp.dot(
        first_low, inner_weight, preferred_element_type=jnp.float32
    ) + inner_bias.astype(jnp.float32)
    activated, gelu_pull = jax.vjp(exact_gelu, inner_sum)
    activated_low = activated.astype(jnp.bfloat16)
    second = jnp.dot(
        activated_low, outer_weight, preferred_element_type=jnp.float32
    ) + outer_bias.astype(jnp.float32)
    result, normed_two, root_two = norm_forward(first_out + second, second_gain, second_shift)
    output = result.astype(jnp.bfloat16)[None]
    upstream = cotangent[0].astype(jnp.float32)
    gradient_second_gain = jnp.sum(upstream * normed_two, axis=0)
    gradient_second_shift = jnp.sum(upstream, axis=0)
    delta_two = norm_backward(upstream, normed_two, root_two, second_gain)
    delta_second = delta_two.astype(jnp.bfloat16)
    gradient_outer_bias = jnp.sum(delta_second.astype(jnp.float32), axis=0)
    gradient_outer_weight = jnp.einsum(
        "tf,td->fd", activated_low, delta_second, preferred_element_type=jnp.float32
    )
    delta_activated = jnp.einsum(
        "td,fd->tf", delta_second, outer_weight, preferred_element_type=jnp.float32
    )
    delta_inner = gelu_pull(delta_activated)[0].astype(jnp.bfloat16)
    gradient_inner_bias = jnp.sum(delta_inner.astype(jnp.float32), axis=0)
    gradient_inner_weight = jnp.einsum(
        "td,tf->df", first_low, delta_inner, preferred_element_type=jnp.float32
    )
    delta_first = delta_two + jnp.einsum(
        "tf,df->td", delta_inner, inner_weight, preferred_element_type=jnp.float32
    )
    gradient_first_gain = jnp.sum(delta_first * normed_one, axis=0)
    gradient_first_shift = jnp.sum(delta_first, axis=0)
    delta_one = norm_backward(delta_first, normed_one, root_one, first_gain)
    delta_branch = delta_one.astype(jnp.bfloat16)
    gradient_out_bias = jnp.sum(delta_branch.astype(jnp.float32), axis=0)
    gradient_out_weight = jnp.einsum(
        "td,te->de", attended_rows, delta_branch, preferred_element_type=jnp.float32
    )
    delta_attended = jnp.einsum(
        "te,de->td", delta_branch, out_weight, preferred_element_type=jnp.float32
    ).astype(jnp.bfloat16)
    delta_rows = delta_attended.reshape(row_count, head_count, head_dim).transpose(1, 0, 2)
    send_grads = scatter_rows(delta_rows, send_matrix, seq_count)
    grad_arrived = lax.all_to_all(send_grads, "seq", split_axis=0, concat_axis=0, tiled=True)
    kept_queries, kept_keys, kept_values, kept_segments = (
        queries,
        keys_in,
        values,
        cluster_segments,
    )
    grad_cluster = collect_rows(grad_arrived, arrive_matrix, head_dim).reshape(
        head_count * per_owner, cluster, head_dim
    )
    three_grads = cluster_backward(
        kept_queries, kept_keys, kept_values, kept_segments, log_total, grad_cluster, score_scale
    )
    leaving_grads = scatter_rows(
        three_grads.reshape(head_count, row_count, 3 * head_dim), arrive_matrix, seq_count
    )
    returned_grads = lax.all_to_all(leaving_grads, "seq", split_axis=0, concat_axis=0, tiled=True)
    delta_three = (
        collect_rows(returned_grads, send_matrix, 3 * head_dim)
        .reshape(head_count, row_count, 3, head_dim)
        .transpose(1, 2, 0, 3)
        .reshape(row_count, 3 * model_width)
    )
    bias_grads = jnp.sum(delta_three.astype(jnp.float32), axis=0)
    weight_grads = jnp.einsum(
        "td,te->de", flat_tokens, delta_three, preferred_element_type=jnp.float32
    )
    gradient_tokens = (
        delta_one
        + jnp.einsum("te,de->td", delta_three, w_three, preferred_element_type=jnp.float32)
    ).astype(jnp.bfloat16)[None]
    gradient_query_weight = weight_grads[:, :model_width]
    gradient_key_weight = weight_grads[:, model_width : 2 * model_width]
    gradient_value_weight = weight_grads[:, 2 * model_width :]
    gradient_query_bias = bias_grads[:model_width]
    gradient_value_bias = bias_grads[2 * model_width :]
    pieces = (
        lax.psum_scatter(gradient_query_weight, "seq", scatter_dimension=0, tiled=True),
        lax.psum_scatter(gradient_query_bias, "seq", scatter_dimension=0, tiled=True),
        lax.psum_scatter(gradient_key_weight, "seq", scatter_dimension=0, tiled=True),
        lax.psum_scatter(gradient_value_weight, "seq", scatter_dimension=0, tiled=True),
        lax.psum_scatter(gradient_value_bias, "seq", scatter_dimension=0, tiled=True),
        lax.psum_scatter(gradient_out_weight, "seq", scatter_dimension=0, tiled=True),
        lax.psum_scatter(gradient_out_bias, "seq", scatter_dimension=0, tiled=True),
        lax.psum_scatter(gradient_first_gain, "seq", scatter_dimension=0, tiled=True),
        lax.psum_scatter(gradient_first_shift, "seq", scatter_dimension=0, tiled=True),
        lax.psum_scatter(gradient_inner_weight, "seq", scatter_dimension=0, tiled=True),
        lax.psum_scatter(gradient_inner_bias, "seq", scatter_dimension=0, tiled=True),
        lax.psum_scatter(gradient_outer_weight, "seq", scatter_dimension=0, tiled=True),
        lax.psum_scatter(gradient_outer_bias, "seq", scatter_dimension=0, tiled=True),
        lax.psum_scatter(gradient_second_gain, "seq", scatter_dimension=0, tiled=True),
        lax.psum_scatter(gradient_second_shift, "seq", scatter_dimension=0, tiled=True),
    )
    summed = (
        lax.psum(pieces[0].astype(jnp.bfloat16), "rep").astype(jnp.float32),
        lax.psum(pieces[1].astype(jnp.bfloat16), "rep").astype(jnp.float32),
        lax.psum(pieces[2].astype(jnp.bfloat16), "rep").astype(jnp.float32),
        lax.psum(pieces[3].astype(jnp.bfloat16), "rep").astype(jnp.float32),
        lax.psum(pieces[4].astype(jnp.bfloat16), "rep").astype(jnp.float32),
        lax.psum(pieces[5].astype(jnp.bfloat16), "rep").astype(jnp.float32),
        lax.psum(pieces[6].astype(jnp.bfloat16), "rep").astype(jnp.float32),
        lax.psum(pieces[7].astype(jnp.bfloat16), "rep").astype(jnp.float32),
        lax.psum(pieces[8].astype(jnp.bfloat16), "rep").astype(jnp.float32),
        lax.psum(pieces[9].astype(jnp.bfloat16), "rep").astype(jnp.float32),
        lax.psum(pieces[10].astype(jnp.bfloat16), "rep").astype(jnp.float32),
        lax.psum(pieces[11].astype(jnp.bfloat16), "rep").astype(jnp.float32),
        lax.psum(pieces[12].astype(jnp.bfloat16), "rep").astype(jnp.float32),
        lax.psum(pieces[13].astype(jnp.bfloat16), "rep").astype(jnp.float32),
        lax.psum(pieces[14].astype(jnp.bfloat16), "rep").astype(jnp.float32),
    )
    return (output, gradient_tokens) + tuple(summed) + (cluster_stats,)


def square_body(
    tokens,
    segments,
    orders,
    owners,
    query_weight,
    query_bias,
    key_weight,
    value_weight,
    value_bias,
    out_weight,
    out_bias,
    first_gain,
    first_shift,
    inner_weight,
    inner_bias,
    outer_weight,
    outer_bias,
    second_gain,
    second_shift,
    cotangent,
):
    (
        wsel,
        order,
        stats,
        x_all,
        sorted_rows,
        prob,
        att,
        low_first,
        act,
        output,
        dsecond,
        dinner,
        delta,
        dbranch,
        vector_grads,
        datt,
    ) = forward_layer(
        tokens[0],
        cotangent[0],
        segments,
        orders.transpose(1, 0, 2),
        owners.transpose(1, 0, 2),
        (
            query_bias,
            value_bias,
            out_bias,
            first_gain,
            first_shift,
            outer_bias,
            second_gain,
            second_shift,
            inner_bias,
        ),
        (query_weight, key_weight, value_weight, out_weight, inner_weight, outer_weight),
    )
    output, grad, reduced, w_all, totals = backward_attention(
        datt,
        order,
        output,
        stats,
        vector_grads,
        att,
        dbranch,
        low_first,
        dsecond,
        act,
        dinner,
        sorted_rows,
        prob,
        wsel,
        x_all,
        delta,
        6,
    )
    return finish(reduced, w_all, output, grad, totals, orders.shape[1], inner_weight.shape[1])


def solution(mesh):
    square = mesh.shape["seq"] == 8 and mesh.shape["rep"] == 4
    placed = (
        P("rep", "seq", None),
        P("rep", "seq"),
        P("rep", None, None),
        P("rep", None, None),
        P(),
        P(),
        P(),
        P(),
        P(),
        P(),
        P(),
        P(),
        P(),
        P(),
        P(),
        P(),
        P(),
        P(),
        P(),
        P("rep", "seq", None),
    )
    return jax.shard_map(
        square_body if square else body,
        mesh=mesh,
        in_specs=placed,
        out_specs=(
            P("rep", "seq", None),
            P("rep", "seq", None),
            P("seq", None),
            P("seq"),
            P("seq", None),
            P("seq", None),
            P("seq"),
            P("seq", None),
            P("seq"),
            P("seq"),
            P("seq"),
            P("seq", None),
            P("seq"),
            P("seq", None),
            P("seq"),
            P("seq"),
            P("seq"),
            P(),
        ),
        check_vma=False,
    )
```
